32 devices in a mesh: blk: 4 (over z), ep: 8 (over y, x, core).
Axes of the slice: x: 2, y: 2, z: 4, core: 2. Of those that a mesh axis runs over, the one named last changes fastest.
Arguments:
- hidden_in: bfloat16 [16, 1024, 768], P('ep', 'blk'), may hold values from -6 to 6
- cotangent: bfloat16 [16, 1024, 768], P('ep', 'blk'), may hold values from -6 to 6
- query_weight: bfloat16 [768, 768], replicated, may hold values from -0.3125 to 0.3125
- key_weight: bfloat16 [768, 768], replicated, may hold values from -0.3125 to 0.3125
- value_weight: bfloat16 [768, 768], replicated, may hold values from -0.21875 to 0.21875
- output_weight: bfloat16 [768, 768], replicated, may hold values from -0.875 to 0.875
- gain_one: float32 [768], replicated, may hold values from 0.5 to 1.5
- shift_one: float32 [768], replicated, may hold values from -1.75 to 1.75
- gain_two: float32 [768], replicated, may hold values from 0.5 to 1.5
- shift_two: float32 [768], replicated, may hold values from -1.75 to 1.75
- w_router: bfloat16 [768, 4], replicated, may hold values from -0.15625 to 0.15625
- w_inner: bfloat16 [8, 768, 1536], P('ep', None, 'blk'), may hold values from -0.21875 to 0.21875
- w_outer: bfloat16 [8, 1536, 768], P('ep', 'blk'), may hold values from -0.3125 to 0.3125
- expert_ids: int32 [8, 4, 2, 256, 1], P('ep', 'blk'), may hold values from 0 to 3; in each aligned block of 512 rows (0 to 511, 512 to 1023, ..., all dimensions but the last counted through in order) at most 256 rows name the same one
- seq_lengths: int32 [16], P('ep'), may hold values from 1 to 1024, as said below
Outputs:
- output: bfloat16 [16, 1024, 768], P('ep', 'blk')
- grad_hidden: float32 [16, 1024, 768], P('ep', 'blk')
- grad_query: float32 [768, 768], replicated
- grad_key: float32 [768, 768], replicated
- grad_value: float32 [768, 768], replicated
- grad_out: float32 [768, 768], replicated
- grad_gain_one: float32 [768], replicated
- grad_shift_one: float32 [768], replicated
- grad_gain_two: float32 [768], replicated
- grad_shift_two: float32 [768], replicated
- grad_router: float32 [768, 4], replicated
- grad_inner: float32 [8, 768, 1536], P('ep', None, 'blk')
- grad_outer: float32 [8, 1536, 768], P('ep', 'blk')
- balance: float32 [], replicated
The draws below stay inside these ranges and needn't reach their ends.
Inputs may be any that keep to these rules, and one draw needn't show every extreme that they name: `expert_ids`: each aligned block of 512 rows (the tokens of one device, in the array's order) names one expert at most 256 times. `seq_lengths`: of the 2 sequences held by one index of ep, one has all 1024 tokens.
All inputs are finite; a program needn't handle non-finite values.
Results may differ from the reference program's by a relative error of at most 0.018.
Values may be sent and summed in bfloat16 or wider, within the bound.
A program may use at most 256 MiB of HBM per device.

```python
import math
import jax
import jax.numpy as jnp
import numpy as np
from jax import lax

D = 768
HEADS = 12
HEAD = 64
FF = 3072
LEN = 1024
SEQ_DEV = 2
EXPERTS = 4
SPAN = 256
TOK_DEV = 512
SEQS = 16
CAP = 256
N_BLK = 4
N_EP = 8


def draw_seq_lengths(key, part):
    key = jax.random.fold_in(key, 7)
    length_key, chosen_key = jax.random.split(key)
    groups = SEQS // SEQ_DEV
    drawn = jax.random.randint(length_key, (groups, SEQ_DEV), 1, LEN + 1)
    chosen = jax.random.randint(chosen_key, (groups, 1), 0, SEQ_DEV)
    full_rows = jnp.arange(SEQ_DEV)[None, :] == chosen
    return jnp.where(full_rows, LEN, drawn).reshape(SEQS).astype(jnp.int32)


def block_levels(stream_key, shape, shards, low, largest):
    def one(position, blocks):
        heights = jax.random.uniform(jax.random.fold_in(jax.random.fold_in(stream_key, 6), position), (blocks,), jnp.float32, low / len(shards), largest / len(shards))
        return jnp.repeat(jnp.exp(heights), shape[position] // blocks).reshape((-1,) + (1,) * (len(shape) - position - 1))

    level = one(*shards[0])
    for cut in shards[1:]:
        level = level * one(*cut)
    return level


def deal_out(key, own, number, rows, count, top, limit, skew):
    order = jax.random.permutation(key, count)
    heavy_load, ordinary = load_shares(count, rows * top, limit, skew, True), load_shares(count, rows * top, limit, skew, False)
    places = jnp.arange(count)

    def named(sizes, rotation):
        used = int((sizes > 0).sum())
        fixed = max(1, used // 4)
        shifted = fixed + (places - fixed + rotation * (used - fixed)) % max(1, count - fixed)
        return jnp.zeros((count,), jnp.int32).at[order[jnp.where(places < fixed, places, shifted)]].set(jnp.asarray(sizes, jnp.int32))

    sizes = jnp.where(number % 4 == 0, named(heavy_load, number // 4), named(ordinary, number - number // 4 - 1))
    mixed = jax.random.permutation(jax.random.fold_in(own, 3), count)
    source_of, sink = mixed[0:count // 2 * 2:2], mixed[1:count // 2 * 2:2]
    margin = jnp.minimum(sizes[source_of] - 1, limit - sizes[sink]) // 2
    margin = jnp.where((source_of == order[0]) | (sink == order[0]) | (sizes[sink] == 0), 0, jnp.maximum(margin, 0))
    shifted = jax.random.randint(jax.random.fold_in(own, 4), (count // 2,), 0, 1 << 20) % (margin + 1)
    sizes = sizes.at[source_of].add(-shifted).at[sink].add(shifted)
    members = jnp.searchsorted(jnp.cumsum(sizes), jnp.arange(rows * top), side="right").astype(jnp.int32)
    grid = members.reshape(top, rows).T
    grid = grid[jax.random.permutation(jax.random.fold_in(own, 1), rows)]
    rotation = jax.random.randint(jax.random.fold_in(own, 2), (rows, 1), 0, top)
    return jnp.take_along_axis(grid, (jnp.arange(top)[None, :] + rotation) % top, axis=1)


def load_shares(number_of, total, bound, skew, full):
    weights = [(1 << 20) // math.isqrt(grade ** skew) + 1 for grade in range(1, number_of + 1)]
    largest = bound if full else min(bound, max(-(-total // number_of), total * weights[0] // sum(weights)))
    least = 1 if total - largest >= number_of - 1 else 0
    holding, rest = [largest] + [least] * (number_of - 1), total - largest - least * (number_of - 1)
    while rest > 0:
        free = [i for i in range(1, number_of) if holding[i] < largest] or [i for i in range(1, number_of) if holding[i] < bound]
        pool, budget = sum([weights[i] for i in free]), rest
        for i in free:
            addition = min(bound - holding[i], max(1, budget * weights[i] // pool), rest)
            holding[i] = holding[i] + addition
            rest = rest - addition
    return np.array(holding)


def normal_values(stream_key, dims, spread, limit, pieces=(), kind=jnp.bfloat16):
    factor_of = block_levels(stream_key, dims, pieces, -0.22, 0.18) if pieces else 1.0
    values = jax.random.normal(stream_key, dims, jnp.float32) * spread * factor_of
    return jnp.minimum(jnp.maximum(values, -limit), limit).astype(kind)


def setup_inputs(seed: int = 0) -> dict:
    streams_of = jax.random.split(jax.random.key(seed), 16)
    hidden_in = normal_values(streams_of[0], (SEQS, LEN, D), 1.0, 6.0, ((0, 8), (1, 4)))
    cotangent = normal_values(streams_of[1], (SEQS, LEN, D), 1.0, 6.0, ((0, 8), (1, 4)))
    query_weight = normal_values(streams_of[2], (D, D), (D // 2) ** -0.5, 0.3125)
    key_weight = normal_values(streams_of[3], (D, D), (D // 2) ** -0.5, 0.3125)
    value_weight = normal_values(streams_of[4], (D, D), D ** -0.5, 0.21875)
    output_weight = normal_values(streams_of[5], (D, D), (D // 16) ** -0.5, 0.875)
    gain_one = jnp.clip(1.0 + 0.1 * jax.random.normal(streams_of[6], (D,), jnp.float32), 0.5, 1.5)
    shift_one = normal_values(streams_of[7], (D,), 0.3, 1.75, (), jnp.float32)
    gain_two = jnp.clip(1.0 + 0.1 * jax.random.normal(streams_of[8], (D,), jnp.float32), 0.5, 1.5)
    shift_two = normal_values(streams_of[9], (D,), 0.3, 1.75, (), jnp.float32)
    w_router = normal_values(streams_of[10], (D, EXPERTS), (2 * D) ** -0.5, 0.15625)
    w_inner = normal_values(streams_of[11], (N_EP, D, FF // 2), D ** -0.5, 0.21875, ((0, 8), (2, 4)))
    w_outer = normal_values(streams_of[12], (N_EP, FF // 2, D), (FF // 8) ** -0.5, 0.3125, ((0, 8), (1, 4)))
    expert_ids_keys = jax.random.split(jax.random.fold_in(streams_of[13], 1), N_EP * N_BLK * SEQ_DEV * SPAN // TOK_DEV)
    expert_ids_turns = jax.random.permutation(jax.random.fold_in(streams_of[13], 3), N_EP * N_BLK * SEQ_DEV * SPAN // TOK_DEV)
    expert_ids = jax.vmap(lambda own, number: deal_out(jax.random.fold_in(streams_of[13], 2), own, number, TOK_DEV, EXPERTS, 1, CAP, 2))(expert_ids_keys, expert_ids_turns).reshape((N_EP, N_BLK, SEQ_DEV, SPAN, 1))
    seq_lengths = draw_seq_lengths(jax.random.fold_in(streams_of[15], 71), 0)
    return dict(hidden_in=hidden_in, cotangent=cotangent, query_weight=query_weight, key_weight=key_weight, value_weight=value_weight, output_weight=output_weight, gain_one=gain_one, shift_one=shift_one, gain_two=gain_two, shift_two=shift_two, w_router=w_router, w_inner=w_inner, w_outer=w_outer, expert_ids=expert_ids, seq_lengths=seq_lengths)


@jax.custom_vjp
def lower_precision(v):
    return lax.optimization_barrier(v.astype(jnp.bfloat16)).astype(jnp.float32)

@jax.custom_vjp
def lower_precision_backward(v):
    return v

def low_keep(v):
    return (lower_precision(v), None)

def low_pass(kept, grad):
    return (grad,)

def back_keep(v):
    return (v, None)

def back_low(kept, grad):
    return (lower_precision(grad),)
lower_precision.defvjp(low_keep, low_pass)
lower_precision_backward.defvjp(back_keep, back_low)
epsilon = 1e-05
balance_weight = 6.0
highest_precision = lax.Precision.HIGHEST

def layer_norm(inputs, norm_gain, norm_shift):
    centered = inputs - lax.optimization_barrier(jnp.mean(inputs, axis=-1, keepdims=True))
    variance = lax.optimization_barrier(jnp.mean(centered * centered, axis=-1, keepdims=True))
    return centered * lax.rsqrt(variance + epsilon) * norm_gain + norm_shift

def attend_one(operands):
    query_seq, key_seq, value_seq, length = operands
    query_heads = query_seq.reshape(LEN, HEADS, HEAD)
    key_heads = key_seq.reshape(LEN, HEADS, HEAD)
    value_heads = value_seq.reshape(LEN, HEADS, HEAD)
    scores = jnp.einsum('qhe,khe->hqk', query_heads, key_heads, precision=highest_precision) * HEAD ** (-0.5)
    scores = lower_precision_backward(scores)
    places = jnp.arange(LEN, dtype=jnp.int32)
    allowed = (places[None, :] <= places[:, None]) & (places[None, :] < length)
    masked = jnp.where(allowed[None], scores, -1e+30)
    log_total = jax.nn.logsumexp(masked, axis=-1, keepdims=True)
    prob_rows = jnp.where(allowed[None], jnp.exp(masked - log_total), 0.0)
    weights = lower_precision(prob_rows)
    attended_rows = jnp.einsum('hqk,khe->qhe', weights, value_heads, precision=highest_precision)
    return attended_rows.reshape(LEN, HEADS * HEAD)

def expert_one(operands):
    row_block, inner_weight, outer_weight = operands
    row_block = lower_precision_backward(row_block)
    pre_act = lower_precision_backward(jnp.dot(row_block, inner_weight, precision=highest_precision, preferred_element_type=jnp.float32))
    activation = lower_precision(jax.nn.gelu(pre_act, approximate=False))
    produced = jnp.dot(activation, outer_weight, precision=highest_precision, preferred_element_type=jnp.float32)
    return lower_precision_backward(lower_precision(produced))

def forward(hidden_in, query_weight, key_weight, value_weight, output_weight, gain_one, shift_one, gain_two, shift_two, w_router, w_inner, w_outer, token_experts, seq_lengths):
    normalized_input = lower_precision(layer_norm(hidden_in, gain_one, shift_one))
    query_rows = lower_precision_backward(lower_precision(jnp.einsum('pto,ox->ptx', normalized_input, query_weight, precision=highest_precision)))
    projected_keys = lower_precision_backward(lower_precision(jnp.einsum('pto,ox->ptx', normalized_input, key_weight, precision=highest_precision)))
    projected_values = lower_precision_backward(lower_precision(jnp.einsum('pto,ox->ptx', normalized_input, value_weight, precision=highest_precision)))
    attended_rows = lax.map(jax.checkpoint(attend_one), (query_rows, projected_keys, projected_values, seq_lengths))
    attended_rows = lower_precision_backward(lower_precision(attended_rows))
    branch_output = lower_precision_backward(jnp.einsum('pto,ox->ptx', attended_rows, output_weight, precision=highest_precision))
    middle = hidden_in + branch_output
    normed_two = lower_precision(layer_norm(middle, gain_two, shift_two))
    flat_rows = normed_two.reshape(SEQS * LEN, D)
    logits = lower_precision_backward(jnp.dot(flat_rows, w_router, precision=highest_precision, preferred_element_type=jnp.float32))
    flat_ids = token_experts.reshape(SEQS * LEN)
    onehot = flat_ids[:, None] == jnp.arange(EXPERTS, dtype=jnp.int32)[None, :]
    onehot_f = onehot.astype(jnp.float32)
    gate_values = jax.nn.sigmoid(lax.optimization_barrier(jnp.sum(logits * onehot_f, axis=1)))
    places = jnp.arange(LEN, dtype=jnp.int32)
    valid_rows = (places[None, :] < seq_lengths[:, None]).astype(jnp.float32).reshape(SEQS * LEN)
    counts = lax.optimization_barrier(jnp.sum(onehot_f * valid_rows[:, None], axis=0))
    mean_load = jnp.sum(counts) / EXPERTS
    load_ratio = (counts - mean_load) / mean_load
    onehot_int = onehot.astype(jnp.int32)
    slot_ranks = lax.optimization_barrier(jnp.sum(jnp.cumsum(onehot_int, axis=0) * onehot_int, axis=1)) - 1
    room_rows = N_BLK * N_EP * CAP
    slot_rows = (flat_ids * room_rows + slot_ranks).astype(jnp.int32)
    buffer = jnp.zeros((EXPERTS * room_rows, D), jnp.float32).at[slot_rows].set(flat_rows)
    inner_full = w_inner.reshape(EXPERTS, 2, D, FF // 2).transpose(0, 2, 1, 3).reshape(EXPERTS, D, FF)
    outer_full = w_outer.reshape(EXPERTS, FF, D)
    produced = lax.map(jax.checkpoint(expert_one), (buffer.reshape(EXPERTS, room_rows, D), inner_full, outer_full))
    expert_out = produced.reshape(EXPERTS * room_rows, D)[slot_rows]
    scale_rows = valid_rows * gate_values
    output = middle + (scale_rows[:, None] * expert_out).reshape(SEQS, LEN, D)
    balance_sum = jnp.sum(scale_rows * lax.optimization_barrier(jnp.sum(onehot_f * load_ratio[None, :], axis=1)))
    return (output, balance_sum)

def reference(hidden_in, cotangent, query_weight, key_weight, value_weight, output_weight, gain_one, shift_one, gain_two, shift_two, w_router, w_inner, w_outer, expert_ids, seq_lengths):
    floats = [arg.astype(jnp.float32) for arg in (hidden_in, query_weight, key_weight, value_weight, output_weight, gain_one, shift_one, gain_two, shift_two, w_router, w_inner, w_outer)]
    token_experts = expert_ids.reshape(N_EP, N_BLK, SEQ_DEV, SPAN).transpose(0, 2, 1, 3).reshape(SEQS, LEN)

    def apply_block(*params):
        return forward(*params, token_experts, seq_lengths)
    (output, balance_sum), pullback = jax.vjp(apply_block, *floats)
    gradients = pullback((cotangent.astype(jnp.float32), jnp.asarray(balance_weight, jnp.float32)))
    valid_total = jnp.sum(seq_lengths).astype(jnp.float32)
    return (output.astype(jnp.bfloat16), gradients[0], gradients[1], gradients[2], gradients[3], gradients[4], gradients[5], gradients[6], gradients[7], gradients[8], gradients[9], gradients[10], gradients[11], balance_sum / valid_total)
```

```python
import functools

import jax
import jax.numpy as jnp
from jax import lax
from jax.experimental import pallas as pl
from jax.experimental.pallas import tpu as pltpu
from jax.sharding import PartitionSpec as P

HEAD = 64
MESH = pl.DeviceIdType.MESH
ANY = pl.BlockSpec(memory_space=pl.ANY)
VMEM = pl.BlockSpec(memory_space=pltpu.VMEM)
SMEM = pl.BlockSpec(memory_space=pltpu.SMEM)
DMA = pltpu.SemaphoreType.DMA
f32 = jnp.float32
bf16 = jnp.bfloat16

epsilon = 1e-05
balance_weight = 6.0
masked_fill = -1e30
VMEM_BYTES = 50 * 1024 * 1024


def dot(a, b):
    return lax.dot_general(a, b, (((1,), (0,)), ((), ())), preferred_element_type=f32)


def dot_nt(a, b):
    return lax.dot_general(a, b, (((1,), (1,)), ((), ())), preferred_element_type=f32)


def dot_tn(a, b):
    return lax.dot_general(a, b, (((0,), (0,)), ((), ())), preferred_element_type=f32)


def place():
    z = lax.axis_index("blk")
    e = lax.axis_index("ep")
    c = lax.rem(e, 2)
    return z, e, c, e - c


def remote(src, dst, send_sem, recv_sem, z, e):
    return pltpu.make_async_remote_copy(
        src, dst, send_sem, recv_sem, device_id=(z, e), device_id_type=MESH
    )


def greet(partners):
    barrier = pltpu.get_barrier_semaphore()
    for z, e in partners:
        pl.semaphore_signal(barrier, inc=1, device_id=(z, e), device_id_type=MESH)
    pl.semaphore_wait(barrier, len(partners))


def column_partners(blocks, z, c, base):
    found = [(z, base + 1 - c)]
    for step in range(1, blocks):
        for k in range(2):
            found.append((lax.rem(z + step, blocks), base + k))
    return found


def params(collective_id):
    return pltpu.CompilerParams(
        collective_id=collective_id, has_side_effects=True, vmem_limit_bytes=VMEM_BYTES
    )


def normed_exchange(normed, blocks):
    seqs, span, width = normed.shape
    half = span // 2

    def kernel(n_ref, x_ref, loc_sem, send_sem, recv_sem, fsend_sem, frecv_sem):
        z, e, c, base = place()
        seq_core = z // 2
        greet(column_partners(blocks, z, c, base))

        def outgoing(s, k):
            return remote(
                n_ref.at[s, k], x_ref.at[z, k], send_sem.at[s, k], recv_sem.at[z], 2 * c + s, base + k
            )

        def own(s, k):
            return pltpu.make_async_copy(n_ref.at[s, k], x_ref.at[z, k], loc_sem)

        for s in range(seqs):
            for k in range(2):
                to_self = (2 * c + s == z) & (c == k)

                @pl.when(to_self)
                def _():
                    own(s, k).start()

                @pl.when(jnp.logical_not(to_self))
                def _():
                    outgoing(s, k).start()

        def forward(zs):
            return remote(
                x_ref.at[zs, c], x_ref.at[zs, c], fsend_sem.at[zs], frecv_sem.at[zs], z, base + 1 - c
            )

        for step in range(blocks):
            zs = lax.rem(z + step, blocks)
            if step == 0:

                @pl.when(c == seq_core)
                def _():
                    pltpu.make_async_copy(n_ref.at[0, 0], x_ref.at[z, c], loc_sem).wait()

                @pl.when(c != seq_core)
                def _():
                    remote(n_ref.at[0, 0], x_ref.at[z, c], send_sem.at[0, 0], recv_sem.at[z], z, base).wait_recv()
            else:
                remote(n_ref.at[0, 0], x_ref.at[zs, c], send_sem.at[0, 0], recv_sem.at[zs], z, base).wait_recv()
            forward(zs).start()
        for step in range(blocks):
            zs = lax.rem(z + step, blocks)
            forward(zs).wait_send()
            remote(
                x_ref.at[zs, 1 - c], x_ref.at[zs, 1 - c], fsend_sem.at[zs], frecv_sem.at[zs], z, base + 1 - c
            ).wait_recv()
        for s in range(seqs):
            for k in range(2):

                @pl.when(jnp.logical_not((2 * c + s == z) & (c == k)))
                def _():
                    outgoing(s, k).wait_send()

    return pl.pallas_call(
        kernel,
        name="normed_exchange",
        out_shape=jax.ShapeDtypeStruct((blocks, 2, half, width), bf16),
        in_specs=[ANY],
        out_specs=ANY,
        scratch_shapes=[DMA, DMA((seqs, 2)), DMA((blocks,)), DMA((blocks,)), DMA((blocks,))],
        compiler_params=params(1),
    )(normed.reshape(seqs, 2, half, width)).reshape(blocks * span, width)


def attended_exchange(att, blocks):
    _, span, width = att.shape
    seqs = 2

    def kernel(a_ref, t_ref, loc_sem, send_sem, recv_sem):
        z, e, c, base = place()
        seq_core, seq = z // 2, lax.rem(z, 2)
        greet(column_partners(blocks, z, c, base))

        def outgoing(j):
            return remote(
                a_ref.at[j], t_ref.at[seq, c], send_sem.at[j], recv_sem.at[seq, c], j, base + seq_core
            )

        def own():
            return pltpu.make_async_copy(a_ref.at[z], t_ref.at[seq, c], loc_sem)

        for step in range(1, blocks):
            outgoing(lax.rem(z + step, blocks)).start()

        @pl.when(seq_core == c)
        def _():
            own().start()

        @pl.when(seq_core != c)
        def _():
            outgoing(z).start()

        for s in range(seqs):
            for k in range(2):
                from_self = (2 * c + s == z) & (c == k)

                @pl.when(jnp.logical_not(from_self))
                def _():
                    remote(a_ref.at[0], t_ref.at[s, k], send_sem.at[0], recv_sem.at[s, k], z, base).wait_recv()

        for step in range(1, blocks):
            outgoing(lax.rem(z + step, blocks)).wait_send()

        @pl.when(seq_core == c)
        def _():
            own().wait()

        @pl.when(seq_core != c)
        def _():
            outgoing(z).wait_send()

    return pl.pallas_call(
        kernel,
        name="attended_exchange",
        out_shape=jax.ShapeDtypeStruct((seqs, 2, span, width), bf16),
        in_specs=[ANY],
        out_specs=ANY,
        scratch_shapes=[DMA, DMA((blocks,)), DMA((seqs, 2))],
        compiler_params=params(2),
    )(att)


def d_attended_exchange(rows, blocks):
    seqs, _, span, width = rows.shape

    def kernel(t_ref, a_ref, loc_sem, send_sem, recv_sem):
        z, e, c, base = place()
        seq_core = z // 2
        greet(column_partners(blocks, z, c, base))

        def outgoing(s, k):
            return remote(
                t_ref.at[s, k], a_ref.at[z], send_sem.at[s, k], recv_sem.at[z], 2 * c + s, base + k
            )

        def own(s, k):
            return pltpu.make_async_copy(t_ref.at[s, k], a_ref.at[z], loc_sem)

        for s in range(seqs):
            for k in range(2):
                to_self = (2 * c + s == z) & (c == k)

                @pl.when(to_self)
                def _():
                    own(s, k).start()

                @pl.when(jnp.logical_not(to_self))
                def _():
                    outgoing(s, k).start()

        for step in range(blocks):
            zs = lax.rem(z + step, blocks)
            if step == 0:

                @pl.when(c == seq_core)
                def _():
                    own(0, 0).wait()

                @pl.when(c != seq_core)
                def _():
                    remote(t_ref.at[0, 0], a_ref.at[z], send_sem.at[0, 0], recv_sem.at[z], z, base).wait_recv()
            else:
                remote(t_ref.at[0, 0], a_ref.at[zs], send_sem.at[0, 0], recv_sem.at[zs], z, base).wait_recv()
        for s in range(seqs):
            for k in range(2):

                @pl.when(jnp.logical_not((2 * c + s == z) & (c == k)))
                def _():
                    outgoing(s, k).wait_send()

    return pl.pallas_call(
        kernel,
        name="d_attended_exchange",
        out_shape=jax.ShapeDtypeStruct((blocks, span, width), bf16),
        in_specs=[ANY],
        out_specs=ANY,
        scratch_shapes=[DMA, DMA((seqs, 2)), DMA((blocks,))],
        compiler_params=params(3),
    )(rows)


def d_normed_exchange(part, blocks):
    _, _, half, width = part.shape
    seqs = 2

    def kernel(p_ref, t_ref, sib_ref, sum_ref, loc_sem, ssend_sem, srecv_sem, send_sem, recv_sem):
        z, e, c, base = place()
        seq_core, seq = z // 2, lax.rem(z, 2)
        greet(column_partners(blocks, z, c, base))

        def to_sibling(j):
            return remote(
                p_ref.at[j, 1 - c], sib_ref.at[j], ssend_sem.at[j], srecv_sem.at[j], z, base + 1 - c
            )

        def outgoing(j):
            return remote(
                sum_ref.at[j], t_ref.at[seq, c], send_sem.at[j], recv_sem.at[seq, c], j, base + seq_core
            )

        def own():
            return pltpu.make_async_copy(sum_ref.at[z], t_ref.at[seq, c], loc_sem)

        order = [lax.rem(z + step, blocks) for step in (2, 3, 1, 0)] if blocks == 4 else [
            lax.rem(z + step + 1, blocks) for step in range(blocks)
        ]
        for j in order:
            to_sibling(j).start()
        for i, j in enumerate(order):
            to_sibling(j).wait_recv()
            sum_ref[j] = (p_ref[j, c].astype(f32) + sib_ref[j].astype(f32)).astype(bf16)
            if i < blocks - 1:
                outgoing(j).start()
            else:

                @pl.when(seq_core == c)
                def _():
                    own().start()

                @pl.when(seq_core != c)
                def _():
                    outgoing(j).start()

        for s in range(seqs):
            for k in range(2):
                from_self = (2 * c + s == z) & (c == k)

                @pl.when(jnp.logical_not(from_self))
                def _():
                    remote(sum_ref.at[0], t_ref.at[s, k], send_sem.at[0], recv_sem.at[s, k], z, base).wait_recv()

        for i, j in enumerate(order):
            to_sibling(j).wait_send()
            if i < blocks - 1:
                outgoing(j).wait_send()

        @pl.when(seq_core == c)
        def _():
            own().wait()

        @pl.when(seq_core != c)
        def _():
            outgoing(z).wait_send()

    return pl.pallas_call(
        kernel,
        name="d_normed_exchange",
        out_shape=jax.ShapeDtypeStruct((seqs, 2, half, width), bf16),
        in_specs=[VMEM],
        out_specs=VMEM,
        scratch_shapes=[
            pltpu.VMEM((blocks, half, width), bf16),
            pltpu.VMEM((blocks, half, width), bf16),
            DMA,
            DMA((blocks,)),
            DMA((blocks,)),
            DMA((blocks,)),
            DMA((seqs, 2)),
        ],
        compiler_params=params(4),
    )(part)


def plane_exchange(arrays, columns, collective_id, name):
    count = len(arrays)

    def kernel(*refs):
        sources, targets = refs[:count], refs[count : 2 * count]
        loc_sem, send_sem, recv_sem = refs[2 * count :]
        z, e, c, base = place()
        col = e // 2
        others = [lax.rem(col + step, columns) for step in range(1, columns)]
        greet([(z, 2 * t + c) for t in others])
        for i in range(count):
            for t in others:
                remote(
                    sources[i].at[t], targets[i].at[col], send_sem.at[i, t], recv_sem.at[i, col], z, 2 * t + c
                ).start()
            pltpu.make_async_copy(sources[i].at[col], targets[i].at[col], loc_sem.at[i]).start()
        for i in range(count):
            pltpu.make_async_copy(sources[i].at[col], targets[i].at[col], loc_sem.at[i]).wait()
            for t in others:
                remote(
                    sources[i].at[t], targets[i].at[t], send_sem.at[i, t], recv_sem.at[i, t], z, 2 * t + c
                ).wait()

    return pl.pallas_call(
        kernel,
        name=name,
        out_shape=[jax.ShapeDtypeStruct(a.shape, a.dtype) for a in arrays],
        in_specs=[ANY] * count,
        out_specs=[ANY] * count,
        scratch_shapes=[DMA((count,)), DMA((count, columns)), DMA((count, columns))],
        compiler_params=params(collective_id),
    )(*arrays)


def attention_forward(length, rows, weights, span):
    total, width = rows.shape
    half = weights.shape[1] // 3
    pairs = half // 128
    blocks = total // span

    def kernel(len_ref, x_ref, w_ref, qkv_ref, att_ref, attt_ref, lse_ref, vt_ref):
        seq_len = len_ref[0]
        for j in range(blocks):
            r = pl.ds(j * span, span)
            qkv_ref[r, :] = dot(x_ref[r, :], w_ref[...]).astype(bf16)
        lane = lax.broadcasted_iota(jnp.int32, (1, 128), 1)
        key_place = lax.broadcasted_iota(jnp.int32, (total, 1), 0)
        key_bias = jnp.where(key_place < seq_len, 0.0, masked_fill)
        later = lax.broadcasted_iota(jnp.int32, (span, span), 0) > lax.broadcasted_iota(
            jnp.int32, (span, span), 1
        )

        def pair_step(p, _):
            first = pl.multiple_of(p * 128, 128)
            k_all = qkv_ref[:, pl.ds(half + first, 128)]
            vt_ref[...] = jnp.transpose(qkv_ref[:, pl.ds(2 * half + first, 128)])
            k_heads = []
            for h in range(2):
                inside = (lane // HEAD) == h
                spare = lane == (1 - h) * HEAD
                k_heads.append(
                    jnp.where(
                        inside, k_all.astype(f32), jnp.where(spare, key_bias, 0.0)
                    ).astype(bf16)
                )
            for j in range(blocks):
                n = (j + 1) * span
                r = pl.ds(j * span, span)
                q = qkv_ref[r, pl.ds(first, 128)].astype(f32) * (HEAD**-0.5)
                out_t = []
                for h in range(2):
                    inside = (lane // HEAD) == h
                    spare = lane == (1 - h) * HEAD
                    q_h = jnp.where(inside, q, jnp.where(spare, 1.0, 0.0)).astype(bf16)
                    s = dot_nt(k_heads[h][:n], q_h)
                    last = jnp.where(later, masked_fill, s[n - span :])
                    s = last if j == 0 else jnp.concatenate([s[: n - span], last], axis=0)
                    top = jnp.max(s, axis=0, keepdims=True)
                    w = jnp.exp(s - top)
                    total_w = jnp.sum(w, axis=0, keepdims=True)
                    o_t = dot(vt_ref[h * HEAD : (h + 1) * HEAD, :n], w.astype(bf16))
                    out_t.append(o_t / total_w)
                    lse_ref[pl.ds(2 * p + h, 1), r] = top + jnp.log(total_w)
                o = jnp.concatenate(out_t, axis=0)
                attt_ref[pl.ds(first, 128), r] = o
                att_ref[j, :, pl.ds(first, 128)] = jnp.transpose(o).astype(bf16)
            return 0

        lax.fori_loop(0, pairs, pair_step, 0)

    return pl.pallas_call(
        kernel,
        name="attention_forward",
        out_shape=[
            jax.ShapeDtypeStruct((total, 3 * half), bf16),
            jax.ShapeDtypeStruct((blocks, span, half), bf16),
            jax.ShapeDtypeStruct((half, total), f32),
            jax.ShapeDtypeStruct((2 * pairs, total), f32),
        ],
        in_specs=[SMEM, VMEM, VMEM],
        out_specs=[VMEM] * 4,
        scratch_shapes=[pltpu.VMEM((128, total), bf16)],
        compiler_params=pltpu.CompilerParams(vmem_limit_bytes=VMEM_BYTES),
        cost_estimate=pl.CostEstimate(flops=20 * 10**9, bytes_accessed=10**7, transcendentals=0),
    )(length, rows, weights)


def attention_backward(length, rows, weights, qkv, att_t, lse, d_att, span):
    total, width = rows.shape
    half = weights.shape[1] // 3
    pairs = half // 128
    blocks = total // span
    scale = HEAD**-0.5

    def kernel(
        len_ref, x_ref, w_ref, qkv_ref, attt_ref, lse_ref, do_ref, gw_ref, dn_ref, dqkv_ref, kt_ref, dk_ref, dv_ref
    ):
        seq_len = len_ref[0]
        lane = lax.broadcasted_iota(jnp.int32, (1, 128), 1)
        key_place = lax.broadcasted_iota(jnp.int32, (total, 1), 0)
        key_bias = jnp.where(key_place < seq_len, 0.0, masked_fill)
        later = lax.broadcasted_iota(jnp.int32, (span, span), 0) > lax.broadcasted_iota(
            jnp.int32, (span, span), 1
        )

        def pair_step(p, _):
            first = pl.multiple_of(p * 128, 128)
            k_all = qkv_ref[:, pl.ds(half + first, 128)]
            kt_ref[...] = jnp.transpose(k_all)
            v_all = qkv_ref[:, pl.ds(2 * half + first, 128)]
            k_heads = []
            for h in range(2):
                inside = (lane // HEAD) == h
                spare = lane == (1 - h) * HEAD
                k_heads.append(
                    jnp.where(
                        inside, k_all.astype(f32), jnp.where(spare, key_bias, 0.0)
                    ).astype(bf16)
                )
            dk_ref[...] = jnp.zeros_like(dk_ref)
            dv_ref[...] = jnp.zeros_like(dv_ref)
            for j in range(blocks):
                n = (j + 1) * span
                r = pl.ds(j * span, span)
                q = qkv_ref[r, pl.ds(first, 128)].astype(f32) * scale
                d_o = do_ref[r, pl.ds(first, 128)].astype(f32)
                prod_t = jnp.transpose(d_o) * attt_ref[pl.ds(first, 128), r]
                dq_t = []
                for h in range(2):
                    inside = (lane // HEAD) == h
                    spare = lane == (1 - h) * HEAD
                    q_h = jnp.where(inside, q, jnp.where(spare, 1.0, 0.0)).astype(bf16)
                    q_only = jnp.where(inside, q, 0.0).astype(bf16)
                    do_h = jnp.where(inside, d_o, 0.0).astype(bf16)
                    delta = jnp.sum(prod_t[h * HEAD : (h + 1) * HEAD], axis=0, keepdims=True)
                    s = dot_nt(k_heads[h][:n], q_h)
                    last = jnp.where(later, masked_fill, s[n - span :])
                    s = last if j == 0 else jnp.concatenate([s[: n - span], last], axis=0)
                    w = jnp.exp(s - lse_ref[pl.ds(2 * p + h, 1), r])
                    d_w = dot_nt(v_all[:n], do_h)
                    d_s = (w * (d_w - delta)).astype(bf16)
                    dv_ref[:n] += dot(w.astype(bf16), do_h)
                    dk_ref[:n] += dot(d_s, q_only)
                    dq_t.append(dot(kt_ref[h * HEAD : (h + 1) * HEAD, :n], d_s))
                dq = jnp.transpose(jnp.concatenate(dq_t, axis=0)) * scale
                dqkv_ref[r, pl.ds(first, 128)] = dq.astype(bf16)
            dqkv_ref[:, pl.ds(half + first, 128)] = dk_ref[...].astype(bf16)
            dqkv_ref[:, pl.ds(2 * half + first, 128)] = dv_ref[...].astype(bf16)
            return 0

        lax.fori_loop(0, pairs, pair_step, 0)
        for j in range(blocks):
            r = pl.ds(j * span, span)
            dn_ref[j] = dot_nt(dqkv_ref[r, :], w_ref[...]).astype(bf16)
        for m in range(3):
            gw_ref[m] = dot_tn(x_ref[...], dqkv_ref[:, m * half : (m + 1) * half]).astype(bf16)

    return pl.pallas_call(
        kernel,
        name="attention_backward",
        out_shape=[
            jax.ShapeDtypeStruct((3, width, half), bf16),
            jax.ShapeDtypeStruct((blocks, span, width), bf16),
        ],
        in_specs=[SMEM] + [VMEM] * 6,
        out_specs=[VMEM] * 2,
        scratch_shapes=[
            pltpu.VMEM((total, 3 * half), bf16),
            pltpu.VMEM((128, total), bf16),
            pltpu.VMEM((total, 128), f32),
            pltpu.VMEM((total, 128), f32),
        ],
        compiler_params=pltpu.CompilerParams(vmem_limit_bytes=VMEM_BYTES),
        cost_estimate=pl.CostEstimate(flops=40 * 10**9, bytes_accessed=10**7, transcendentals=0),
    )(length, rows, weights, qkv, att_t, lse, d_att)


def experts(rows, d_out, inner_own, inner_sib, outer_own, outer_sib):
    total, width = rows.shape
    steps, _, part = inner_own.shape
    block = 256

    def kernel(
        x_ref, d_ref, io_ref, is_ref, oo_ref, os_ref,
        out_ref, dx_ref, gio_ref, gis_ref, goo_ref, gos_ref,
        oacc_ref, dacc_ref, act_ref, dpre_ref, wi_ref, wo_ref,
    ):
        g = pl.program_id(0)
        wi_ref[:, :part] = io_ref[0]
        wi_ref[:, part:] = is_ref[0]
        wo_ref[:part] = oo_ref[0]
        wo_ref[part:] = os_ref[0]

        @pl.when(g == 0)
        def _():
            oacc_ref[...] = jnp.zeros_like(oacc_ref)
            dacc_ref[...] = jnp.zeros_like(dacc_ref)

        def row_step(b, _):
            r = pl.ds(pl.multiple_of(b * block, block), block)
            pre = dot(x_ref[r, :], wi_ref[...])
            cdf = 0.5 * (1.0 + lax.erf(pre * (0.5**0.5)))
            act = (pre * cdf).astype(bf16)
            slope = cdf + pre * (jnp.exp(-0.5 * pre * pre) * ((2 * jnp.pi) ** -0.5))
            d_act = dot_nt(d_ref[r, :], wo_ref[...])
            d_pre = (d_act * slope).astype(bf16)
            act_ref[r, :] = act
            dpre_ref[r, :] = d_pre
            oacc_ref[r, :] += dot(act, wo_ref[...])
            dacc_ref[r, :] += dot_nt(d_pre, wi_ref[...])
            return 0

        lax.fori_loop(0, total // block, row_step, 0)
        g_inner = dot_tn(x_ref[...], dpre_ref[...]).astype(bf16)
        gio_ref[0] = g_inner[:, :part]
        gis_ref[0] = g_inner[:, part:]
        g_outer = dot_tn(act_ref[...], d_ref[...]).astype(bf16)
        goo_ref[0] = g_outer[:part]
        gos_ref[0] = g_outer[part:]

        @pl.when(g == steps - 1)
        def _():
            out_ref[...] = oacc_ref[...].astype(bf16)
            dx_ref[...] = dacc_ref[...].astype(bf16)

    whole = pl.BlockSpec((total, width), lambda g: (0, 0))
    inner = pl.BlockSpec((1, width, part), lambda g: (g, 0, 0))
    outer = pl.BlockSpec((1, part, width), lambda g: (g, 0, 0))
    return pl.pallas_call(
        kernel,
        name="experts",
        grid=(steps,),
        out_shape=[
            jax.ShapeDtypeStruct((total, width), bf16),
            jax.ShapeDtypeStruct((total, width), bf16),
            jax.ShapeDtypeStruct((steps, width, part), bf16),
            jax.ShapeDtypeStruct((steps, width, part), bf16),
            jax.ShapeDtypeStruct((steps, part, width), bf16),
            jax.ShapeDtypeStruct((steps, part, width), bf16),
        ],
        in_specs=[whole, whole, inner, inner, outer, outer],
        out_specs=[whole, whole, inner, inner, outer, outer],
        scratch_shapes=[
            pltpu.VMEM((total, width), f32),
            pltpu.VMEM((total, width), f32),
            pltpu.VMEM((total, 2 * part), bf16),
            pltpu.VMEM((total, 2 * part), bf16),
            pltpu.VMEM((width, 2 * part), bf16),
            pltpu.VMEM((2 * part, width), bf16),
        ],
        compiler_params=pltpu.CompilerParams(
            vmem_limit_bytes=VMEM_BYTES, dimension_semantics=("arbitrary",)
        ),
        cost_estimate=pl.CostEstimate(flops=40 * 10**9, bytes_accessed=3 * 10**7, transcendentals=0),
    )(rows, d_out, inner_own, inner_sib, outer_own, outer_sib)


def expert_grad_sum(gi_own, gi_sib, go_own, go_sib):
    blocks, width, part = gi_own.shape

    def kernel(
        gio_ref, gis_ref, goo_ref, gos_ref, fi_ref, fo_ref,
        oi, oo, si, so, zi, zo, loc_sem, ssend_sem, srecv_sem, send_sem, recv_sem,
    ):
        z, e, c, base = place()
        greet(column_partners(blocks, z, c, base))
        order = [lax.rem(z + step, blocks) for step in (2, 1, 3, 0)] if blocks == 4 else [
            lax.rem(z + step + 1, blocks) for step in range(blocks)
        ]

        def sibling(i, src, dst, j):
            return remote(src.at[j], dst.at[j], ssend_sem.at[i, j], srecv_sem.at[i, j], z, base + 1 - c)

        def local(i, src, dst, j):
            return pltpu.make_async_copy(src.at[j], dst.at[j], loc_sem.at[i, j])

        def over_z(i, src, dst, j):
            return remote(src.at[j], dst.at[z], send_sem.at[i, j], recv_sem.at[i, z], j, e)

        for j in order:
            sibling(0, gis_ref, si, j).start()
            sibling(1, gos_ref, so, j).start()
            local(0, gio_ref, oi, j).start()
            local(1, goo_ref, oo, j).start()
        for n, j in enumerate(order):
            for i, (own, sib, src, ssrc) in enumerate(((oi, si, gio_ref, gis_ref), (oo, so, goo_ref, gos_ref))):
                local(i, src, own, j).wait()
                sibling(i, ssrc, sib, j).wait_recv()
                own[j] = (own[j].astype(f32) + sib[j].astype(f32)).astype(bf16)
                if n < blocks - 1:
                    over_z(i, own, (zi, zo)[i], j).start()
        for i, (own, into, out) in enumerate(((oi, zi, fi_ref), (oo, zo, fo_ref))):
            for step in range(1, blocks):
                zs = lax.rem(z + step, blocks)
                remote(own.at[0], into.at[zs], send_sem.at[i, 0], recv_sem.at[i, zs], z, e).wait_recv()
            into[z] = own[z]
            acc = into[0].astype(f32)
            for j in range(1, blocks):
                acc = acc + into[j].astype(f32)
            out[...] = acc
        for n, j in enumerate(order):
            for i, (own, ssrc, sib) in enumerate(((oi, gis_ref, si), (oo, gos_ref, so))):
                sibling(i, ssrc, sib, j).wait_send()
                if n < blocks - 1:
                    over_z(i, own, (zi, zo)[i], j).wait_send()

    return pl.pallas_call(
        kernel,
        name="expert_grad_sum",
        out_shape=[
            jax.ShapeDtypeStruct((width, part), f32),
            jax.ShapeDtypeStruct((part, width), f32),
        ],
        in_specs=[ANY] * 4,
        out_specs=[VMEM] * 2,
        scratch_shapes=[
            pltpu.VMEM((blocks, width, part), bf16),
            pltpu.VMEM((blocks, part, width), bf16),
            pltpu.VMEM((blocks, width, part), bf16),
            pltpu.VMEM((blocks, part, width), bf16),
            pltpu.VMEM((blocks, width, part), bf16),
            pltpu.VMEM((blocks, part, width), bf16),
            DMA((2, blocks)),
            DMA((2, blocks)),
            DMA((2, blocks)),
            DMA((2, blocks)),
            DMA((2, blocks)),
        ],
        compiler_params=params(5),
    )(gi_own, gi_sib, go_own, go_sib)


def dense_grad_sum(qkv_part, out_part, small, blocks, columns):
    _, width, half = qkv_part.shape
    bits = max(1, columns.bit_length() - 1)
    assert columns == 1 << bits and bits >= 2
    piece = 4 * width // (8 * blocks)
    rest = bits - 2

    def kernel(
        q_ref, o_ref, s_ref, g_ref, t_ref,
        work, got1, got2, got3, gotr, osib, sgot, szgot, sem, rsem, zsem, zrsem, ssem, srsem,
    ):
        z, e, c, base = place()
        col = e // 2
        sib = base + 1 - c
        bit = [lax.rem(col // (1 << i), 2) for i in range(bits)]
        mate = [2 * (col + (1 - 2 * bit[i]) * (1 << i)) + c for i in range(bits)]
        greet(
            [(z, sib)]
            + [(z, mate[i]) for i in range(bits)]
            + [(lax.rem(z + step, blocks), e) for step in range(1, blocks)]
        )
        count = [0]

        def swap(src, dst, target_z, target_e):
            i = count[0]
            count[0] += 1
            copy = remote(src, dst, sem.at[i], rsem.at[i], target_z, target_e)
            copy.start()
            return copy

        def add(into, index, received):
            into[index] = (into[index].astype(f32) + received.astype(f32)).astype(bf16)

        scount = [0]

        def small_swap(target_z, target_e):
            i = scount[0]
            scount[0] += 1
            copy = remote(t_ref, sgot.at[i], ssem.at[i], srsem.at[i], target_z, target_e)
            copy.start()
            return copy, i

        def small_add(copy, i):
            copy.wait()
            t_ref[...] = t_ref[...] + sgot[i]

        t_ref[...] = s_ref[...]
        first = swap(o_ref.at[1 - c], osib, z, sib)
        tiny, n = small_swap(z, sib)
        rows = 2 * 2 * blocks * piece
        work[0] = jnp.concatenate([q_ref[0], q_ref[1]], axis=0).reshape(2, 2, blocks, piece, half)
        first.wait()
        o_sum = (o_ref[c].astype(f32) + osib[...].astype(f32)).astype(bf16)
        work[1] = jnp.concatenate([q_ref[2], o_sum], axis=0).reshape(2, 2, blocks, piece, half)
        small_add(tiny, n)
        one = [swap(work.at[i, 1 - bit[i]], got1.at[i], z, mate[i]) for i in range(2)]
        tiny, n = small_swap(z, mate[0])
        for i in range(2):
            one[i].wait()
            work[i, bit[i]] = (work[i, bit[i]].astype(f32) + got1[i].astype(f32)).astype(bf16)
        small_add(tiny, n)
        two = [swap(work.at[i, bit[i], 1 - bit[1 - i]], got2.at[i], z, mate[1 - i]) for i in range(2)]
        tiny, n = small_swap(z, mate[1])
        for i in range(2):
            two[i].wait()
            work[i, bit[i], bit[1 - i]] = (
                work[i, bit[i], bit[1 - i]].astype(f32) + got2[i].astype(f32)
            ).astype(bf16)
        small_add(tiny, n)
        sends = []
        for step in range(1, blocks):
            zt = lax.rem(z + step, blocks)
            for i in range(2):
                copy = remote(
                    work.at[i, bit[i], bit[1 - i], zt], got3.at[i, z], zsem.at[i, zt], zrsem.at[i, z], zt, e
                )
                copy.start()
                sends.append(copy)
            copy = remote(t_ref, szgot.at[z], zsem.at[2, zt], zrsem.at[4, z], zt, e)
            copy.start()
            sends.append(copy)
        for step in range(1, blocks):
            zs = lax.rem(z + step, blocks)
            for i in range(2):
                remote(got3.at[i, 0], got3.at[i, zs], zsem.at[i, zs], zrsem.at[i, zs], z, e).wait_recv()
            remote(t_ref, szgot.at[zs], zsem.at[2, zs], zrsem.at[4, zs], z, e).wait_recv()
        for copy in sends:
            copy.wait_send()
        szgot[z] = t_ref[...]
        tot = szgot[0]
        for j in range(1, blocks):
            tot = tot + szgot[j]
        t_ref[...] = tot
        for i in range(2):
            got3[i, z] = work[i, bit[i], bit[1 - i], z]
            tot = got3[i, 0].astype(f32)
            for j in range(1, blocks):
                tot = tot + got3[i, j].astype(f32)
            g_ref[c, i, bit[i], bit[1 - i], z] = tot.astype(bf16)
        for b in range(rest):
            got = [
                swap(g_ref.at[c, i, bit[i], bit[1 - i], z], gotr.at[b, i], z, mate[2 + b]) for i in range(2)
            ]
            tiny, n = small_swap(z, mate[2 + b])
            for i in range(2):
                got[i].wait()
                g_ref[c, i, bit[i], bit[1 - i], z] = (
                    g_ref[c, i, bit[i], bit[1 - i], z].astype(f32) + gotr[b, i].astype(f32)
                ).astype(bf16)
            small_add(tiny, n)
        sends = []
        for step in range(1, blocks):
            zt = lax.rem(z + step, blocks)
            for i in range(2):
                at = g_ref.at[c, i, bit[i], bit[1 - i], z]
                copy = remote(at, at, zsem.at[i, zt], zrsem.at[2 + i, z], zt, e)
                copy.start()
                sends.append(copy)
        for step in range(1, blocks):
            zs = lax.rem(z + step, blocks)
            for i in range(2):
                at = g_ref.at[c, i, bit[i], bit[1 - i], zs]
                remote(at, at, zsem.at[i, zs], zrsem.at[2 + i, zs], z, e).wait_recv()
        for copy in sends:
            copy.wait_send()
        two = []
        for i in range(2):
            at = g_ref.at[c, i, bit[i], bit[1 - i]]
            two.append(swap(at, at, z, mate[1 - i]))
        for copy in two:
            copy.wait()
        one = []
        for i in range(2):
            at = g_ref.at[c, i, bit[i]]
            one.append(swap(at, at, z, mate[i]))
        for copy in one:
            copy.wait()
        swap(g_ref.at[c], g_ref.at[c], z, sib).wait()

    lanes = small.shape
    stages = 2 + 2 + 2 + 2 * rest + 2 + 2 + 2
    work_shape = (2, 2, 2, blocks, piece, half)
    grads, sums = pl.pallas_call(
        kernel,
        name="dense_grad_sum",
        out_shape=[
            jax.ShapeDtypeStruct((2,) + work_shape, bf16),
            jax.ShapeDtypeStruct(lanes, f32),
        ],
        in_specs=[VMEM] * 3,
        out_specs=[VMEM] * 2,
        scratch_shapes=[
            pltpu.VMEM(work_shape, bf16),
            pltpu.VMEM((2, 2, blocks, piece, half), bf16),
            pltpu.VMEM((2, blocks, piece, half), bf16),
            pltpu.VMEM((2, blocks, piece, half), bf16),
            pltpu.VMEM((max(1, rest), 2, piece, half), bf16),
            pltpu.VMEM((width, half), bf16),
            pltpu.VMEM((1 + bits,) + lanes, f32),
            pltpu.VMEM((blocks,) + lanes, f32),
            DMA((stages,)),
            DMA((stages,)),
            DMA((3, blocks)),
            DMA((5, blocks)),
            DMA((1 + bits,)),
            DMA((1 + bits,)),
        ],
        compiler_params=params(6),
    )(qkv_part, out_part, small)
    return grads.reshape(2, 4, width, half), sums


def layer_norm(inputs, norm_gain, norm_shift):
    centered = inputs - jnp.mean(inputs, axis=-1, keepdims=True)
    variance = jnp.mean(centered * centered, axis=-1, keepdims=True)
    return centered * lax.rsqrt(variance + epsilon) * norm_gain + norm_shift


def on_device(
    hidden_in,
    cotangent,
    query_weight,
    key_weight,
    value_weight,
    output_weight,
    gain_one,
    shift_one,
    gain_two,
    shift_two,
    w_router,
    w_inner,
    w_outer,
    expert_ids,
    seq_lengths,
):
    seqs, span, width = hidden_in.shape
    tokens = seqs * span
    blocks = lax.axis_size("blk")
    columns = lax.axis_size("ep") // 2
    experts_n = w_router.shape[1]
    capacity = max(2, 2 * tokens // experts_n)
    slots = experts_n * capacity
    half = width // 2
    assert seqs * 2 == blocks and experts_n == columns
    z, e, c, base = place()

    inner_own = lax.all_gather(w_inner[0], "blk", axis=0)
    outer_own = lax.all_gather(w_outer[0], "blk", axis=0)
    flip = [(i, i ^ 1) for i in range(2 * columns)]
    inner_sib = lax.ppermute(inner_own, "ep", flip)
    outer_sib = lax.ppermute(outer_own, "ep", flip)

    inputs = hidden_in.astype(f32)
    normed_f, norm_one_pull = jax.vjp(layer_norm, inputs, gain_one, shift_one)
    normed = normed_f.astype(bf16)

    token_experts = expert_ids.reshape(tokens)
    onehot = token_experts[:, None] == jnp.arange(experts_n, dtype=jnp.int32)[None, :]
    onehot_f = onehot.astype(f32)
    onehot_int = onehot.astype(jnp.int32)
    places = z * span + jnp.arange(span, dtype=jnp.int32)
    valid_rows = (places[None, :] < seq_lengths[:, None]).astype(f32).reshape(tokens)
    counts = lax.psum(jnp.sum(onehot_f * valid_rows[:, None], axis=0), ("blk", "ep"))
    mean_load = jnp.sum(counts) / experts_n
    load_ratio = (counts - mean_load) / mean_load
    slot_ranks = jnp.sum(jnp.cumsum(onehot_int, axis=0) * onehot_int, axis=1) - 1
    slot_rows = token_experts * capacity + slot_ranks
    to_slots = (jnp.arange(slots, dtype=jnp.int32)[:, None] == slot_rows[None, :]).astype(bf16)
    from_slots = (slot_rows[:, None] == jnp.arange(slots, dtype=jnp.int32)[None, :]).astype(bf16)

    column_lengths = lax.all_gather(seq_lengths, "ep")
    length = lax.dynamic_slice(
        column_lengths, (base + z // 2, lax.rem(z, 2)), (1, 1)
    ).reshape(1)

    def half_columns(weight):
        return lax.dynamic_slice_in_dim(weight, c * half, half, axis=1)

    w_qkv = jnp.concatenate(
        [half_columns(query_weight), half_columns(key_weight), half_columns(value_weight)], axis=1
    )

    rows_all = normed_exchange(normed, blocks)
    qkv, att, att_t, lse = attention_forward(length, rows_all, w_qkv, span)
    attended = attended_exchange(att, blocks)

    branch = jnp.einsum(
        "skqd,kde->sqe", attended, output_weight.reshape(2, half, width), preferred_element_type=f32
    )
    middle = (inputs + branch).reshape(tokens, width)
    normed_two_f, norm_two_pull = jax.vjp(layer_norm, middle, gain_two, shift_two)
    flat_rows = normed_two_f.astype(bf16)
    logits = jnp.dot(flat_rows, w_router, preferred_element_type=f32)
    gate_values = jax.nn.sigmoid(jnp.sum(logits * onehot_f, axis=1))
    scale_rows = valid_rows * gate_values
    grad_flat = cotangent.astype(f32).reshape(tokens, width)
    d_expert = (scale_rows[:, None] * grad_flat).astype(bf16)

    sent = jnp.dot(to_slots, jnp.concatenate([flat_rows, d_expert], axis=1), preferred_element_type=f32).astype(bf16)
    to_rows = sent[:, :width].reshape(columns, capacity, width)
    to_grads = sent[:, width:].reshape(columns, capacity, width)
    got_rows, got_grads = plane_exchange([to_rows, to_grads], columns, 7, "dispatch_exchange")
    produced, d_rows, gi_own, gi_sib, go_own, go_sib = experts(
        got_rows.reshape(-1, width),
        got_grads.reshape(-1, width),
        inner_own,
        inner_sib,
        outer_own,
        outer_sib,
    )
    back_rows, back_grads = plane_exchange(
        [
            produced.reshape(columns, capacity, width),
            d_rows.reshape(columns, capacity, width),
        ],
        columns,
        8,
        "return_exchange",
    )
    expert_out = jnp.dot(from_slots, back_rows.reshape(slots, width), preferred_element_type=f32)
    d_expert_rows = jnp.dot(from_slots, back_grads.reshape(slots, width), preferred_element_type=f32)

    output = (middle + scale_rows[:, None] * expert_out).reshape(seqs, span, width).astype(bf16)
    ratio_rows = jnp.sum(onehot_f * load_ratio[None, :], axis=1)
    local_balance = jnp.sum(scale_rows * ratio_rows)
    d_gate = valid_rows * (jnp.sum(grad_flat * expert_out, axis=1) + balance_weight * ratio_rows)
    d_logits = (onehot_f * (d_gate * gate_values * (1.0 - gate_values))[:, None]).astype(bf16)
    grad_router = jnp.einsum("td,te->ed", flat_rows, d_logits, preferred_element_type=f32)
    d_router_rows = jnp.einsum("te,de->td", d_logits, w_router, preferred_element_type=f32)
    d_middle_norm, grad_gain_two, grad_shift_two = norm_two_pull(d_expert_rows + d_router_rows)
    d_middle = (grad_flat + d_middle_norm).reshape(seqs, span, width)
    d_branch = d_middle.astype(bf16)
    out_part = jnp.einsum(
        "skqd,sqhe->hkde", attended, d_branch.reshape(seqs, span, 2, half), preferred_element_type=f32
    ).astype(bf16).reshape(2, width, half)
    d_attended = jnp.einsum(
        "sqe,kde->skqd", d_branch, output_weight.reshape(2, half, width), preferred_element_type=f32
    ).astype(bf16)
    d_att = d_attended_exchange(d_attended, blocks)
    qkv_part, d_norm_part = attention_backward(
        length, rows_all, w_qkv, qkv, att_t, lse, d_att.reshape(blocks * span, half), span
    )
    d_normed = d_normed_exchange(d_norm_part.reshape(blocks, 2, span // 2, width), blocks)
    d_input_norm, grad_gain_one, grad_shift_one = norm_one_pull(
        d_normed.reshape(seqs, span, width).astype(f32)
    )
    grad_hidden = d_middle + d_input_norm

    vectors = jnp.concatenate(
        [
            grad_gain_one[None],
            grad_shift_one[None],
            grad_gain_two[None],
            grad_shift_two[None],
            grad_router,
            jnp.full((1, width), local_balance, f32),
        ],
        axis=0,
    )
    pad = -vectors.shape[0] % 8
    vectors = jnp.pad(vectors, ((0, pad), (0, 0)))
    grads, sums = dense_grad_sum(qkv_part, out_part, vectors, blocks, columns)
    dense = [
        jnp.concatenate([grads[0, m], grads[1, m]], axis=1).astype(f32) for m in range(4)
    ]
    grad_inner, grad_outer = expert_grad_sum(gi_own, gi_sib, go_own, go_sib)
    balance = sums[4 + experts_n, 0] / jnp.sum(counts)
    return (
        output,
        grad_hidden,
        dense[0],
        dense[1],
        dense[2],
        dense[3],
        sums[0],
        sums[1],
        sums[2],
        sums[3],
        jnp.transpose(sums[4 : 4 + experts_n]),
        grad_inner[None],
        grad_outer[None],
        balance,
    )


def solution(mesh):
    tokens = P("ep", "blk", None)
    return jax.shard_map(
        on_device,
        mesh=mesh,
        in_specs=(tokens, tokens)
        + (P(),) * 9
        + (P("ep", None, "blk"), P("ep", "blk", None), P("ep", "blk", None, None, None), P("ep")),
        out_specs=(tokens, tokens) + (P(),) * 9 + (P("ep", None, "blk"), P("ep", "blk", None), P()),
        check_vma=False,
    )
```

```python
import functools

import jax
import jax.numpy as jnp
from jax import lax
from jax.experimental import pallas as pl
from jax.experimental.pallas import tpu as pltpu
from jax.sharding import PartitionSpec as P

HEAD = 64
MESH = pl.DeviceIdType.MESH
ANY = pl.BlockSpec(memory_space=pl.ANY)
VMEM = pl.BlockSpec(memory_space=pltpu.VMEM)
SMEM = pl.BlockSpec(memory_space=pltpu.SMEM)
DMA = pltpu.SemaphoreType.DMA
f32 = jnp.float32
bf16 = jnp.bfloat16

epsilon = 1e-05
balance_weight = 6.0
masked_fill = -1e30
VMEM_BYTES = 50 * 1024 * 1024


def dot(a, b):
    return lax.dot_general(a, b, (((1,), (0,)), ((), ())), preferred_element_type=f32)


def dot_nt(a, b):
    return lax.dot_general(a, b, (((1,), (1,)), ((), ())), preferred_element_type=f32)


def dot_tn(a, b):
    return lax.dot_general(a, b, (((0,), (0,)), ((), ())), preferred_element_type=f32)


def place():
    z = lax.axis_index("blk")
    e = lax.axis_index("ep")
    c = lax.rem(e, 2)
    return z, e, c, e - c


def remote(src, dst, send_sem, recv_sem, z, e):
    return pltpu.make_async_remote_copy(
        src, dst, send_sem, recv_sem, device_id=(z, e), device_id_type=MESH
    )


def greet(partners):
    barrier = pltpu.get_barrier_semaphore()
    for z, e in partners:
        pl.semaphore_signal(barrier, inc=1, device_id=(z, e), device_id_type=MESH)
    pl.semaphore_wait(barrier, len(partners))


def column_partners(blocks, z, c, base):
    found = [(z, base + 1 - c)]
    for step in range(1, blocks):
        for k in range(2):
            found.append((lax.rem(z + step, blocks), base + k))
    return found


def params(collective_id):
    return pltpu.CompilerParams(
        collective_id=collective_id, has_side_effects=True, vmem_limit_bytes=VMEM_BYTES
    )


def normed_exchange(normed, blocks):
    seqs, span, width = normed.shape
    half = span // 2

    def kernel(n_ref, x_ref, loc_sem, send_sem, recv_sem, fsend_sem, frecv_sem):
        z, e, c, base = place()
        seq_core = z // 2
        greet(column_partners(blocks, z, c, base))

        def outgoing(s, k):
            return remote(
                n_ref.at[s, k], x_ref.at[z, k], send_sem.at[s, k], recv_sem.at[z], 2 * c + s, base + k
            )

        def own(s, k):
            return pltpu.make_async_copy(n_ref.at[s, k], x_ref.at[z, k], loc_sem)

        for s in range(seqs):
            for k in range(2):
                to_self = (2 * c + s == z) & (c == k)

                @pl.when(to_self)
                def _():
                    own(s, k).start()

                @pl.when(jnp.logical_not(to_self))
                def _():
                    outgoing(s, k).start()

        def forward(zs):
            return remote(
                x_ref.at[zs, c], x_ref.at[zs, c], fsend_sem.at[zs], frecv_sem.at[zs], z, base + 1 - c
            )

        for step in range(blocks):
            zs = lax.rem(z + step, blocks)
            if step == 0:

                @pl.when(c == seq_core)
                def _():
                    pltpu.make_async_copy(n_ref.at[0, 0], x_ref.at[z, c], loc_sem).wait()

                @pl.when(c != seq_core)
                def _():
                    remote(n_ref.at[0, 0], x_ref.at[z, c], send_sem.at[0, 0], recv_sem.at[z], z, base).wait_recv()
            else:
                remote(n_ref.at[0, 0], x_ref.at[zs, c], send_sem.at[0, 0], recv_sem.at[zs], z, base).wait_recv()
            forward(zs).start()
        for step in range(blocks):
            zs = lax.rem(z + step, blocks)
            forward(zs).wait_send()
            remote(
                x_ref.at[zs, 1 - c], x_ref.at[zs, 1 - c], fsend_sem.at[zs], frecv_sem.at[zs], z, base + 1 - c
            ).wait_recv()
        for s in range(seqs):
            for k in range(2):

                @pl.when(jnp.logical_not((2 * c + s == z) & (c == k)))
                def _():
                    outgoing(s, k).wait_send()

    return pl.pallas_call(
        kernel,
        name="normed_exchange",
        out_shape=jax.ShapeDtypeStruct((blocks, 2, half, width), bf16),
        in_specs=[ANY],
        out_specs=ANY,
        scratch_shapes=[DMA, DMA((seqs, 2)), DMA((blocks,)), DMA((blocks,)), DMA((blocks,))],
        compiler_params=params(1),
    )(normed.reshape(seqs, 2, half, width)).reshape(blocks * span, width)


def attended_exchange(att, blocks):
    _, span, width = att.shape
    seqs = 2

    def kernel(a_ref, t_ref, loc_sem, send_sem, recv_sem):
        z, e, c, base = place()
        seq_core, seq = z // 2, lax.rem(z, 2)
        greet(column_partners(blocks, z, c, base))

        def outgoing(j):
            return remote(
                a_ref.at[j], t_ref.at[seq, c], send_sem.at[j], recv_sem.at[seq, c], j, base + seq_core
            )

        def own():
            return pltpu.make_async_copy(a_ref.at[z], t_ref.at[seq, c], loc_sem)

        for step in range(1, blocks):
            outgoing(lax.rem(z + step, blocks)).start()

        @pl.when(seq_core == c)
        def _():
            own().start()

        @pl.when(seq_core != c)
        def _():
            outgoing(z).start()

        for s in range(seqs):
            for k in range(2):
                from_self = (2 * c + s == z) & (c == k)

                @pl.when(jnp.logical_not(from_self))
                def _():
                    remote(a_ref.at[0], t_ref.at[s, k], send_sem.at[0], recv_sem.at[s, k], z, base).wait_recv()

        for step in range(1, blocks):
            outgoing(lax.rem(z + step, blocks)).wait_send()

        @pl.when(seq_core == c)
        def _():
            own().wait()

        @pl.when(seq_core != c)
        def _():
            outgoing(z).wait_send()

    return pl.pallas_call(
        kernel,
        name="attended_exchange",
        out_shape=jax.ShapeDtypeStruct((seqs, 2, span, width), bf16),
        in_specs=[ANY],
        out_specs=ANY,
        scratch_shapes=[DMA, DMA((blocks,)), DMA((seqs, 2))],
        compiler_params=params(2),
    )(att)


def plane_exchange(arrays, columns, collective_id, name):
    count = len(arrays)

    def kernel(*refs):
        sources, targets = refs[:count], refs[count : 2 * count]
        loc_sem, send_sem, recv_sem = refs[2 * count :]
        z, e, c, base = place()
        col = e // 2
        others = [lax.rem(col + step, columns) for step in range(1, columns)]
        greet([(z, 2 * t + c) for t in others])
        for i in range(count):
            for t in others:
                remote(
                    sources[i].at[t], targets[i].at[col], send_sem.at[i, t], recv_sem.at[i, col], z, 2 * t + c
                ).start()
            pltpu.make_async_copy(sources[i].at[col], targets[i].at[col], loc_sem.at[i]).start()
        for i in range(count):
            pltpu.make_async_copy(sources[i].at[col], targets[i].at[col], loc_sem.at[i]).wait()
            for t in others:
                remote(
                    sources[i].at[t], targets[i].at[t], send_sem.at[i, t], recv_sem.at[i, t], z, 2 * t + c
                ).wait()

    return pl.pallas_call(
        kernel,
        name=name,
        out_shape=[jax.ShapeDtypeStruct(a.shape, a.dtype) for a in arrays],
        in_specs=[ANY] * count,
        out_specs=[ANY] * count,
        scratch_shapes=[DMA((count,)), DMA((count, columns)), DMA((count, columns))],
        compiler_params=params(collective_id),
    )(*arrays)


def attention_forward(length, rows, weights, span):
    total, width = rows.shape
    half = weights.shape[1] // 3
    pairs = half // 128
    blocks = total // span

    def kernel(len_ref, x_ref, w_ref, qkv_ref, att_ref, attt_ref, lse_ref, vt_ref):
        seq_len = len_ref[0]
        for j in range(blocks):
            r = pl.ds(j * span, span)
            qkv_ref[r, :] = dot(x_ref[r, :], w_ref[...]).astype(bf16)
        lane = lax.broadcasted_iota(jnp.int32, (1, 128), 1)
        key_place = lax.broadcasted_iota(jnp.int32, (total, 1), 0)
        key_bias = jnp.where(key_place < seq_len, 0.0, masked_fill)
        later = lax.broadcasted_iota(jnp.int32, (span, span), 0) > lax.broadcasted_iota(
            jnp.int32, (span, span), 1
        )

        def pair_step(p, _):
            first = pl.multiple_of(p * 128, 128)
            k_all = qkv_ref[:, pl.ds(half + first, 128)]
            vt_ref[...] = jnp.transpose(qkv_ref[:, pl.ds(2 * half + first, 128)])
            k_heads = []
            for h in range(2):
                inside = (lane // HEAD) == h
                spare = lane == (1 - h) * HEAD
                k_heads.append(
                    jnp.where(
                        inside, k_all.astype(f32), jnp.where(spare, key_bias, 0.0)
                    ).astype(bf16)
                )
            for j in range(blocks):
                n = (j + 1) * span
                r = pl.ds(j * span, span)
                q = qkv_ref[r, pl.ds(first, 128)].astype(f32) * (HEAD**-0.5)
                out_t = []
                for h in range(2):
                    inside = (lane // HEAD) == h
                    spare = lane == (1 - h) * HEAD
                    q_h = jnp.where(inside, q, jnp.where(spare, 1.0, 0.0)).astype(bf16)
                    s = dot_nt(k_heads[h][:n], q_h)
                    last = jnp.where(later, masked_fill, s[n - span :])
                    s = last if j == 0 else jnp.concatenate([s[: n - span], last], axis=0)
                    top = jnp.max(s, axis=0, keepdims=True)
                    w = jnp.exp(s - top)
                    total_w = jnp.sum(w, axis=0, keepdims=True)
                    o_t = dot(vt_ref[h * HEAD : (h + 1) * HEAD, :n], w.astype(bf16))
                    out_t.append(o_t / total_w)
                    lse_ref[pl.ds(2 * p + h, 1), r] = top + jnp.log(total_w)
                o = jnp.concatenate(out_t, axis=0)
                attt_ref[pl.ds(first, 128), r] = o
                att_ref[j, :, pl.ds(first, 128)] = jnp.transpose(o).astype(bf16)
            return 0

        lax.fori_loop(0, pairs, pair_step, 0)

    return pl.pallas_call(
        kernel,
        name="attention_forward",
        out_shape=[
            jax.ShapeDtypeStruct((total, 3 * half), bf16),
            jax.ShapeDtypeStruct((blocks, span, half), bf16),
            jax.ShapeDtypeStruct((half, total), f32),
            jax.ShapeDtypeStruct((2 * pairs, total), f32),
        ],
        in_specs=[SMEM, VMEM, VMEM],
        out_specs=[VMEM] * 4,
        scratch_shapes=[pltpu.VMEM((128, total), bf16)],
        compiler_params=pltpu.CompilerParams(vmem_limit_bytes=VMEM_BYTES),
        cost_estimate=pl.CostEstimate(flops=20 * 10**9, bytes_accessed=10**7, transcendentals=0),
    )(length, rows, weights)


def experts(rows, d_out, inner_own, inner_sib, outer_own, outer_sib):
    total, width = rows.shape
    steps, _, part = inner_own.shape
    block = 256

    def kernel(
        x_ref, d_ref, io_ref, is_ref, oo_ref, os_ref,
        out_ref, dx_ref, gio_ref, gis_ref, goo_ref, gos_ref,
        oacc_ref, dacc_ref, act_ref, dpre_ref, wi_ref, wo_ref,
    ):
        g = pl.program_id(0)
        wi_ref[:, :part] = io_ref[0]
        wi_ref[:, part:] = is_ref[0]
        wo_ref[:part] = oo_ref[0]
        wo_ref[part:] = os_ref[0]

        @pl.when(g == 0)
        def _():
            oacc_ref[...] = jnp.zeros_like(oacc_ref)
            dacc_ref[...] = jnp.zeros_like(dacc_ref)

        def row_step(b, _):
            r = pl.ds(pl.multiple_of(b * block, block), block)
            pre = dot(x_ref[r, :], wi_ref[...])
            cdf = 0.5 * (1.0 + lax.erf(pre * (0.5**0.5)))
            act = (pre * cdf).astype(bf16)
            slope = cdf + pre * (jnp.exp(-0.5 * pre * pre) * ((2 * jnp.pi) ** -0.5))
            d_act = dot_nt(d_ref[r, :], wo_ref[...])
            d_pre = (d_act * slope).astype(bf16)
            act_ref[r, :] = act
            dpre_ref[r, :] = d_pre
            oacc_ref[r, :] += dot(act, wo_ref[...])
            dacc_ref[r, :] += dot_nt(d_pre, wi_ref[...])
            return 0

        lax.fori_loop(0, total // block, row_step, 0)
        g_inner = dot_tn(x_ref[...], dpre_ref[...]).astype(bf16)
        gio_ref[0] = g_inner[:, :part]
        gis_ref[0] = g_inner[:, part:]
        g_outer = dot_tn(act_ref[...], d_ref[...]).astype(bf16)
        goo_ref[0] = g_outer[:part]
        gos_ref[0] = g_outer[part:]

        @pl.when(g == steps - 1)
        def _():
            out_ref[...] = oacc_ref[...].astype(bf16)
            dx_ref[...] = dacc_ref[...].astype(bf16)

    whole = pl.BlockSpec((total, width), lambda g: (0, 0))
    inner = pl.BlockSpec((1, width, part), lambda g: (g, 0, 0))
    outer = pl.BlockSpec((1, part, width), lambda g: (g, 0, 0))
    return pl.pallas_call(
        kernel,
        name="experts",
        grid=(steps,),
        out_shape=[
            jax.ShapeDtypeStruct((total, width), bf16),
            jax.ShapeDtypeStruct((total, width), bf16),
            jax.ShapeDtypeStruct((steps, width, part), bf16),
            jax.ShapeDtypeStruct((steps, width, part), bf16),
            jax.ShapeDtypeStruct((steps, part, width), bf16),
            jax.ShapeDtypeStruct((steps, part, width), bf16),
        ],
        in_specs=[whole, whole, inner, inner, outer, outer],
        out_specs=[whole, whole, inner, inner, outer, outer],
        scratch_shapes=[
            pltpu.VMEM((total, width), f32),
            pltpu.VMEM((total, width), f32),
            pltpu.VMEM((total, 2 * part), bf16),
            pltpu.VMEM((total, 2 * part), bf16),
            pltpu.VMEM((width, 2 * part), bf16),
            pltpu.VMEM((2 * part, width), bf16),
        ],
        compiler_params=pltpu.CompilerParams(
            vmem_limit_bytes=VMEM_BYTES, dimension_semantics=("arbitrary",)
        ),
        cost_estimate=pl.CostEstimate(flops=40 * 10**9, bytes_accessed=3 * 10**7, transcendentals=0),
    )(rows, d_out, inner_own, inner_sib, outer_own, outer_sib)


class PieceSum:
    def __init__(self, at, part, got1, got2, got3, gotr, full, sem, rsem, zsem, zrsem, order):
        self.at, self.part, self.full = at, part, full
        self.got1, self.got2, self.got3, self.gotr = got1, got2, got3, gotr
        self.sem, self.rsem, self.zsem, self.zrsem = sem, rsem, zsem, zrsem
        z, e, c, bit, mate, blocks, sib = at
        self.first, self.second = order
        self.rest = len(bit) - 2

    def swap(self, n, src, dst, e):
        return remote(src, dst, self.sem.at[n], self.rsem.at[n], self.at[0], e)

    def halves(self):
        z, e, c, bit, mate, blocks, sib = self.at
        return self.swap(0, self.part.at[1 - bit[self.first]], self.got1, mate[self.first])

    def quarters(self):
        z, e, c, bit, mate, blocks, sib = self.at
        b1, b2 = bit[self.first], bit[self.second]
        return self.swap(1, self.part.at[b1, 1 - b2], self.got2, mate[self.second])

    def to_z(self, zt):
        z, e, c, bit, mate, blocks, sib = self.at
        b1, b2 = bit[self.first], bit[self.second]
        return remote(
            self.part.at[b1, b2, zt], self.got3.at[z], self.zsem.at[0, zt], self.zrsem.at[0, z], zt, e
        )

    def own(self):
        z, e, c, bit, mate, blocks, sib = self.at
        return self.full.at[c, bit[self.first], bit[self.second], z]

    def back_z(self, zt):
        z, e, c, bit, mate, blocks, sib = self.at
        return remote(self.own(), self.own(), self.zsem.at[1, zt], self.zrsem.at[1, z], zt, e)

    def back_quarter(self):
        z, e, c, bit, mate, blocks, sib = self.at
        at = self.full.at[c, bit[self.first], bit[self.second]]
        return self.swap(2, at, at, mate[self.second])

    def back_half(self):
        z, e, c, bit, mate, blocks, sib = self.at
        at = self.full.at[c, bit[self.first]]
        return self.swap(3, at, at, mate[self.first])

    def to_sibling(self):
        z, e, c, bit, mate, blocks, sib = self.at
        return self.swap(4, self.full.at[c], self.full.at[c], sib)

    def step(self, n):
        z, e, c, bit, mate, blocks, sib = self.at
        b1, b2 = bit[self.first], bit[self.second]
        others = [lax.rem(z + step, blocks) for step in range(1, blocks)]
        if n == 0:
            self.halves().start()
        elif n == 1:
            self.halves().wait()
            self.part[b1] = (self.part[b1].astype(f32) + self.got1[...].astype(f32)).astype(bf16)
            self.quarters().start()
        elif n == 2:
            self.quarters().wait()
            self.part[b1, b2] = (self.part[b1, b2].astype(f32) + self.got2[...].astype(f32)).astype(bf16)
            for zt in others:
                self.to_z(zt).start()
        elif n == 3:
            for zs in others:
                remote(
                    self.got3.at[0], self.got3.at[zs], self.zsem.at[0, zs], self.zrsem.at[0, zs], z, e
                ).wait_recv()
            for zt in others:
                self.to_z(zt).wait_send()
            self.got3[z] = self.part[b1, b2, z]
            total = self.got3[0].astype(f32)
            for j in range(1, blocks):
                total = total + self.got3[j].astype(f32)
            own = self.own()
            own[...] = total.astype(bf16)
            for r in range(self.rest):
                copy = self.swap(5 + r, own, self.gotr.at[r], mate[2 + r])
                copy.start()
                copy.wait()
                own[...] = (own[...].astype(f32) + self.gotr[r].astype(f32)).astype(bf16)
            for zt in others:
                self.back_z(zt).start()
        elif n == 4:
            for zs in others:
                at = self.full.at[c, b1, b2, zs]
                remote(at, at, self.zsem.at[1, zs], self.zrsem.at[1, zs], z, e).wait_recv()
            for zt in others:
                self.back_z(zt).wait_send()
            self.back_quarter().start()
        elif n == 5:
            self.back_quarter().wait()
            self.back_half().start()
        elif n == 6:
            self.back_half().wait()
            self.to_sibling().start()
        elif n == 7:
            self.to_sibling().wait()

    @staticmethod
    def scratch(blocks, piece, lanes, rest):
        return [
            pltpu.VMEM((2, 2, blocks, piece, lanes), bf16),
            pltpu.VMEM((2, blocks, piece, lanes), bf16),
            pltpu.VMEM((blocks, piece, lanes), bf16),
            pltpu.VMEM((blocks, piece, lanes), bf16),
            pltpu.VMEM((max(1, rest), piece, lanes), bf16),
            DMA((5 + rest,)),
            DMA((5 + rest,)),
            DMA((2, blocks)),
            DMA((2, blocks)),
        ]


def backward(
    length, rows, weights, qkv, att_t, lse, d_attended, out_part, small, hidden, gain, d_middle,
    gi_own, gi_sib, go_own, go_sib, span, columns,
):
    total, width = rows.shape
    half = weights.shape[1] // 3
    pairs = half // 128
    blocks = total // span
    seqs = d_attended.shape[0]
    hs = span // 2
    scale = HEAD**-0.5
    part = gi_own.shape[2]
    bits = columns.bit_length() - 1
    assert columns == 1 << bits and bits >= 2
    rest = bits - 2
    small_rows = small.shape[0]
    out_piece, pair_piece = width // (4 * blocks), 3 * width // (4 * blocks)
    n_sum = 9

    def kernel(*refs):
        (
            len_ref, x_ref, w_ref, qkv_ref, attt_ref, lse_ref, datt_ref, op_ref, small_ref, hid_ref, gain_ref, dmid_ref,
            gio_ref, gis_ref, goo_ref, gos_ref,
        ) = refs[:16]
        gout_ref, gpair_ref, sums_ref, fi_ref, fo_ref, gh_ref = refs[16:22]
        (
            do_ref, dqkv_ref, kt_ref, dk_ref, dv_ref, xt_ref, dn_ref, dsib_ref, dsum_ref, dnt_ref,
            oi, oo, si, so, zi, zo, osib, sgot, szgot,
            loc_sem, dsend, drecv, rloc, rssend, rsrecv, rsend, rrecv,
            nsend, nrecv, ssend, srecv, osend, orecv, tsend, trecv, tzsend, tzrecv,
        ) = refs[22:59]
        sums_scratch = refs[59:]
        z, e, c, base = place()
        col = e // 2
        sib = base + 1 - c
        seq_core, seq = z // 2, lax.rem(z, 2)
        bit = [lax.rem(col // (1 << i), 2) for i in range(bits)]
        mate = [2 * (col + (1 - 2 * bit[i]) * (1 << i)) + c for i in range(bits)]
        others = [lax.rem(z + step, blocks) for step in range(1, blocks)]
        greet(column_partners(blocks, z, c, base) + [(z, mate[i]) for i in range(bits)])

        at = (z, e, c, bit, mate, blocks, sib)
        out_sum = PieceSum(at, *sums_scratch[0:5], gout_ref, *sums_scratch[5:9], (0, 1))
        pair_sums = [
            PieceSum(
                at,
                *sums_scratch[n_sum * (p + 1) : n_sum * (p + 1) + 5],
                gpair_ref.at[p],
                *sums_scratch[n_sum * (p + 1) + 5 : n_sum * (p + 2)],
                (1, 0) if p % 2 == 0 else (0, 1),
            )
            for p in range(pairs)
        ]

        def d_out(s, k):
            return remote(
                datt_ref.at[s, k], do_ref.at[z], dsend.at[s, k], drecv.at[z], 2 * c + s, base + k
            )

        def d_own(s, k):
            return pltpu.make_async_copy(datt_ref.at[s, k], do_ref.at[z], loc_sem.at[0])

        for s in range(seqs):
            for k in range(2):
                to_self = (2 * c + s == z) & (c == k)

                @pl.when(to_self)
                def _():
                    d_own(s, k).start()

                @pl.when(jnp.logical_not(to_self))
                def _():
                    d_out(s, k).start()

        r_order = others[1:2] + others[0:1] + others[2:] + [z]
        kinds = ((0, gio_ref, gis_ref, oi, si, zi, fi_ref), (1, goo_ref, gos_ref, oo, so, zo, fo_ref))

        def r_sib(i, src, dst, j):
            return remote(src.at[j], dst.at[j], rssend.at[i, j], rsrecv.at[i, j], z, sib)

        def r_loc(i, src, dst, j):
            return pltpu.make_async_copy(src.at[j], dst.at[j], rloc.at[i, j])

        def r_z(i, src, dst, j):
            return remote(src.at[j], dst.at[z], rsend.at[i, j], rrecv.at[i, z], j, e)

        o_first = remote(op_ref.at[1 - c], osib, osend, orecv, z, sib)
        o_first.start()
        for j in r_order:
            for i, own, sibs, own_buf, sib_buf, z_buf, final in kinds:
                r_sib(i, sibs, sib_buf, j).start()
                r_loc(i, own, own_buf, j).start()

        xt_ref[...] = jnp.transpose(x_ref[...])
        o_first.wait()
        out_sum.part[...] = (op_ref[c].astype(f32) + osib[...].astype(f32)).astype(bf16).reshape(
            2, 2, blocks, out_piece, half
        )
        out_sum.step(0)
        for n, j in enumerate(r_order):
            for i, own, sibs, own_buf, sib_buf, z_buf, final in kinds:
                r_loc(i, own, own_buf, j).wait()
                r_sib(i, sibs, sib_buf, j).wait_recv()
                own_buf[j] = (own_buf[j].astype(f32) + sib_buf[j].astype(f32)).astype(bf16)

        @pl.when(c == seq_core)
        def _():
            d_own(0, 0).wait()

        @pl.when(c != seq_core)
        def _():
            remote(datt_ref.at[0, 0], do_ref.at[z], dsend.at[0, 0], drecv.at[z], z, base).wait_recv()

        for zs in others:
            remote(datt_ref.at[0, 0], do_ref.at[zs], dsend.at[0, 0], drecv.at[zs], z, base).wait_recv()

        for j in r_order[:-1]:
            for i, own, sibs, own_buf, sib_buf, z_buf, final in kinds:
                r_z(i, own_buf, z_buf, j).start()

        seq_len = len_ref[0]
        lane = lax.broadcasted_iota(jnp.int32, (1, 128), 1)
        key_place = lax.broadcasted_iota(jnp.int32, (total, 1), 0)
        key_bias = jnp.where(key_place < seq_len, 0.0, masked_fill)
        later = lax.broadcasted_iota(jnp.int32, (span, span), 0) > lax.broadcasted_iota(
            jnp.int32, (span, span), 1
        )

        def pair_step(p):
            first = p * 128
            k_all = qkv_ref[:, pl.ds(half + first, 128)]
            kt_ref[...] = jnp.transpose(k_all)
            v_all = qkv_ref[:, pl.ds(2 * half + first, 128)]
            k_heads = []
            for h in range(2):
                inside = (lane // HEAD) == h
                spare = lane == (1 - h) * HEAD
                k_heads.append(
                    jnp.where(
                        inside, k_all.astype(f32), jnp.where(spare, key_bias, 0.0)
                    ).astype(bf16)
                )
            dk_ref[...] = jnp.zeros_like(dk_ref)
            dv_ref[...] = jnp.zeros_like(dv_ref)
            for j in range(blocks):
                n = (j + 1) * span
                r = pl.ds(j * span, span)
                q = qkv_ref[r, pl.ds(first, 128)].astype(f32) * scale
                d_o = do_ref[j, :, pl.ds(first, 128)].astype(f32)
                prod_t = jnp.transpose(d_o) * attt_ref[pl.ds(first, 128), r]
                dq_t = []
                for h in range(2):
                    inside = (lane // HEAD) == h
                    spare = lane == (1 - h) * HEAD
                    q_h = jnp.where(inside, q, jnp.where(spare, 1.0, 0.0)).astype(bf16)
                    q_only = jnp.where(inside, q, 0.0).astype(bf16)
                    do_h = jnp.where(inside, d_o, 0.0).astype(bf16)
                    delta = jnp.sum(prod_t[h * HEAD : (h + 1) * HEAD], axis=0, keepdims=True)
                    s = dot_nt(k_heads[h][:n], q_h)
                    last = jnp.where(later, masked_fill, s[n - span :])
                    s = last if j == 0 else jnp.concatenate([s[: n - span], last], axis=0)
                    w = jnp.exp(s - lse_ref[pl.ds(2 * p + h, 1), r])
                    d_w = dot_nt(v_all[:n], do_h)
                    d_s = (w * (d_w - delta)).astype(bf16)
                    dv_ref[:n] += dot(w.astype(bf16), do_h)
                    dk_ref[:n] += dot(d_s, q_only)
                    dq_t.append(dot(kt_ref[h * HEAD : (h + 1) * HEAD, :n], d_s))
                dq = jnp.transpose(jnp.concatenate(dq_t, axis=0)) * scale
                dqkv_ref[r, pl.ds(first, 128)] = dq.astype(bf16)
            dqkv_ref[:, pl.ds(half + first, 128)] = dk_ref[...].astype(bf16)
            dqkv_ref[:, pl.ds(2 * half + first, 128)] = dv_ref[...].astype(bf16)
            joined = jnp.concatenate(
                [dqkv_ref[:, pl.ds(m * half + first, 128)] for m in range(3)], axis=1
            )
            grads = dot(xt_ref[...], joined).astype(bf16)
            pair_sums[p].part[...] = jnp.concatenate(
                [grads[:, m * 128 : (m + 1) * 128] for m in range(3)], axis=0
            ).reshape(2, 2, blocks, pair_piece, 128)

        todo = [(out_sum, 1)]
        for p in range(pairs):
            pair_step(p)
            nexts = []
            for one, n in todo:
                one.step(n)
                if n < 7:
                    nexts.append((one, n + 1))
            pair_sums[p].step(0)
            todo = nexts + [(pair_sums[p], 1)]

        for j in range(blocks):
            r = pl.ds(j * span, span)
            dn_ref[j] = dot_nt(dqkv_ref[r, :], w_ref[...]).astype(bf16).reshape(2, hs, width)

        def n_sib(j):
            return remote(dn_ref.at[j, 1 - c], dsib_ref.at[j], nsend.at[j], nrecv.at[j], z, sib)

        def n_out(j):
            return remote(
                dsum_ref.at[j], dnt_ref.at[seq, c], ssend.at[j], srecv.at[seq, c], j, base + seq_core
            )

        def n_own():
            return pltpu.make_async_copy(dsum_ref.at[z], dnt_ref.at[seq, c], loc_sem.at[1])

        n_order = others[1:2] + others[0:1] + others[2:] + [z]
        for j in n_order:
            n_sib(j).start()
        for i, j in enumerate(n_order):
            n_sib(j).wait_recv()
            dsum_ref[j] = (dn_ref[j, c].astype(f32) + dsib_ref[j].astype(f32)).astype(bf16)
            if i < blocks - 1:
                n_out(j).start()
            else:

                @pl.when(seq_core == c)
                def _():
                    n_own().start()

                @pl.when(seq_core != c)
                def _():
                    n_out(j).start()

        def advance():
            nexts = []
            for one, n in todo:
                one.step(n)
                if n < 7:
                    nexts.append((one, n + 1))
            todo[:] = nexts

        advance()
        for s in range(seqs):
            for k in range(2):
                from_self = (2 * c + s == z) & (c == k)

                @pl.when(jnp.logical_not(from_self))
                def _():
                    remote(
                        dsum_ref.at[0], dnt_ref.at[s, k], ssend.at[0], srecv.at[s, k], z, base
                    ).wait_recv()

                @pl.when(from_self)
                def _():
                    n_own().wait()

        gains = gain_ref[...]
        gain_sum = jnp.zeros((1, width), f32)
        shift_sum = jnp.zeros((1, width), f32)
        for s in range(seqs):
            for k in range(2):
                v = hid_ref[s, k].astype(f32)
                centered = v - jnp.mean(v, axis=-1, keepdims=True)
                inverse = lax.rsqrt(jnp.mean(centered * centered, axis=-1, keepdims=True) + epsilon)
                unit = centered * inverse
                dy = dnt_ref[s, k].astype(f32)
                gain_sum = gain_sum + jnp.sum(dy * unit, axis=0, keepdims=True)
                shift_sum = shift_sum + jnp.sum(dy, axis=0, keepdims=True)
                du = dy * gains
                dx = inverse * (
                    du
                    - jnp.mean(du, axis=-1, keepdims=True)
                    - unit * jnp.mean(du * unit, axis=-1, keepdims=True)
                )
                gh_ref[s, k] = dmid_ref[s, k] + dx

        sums_ref[...] = small_ref[...]
        sums_ref[0:1] = gain_sum
        sums_ref[1:2] = shift_sum

        def t_swap(n, te):
            return remote(sums_ref, sgot.at[n], tsend.at[n], trecv.at[n], z, te)

        partners = [sib] + mate
        for n, te in enumerate(partners):
            copy = t_swap(n, te)
            copy.start()
            if n in (1, 2):
                advance()
            copy.wait()
            sums_ref[...] = sums_ref[...] + sgot[n]

        def t_z(zt):
            return remote(sums_ref, szgot.at[z], tzsend.at[zt], tzrecv.at[z], zt, e)

        for zt in others:
            t_z(zt).start()
        advance()
        for zs in others:
            remote(sums_ref, szgot.at[zs], tzsend.at[zs], tzrecv.at[zs], z, e).wait_recv()
        for zt in others:
            t_z(zt).wait_send()
        szgot[z] = sums_ref[...]
        tot = szgot[0]
        for j in range(1, blocks):
            tot = tot + szgot[j]
        sums_ref[...] = tot

        advance()
        for i, own, sibs, own_buf, sib_buf, z_buf, final in kinds:
            for zs in others:
                remote(own_buf.at[0], z_buf.at[zs], rsend.at[i, 0], rrecv.at[i, zs], z, e).wait_recv()
            z_buf[z] = own_buf[z]
            acc = z_buf[0].astype(f32)
            for j in range(1, blocks):
                acc = acc + z_buf[j].astype(f32)
            final[...] = acc
            advance()
        while todo:
            advance()

        for s in range(seqs):
            for k in range(2):

                @pl.when(jnp.logical_not((2 * c + s == z) & (c == k)))
                def _():
                    d_out(s, k).wait_send()

        for j in n_order[:-1]:
            n_out(j).wait_send()

        @pl.when(seq_core != c)
        def _():
            n_out(z).wait_send()

        for j in n_order:
            n_sib(j).wait_send()
            for i, own, sibs, own_buf, sib_buf, z_buf, final in kinds:
                r_sib(i, sibs, sib_buf, j).wait_send()
        for j in r_order[:-1]:
            for i, own, sibs, own_buf, sib_buf, z_buf, final in kinds:
                r_z(i, own_buf, z_buf, j).wait_send()

    stage = blocks
    scratch = [
        pltpu.VMEM((blocks, span, half), bf16),
        pltpu.VMEM((total, 3 * half), bf16),
        pltpu.VMEM((128, total), bf16),
        pltpu.VMEM((total, 128), f32),
        pltpu.VMEM((total, 128), f32),
        pltpu.VMEM((width, total), bf16),
        pltpu.VMEM((blocks, 2, hs, width), bf16),
        pltpu.VMEM((blocks, hs, width), bf16),
        pltpu.VMEM((blocks, hs, width), bf16),
        pltpu.VMEM((seqs, 2, hs, width), bf16),
        pltpu.VMEM((blocks, width, part), bf16),
        pltpu.VMEM((blocks, part, width), bf16),
        pltpu.VMEM((blocks, width, part), bf16),
        pltpu.VMEM((blocks, part, width), bf16),
        pltpu.VMEM((blocks, width, part), bf16),
        pltpu.VMEM((blocks, part, width), bf16),
        pltpu.VMEM((width, half), bf16),
        pltpu.VMEM((1 + bits, small_rows, width), f32),
        pltpu.VMEM((blocks, small_rows, width), f32),
        DMA((2,)),
        DMA((seqs, 2)),
        DMA((stage,)),
        DMA((2, stage)),
        DMA((2, stage)),
        DMA((2, stage)),
        DMA((2, stage)),
        DMA((2, stage)),
        DMA((stage,)),
        DMA((stage,)),
        DMA((stage,)),
        DMA((seqs, 2)),
        DMA,
        DMA,
        DMA((1 + bits,)),
        DMA((1 + bits,)),
        DMA((stage,)),
        DMA((stage,)),
    ]
    scratch += PieceSum.scratch(blocks, out_piece, half, rest)
    for _ in range(pairs):
        scratch += PieceSum.scratch(blocks, pair_piece, 128, rest)
    gout, gpair, sums, g_inner, g_outer, g_hidden = pl.pallas_call(
        kernel,
        name="backward",
        out_shape=[
            jax.ShapeDtypeStruct((2, 2, 2, blocks, out_piece, half), bf16),
            jax.ShapeDtypeStruct((pairs, 2, 2, 2, blocks, pair_piece, 128), bf16),
            jax.ShapeDtypeStruct(small.shape, f32),
            jax.ShapeDtypeStruct((width, part), f32),
            jax.ShapeDtypeStruct((part, width), f32),
            jax.ShapeDtypeStruct((seqs, 2, hs, width), f32),
        ],
        in_specs=[SMEM] + [VMEM] * 11 + [ANY] * 4,
        out_specs=[VMEM] * 6,
        scratch_shapes=scratch,
        compiler_params=params(3),
    )(
        length, rows, weights, qkv, att_t, lse, d_attended, out_part, small,
        hidden.reshape(seqs, 2, hs, width), gain.reshape(1, width), d_middle.reshape(seqs, 2, hs, width),
        gi_own, gi_sib, go_own, go_sib,
    )
    g_out = gout.reshape(2, width, half).transpose(1, 0, 2).reshape(width, width)
    g_pair = gpair.reshape(pairs, 2, 3, width, 128).transpose(2, 3, 1, 0, 4).reshape(3, width, width)
    return g_out, g_pair, sums, g_inner, g_outer, g_hidden.reshape(seqs, span, width)


def layer_norm(inputs, norm_gain, norm_shift):
    centered = inputs - jnp.mean(inputs, axis=-1, keepdims=True)
    variance = jnp.mean(centered * centered, axis=-1, keepdims=True)
    return centered * lax.rsqrt(variance + epsilon) * norm_gain + norm_shift


def on_device(
    hidden_in,
    cotangent,
    query_weight,
    key_weight,
    value_weight,
    output_weight,
    gain_one,
    shift_one,
    gain_two,
    shift_two,
    w_router,
    w_inner,
    w_outer,
    expert_ids,
    seq_lengths,
):
    seqs, span, width = hidden_in.shape
    tokens = seqs * span
    blocks = lax.axis_size("blk")
    columns = lax.axis_size("ep") // 2
    experts_n = w_router.shape[1]
    capacity = max(2, 2 * tokens // experts_n)
    slots = experts_n * capacity
    half = width // 2
    assert seqs * 2 == blocks and experts_n == columns
    z, e, c, base = place()

    inner_own = lax.all_gather(w_inner[0], "blk", axis=0)
    outer_own = lax.all_gather(w_outer[0], "blk", axis=0)
    flip = [(i, i ^ 1) for i in range(2 * columns)]
    inner_sib = lax.ppermute(inner_own, "ep", flip)
    outer_sib = lax.ppermute(outer_own, "ep", flip)

    inputs = hidden_in.astype(f32)
    normed = layer_norm(inputs, gain_one, shift_one).astype(bf16)

    token_experts = expert_ids.reshape(tokens)
    onehot = token_experts[:, None] == jnp.arange(experts_n, dtype=jnp.int32)[None, :]
    onehot_f = onehot.astype(f32)
    onehot_int = onehot.astype(jnp.int32)
    places = z * span + jnp.arange(span, dtype=jnp.int32)
    valid_rows = (places[None, :] < seq_lengths[:, None]).astype(f32).reshape(tokens)
    counts = lax.psum(jnp.sum(onehot_f * valid_rows[:, None], axis=0), ("blk", "ep"))
    mean_load = jnp.sum(counts) / experts_n
    load_ratio = (counts - mean_load) / mean_load
    slot_ranks = jnp.sum(jnp.cumsum(onehot_int, axis=0) * onehot_int, axis=1) - 1
    slot_rows = token_experts * capacity + slot_ranks
    to_slots = (jnp.arange(slots, dtype=jnp.int32)[:, None] == slot_rows[None, :]).astype(bf16)
    from_slots = (slot_rows[:, None] == jnp.arange(slots, dtype=jnp.int32)[None, :]).astype(bf16)

    column_lengths = lax.all_gather(seq_lengths, "ep")
    length = lax.dynamic_slice(
        column_lengths, (base + z // 2, lax.rem(z, 2)), (1, 1)
    ).reshape(1)

    def half_columns(weight):
        return lax.dynamic_slice_in_dim(weight, c * half, half, axis=1)

    w_qkv = jnp.concatenate(
        [half_columns(query_weight), half_columns(key_weight), half_columns(value_weight)], axis=1
    )

    rows_all = normed_exchange(normed, blocks)
    qkv, att, att_t, lse = attention_forward(length, rows_all, w_qkv, span)
    attended = attended_exchange(att, blocks)

    branch = jnp.einsum(
        "skqd,kde->sqe", attended, output_weight.reshape(2, half, width), preferred_element_type=f32
    )
    middle = (inputs + branch).reshape(tokens, width)
    normed_two_f, norm_two_pull = jax.vjp(layer_norm, middle, gain_two, shift_two)
    flat_rows = normed_two_f.astype(bf16)
    logits = jnp.dot(flat_rows, w_router, preferred_element_type=f32)
    gate_values = jax.nn.sigmoid(jnp.sum(logits * onehot_f, axis=1))
    scale_rows = valid_rows * gate_values
    grad_flat = cotangent.astype(f32).reshape(tokens, width)
    d_expert = (scale_rows[:, None] * grad_flat).astype(bf16)

    sent = jnp.dot(to_slots, jnp.concatenate([flat_rows, d_expert], axis=1), preferred_element_type=f32).astype(bf16)
    to_rows = sent[:, :width].reshape(columns, capacity, width)
    to_grads = sent[:, width:].reshape(columns, capacity, width)
    got_rows, got_grads = plane_exchange([to_rows, to_grads], columns, 7, "dispatch_exchange")
    produced, d_rows, gi_own, gi_sib, go_own, go_sib = experts(
        got_rows.reshape(-1, width),
        got_grads.reshape(-1, width),
        inner_own,
        inner_sib,
        outer_own,
        outer_sib,
    )
    back_rows, back_grads = plane_exchange(
        [
            produced.reshape(columns, capacity, width),
            d_rows.reshape(columns, capacity, width),
        ],
        columns,
        8,
        "return_exchange",
    )
    expert_out = jnp.dot(from_slots, back_rows.reshape(slots, width), preferred_element_type=f32)
    d_expert_rows = jnp.dot(from_slots, back_grads.reshape(slots, width), preferred_element_type=f32)

    output = (middle + scale_rows[:, None] * expert_out).reshape(seqs, span, width).astype(bf16)
    ratio_rows = jnp.sum(onehot_f * load_ratio[None, :], axis=1)
    local_balance = jnp.sum(scale_rows * ratio_rows)
    d_gate = valid_rows * (jnp.sum(grad_flat * expert_out, axis=1) + balance_weight * ratio_rows)
    d_logits = (onehot_f * (d_gate * gate_values * (1.0 - gate_values))[:, None]).astype(bf16)
    grad_router = jnp.einsum("td,te->ed", flat_rows, d_logits, preferred_element_type=f32)
    d_router_rows = jnp.einsum("te,de->td", d_logits, w_router, preferred_element_type=f32)
    d_middle_norm, grad_gain_two, grad_shift_two = norm_two_pull(d_expert_rows + d_router_rows)
    d_middle = (grad_flat + d_middle_norm).reshape(seqs, span, width)
    d_branch = d_middle.astype(bf16)
    out_part = jnp.einsum(
        "skqd,sqhe->hkde", attended, d_branch.reshape(seqs, span, 2, half), preferred_element_type=f32
    ).astype(bf16).reshape(2, width, half)
    d_attended = jnp.einsum(
        "sqe,kde->skqd", d_branch, output_weight.reshape(2, half, width), preferred_element_type=f32
    ).astype(bf16)
    vectors = jnp.concatenate(
        [
            jnp.zeros((2, width), f32),
            grad_gain_two[None],
            grad_shift_two[None],
            grad_router,
            jnp.full((1, width), local_balance, f32),
        ],
        axis=0,
    )
    vectors = jnp.pad(vectors, ((0, -vectors.shape[0] % 8), (0, 0)))
    g_out, g_qkv, sums, grad_inner, grad_outer, grad_hidden = backward(
        length, rows_all, w_qkv, qkv, att_t, lse, d_attended, out_part, vectors, hidden_in, gain_one, d_middle,
        gi_own, gi_sib, go_own, go_sib, span, columns,
    )
    dense = [g_qkv[0].astype(f32), g_qkv[1].astype(f32), g_qkv[2].astype(f32), g_out.astype(f32)]
    balance = sums[4 + experts_n, 0] / jnp.sum(counts)
    return (
        output,
        grad_hidden,
        dense[0],
        dense[1],
        dense[2],
        dense[3],
        sums[0],
        sums[1],
        sums[2],
        sums[3],
        jnp.transpose(sums[4 : 4 + experts_n]),
        grad_inner[None],
        grad_outer[None],
        balance,
    )


def solution(mesh):
    tokens = P("ep", "blk", None)
    return jax.shard_map(
        on_device,
        mesh=mesh,
        in_specs=(tokens, tokens)
        + (P(),) * 9
        + (P("ep", None, "blk"), P("ep", "blk", None), P("ep", "blk", None, None, None), P("ep")),
        out_specs=(tokens, tokens) + (P(),) * 9 + (P("ep", None, "blk"), P("ep", "blk", None), P()),
        check_vma=False,
    )
```

```python
import functools

import jax
import jax.numpy as jnp
from jax import lax
from jax.experimental import pallas as pl
from jax.experimental.pallas import tpu as pltpu
from jax.sharding import PartitionSpec as P

HEAD = 64
MESH = pl.DeviceIdType.MESH
ANY = pl.BlockSpec(memory_space=pl.ANY)
VMEM = pl.BlockSpec(memory_space=pltpu.VMEM)
SMEM = pl.BlockSpec(memory_space=pltpu.SMEM)
DMA = pltpu.SemaphoreType.DMA
f32 = jnp.float32
bf16 = jnp.bfloat16

epsilon = 1e-05
balance_weight = 6.0
masked_fill = -1e30
VMEM_BYTES = 50 * 1024 * 1024


def dot(a, b):
    return lax.dot_general(a, b, (((1,), (0,)), ((), ())), preferred_element_type=f32)


def dot_nt(a, b):
    return lax.dot_general(a, b, (((1,), (1,)), ((), ())), preferred_element_type=f32)


def dot_tn(a, b):
    return lax.dot_general(a, b, (((0,), (0,)), ((), ())), preferred_element_type=f32)


def place():
    z = lax.axis_index("blk")
    e = lax.axis_index("ep")
    c = lax.rem(e, 2)
    return z, e, c, e - c


def remote(src, dst, send_sem, recv_sem, z, e):
    return pltpu.make_async_remote_copy(
        src, dst, send_sem, recv_sem, device_id=(z, e), device_id_type=MESH
    )


def greet(partners):
    barrier = pltpu.get_barrier_semaphore()
    for z, e in partners:
        pl.semaphore_signal(barrier, inc=1, device_id=(z, e), device_id_type=MESH)
    pl.semaphore_wait(barrier, len(partners))


def column_partners(blocks, z, c, base):
    found = [(z, base + 1 - c)]
    for step in range(1, blocks):
        for k in range(2):
            found.append((lax.rem(z + step, blocks), base + k))
    return found


def params(collective_id):
    return pltpu.CompilerParams(
        collective_id=collective_id, has_side_effects=True, vmem_limit_bytes=VMEM_BYTES
    )


def lane_of(shape, dimension):
    return lax.broadcasted_iota(jnp.int32, shape, dimension)


def key_heads(k_all, key_bias):
    lane = lane_of((1, 128), 1)
    found = []
    for h in range(2):
        inside = (lane // HEAD) == h
        spare = lane == (1 - h) * HEAD
        found.append(
            jnp.where(inside, k_all.astype(f32), jnp.where(spare, key_bias, 0.0)).astype(bf16)
        )
    return found


def forward(
    hidden, cotangent, gain_one, shift_one, gain_two, shift_two, w_query, w_key, w_value, w_output, w_router,
    ids, lengths, w_inner, w_outer, blocks, columns, capacity, experts_n,
):
    seqs, span, width = hidden.shape
    hs = span // 2
    half = width // 2
    pairs = half // 128
    total = blocks * span
    tokens = seqs * span
    slots = experts_n * capacity
    part = w_inner.shape[1]
    cap_lanes = max(128, capacity)

    def kernel(*refs):
        (
            hid_ref, cot_ref, g1_ref, s1_ref, g2_ref, s2_ref, wq_ref, wk_ref, wv_ref, wo_ref, wr_ref,
            ids_ref, lens_ref, wi_ref, we_ref,
        ) = refs[:15]
        (
            x_ref, w_ref, qkv_ref, attt_ref, lse_ref, t_ref, mid_ref, flat_ref, gate_ref, slot_ref,
            rows_ref, sc_ref, cote_ref, len_ref, cnt_ref, li_ref, lo_ref, bi_ref, bo_ref,
        ) = refs[15:34]
        (
            nb_ref, kh_ref, vt_ref, att_ref, cots_ref, lgot_ref, cown_ref, cgot_ref,
            wload, nloc, nsend, nrecv, fsend, frecv, aloc, asend, arecv, closs, csend, crecv,
            lsend, lrecv, ksend, krecv, hsend, hrecv, bsend, brecv,
        ) = refs[34:]
        z, e, c, base = place()
        col = e // 2
        sib = base + 1 - c
        seq_core, seq = z // 2, lax.rem(z, 2)
        others = [lax.rem(z + step, blocks) for step in range(1, blocks)]
        plane = [lax.rem(col + step, columns) for step in range(1, columns)]
        column = column_partners(blocks, z, c, base)

        def load_w(m, ref):
            return pltpu.make_async_copy(
                ref.at[:, pl.ds(pl.multiple_of(c * half, half), half)],
                w_ref.at[:, pl.ds(m * half, half)],
                wload.at[m],
            )

        for m, ref in enumerate((wq_ref, wk_ref, wv_ref)):
            load_w(m, ref).start()
        for s in range(seqs):
            for k in range(2):
                v = hid_ref[s, k].astype(f32)
                centered = v - jnp.mean(v, axis=-1, keepdims=True)
                inverse = lax.rsqrt(jnp.mean(centered * centered, axis=-1, keepdims=True) + epsilon)
                nb_ref[s, k] = (centered * inverse * g1_ref[...] + s1_ref[...]).astype(bf16)
        greet(column + [(z, 2 * t + c) for t in plane])

        def n_out(s, k):
            return remote(
                nb_ref.at[s, k], x_ref.at[z, k], nsend.at[s, k], nrecv.at[z], 2 * c + s, base + k
            )

        def n_own(s, k):
            return pltpu.make_async_copy(nb_ref.at[s, k], x_ref.at[z, k], nloc)

        for s in range(seqs):
            for k in range(2):
                to_self = (2 * c + s == z) & (c == k)

                @pl.when(to_self)
                def _():
                    n_own(s, k).start()

                @pl.when(jnp.logical_not(to_self))
                def _():
                    n_out(s, k).start()

        to_lens = remote(lens_ref, lgot_ref, lsend, lrecv, z, sib)
        to_lens.start()
        lane = lane_of((tokens, 128), 1)
        onehot = (lane == ids_ref[...]).astype(f32)
        place_in = z * span + lane_of((span, 1), 0)
        valid = jnp.concatenate(
            [(place_in < lens_ref[s, 0:1, 0:1]).astype(f32) for s in range(seqs)], axis=0
        )
        cown_ref[...] = jnp.broadcast_to(jnp.sum(onehot * valid, axis=0, keepdims=True), (8, 128))

        def k_out(n, to_z, to_e):
            return remote(cown_ref, cgot_ref.at[z, c], ksend.at[n], krecv.at[z, c], to_z, to_e)

        for n, (to_z, to_e) in enumerate(column):
            k_out(n, to_z, to_e).start()
        earlier = (lane_of((tokens, tokens), 0) > lane_of((tokens, tokens), 1)).astype(f32).astype(bf16)
        rank = dot(earlier, onehot.astype(bf16))
        slot = jnp.sum(onehot * (rank + (lane * capacity).astype(f32)), axis=1, keepdims=True)
        slot_ref[...] = slot
        slot_row = jnp.transpose(jnp.broadcast_to(slot, (tokens, 128)))[0:1]
        to_slots = (lane_of((slots, tokens), 0).astype(f32) == slot_row).astype(f32).astype(bf16)
        cots_ref[...] = (
            dot(to_slots, cot_ref[...]).astype(bf16).reshape(columns, capacity, width)
        )

        def c_out(t):
            return remote(cots_ref.at[t], cote_ref.at[col], csend.at[t], crecv.at[col], z, 2 * t + c)

        c_own = pltpu.make_async_copy(cots_ref.at[col], cote_ref.at[col], closs)
        c_own.start()
        for t in plane:
            c_out(t).start()
        for m, ref in enumerate((wq_ref, wk_ref, wv_ref)):
            load_w(m, ref).wait()

        def n_sib(zs):
            return remote(x_ref.at[zs, c], x_ref.at[zs, c], fsend.at[zs], frecv.at[zs], z, sib)

        for zs in [z] + others:
            if zs is z:

                @pl.when(c == seq_core)
                def _():
                    n_own(0, 0).wait()

                @pl.when(c != seq_core)
                def _():
                    remote(nb_ref.at[0, 0], x_ref.at[z, c], nsend.at[0, 0], nrecv.at[z], z, base).wait_recv()
            else:
                remote(nb_ref.at[0, 0], x_ref.at[zs, c], nsend.at[0, 0], nrecv.at[zs], z, base).wait_recv()
            n_sib(zs).start()

        def h_out(i, step):
            src, dst = ((wi_ref, li_ref), (we_ref, lo_ref))[i]
            side = 0 if step == 1 else 1
            return remote(src, dst.at[side], hsend.at[i, side], hrecv.at[i, side], z + step, e)

        def b_out(i):
            src, dst = ((wi_ref, bi_ref), (we_ref, bo_ref))[i]
            return remote(src, dst, bsend.at[i], brecv.at[i], z, sib)

        for i in range(2):

            @pl.when(z < blocks - 1)
            def _():
                h_out(i, 1).start()

            @pl.when(z > 0)
            def _():
                h_out(i, -1).start()

        for zs in [z] + others:
            remote(
                x_ref.at[zs, 1 - c], x_ref.at[zs, 1 - c], fsend.at[zs], frecv.at[zs], z, sib
            ).wait_recv()
            qkv_ref[zs] = dot(x_ref[zs].reshape(span, width), w_ref[...]).astype(bf16)
        for i in range(2):
            b_out(i).start()
        to_lens.wait()
        seq_len = jnp.where(c == seq_core, lens_ref[seq], lgot_ref[seq])
        len_ref[...] = seq_len
        key_bias = jnp.where(lane_of((total, 1), 0) < seq_len[0:1, 0:1], 0.0, masked_fill)
        for p in range(pairs):
            k_all = jnp.concatenate(
                [qkv_ref[j, :, half + p * 128 : half + (p + 1) * 128] for j in range(blocks)], axis=0
            )
            for h, k_h in enumerate(key_heads(k_all, key_bias)):
                kh_ref[2 * p + h] = k_h
            for j in range(blocks):
                vt_ref[p * 128 : (p + 1) * 128, j * span : (j + 1) * span] = jnp.transpose(
                    qkv_ref[j, :, 2 * half + p * 128 : 2 * half + (p + 1) * 128]
                )
        later = lane_of((span, span), 0) > lane_of((span, span), 1)
        lane_row = lane_of((1, 128), 1)

        def a_out(j):
            return remote(
                att_ref.at[j], t_ref.at[seq, c], asend.at[j], arecv.at[seq, c], j, base + seq_core
            )

        def a_own(j):
            return pltpu.make_async_copy(att_ref.at[j], t_ref.at[seq, c], aloc)

        for j in reversed(range(blocks)):
            n = (j + 1) * span

            def pair_step(p, _):
                first = pl.multiple_of(p * 128, 128)
                q = qkv_ref[j, :, pl.ds(first, 128)].astype(f32) * (HEAD**-0.5)
                out_t = []
                for h in range(2):
                    inside = (lane_row // HEAD) == h
                    spare = lane_row == (1 - h) * HEAD
                    q_h = jnp.where(inside, q, jnp.where(spare, 1.0, 0.0)).astype(bf16)
                    s = dot_nt(kh_ref[2 * p + h, :n], q_h)
                    last = jnp.where(later, masked_fill, s[n - span :])
                    s = last if j == 0 else jnp.concatenate([s[: n - span], last], axis=0)
                    top = jnp.max(s, axis=0, keepdims=True)
                    w = jnp.exp(s - top)
                    total_w = jnp.sum(w, axis=0, keepdims=True)
                    o_t = dot(vt_ref[pl.ds(pl.multiple_of(first + h * HEAD, HEAD), HEAD), :n], w.astype(bf16))
                    out_t.append(o_t / total_w)
                    lse_ref[pl.ds(2 * p + h, 1), pl.ds(j * span, span)] = top + jnp.log(total_w)
                o = jnp.concatenate(out_t, axis=0)
                attt_ref[pl.ds(first, 128), pl.ds(j * span, span)] = o
                att_ref[j, :, pl.ds(first, 128)] = jnp.transpose(o).astype(bf16)
                return 0

            lax.fori_loop(0, pairs, pair_step, 0)
            to_self = (z == j) & (c == seq_core)

            @pl.when(to_self)
            def _():
                a_own(j).start()

            @pl.when(jnp.logical_not(to_self))
            def _():
                a_out(j).start()

        for s in range(seqs):
            for k in range(2):
                from_self = (2 * c + s == z) & (c == k)

                @pl.when(from_self)
                def _():
                    a_own(0).wait()

                @pl.when(jnp.logical_not(from_self))
                def _():
                    remote(att_ref.at[0], t_ref.at[s, k], asend.at[0], arecv.at[s, k], z, base).wait_recv()

        for s in range(seqs):
            r = pl.ds(s * span, span)
            branch = dot(t_ref[s, 0], wo_ref[0:half]) + dot(t_ref[s, 1], wo_ref[half:])
            v = hid_ref[s].reshape(span, width).astype(f32) + branch
            mid_ref[r, :] = v
            centered = v - jnp.mean(v, axis=-1, keepdims=True)
            inverse = lax.rsqrt(jnp.mean(centered * centered, axis=-1, keepdims=True) + epsilon)
            flat_ref[r, :] = (centered * inverse * g2_ref[...] + s2_ref[...]).astype(bf16)
        logits = dot(flat_ref[...], wr_ref[...])
        gate = jax.nn.sigmoid(jnp.sum(logits * onehot, axis=1, keepdims=True))
        gate_ref[...] = gate
        rows_ref[...] = (
            dot(to_slots, flat_ref[...]).astype(bf16).reshape(columns, capacity, width)
        )
        from_slots = lane_of((tokens, slots), 1).astype(f32) == slot_ref[...]
        scales = jnp.sum(jnp.where(from_slots, valid * gate, 0.0), axis=0, keepdims=True)
        if cap_lanes != capacity:
            sc_ref[...] = jnp.zeros_like(sc_ref)
        for t in range(columns):
            sc_ref[t, :, 0:capacity] = jnp.broadcast_to(
                scales[:, t * capacity : (t + 1) * capacity], (8, capacity)
            )

        for n, (to_z, to_e) in enumerate(column):
            remote(cown_ref, cgot_ref.at[to_z, lax.rem(to_e, 2)], ksend.at[n], krecv.at[to_z, lax.rem(to_e, 2)], z, sib).wait_recv()
            k_out(n, to_z, to_e).wait_send()
        cgot_ref[z, c] = cown_ref[...]
        tot = jnp.zeros((8, 128), f32)
        for zs in range(blocks):
            for k in range(2):
                tot = tot + cgot_ref[zs, k]
        cnt_ref[...] = tot
        c_own.wait()
        for t in plane:
            c_out(t).wait_send()
            remote(cots_ref.at[t], cote_ref.at[t], csend.at[t], crecv.at[t], z, e).wait_recv()
        for s in range(seqs):
            for k in range(2):

                @pl.when(jnp.logical_not((2 * c + s == z) & (c == k)))
                def _():
                    n_out(s, k).wait_send()

        for zs in [z] + others:
            n_sib(zs).wait_send()
        for j in range(blocks):

            @pl.when(jnp.logical_not((z == j) & (c == seq_core)))
            def _():
                a_out(j).wait_send()

        for i in range(2):
            b_out(i).wait()

            @pl.when(z < blocks - 1)
            def _():
                h_out(i, 1).wait_send()
                src, dst = ((wi_ref, li_ref), (we_ref, lo_ref))[i]
                remote(src, dst.at[1], hsend.at[i, 1], hrecv.at[i, 1], z, e).wait_recv()

            @pl.when(z > 0)
            def _():
                h_out(i, -1).wait_send()
                src, dst = ((wi_ref, li_ref), (we_ref, lo_ref))[i]
                remote(src, dst.at[0], hsend.at[i, 0], hrecv.at[i, 0], z, e).wait_recv()

    out_shapes = [
        ((blocks, 2, hs, width), bf16),
        ((width, 3 * half), bf16),
        ((blocks, span, 3 * half), bf16),
        ((half, total), f32),
        ((2 * pairs, total), f32),
        ((seqs, 2, span, half), bf16),
        ((tokens, width), f32),
        ((tokens, width), bf16),
        ((tokens, 1), f32),
        ((tokens, 1), f32),
        ((columns, capacity, width), bf16),
        ((columns, 8, cap_lanes), f32),
        ((columns, capacity, width), bf16),
        ((8, 128), jnp.int32),
        ((8, 128), f32),
        ((2, width, part), bf16),
        ((2, part, width), bf16),
        ((width, part), bf16),
        ((part, width), bf16),
    ]
    return pl.pallas_call(
        kernel,
        name="forward",
        out_shape=[jax.ShapeDtypeStruct(a, b) for a, b in out_shapes],
        in_specs=[VMEM] * 6 + [ANY] * 3 + [VMEM] * 4 + [ANY] * 2,
        out_specs=[VMEM] * 12 + [ANY] + [VMEM] * 2 + [ANY] * 4,
        scratch_shapes=[
            pltpu.VMEM((seqs, 2, hs, width), bf16),
            pltpu.VMEM((2 * pairs, total, 128), bf16),
            pltpu.VMEM((half, total), bf16),
            pltpu.VMEM((blocks, span, half), bf16),
            pltpu.VMEM((columns, capacity, width), bf16),
            pltpu.VMEM((seqs, 8, 128), jnp.int32),
            pltpu.VMEM((8, 128), f32),
            pltpu.VMEM((blocks, 2, 8, 128), f32),
            DMA((3,)),
            DMA,
            DMA((seqs, 2)),
            DMA((blocks,)),
            DMA((blocks,)),
            DMA((blocks,)),
            DMA,
            DMA((blocks,)),
            DMA((seqs, 2)),
            DMA,
            DMA((columns,)),
            DMA((columns,)),
            DMA,
            DMA,
            DMA((2 * blocks - 1,)),
            DMA((blocks, 2)),
            DMA((2, 2)),
            DMA((2, 2)),
            DMA((2,)),
            DMA((2,)),
        ],
        compiler_params=params(1),
    )(
        hidden.reshape(seqs, 2, hs, width), cotangent.reshape(tokens, width),
        gain_one.reshape(1, width), shift_one.reshape(1, width), gain_two.reshape(1, width), shift_two.reshape(1, width),
        w_query, w_key, w_value, w_output, w_router, ids, lengths, w_inner, w_outer,
    )


def slice_order(z):
    return [z, z + 1 - 2 * lax.rem(z, 2), jnp.where(z < 2, 2, 1), jnp.where(z < 2, 3, 0)]


def experts(rows, scales, cot, counts, w_inner, w_outer, sib_inner, sib_outer, near_inner, near_outer, blocks):
    columns, capacity, width = rows.shape
    cap_lanes = scales.shape[2]
    total = columns * capacity
    part = w_inner.shape[1]
    block = 256
    count = total // block
    per = block // capacity
    assert blocks == 4 and columns == count * per

    def kernel(*refs):
        rows_ref, sc_ref, cot_ref, cnt_ref, wi_ref, we_ref, bi_ref, bo_ref, li_ref, lo_ref = refs[:10]
        back_ref, dots_ref, made_ref, tot_ref, gi_ref, go_ref, ei_ref, eo_ref = refs[10:18]
        (
            x_ref, xt_ref, d_ref, scg_ref, cntg_ref, in_ref, out_ref, oacc, dacc, act_ref, dpre_ref,
            dr_ref, dots_own, sgi_ref, sgo_ref, ggi_ref, ggo_ref,
            xloc, xsend, xrecv, scsend, screcv, ksend, krecv, wloc, wsend, wrecv, vsend, vrecv,
            bloc, dsend, drecv, gsend, grecv, ssend, srecv,
        ) = refs[18:]
        z, e, c, base = place()
        col = e // 2
        sib = base + 1 - c
        inner = (z > 0) & (z < blocks - 1)
        end = jnp.logical_not(inner)
        plane = [lax.rem(col + step, columns) for step in range(1, columns)]
        greet(column_partners(blocks, z, c, base) + [(z, 2 * t + c) for t in plane])

        def x_out(t):
            return remote(rows_ref.at[t], x_ref.at[col], xsend.at[t], xrecv.at[col], z, 2 * t + c)

        def sc_out(t):
            return remote(sc_ref.at[t], scg_ref.at[col], scsend.at[t], screcv.at[col], z, 2 * t + c)

        def cnt_out(t):
            return remote(cnt_ref, cntg_ref.at[col], ksend.at[t], krecv.at[col], z, 2 * t + c)

        x_own = pltpu.make_async_copy(rows_ref.at[col], x_ref.at[col], xloc)
        x_own.start()
        for t in plane:
            sc_out(t).start()
            x_out(t).start()
            cnt_out(t).start()
        scg_ref[col] = sc_ref[col]
        cntg_ref[col] = cnt_ref[...]

        lo_half, hi_half = pl.ds(0, part), pl.ds(part, part)

        def views(s, which):
            return (in_ref.at[s, :, which], out_ref.at[s, which])

        sources = ((wi_ref, we_ref), (bi_ref, bo_ref))

        def w_own(i, k):
            return pltpu.make_async_copy(
                sources[k][i], views(z, (lo_half, hi_half)[k])[i], wloc.at[i, k]
            )

        def w_near(i, side):
            s = z - 1 if side == 0 else z + 1
            return pltpu.make_async_copy((li_ref, lo_ref)[i].at[side], views(s, lo_half)[i], wloc.at[i, 2 + side])

        def w_near_sib(i, side):
            s = z - 1 if side == 0 else z + 1
            return remote(
                (li_ref, lo_ref)[i].at[side], views(s, hi_half)[i], vsend.at[i, s], vrecv.at[i, s], z, sib
            )

        def w_pass(i, side):
            s = z - 1 if side == 0 else z + 1
            to = z + 1 if side == 0 else z - 1
            return remote((li_ref, lo_ref)[i].at[side], views(s, lo_half)[i], wsend.at[i, side], wrecv.at[i, s], to, e)

        def w_got(i, s):
            return remote(views(s, lo_half)[i], views(s, lo_half)[i], wsend.at[i, 0], wrecv.at[i, s], z, e)

        def w_sib(i, s):
            return remote(views(s, lo_half)[i], views(s, hi_half)[i], vsend.at[i, s], vrecv.at[i, s], z, sib)

        def w_last(i, s, to):
            return remote(views(s, lo_half)[i], views(s, lo_half)[i], wsend.at[i, 2], wrecv.at[i, s], to, e)

        def has(side):
            return z > 0 if side == 0 else z < blocks - 1

        for i in range(2):
            for k in range(2):
                w_own(i, k).start()
        for side in range(2):
            for i in range(2):

                @pl.when(inner)
                def _():
                    w_pass(i, side).start()

        for side in range(2):
            for i in range(2):

                @pl.when(has(side))
                def _():
                    w_near(i, side).start()
                    w_near_sib(i, side).start()

        hop_two = lax.rem(z + 2, blocks)
        order = slice_order(z)
        far = order[3]
        oacc[...] = jnp.zeros_like(oacc)
        dacc[...] = jnp.zeros_like(dacc)
        first_block = col // per

        def at_block(b):
            return pl.ds(pl.multiple_of(b * per, per), per)

        def row_step(s, b, fresh):
            x_b = x_ref[at_block(b)].reshape(block, width)
            r = pl.ds(pl.multiple_of(b * block, block), block)
            if fresh:
                row = jnp.concatenate(
                    [scg_ref[b * per + i, :, 0:capacity] for i in range(per)], axis=1
                )
                column = jnp.transpose(row)[:, 0:1]
                cots = cot_ref[at_block(b)].reshape(block, width).astype(f32)
                d_ref[r, :] = (column * cots).astype(bf16)
            pre = dot(x_b, in_ref[s])
            cdf = 0.5 * (1.0 + lax.erf(pre * (0.5**0.5)))
            act = (pre * cdf).astype(bf16)
            slope = cdf + pre * (jnp.exp(-0.5 * pre * pre) * ((2 * jnp.pi) ** -0.5))
            d_act = dot_nt(d_ref[r, :], out_ref[s])
            d_pre = (d_act * slope).astype(bf16)
            act_ref[r, :] = act
            dpre_ref[r, :] = d_pre
            oacc[r, :] += dot(act, out_ref[s])
            dacc[r, :] += dot_nt(d_pre, in_ref[s])

        def grads(s):
            g_inner = dot(xt_ref[...], dpre_ref[...])
            gi_ref[s] = g_inner[:, :part].astype(bf16)
            sgi_ref[s] = g_inner[:, part:].astype(bf16)
            g_outer = dot_tn(act_ref[...], d_ref[...])
            go_ref[s] = g_outer[:part].astype(bf16)
            sgo_ref[s] = g_outer[part:].astype(bf16)
            for i in range(2):
                g_sib(i, s).start()

        def g_sib(i, s):
            src, dst = ((sgi_ref, ggi_ref), (sgo_ref, ggo_ref))[i]
            return remote(src.at[s], dst.at[s], gsend.at[i, s], grecv.at[i, s], z, sib)

        def join(s):
            for i, (total_ref, got_ref) in enumerate(((gi_ref, ggi_ref), (go_ref, ggo_ref))):
                g_sib(i, s).wait_recv()
                total_ref[s] = (total_ref[s].astype(f32) + got_ref[s].astype(f32)).astype(bf16)

        def s_out(i, s):
            src, dst = ((gi_ref, ei_ref), (go_ref, eo_ref))[i]
            return remote(src.at[s], dst.at[z], ssend.at[i, s], srecv.at[i, z], s, e)

        def block_at(m):
            return lax.rem(first_block + count - m, count)

        for i in range(2):
            for k in range(2):
                w_own(i, k).wait()
        for m in range(count):
            b = block_at(m)
            for i in range(per):
                t = b * per + i

                @pl.when(t == col)
                def _():
                    x_own.wait()

                @pl.when(t != col)
                def _():
                    remote(sc_ref.at[0], scg_ref.at[t], scsend.at[t], screcv.at[t], z, e).wait_recv()
                    remote(rows_ref.at[0], x_ref.at[t], xsend.at[t], xrecv.at[t], z, e).wait_recv()

            row_step(order[0], b, True)
        xt_ref[...] = jnp.transpose(x_ref[...].reshape(total, width))
        grads(order[0])

        for i in range(2):
            for side in range(2):

                @pl.when(has(side))
                def _():
                    w_near(i, side).wait()
                    remote(
                        li_ref.at[0] if i == 0 else lo_ref.at[0],
                        views(z - 1 if side == 0 else z + 1, hi_half)[i],
                        vsend.at[i, z],
                        vrecv.at[i, z - 1 if side == 0 else z + 1],
                        z,
                        sib,
                    ).wait_recv()

        def loop(s):
            def body(b, _):
                row_step(s, b, False)
                return 0

            lax.fori_loop(0, count, body, 0)

        loop(order[1])
        for i in range(2):
            w_got(i, hop_two).wait_recv()
            w_sib(i, hop_two).start()

            @pl.when(inner)
            def _():
                w_last(i, hop_two, jnp.where(z == 1, 0, blocks - 1)).start()

        grads(order[1])
        join(order[0])
        for i in range(2):
            remote(
                views(hop_two, lo_half)[i], views(hop_two, hi_half)[i], vsend.at[i, z], vrecv.at[i, hop_two], z, sib
            ).wait_recv()
        loop(order[2])

        @pl.when(end)
        def _():
            for i in range(2):
                w_got(i, far).wait_recv()
                w_sib(i, far).start()

        grads(order[2])
        join(order[1])
        for i in range(2):
            s_out(i, order[1]).start()

        @pl.when(end)
        def _():
            for i in range(2):
                remote(
                    views(far, lo_half)[i], views(far, hi_half)[i], vsend.at[i, z], vrecv.at[i, far], z, sib
                ).wait_recv()

        def d_out(t):
            return remote(dr_ref.at[t], back_ref.at[col], dsend.at[0, t], drecv.at[0, col], z, 2 * t + c)

        def dots_out(t):
            return remote(dots_own.at[t], dots_ref.at[col], dsend.at[1, t], drecv.at[1, col], z, 2 * t + c)

        b_own = pltpu.make_async_copy(dr_ref.at[col], back_ref.at[col], bloc)
        for m in list(range(1, count)) + [0]:
            b = block_at(m)
            row_step(order[3], b, False)
            if m == 1:
                join(order[2])
                s_out(0, order[2]).start()
            r = pl.ds(pl.multiple_of(b * block, block), block)
            made = oacc[r, :].astype(bf16)
            made_ref[at_block(b)] = made.reshape(per, capacity, width)
            dr_ref[at_block(b)] = dacc[r, :].astype(bf16).reshape(per, capacity, width)
            cots = cot_ref[at_block(b)].reshape(block, width).astype(f32)
            sums = jnp.sum(cots * made.astype(f32), axis=1, keepdims=True)
            row = jnp.transpose(jnp.broadcast_to(sums, (block, 128)))[0:8]
            for i in range(per):
                t = b * per + i
                if cap_lanes != capacity:
                    dots_own[t] = jnp.zeros((8, cap_lanes), f32)
                dots_own[t, :, 0:capacity] = row[:, i * capacity : (i + 1) * capacity]

                @pl.when(t == col)
                def _():
                    b_own.start()
                    dots_ref[t] = dots_own[t]

                @pl.when(t != col)
                def _():
                    d_out(t).start()
                    dots_out(t).start()

        grads(order[3])
        join(order[3])

        for t in plane:
            x_out(t).wait_send()
            sc_out(t).wait_send()
            cnt_out(t).wait_send()
            remote(cnt_ref, cntg_ref.at[t], ksend.at[t], krecv.at[t], z, e).wait_recv()
        tot = cntg_ref[0]
        for t in range(1, columns):
            tot = tot + cntg_ref[t]
        tot_ref[...] = tot
        for i in range(2):
            for side in range(2):

                @pl.when(has(side))
                def _():
                    w_near_sib(i, side).wait_send()

                @pl.when(inner)
                def _():
                    w_pass(i, side).wait_send()

            w_sib(i, hop_two).wait_send()

            @pl.when(inner)
            def _():
                w_last(i, hop_two, z).wait_send()

            @pl.when(end)
            def _():
                w_sib(i, far).wait_send()

            for s in range(blocks):
                g_sib(i, s).wait_send()
            s_out(i, order[1]).wait_send()
            got = (ei_ref, eo_ref)[i]
            remote(got.at[0], got.at[order[1]], ssend.at[i, 0], srecv.at[i, order[1]], z, e).wait_recv()
        s_out(0, order[2]).wait_send()

        @pl.when(inner)
        def _():
            for k in range(2):
                zs = lax.rem(2 * (z // 2) + 2 + k, blocks)
                remote(ei_ref.at[0], ei_ref.at[zs], ssend.at[0, 0], srecv.at[0, zs], z, e).wait_recv()

        b_own.wait()
        for t in plane:
            d_out(t).wait_send()
            dots_out(t).wait_send()
            remote(dr_ref.at[0], back_ref.at[t], dsend.at[0, t], drecv.at[0, t], z, e).wait_recv()
            remote(dots_own.at[0], dots_ref.at[t], dsend.at[1, t], drecv.at[1, t], z, e).wait_recv()

    out_shapes = [
        ((columns, capacity, width), bf16),
        ((columns, 8, cap_lanes), f32),
        ((columns, capacity, width), bf16),
        ((8, 128), f32),
        ((blocks, width, part), bf16),
        ((blocks, part, width), bf16),
        ((blocks, width, part), bf16),
        ((blocks, part, width), bf16),
    ]
    return pl.pallas_call(
        kernel,
        name="experts",
        out_shape=[jax.ShapeDtypeStruct(a, b) for a, b in out_shapes],
        in_specs=[VMEM] * 4 + [ANY] * 6,
        out_specs=[VMEM] * 6 + [ANY] * 2,
        scratch_shapes=[
            pltpu.VMEM((columns, capacity, width), bf16),
            pltpu.VMEM((width, total), bf16),
            pltpu.VMEM((total, width), bf16),
            pltpu.VMEM((columns, 8, cap_lanes), f32),
            pltpu.VMEM((columns, 8, 128), f32),
            pltpu.VMEM((blocks, width, 2 * part), bf16),
            pltpu.VMEM((blocks, 2 * part, width), bf16),
            pltpu.VMEM((total, width), f32),
            pltpu.VMEM((total, width), f32),
            pltpu.VMEM((total, 2 * part), bf16),
            pltpu.VMEM((total, 2 * part), bf16),
            pltpu.VMEM((columns, capacity, width), bf16),
            pltpu.VMEM((columns, 8, cap_lanes), f32),
            pltpu.VMEM((blocks, width, part), bf16),
            pltpu.VMEM((blocks, part, width), bf16),
            pltpu.VMEM((blocks, width, part), bf16),
            pltpu.VMEM((blocks, part, width), bf16),
            DMA,
            DMA((columns,)),
            DMA((columns,)),
            DMA((columns,)),
            DMA((columns,)),
            DMA((columns,)),
            DMA((columns,)),
            DMA((2, 4)),
            DMA((2, 3)),
            DMA((2, blocks)),
            DMA((2, blocks)),
            DMA((2, blocks)),
            DMA,
            DMA((2, columns)),
            DMA((2, columns)),
            DMA((2, blocks)),
            DMA((2, blocks)),
            DMA((2, blocks)),
            DMA((2, blocks)),
        ],
        compiler_params=params(2),
    )(rows, scales, cot, counts, w_inner, w_outer, sib_inner, sib_outer, near_inner, near_outer)


class PieceSum:
    def __init__(self, at, part, got1, got2, got3, gotr, full, sem, rsem, zsem, zrsem, order):
        self.at, self.part, self.full = at, part, full
        self.got1, self.got2, self.got3, self.gotr = got1, got2, got3, gotr
        self.sem, self.rsem, self.zsem, self.zrsem = sem, rsem, zsem, zrsem
        z, e, c, bit, mate, blocks, sib = at
        self.first, self.second = order
        self.rest = len(bit) - 2

    def swap(self, n, src, dst, e):
        return remote(src, dst, self.sem.at[n], self.rsem.at[n], self.at[0], e)

    def halves(self):
        z, e, c, bit, mate, blocks, sib = self.at
        return self.swap(0, self.part.at[1 - bit[self.first]], self.got1, mate[self.first])

    def quarters(self):
        z, e, c, bit, mate, blocks, sib = self.at
        b1, b2 = bit[self.first], bit[self.second]
        return self.swap(1, self.part.at[b1, 1 - b2], self.got2, mate[self.second])

    def to_z(self, zt):
        z, e, c, bit, mate, blocks, sib = self.at
        b1, b2 = bit[self.first], bit[self.second]
        return remote(
            self.part.at[b1, b2, zt], self.got3.at[z], self.zsem.at[0, zt], self.zrsem.at[0, z], zt, e
        )

    def own(self):
        z, e, c, bit, mate, blocks, sib = self.at
        return self.full.at[c, bit[self.first], bit[self.second], z]

    def back_z(self, zt):
        z, e, c, bit, mate, blocks, sib = self.at
        return remote(self.own(), self.own(), self.zsem.at[1, zt], self.zrsem.at[1, z], zt, e)

    def back_quarter(self):
        z, e, c, bit, mate, blocks, sib = self.at
        at = self.full.at[c, bit[self.first], bit[self.second]]
        return self.swap(2, at, at, mate[self.second])

    def back_half(self):
        z, e, c, bit, mate, blocks, sib = self.at
        at = self.full.at[c, bit[self.first]]
        return self.swap(3, at, at, mate[self.first])

    def to_sibling(self):
        z, e, c, bit, mate, blocks, sib = self.at
        return self.swap(4, self.full.at[c], self.full.at[c], sib)

    def step(self, n):
        z, e, c, bit, mate, blocks, sib = self.at
        b1, b2 = bit[self.first], bit[self.second]
        others = [lax.rem(z + step, blocks) for step in range(1, blocks)]
        if n == 0:
            self.halves().start()
        elif n == 1:
            self.halves().wait()
            self.part[b1] = (self.part[b1].astype(f32) + self.got1[...].astype(f32)).astype(bf16)
            self.quarters().start()
        elif n == 2:
            self.quarters().wait()
            self.part[b1, b2] = (self.part[b1, b2].astype(f32) + self.got2[...].astype(f32)).astype(bf16)
            for zt in others:
                self.to_z(zt).start()
        elif n == 3:
            for zs in others:
                remote(
                    self.got3.at[0], self.got3.at[zs], self.zsem.at[0, zs], self.zrsem.at[0, zs], z, e
                ).wait_recv()
            for zt in others:
                self.to_z(zt).wait_send()
            self.got3[z] = self.part[b1, b2, z]
            total = self.got3[0].astype(f32)
            for j in range(1, blocks):
                total = total + self.got3[j].astype(f32)
            own = self.own()
            own[...] = total.astype(bf16)
            for r in range(self.rest):
                copy = self.swap(5 + r, own, self.gotr.at[r], mate[2 + r])
                copy.start()
                copy.wait()
                own[...] = (own[...].astype(f32) + self.gotr[r].astype(f32)).astype(bf16)
            for zt in others:
                self.back_z(zt).start()
        elif n == 4:
            for zs in others:
                at = self.full.at[c, b1, b2, zs]
                remote(at, at, self.zsem.at[1, zs], self.zrsem.at[1, zs], z, e).wait_recv()
            for zt in others:
                self.back_z(zt).wait_send()
            self.back_quarter().start()
        elif n == 5:
            self.back_quarter().wait()
            self.back_half().start()
        elif n == 6:
            self.back_half().wait()
            self.to_sibling().start()
        elif n == 7:
            self.to_sibling().wait()

    @staticmethod
    def scratch(blocks, piece, lanes, rest):
        return [
            pltpu.VMEM((2, 2, blocks, piece, lanes), bf16),
            pltpu.VMEM((2, blocks, piece, lanes), bf16),
            pltpu.VMEM((blocks, piece, lanes), bf16),
            pltpu.VMEM((blocks, piece, lanes), bf16),
            pltpu.VMEM((max(1, rest), piece, lanes), bf16),
            DMA((5 + rest,)),
            DMA((5 + rest,)),
            DMA((2, blocks)),
            DMA((2, blocks)),
        ]


def backward(
    rows, weights, qkv, att_t, lse, length, attended, middle, flat, gate, slot, ids, lengths, cotangent,
    back, dots, counts, made, hidden, gain_one, gain_two, w_output, w_router, g_inner, g_outer, e_inner, e_outer,
    experts_n,
):
    total, width = rows.shape
    half = weights.shape[1] // 3
    pairs = half // 128
    seqs, _, span, _ = attended.shape
    blocks = total // span
    columns, capacity, _ = back.shape
    slots = columns * capacity
    tokens = seqs * span
    hs = span // 2
    scale = HEAD**-0.5
    part = g_inner.shape[2]
    bits = columns.bit_length() - 1
    assert columns == 1 << bits and bits >= 2 and blocks == 4
    rest = bits - 2
    small_rows = -(-(5 + experts_n) // 8) * 8
    out_piece, pair_piece = width // (4 * blocks), 3 * width // (4 * blocks)
    n_sum = 9

    def kernel(*refs):
        (
            x_ref, w_ref, qkv_ref, attt_ref, lse_ref, len_ref, t_ref, mid_ref, flat_ref, gate_ref, slot_ref, ids_ref,
            lens_ref, cot_ref, back_ref, dots_ref, cnt_ref, made_ref, hid_ref, g1_ref, g2_ref, wo_ref, wr_ref,
            gi_ref, go_ref, ei_ref, eo_ref,
        ) = refs[:27]
        gout_ref, gpair_ref, sums_ref, fi_ref, fo_ref, gh_ref, y_ref = refs[27:34]
        (
            do_ref, dqkv_ref, kt_ref, dk_ref, dv_ref, xt_ref, dn_ref, dsib_ref, dsum_ref, dnt_ref,
            zi, zo, osib, sgot, szgot, datt_ref, op_ref, dmid_ref, mg_ref,
            loc_sem, dsend, drecv, rloc, rsend, rrecv,
            nsend, nrecv, ssend, srecv, osend, orecv, tsend, trecv, tzsend, tzrecv, msend, mrecv,
        ) = refs[34:71]
        sums_scratch = refs[71:]
        z, e, c, base = place()
        col = e // 2
        sib = base + 1 - c
        seq_core, seq = z // 2, lax.rem(z, 2)
        bit = [lax.rem(col // (1 << i), 2) for i in range(bits)]
        mate = [2 * (col + (1 - 2 * bit[i]) * (1 << i)) + c for i in range(bits)]
        others = [lax.rem(z + step, blocks) for step in range(1, blocks)]
        plane = [lax.rem(col + step, columns) for step in range(1, columns)]
        inner = (z > 0) & (z < blocks - 1)
        order = slice_order(z)
        across = [lax.rem(2 * (z // 2) + 2 + k, blocks) for k in range(2)]
        greet(column_partners(blocks, z, c, base) + [(z, 2 * t + c) for t in plane])

        def m_out(t):
            return remote(made_ref.at[t], mg_ref.at[col], msend.at[t], mrecv.at[col], z, 2 * t + c)

        m_own = pltpu.make_async_copy(made_ref.at[col], mg_ref.at[col], loc_sem.at[2])
        m_own.start()
        for t in plane:
            m_out(t).start()

        def r_z(i, s):
            src, dst = ((gi_ref, zi), (go_ref, zo))[i]
            return remote(src.at[s], dst.at[z], rsend.at[i, s], rrecv.at[i, z], s, e)

        def r_loc(i, n):
            s = [z, order[1], across[0], across[1]][n]
            src = ((gi_ref, ei_ref), (go_ref, eo_ref))[i][0 if n == 0 else 1]
            return pltpu.make_async_copy(src.at[s], (zi, zo)[i].at[s], rloc.at[i, n])

        r_z(1, order[2]).start()
        for i in range(2):
            for n in range(2):
                r_loc(i, n).start()

        @pl.when(inner)
        def _():
            r_loc(0, 2).start()
            r_loc(0, 3).start()

        lane = lane_of((tokens, 128), 1)
        onehot = (lane == ids_ref[...]).astype(f32)
        place_in = z * span + lane_of((span, 1), 0)
        valid = jnp.concatenate(
            [(place_in < lens_ref[s, 0:1, 0:1]).astype(f32) for s in range(seqs)], axis=0
        )
        from_slots = lane_of((tokens, slots), 1).astype(f32) == slot_ref[...]
        dots_row = jnp.concatenate([dots_ref[t, 0:1, 0:capacity] for t in range(columns)], axis=1)
        dot_rows = jnp.sum(jnp.where(from_slots, dots_row, 0.0), axis=1, keepdims=True)
        picks = from_slots.astype(f32).astype(bf16)
        d_rows = dot(picks, back_ref[...].reshape(slots, width))
        count_row = cnt_ref[0:1]
        mean_load = jnp.sum(count_row, axis=1, keepdims=True) / experts_n
        ratio_rows = jnp.sum(onehot * ((count_row - mean_load) / mean_load), axis=1, keepdims=True)
        gates = gate_ref[...]
        d_gate = valid * (dot_rows + balance_weight * ratio_rows)
        d_logits = (onehot * (d_gate * gates * (1.0 - gates))).astype(bf16)
        router_t = dot_tn(d_logits, flat_ref[...])
        balance_part = jnp.sum(valid * gates * ratio_rows, axis=0, keepdims=True)
        gain_sum = jnp.zeros((1, width), f32)
        shift_sum = jnp.zeros((1, width), f32)
        for s in range(seqs):
            lo, hi = s * span, (s + 1) * span
            v = mid_ref[lo:hi]
            centered = v - jnp.mean(v, axis=-1, keepdims=True)
            inverse = lax.rsqrt(jnp.mean(centered * centered, axis=-1, keepdims=True) + epsilon)
            unit = centered * inverse
            dy = d_rows[lo:hi] + dot_nt(d_logits[lo:hi], wr_ref[...])
            gain_sum = gain_sum + jnp.sum(dy * unit, axis=0, keepdims=True)
            shift_sum = shift_sum + jnp.sum(dy, axis=0, keepdims=True)
            du = dy * g2_ref[...]
            dx = inverse * (
                du
                - jnp.mean(du, axis=-1, keepdims=True)
                - unit * jnp.mean(du * unit, axis=-1, keepdims=True)
            )
            dmid_ref[lo:hi] = cot_ref[lo:hi].astype(f32) + dx
            d_branch = dmid_ref[lo:hi].astype(bf16)
            for k in range(2):
                datt_ref[s, k] = dot_nt(d_branch, wo_ref[k * half : (k + 1) * half]).astype(bf16)

        at = (z, e, c, bit, mate, blocks, sib)
        out_sum = PieceSum(at, *sums_scratch[0:5], gout_ref, *sums_scratch[5:9], (0, 1))
        pair_sums = [
            PieceSum(
                at,
                *sums_scratch[n_sum * (p + 1) : n_sum * (p + 1) + 5],
                gpair_ref.at[p],
                *sums_scratch[n_sum * (p + 1) + 5 : n_sum * (p + 2)],
                (1, 0) if p % 2 == 0 else (0, 1),
            )
            for p in range(pairs)
        ]

        def d_out(s, k):
            return remote(
                datt_ref.at[s, k], do_ref.at[z], dsend.at[s, k], drecv.at[z], 2 * c + s, base + k
            )

        def d_own(s, k):
            return pltpu.make_async_copy(datt_ref.at[s, k], do_ref.at[z], loc_sem.at[0])

        for s in range(seqs):
            for k in range(2):
                to_self = (2 * c + s == z) & (c == k)

                @pl.when(to_self)
                def _():
                    d_own(s, k).start()

                @pl.when(jnp.logical_not(to_self))
                def _():
                    d_out(s, k).start()

        sums_ref[...] = jnp.zeros_like(sums_ref)
        sums_ref[2:3] = gain_sum
        sums_ref[3:4] = shift_sum
        sums_ref[4 : 4 + experts_n] = router_t[0:experts_n]
        sums_ref[4 + experts_n : 5 + experts_n] = jnp.broadcast_to(balance_part, (1, width))
        d_branch = dmid_ref[...].astype(bf16)
        for k in range(2):
            att_k = jnp.concatenate([t_ref[s, k] for s in range(seqs)], axis=0)
            made_k = dot_tn(att_k, d_branch).astype(bf16)
            op_ref[0, k * half : (k + 1) * half] = made_k[:, :half]
            op_ref[1, k * half : (k + 1) * half] = made_k[:, half:]
        o_first = remote(op_ref.at[1 - c], osib, osend, orecv, z, sib)
        o_first.start()
        xt_ref[...] = jnp.transpose(x_ref[...])
        o_first.wait()
        out_sum.part[...] = (op_ref[c].astype(f32) + osib[...].astype(f32)).astype(bf16).reshape(
            2, 2, blocks, out_piece, half
        )
        out_sum.step(0)

        @pl.when(c == seq_core)
        def _():
            d_own(0, 0).wait()

        @pl.when(c != seq_core)
        def _():
            remote(datt_ref.at[0, 0], do_ref.at[z], dsend.at[0, 0], drecv.at[z], z, base).wait_recv()

        for zs in others:
            remote(datt_ref.at[0, 0], do_ref.at[zs], dsend.at[0, 0], drecv.at[zs], z, base).wait_recv()

        r_z(0, order[3]).start()
        key_bias = jnp.where(lane_of((total, 1), 0) < len_ref[0:1, 0:1], 0.0, masked_fill)
        lane = lane_of((1, 128), 1)
        later = lax.broadcasted_iota(jnp.int32, (span, span), 0) > lax.broadcasted_iota(
            jnp.int32, (span, span), 1
        )

        def pair_step(p):
            first = p * 128
            k_all = qkv_ref[:, pl.ds(half + first, 128)]
            kt_ref[...] = jnp.transpose(k_all)
            v_all = qkv_ref[:, pl.ds(2 * half + first, 128)]
            k_heads = key_heads(k_all, key_bias)
            dk_ref[...] = jnp.zeros_like(dk_ref)
            dv_ref[...] = jnp.zeros_like(dv_ref)
            for j in range(blocks):
                n = (j + 1) * span
                r = pl.ds(j * span, span)
                q = qkv_ref[r, pl.ds(first, 128)].astype(f32) * scale
                d_o = do_ref[j, :, pl.ds(first, 128)].astype(f32)
                prod_t = jnp.transpose(d_o) * attt_ref[pl.ds(first, 128), r]
                dq_t = []
                for h in range(2):
                    inside = (lane // HEAD) == h
                    spare = lane == (1 - h) * HEAD
                    q_h = jnp.where(inside, q, jnp.where(spare, 1.0, 0.0)).astype(bf16)
                    q_only = jnp.where(inside, q, 0.0).astype(bf16)
                    do_h = jnp.where(inside, d_o, 0.0).astype(bf16)
                    delta = jnp.sum(prod_t[h * HEAD : (h + 1) * HEAD], axis=0, keepdims=True)
                    s = dot_nt(k_heads[h][:n], q_h)
                    last = jnp.where(later, masked_fill, s[n - span :])
                    s = last if j == 0 else jnp.concatenate([s[: n - span], last], axis=0)
                    w = jnp.exp(s - lse_ref[pl.ds(2 * p + h, 1), r])
                    d_w = dot_nt(v_all[:n], do_h)
                    d_s = (w * (d_w - delta)).astype(bf16)
                    dv_ref[:n] += dot(w.astype(bf16), do_h)
                    dk_ref[:n] += dot(d_s, q_only)
                    dq_t.append(dot(kt_ref[h * HEAD : (h + 1) * HEAD, :n], d_s))
                dq = jnp.transpose(jnp.concatenate(dq_t, axis=0)) * scale
                dqkv_ref[r, pl.ds(first, 128)] = dq.astype(bf16)
            dqkv_ref[:, pl.ds(half + first, 128)] = dk_ref[...].astype(bf16)
            dqkv_ref[:, pl.ds(2 * half + first, 128)] = dv_ref[...].astype(bf16)
            joined = jnp.concatenate(
                [dqkv_ref[:, pl.ds(m * half + first, 128)] for m in range(3)], axis=1
            )
            grads = dot(xt_ref[...], joined).astype(bf16)
            pair_sums[p].part[...] = jnp.concatenate(
                [grads[:, m * 128 : (m + 1) * 128] for m in range(3)], axis=0
            ).reshape(2, 2, blocks, pair_piece, 128)

        todo = [(out_sum, 1)]

        def advance(limit=7):
            nexts = []
            for one, n in todo:
                if n <= limit:
                    one.step(n)
                    n += 1
                if n <= 7:
                    nexts.append((one, n))
            todo[:] = nexts

        for p in range(pairs):
            pair_step(p)
            advance(1)
            pair_sums[p].step(0)
            todo.append((pair_sums[p], 1))

        for j in range(blocks):
            r = pl.ds(j * span, span)
            dn_ref[j] = dot_nt(dqkv_ref[r, :], w_ref[...]).astype(bf16).reshape(2, hs, width)

        def n_sib(j):
            return remote(dn_ref.at[j, 1 - c], dsib_ref.at[j], nsend.at[j], nrecv.at[j], z, sib)

        def n_out(j):
            return remote(
                dsum_ref.at[j], dnt_ref.at[seq, c], ssend.at[j], srecv.at[seq, c], j, base + seq_core
            )

        def n_own():
            return pltpu.make_async_copy(dsum_ref.at[z], dnt_ref.at[seq, c], loc_sem.at[1])

        n_order = others[1:2] + others[0:1] + others[2:] + [z]
        for j in n_order:
            n_sib(j).start()
        for i, j in enumerate(n_order):
            n_sib(j).wait_recv()
            dsum_ref[j] = (dn_ref[j, c].astype(f32) + dsib_ref[j].astype(f32)).astype(bf16)
            if i < blocks - 1:
                n_out(j).start()
            else:

                @pl.when(seq_core == c)
                def _():
                    n_own().start()

                @pl.when(seq_core != c)
                def _():
                    n_out(j).start()

        advance(2)
        r_z(1, order[3]).start()
        for t in plane:
            remote(made_ref.at[0], mg_ref.at[t], msend.at[t], mrecv.at[t], z, e).wait_recv()
        m_own.wait()
        scaled = valid * gates
        expert_out = dot(picks, mg_ref[...].reshape(slots, width))
        y_ref[...] = (mid_ref[...] + scaled * expert_out).astype(bf16)
        advance(2)
        for s in range(seqs):
            for k in range(2):
                from_self = (2 * c + s == z) & (c == k)

                @pl.when(jnp.logical_not(from_self))
                def _():
                    remote(
                        dsum_ref.at[0], dnt_ref.at[s, k], ssend.at[0], srecv.at[s, k], z, base
                    ).wait_recv()

                @pl.when(from_self)
                def _():
                    n_own().wait()

        gains = g1_ref[...]
        gain_sum = jnp.zeros((1, width), f32)
        shift_sum = jnp.zeros((1, width), f32)
        for s in range(seqs):
            for k in range(2):
                v = hid_ref[s, k].astype(f32)
                centered = v - jnp.mean(v, axis=-1, keepdims=True)
                inverse = lax.rsqrt(jnp.mean(centered * centered, axis=-1, keepdims=True) + epsilon)
                unit = centered * inverse
                dy = dnt_ref[s, k].astype(f32)
                gain_sum = gain_sum + jnp.sum(dy * unit, axis=0, keepdims=True)
                shift_sum = shift_sum + jnp.sum(dy, axis=0, keepdims=True)
                du = dy * gains
                dx = inverse * (
                    du
                    - jnp.mean(du, axis=-1, keepdims=True)
                    - unit * jnp.mean(du * unit, axis=-1, keepdims=True)
                )
                gh_ref[s, k] = dmid_ref[(2 * s + k) * hs : (2 * s + k + 1) * hs] + dx

        sums_ref[0:1] = gain_sum
        sums_ref[1:2] = shift_sum

        def t_swap(n, te):
            return remote(sums_ref, sgot.at[n], tsend.at[n], trecv.at[n], z, te)

        partners = [sib] + mate
        for n, te in enumerate(partners):
            copy = t_swap(n, te)
            copy.start()
            if n in (1, 2):
                advance()
            copy.wait()
            sums_ref[...] = sums_ref[...] + sgot[n]

        def t_z(zt):
            return remote(sums_ref, szgot.at[z], tzsend.at[zt], tzrecv.at[z], zt, e)

        for zt in others:
            t_z(zt).start()
        advance()
        for zs in others:
            remote(sums_ref, szgot.at[zs], tzsend.at[zs], tzrecv.at[zs], z, e).wait_recv()
        for zt in others:
            t_z(zt).wait_send()
        szgot[z] = sums_ref[...]
        tot = szgot[0]
        for j in range(1, blocks):
            tot = tot + szgot[j]
        sums_ref[...] = tot

        advance()
        for i, (z_buf, final) in enumerate(((zi, fi_ref), (zo, fo_ref))):
            for n in range(2):
                r_loc(i, n).wait()
            for k in range(2):
                arrived = remote(z_buf.at[0], z_buf.at[across[k]], rsend.at[i, 0], rrecv.at[i, across[k]], z, e)
                if i == 0:

                    @pl.when(inner)
                    def _():
                        r_loc(0, 2 + k).wait()

                    @pl.when(jnp.logical_not(inner))
                    def _():
                        arrived.wait_recv()
                else:
                    arrived.wait_recv()
            acc = z_buf[0].astype(f32)
            for j in range(1, blocks):
                acc = acc + z_buf[j].astype(f32)
            final[...] = acc
            advance()
        while todo:
            advance()

        for s in range(seqs):
            for k in range(2):

                @pl.when(jnp.logical_not((2 * c + s == z) & (c == k)))
                def _():
                    d_out(s, k).wait_send()

        for j in n_order[:-1]:
            n_out(j).wait_send()

        @pl.when(seq_core != c)
        def _():
            n_out(z).wait_send()

        for j in n_order:
            n_sib(j).wait_send()
        r_z(1, order[2]).wait_send()
        for i in range(2):
            r_z(i, order[3]).wait_send()
        for t in plane:
            m_out(t).wait_send()

    stage = blocks
    scratch = [
        pltpu.VMEM((blocks, span, half), bf16),
        pltpu.VMEM((total, 3 * half), bf16),
        pltpu.VMEM((128, total), bf16),
        pltpu.VMEM((total, 128), f32),
        pltpu.VMEM((total, 128), f32),
        pltpu.VMEM((width, total), bf16),
        pltpu.VMEM((blocks, 2, hs, width), bf16),
        pltpu.VMEM((blocks, hs, width), bf16),
        pltpu.VMEM((blocks, hs, width), bf16),
        pltpu.VMEM((seqs, 2, hs, width), bf16),
        pltpu.VMEM((blocks, width, part), bf16),
        pltpu.VMEM((blocks, part, width), bf16),
        pltpu.VMEM((width, half), bf16),
        pltpu.VMEM((1 + bits, small_rows, width), f32),
        pltpu.VMEM((blocks, small_rows, width), f32),
        pltpu.VMEM((seqs, 2, span, half), bf16),
        pltpu.VMEM((2, width, half), bf16),
        pltpu.VMEM((tokens, width), f32),
        pltpu.VMEM((columns, capacity, width), bf16),
        DMA((3,)),
        DMA((seqs, 2)),
        DMA((stage,)),
        DMA((2, 4)),
        DMA((2, stage)),
        DMA((2, stage)),
        DMA((stage,)),
        DMA((stage,)),
        DMA((stage,)),
        DMA((seqs, 2)),
        DMA,
        DMA,
        DMA((1 + bits,)),
        DMA((1 + bits,)),
        DMA((stage,)),
        DMA((stage,)),
        DMA((columns,)),
        DMA((columns,)),
    ]
    scratch += PieceSum.scratch(blocks, out_piece, half, rest)
    for _ in range(pairs):
        scratch += PieceSum.scratch(blocks, pair_piece, 128, rest)
    gout, gpair, sums, f_inner, f_outer, g_hidden, output = pl.pallas_call(
        kernel,
        name="backward",
        out_shape=[
            jax.ShapeDtypeStruct((2, 2, 2, blocks, out_piece, half), bf16),
            jax.ShapeDtypeStruct((pairs, 2, 2, 2, blocks, pair_piece, 128), bf16),
            jax.ShapeDtypeStruct((small_rows, width), f32),
            jax.ShapeDtypeStruct((width, part), f32),
            jax.ShapeDtypeStruct((part, width), f32),
            jax.ShapeDtypeStruct((seqs, 2, hs, width), f32),
            jax.ShapeDtypeStruct((tokens, width), bf16),
        ],
        in_specs=[VMEM] * 23 + [ANY] * 4,
        out_specs=[VMEM] * 7,
        scratch_shapes=scratch,
        compiler_params=params(3),
    )(
        rows, weights, qkv, att_t, lse, length, attended, middle, flat, gate, slot, ids, lengths, cotangent,
        back, dots, counts, made, hidden.reshape(seqs, 2, hs, width), gain_one.reshape(1, width),
        gain_two.reshape(1, width), w_output, w_router, g_inner, g_outer, e_inner, e_outer,
    )
    g_out = gout.reshape(2, width, half).transpose(1, 0, 2).reshape(width, width)
    g_pair = gpair.reshape(pairs, 2, 3, width, 128).transpose(2, 3, 1, 0, 4).reshape(3, width, width)
    return (
        g_out, g_pair, sums, f_inner, f_outer, g_hidden.reshape(seqs, span, width), output.reshape(seqs, span, width)
    )


def on_device(
    hidden_in,
    cotangent,
    query_weight,
    key_weight,
    value_weight,
    output_weight,
    gain_one,
    shift_one,
    gain_two,
    shift_two,
    w_router,
    w_inner,
    w_outer,
    expert_ids,
    seq_lengths,
):
    seqs, span, width = hidden_in.shape
    tokens = seqs * span
    blocks = lax.axis_size("blk")
    columns = lax.axis_size("ep") // 2
    experts_n = w_router.shape[1]
    capacity = max(2, 2 * tokens // experts_n)
    total = blocks * span
    half = width // 2
    assert seqs * 2 == blocks and experts_n == columns

    ids = expert_ids.reshape(tokens, 1)
    lengths = jnp.broadcast_to(seq_lengths[:, None, None], (seqs, 8, 128))
    router = jnp.pad(w_router, ((0, 0), (0, 128 - experts_n)))
    cot = cotangent.reshape(tokens, width)
    (
        rows, w_qkv, qkv, att_t, lse, attended, middle, flat, gate, slot, to_rows, scales, cot_rows, length, counts,
        near_inner, near_outer, sib_inner, sib_outer,
    ) = forward(
        hidden_in, cotangent, gain_one, shift_one, gain_two, shift_two, query_weight, key_weight, value_weight,
        output_weight, router, ids, lengths, w_inner[0], w_outer[0], blocks, columns, capacity, experts_n,
    )
    back, dots, made, counts, g_inner, g_outer, e_inner, e_outer = experts(
        to_rows, scales, cot_rows, counts, w_inner[0], w_outer[0], sib_inner, sib_outer, near_inner, near_outer, blocks
    )
    g_out, g_qkv, sums, grad_inner, grad_outer, grad_hidden, output = backward(
        rows.reshape(total, width), w_qkv, qkv.reshape(total, 3 * half), att_t, lse, length, attended, middle, flat, gate,
        slot, ids, lengths, cot, back, dots, counts, made, hidden_in, gain_one, gain_two, output_weight, router,
        g_inner, g_outer, e_inner, e_outer, experts_n,
    )
    balance = sums[4 + experts_n, 0] / jnp.sum(counts[0])
    return (
        output,
        grad_hidden,
        g_qkv[0].astype(f32),
        g_qkv[1].astype(f32),
        g_qkv[2].astype(f32),
        g_out.astype(f32),
        sums[0],
        sums[1],
        sums[2],
        sums[3],
        jnp.transpose(sums[4 : 4 + experts_n]),
        grad_inner[None],
        grad_outer[None],
        balance,
    )


def solution(mesh):
    tokens = P("ep", "blk", None)
    return jax.shard_map(
        on_device,
        mesh=mesh,
        in_specs=(tokens, tokens)
        + (P(),) * 9
        + (P("ep", None, "blk"), P("ep", "blk", None), P("ep", "blk", None, None, None), P("ep")),
        out_specs=(tokens, tokens) + (P(),) * 9 + (P("ep", None, "blk"), P("ep", "blk", None), P()),
        check_vma=False,
    )
```

```python
import functools

import jax
import jax.numpy as jnp
from jax import lax
from jax.experimental import pallas as pl
from jax.experimental.pallas import tpu as pltpu
from jax.sharding import PartitionSpec as P

HEAD = 64
MESH = pl.DeviceIdType.MESH
ANY = pl.BlockSpec(memory_space=pl.ANY)
VMEM = pl.BlockSpec(memory_space=pltpu.VMEM)
SMEM = pl.BlockSpec(memory_space=pltpu.SMEM)
DMA = pltpu.SemaphoreType.DMA
f32 = jnp.float32
bf16 = jnp.bfloat16

epsilon = 1e-05
balance_weight = 6.0
masked_fill = -1e30
VMEM_BYTES = 57 * 1024 * 1024


def dot(a, b):
    return lax.dot_general(a, b, (((1,), (0,)), ((), ())), preferred_element_type=f32)


def dot_nt(a, b):
    return lax.dot_general(a, b, (((1,), (1,)), ((), ())), preferred_element_type=f32)


def dot_tn(a, b):
    return lax.dot_general(a, b, (((0,), (0,)), ((), ())), preferred_element_type=f32)


def place():
    z = lax.axis_index("blk")
    e = lax.axis_index("ep")
    c = lax.rem(e, 2)
    return z, e, c, e - c


def remote(src, dst, send_sem, recv_sem, z, e):
    return pltpu.make_async_remote_copy(
        src, dst, send_sem, recv_sem, device_id=(z, e), device_id_type=MESH
    )


def greet(partners):
    barrier = pltpu.get_barrier_semaphore()
    for z, e in partners:
        pl.semaphore_signal(barrier, inc=1, device_id=(z, e), device_id_type=MESH)
    pl.semaphore_wait(barrier, len(partners))


def column_partners(blocks, z, c, base):
    found = [(z, base + 1 - c)]
    for step in range(1, blocks):
        for k in range(2):
            found.append((lax.rem(z + step, blocks), base + k))
    return found


def params(collective_id):
    return pltpu.CompilerParams(
        collective_id=collective_id, has_side_effects=True, vmem_limit_bytes=VMEM_BYTES
    )


def lane_of(shape, dimension):
    return lax.broadcasted_iota(jnp.int32, shape, dimension)


def key_heads(k_all, key_bias):
    lane = lane_of((1, 128), 1)
    found = []
    for h in range(2):
        inside = (lane // HEAD) == h
        spare = lane == (1 - h) * HEAD
        found.append(
            jnp.where(inside, k_all.astype(f32), jnp.where(spare, key_bias, 0.0)).astype(bf16)
        )
    return found


def forward(
    hidden, cotangent, gain_one, shift_one, gain_two, shift_two, w_query, w_key, w_value, w_output, w_router,
    ids, lengths, w_inner, w_outer, blocks, columns, capacity, experts_n,
):
    seqs, span, width = hidden.shape
    hs = span // 2
    half = width // 2
    pairs = half // 128
    total = blocks * span
    tokens = seqs * span
    slots = experts_n * capacity
    part = w_inner.shape[1]
    cap_lanes = max(128, capacity)

    def kernel(*refs):
        (
            hid_ref, cot_ref, g1_ref, s1_ref, g2_ref, s2_ref, wq_ref, wk_ref, wv_ref, wo_ref, wr_ref,
            ids_ref, lens_ref, wi_ref, we_ref,
        ) = refs[:15]
        (
            xt_ref, w_ref, qkv_ref, attt_ref, lse_ref, t_ref, mid_ref, flat_ref, gate_ref, slot_ref,
            rows_ref, sc_ref, cote_ref, len_ref, cnt_ref, li_ref, bi_ref, bo_ref,
        ) = refs[15:33]
        (
            x_ref, nb_ref, kh_ref, vt_ref, att_ref, cots_ref, lgot_ref, cown_ref, cgot_ref,
            wload, nloc, nsend, nrecv, fsend, frecv, aloc, asend, arecv, closs, csend, crecv,
            lsend, lrecv, ksend, krecv, hsend, hrecv, bsend, brecv,
        ) = refs[33:]
        z, e, c, base = place()
        col = e // 2
        sib = base + 1 - c
        seq_core, seq = z // 2, lax.rem(z, 2)
        others = [lax.rem(z + step, blocks) for step in range(1, blocks)]
        plane = [lax.rem(col + step, columns) for step in range(1, columns)]
        column = column_partners(blocks, z, c, base)

        def load_w(m, ref):
            return pltpu.make_async_copy(
                ref.at[:, pl.ds(pl.multiple_of(c * half, half), half)],
                w_ref.at[:, pl.ds(m * half, half)],
                wload.at[m],
            )

        for m, ref in enumerate((wq_ref, wk_ref, wv_ref)):
            load_w(m, ref).start()
        gain_row, shift_row = g1_ref[...].reshape(1, width), s1_ref[...].reshape(1, width)
        for s in range(seqs):
            for k in range(2):
                v = hid_ref[s, k].astype(f32)
                centered = v - jnp.mean(v, axis=-1, keepdims=True)
                inverse = lax.rsqrt(jnp.mean(centered * centered, axis=-1, keepdims=True) + epsilon)
                nb_ref[s, k] = (centered * inverse * gain_row + shift_row).astype(bf16)
        greet(column + [(z, 2 * t + c) for t in plane])

        def n_out(s, k):
            return remote(
                nb_ref.at[s, k], x_ref.at[z, k], nsend.at[s, k], nrecv.at[z], 2 * c + s, base + k
            )

        def n_own(s, k):
            return pltpu.make_async_copy(nb_ref.at[s, k], x_ref.at[z, k], nloc)

        for k in range(2):
            for s in range(seqs):
                to_self = (2 * c + s == z) & (c == k)

                @pl.when(to_self)
                def _():
                    n_own(s, k).start()

                @pl.when(jnp.logical_not(to_self))
                def _():
                    n_out(s, k).start()

        to_lens = remote(lens_ref, lgot_ref, lsend, lrecv, z, sib)
        to_lens.start()
        lane = lane_of((tokens, 128), 1)
        onehot = (lane == ids_ref[...]).astype(f32)
        place_in = z * span + lane_of((span, 1), 0)
        valid = jnp.concatenate(
            [(place_in < lens_ref[s, 0:1, 0:1]).astype(f32) for s in range(seqs)], axis=0
        )
        cown_ref[...] = jnp.broadcast_to(jnp.sum(onehot * valid, axis=0, keepdims=True), (8, 128))

        def k_out(n, to_z, to_e):
            return remote(cown_ref, cgot_ref.at[z, c], ksend.at[n], krecv.at[z, c], to_z, to_e)

        for n, (to_z, to_e) in enumerate(column):
            k_out(n, to_z, to_e).start()
        earlier = (lane_of((tokens, tokens), 0) > lane_of((tokens, tokens), 1)).astype(f32).astype(bf16)
        rank = dot(earlier, onehot.astype(bf16))
        slot = jnp.sum(onehot * (rank + (lane * capacity).astype(f32)), axis=1, keepdims=True)
        slot_ref[...] = slot
        slot_row = jnp.transpose(jnp.broadcast_to(slot, (tokens, 128)))[0:1]
        to_slots = (lane_of((slots, tokens), 0).astype(f32) == slot_row).astype(f32).astype(bf16)
        cots_ref[...] = (
            dot(to_slots, cot_ref[...]).astype(bf16).reshape(columns, capacity, width)
        )

        def c_out(t):
            return remote(cots_ref.at[t], cote_ref.at[col], csend.at[t], crecv.at[col], z, 2 * t + c)

        c_own = pltpu.make_async_copy(cots_ref.at[col], cote_ref.at[col], closs)
        c_own.start()
        for t in plane:
            c_out(t).start()
        for m, ref in enumerate((wq_ref, wk_ref, wv_ref)):
            load_w(m, ref).wait()

        def n_sib(zs):
            return remote(x_ref.at[zs, c], x_ref.at[zs, c], fsend.at[zs], frecv.at[zs], z, sib)

        for zs in [z] + others:
            if zs is z:

                @pl.when(c == seq_core)
                def _():
                    n_own(0, 0).wait()

                @pl.when(c != seq_core)
                def _():
                    remote(nb_ref.at[0, 0], x_ref.at[z, c], nsend.at[0, 0], nrecv.at[z], z, base).wait_recv()
            else:
                remote(nb_ref.at[0, 0], x_ref.at[zs, c], nsend.at[0, 0], nrecv.at[zs], z, base).wait_recv()
            n_sib(zs).start()

        def h_out(step):
            side = 0 if step == 1 else 1
            return remote(wi_ref, li_ref.at[side], hsend.at[side], hrecv.at[side], z + step, e)

        def b_out(i):
            src, dst = ((wi_ref, bi_ref), (we_ref, bo_ref))[i]
            return remote(src, dst, bsend.at[i], brecv.at[i], z, sib)

        @pl.when(z < blocks - 1)
        def _():
            h_out(1).start()

        @pl.when(z > 0)
        def _():
            h_out(-1).start()

        for zs in [z] + others:
            remote(
                x_ref.at[zs, 1 - c], x_ref.at[zs, 1 - c], fsend.at[zs], frecv.at[zs], z, sib
            ).wait_recv()
            x_z = x_ref[zs].reshape(span, width)
            qkv_ref[zs] = dot(x_z, w_ref[...]).astype(bf16)
            xt_ref[:, pl.ds(pl.multiple_of(zs * span, span), span)] = jnp.transpose(x_z)
        for i in range(2):
            b_out(i).start()
        to_lens.wait()
        seq_len = jnp.where(c == seq_core, lens_ref[seq], lgot_ref[seq])
        len_ref[...] = seq_len
        key_bias = jnp.where(lane_of((total, 1), 0) < seq_len[0:1, 0:1], 0.0, masked_fill)
        for p in range(pairs):
            k_all = jnp.concatenate(
                [qkv_ref[j, :, half + p * 128 : half + (p + 1) * 128] for j in range(blocks)], axis=0
            )
            for h, k_h in enumerate(key_heads(k_all, key_bias)):
                kh_ref[2 * p + h] = k_h
            for j in range(blocks):
                vt_ref[p * 128 : (p + 1) * 128, j * span : (j + 1) * span] = jnp.transpose(
                    qkv_ref[j, :, 2 * half + p * 128 : 2 * half + (p + 1) * 128]
                )
        later = lane_of((span, span), 0) > lane_of((span, span), 1)
        lane_row = lane_of((1, 128), 1)

        def a_out(j):
            return remote(
                att_ref.at[j], t_ref.at[seq, c], asend.at[j], arecv.at[seq, c], j, base + seq_core
            )

        def a_own(j):
            return pltpu.make_async_copy(att_ref.at[j], t_ref.at[seq, c], aloc)

        for j in reversed(range(blocks)):
            n = (j + 1) * span

            def pair_step(p, _):
                first = pl.multiple_of(p * 128, 128)
                q = qkv_ref[j, :, pl.ds(first, 128)].astype(f32) * (HEAD**-0.5)
                out_t = []
                for h in range(2):
                    inside = (lane_row // HEAD) == h
                    spare = lane_row == (1 - h) * HEAD
                    q_h = jnp.where(inside, q, jnp.where(spare, 1.0, 0.0)).astype(bf16)
                    s = dot_nt(kh_ref[2 * p + h, :n], q_h)
                    last = jnp.where(later, masked_fill, s[n - span :])
                    s = last if j == 0 else jnp.concatenate([s[: n - span], last], axis=0)
                    top = jnp.max(s, axis=0, keepdims=True)
                    w = jnp.exp(s - top)
                    total_w = jnp.sum(w, axis=0, keepdims=True)
                    o_t = dot(vt_ref[pl.ds(pl.multiple_of(first + h * HEAD, HEAD), HEAD), :n], w.astype(bf16))
                    out_t.append(o_t / total_w)
                    lse_ref[pl.ds(2 * p + h, 1), pl.ds(j * span, span)] = top + jnp.log(total_w)
                o = jnp.concatenate(out_t, axis=0)
                attt_ref[pl.ds(first, 128), pl.ds(j * span, span)] = o
                att_ref[j, :, pl.ds(first, 128)] = jnp.transpose(o).astype(bf16)
                return 0

            lax.fori_loop(0, pairs, pair_step, 0)
            to_self = (z == j) & (c == seq_core)

            @pl.when(to_self)
            def _():
                a_own(j).start()

            @pl.when(jnp.logical_not(to_self))
            def _():
                a_out(j).start()

        for s in range(seqs):
            for k in range(2):
                from_self = (2 * c + s == z) & (c == k)

                @pl.when(from_self)
                def _():
                    a_own(0).wait()

                @pl.when(jnp.logical_not(from_self))
                def _():
                    remote(att_ref.at[0], t_ref.at[s, k], asend.at[0], arecv.at[s, k], z, base).wait_recv()

        for s in range(seqs):
            r = pl.ds(s * span, span)
            branch = dot(t_ref[s, 0], wo_ref[0:half]) + dot(t_ref[s, 1], wo_ref[half:])
            v = hid_ref[s].reshape(span, width).astype(f32) + branch
            mid_ref[r, :] = v
            centered = v - jnp.mean(v, axis=-1, keepdims=True)
            inverse = lax.rsqrt(jnp.mean(centered * centered, axis=-1, keepdims=True) + epsilon)
            flat_ref[r, :] = (
                centered * inverse * g2_ref[...].reshape(1, width) + s2_ref[...].reshape(1, width)
            ).astype(bf16)
        logits = dot(flat_ref[...], wr_ref[...])
        gate = jax.nn.sigmoid(jnp.sum(logits * onehot, axis=1, keepdims=True))
        gate_ref[...] = gate
        rows_ref[...] = (
            dot(to_slots, flat_ref[...]).astype(bf16).reshape(columns, capacity, width)
        )
        from_slots = lane_of((tokens, slots), 1).astype(f32) == slot_ref[...]
        scales = jnp.sum(jnp.where(from_slots, valid * gate, 0.0), axis=0, keepdims=True)
        if cap_lanes != capacity:
            sc_ref[...] = jnp.zeros_like(sc_ref)
        for t in range(columns):
            sc_ref[t, :, 0:capacity] = jnp.broadcast_to(
                scales[:, t * capacity : (t + 1) * capacity], (8, capacity)
            )

        for n, (to_z, to_e) in enumerate(column):
            remote(cown_ref, cgot_ref.at[to_z, lax.rem(to_e, 2)], ksend.at[n], krecv.at[to_z, lax.rem(to_e, 2)], z, sib).wait_recv()
            k_out(n, to_z, to_e).wait_send()
        cgot_ref[z, c] = cown_ref[...]
        tot = jnp.zeros((8, 128), f32)
        for zs in range(blocks):
            for k in range(2):
                tot = tot + cgot_ref[zs, k]
        cnt_ref[...] = tot
        c_own.wait()
        for t in plane:
            c_out(t).wait_send()
            remote(cots_ref.at[t], cote_ref.at[t], csend.at[t], crecv.at[t], z, e).wait_recv()
        for s in range(seqs):
            for k in range(2):

                @pl.when(jnp.logical_not((2 * c + s == z) & (c == k)))
                def _():
                    n_out(s, k).wait_send()

        for zs in [z] + others:
            n_sib(zs).wait_send()
        for j in range(blocks):

            @pl.when(jnp.logical_not((z == j) & (c == seq_core)))
            def _():
                a_out(j).wait_send()

        for i in range(2):
            b_out(i).wait()

        @pl.when(z < blocks - 1)
        def _():
            h_out(1).wait_send()
            remote(wi_ref, li_ref.at[1], hsend.at[1], hrecv.at[1], z, e).wait_recv()

        @pl.when(z > 0)
        def _():
            h_out(-1).wait_send()
            remote(wi_ref, li_ref.at[0], hsend.at[0], hrecv.at[0], z, e).wait_recv()

    out_shapes = [
        ((width, total), bf16),
        ((width, 3 * half), bf16),
        ((blocks, span, 3 * half), bf16),
        ((half, total), f32),
        ((2 * pairs, total), f32),
        ((seqs, 2, span, half), bf16),
        ((tokens, width), f32),
        ((tokens, width), bf16),
        ((tokens, 1), f32),
        ((tokens, 1), f32),
        ((columns, capacity, width), bf16),
        ((columns, 8, cap_lanes), f32),
        ((columns, capacity, width), bf16),
        ((8, 128), jnp.int32),
        ((8, 128), f32),
        ((2, width, part), bf16),
        ((width, part), bf16),
        ((part, width), bf16),
    ]
    return pl.pallas_call(
        kernel,
        name="forward",
        out_shape=[jax.ShapeDtypeStruct(a, b) for a, b in out_shapes],
        in_specs=[VMEM] * 6 + [ANY] * 3 + [VMEM] * 4 + [ANY] * 2,
        out_specs=[VMEM] * 12 + [ANY] + [VMEM] * 2 + [ANY] * 3,
        scratch_shapes=[
            pltpu.VMEM((blocks, 2, hs, width), bf16),
            pltpu.VMEM((seqs, 2, hs, width), bf16),
            pltpu.VMEM((2 * pairs, total, 128), bf16),
            pltpu.VMEM((half, total), bf16),
            pltpu.VMEM((blocks, span, half), bf16),
            pltpu.VMEM((columns, capacity, width), bf16),
            pltpu.VMEM((seqs, 8, 128), jnp.int32),
            pltpu.VMEM((8, 128), f32),
            pltpu.VMEM((blocks, 2, 8, 128), f32),
            DMA((3,)),
            DMA,
            DMA((seqs, 2)),
            DMA((blocks,)),
            DMA((blocks,)),
            DMA((blocks,)),
            DMA,
            DMA((blocks,)),
            DMA((seqs, 2)),
            DMA,
            DMA((columns,)),
            DMA((columns,)),
            DMA,
            DMA,
            DMA((2 * blocks - 1,)),
            DMA((blocks, 2)),
            DMA((2,)),
            DMA((2,)),
            DMA((2,)),
            DMA((2,)),
        ],
        compiler_params=params(1),
    )(
        hidden.reshape(seqs, 2, hs, width), cotangent.reshape(tokens, width),
        gain_one, shift_one, gain_two, shift_two,
        w_query, w_key, w_value, w_output, w_router, ids, lengths, w_inner, w_outer,
    )


def slice_order(z):
    near = z + 1 - 2 * lax.rem(z, 2)
    across = jnp.where(z < 2, 2, 1)
    inner = (z > 0) & (z < 3)
    return [jnp.where(inner, across, near), jnp.where(inner, near, across), z, jnp.where(z < 2, 3, 0)]


def experts(
    rows, scales, cot, counts, w_inner, w_outer, sib_inner, sib_outer, near_inner, blocks
):
    columns, capacity, width = rows.shape
    cap_lanes = scales.shape[2]
    total = columns * capacity
    part = w_inner.shape[1]
    block = 256
    count = total // block
    per = block // capacity
    assert blocks == 4 and columns == count * per

    def kernel(*refs):
        rows_ref, sc_ref, cot_ref, cnt_ref, wi_ref, we_ref, bi_ref, bo_ref, li_ref = refs[:9]
        back_ref, dots_ref, made_ref, tot_ref, gi_ref, go_ref, ei_ref, eo_ref = refs[9:17]
        (
            x_ref, xt_ref, d_ref, scg_ref, cntg_ref, in_ref, out_ref, oacc, dacc, act_ref, dpre_ref,
            dr_ref, dots_own, sgi_ref, sgo_ref, ggi_ref, ggo_ref,
            xloc, xsend, xrecv, scsend, screcv, ksend, krecv, wloc, wsend, wrecv, vsend, vrecv,
            bloc, dsend, drecv, gsend, grecv, ssend, srecv,
        ) = refs[17:]
        z, e, c, base = place()
        col = e // 2
        sib = base + 1 - c
        inner = (z > 0) & (z < blocks - 1)
        end = jnp.logical_not(inner)
        plane = [lax.rem(col + step, columns) for step in range(1, columns)]
        greet(column_partners(blocks, z, c, base) + [(z, 2 * t + c) for t in plane])

        def x_out(t):
            return remote(rows_ref.at[t], x_ref.at[col], xsend.at[t], xrecv.at[col], z, 2 * t + c)

        def sc_out(t):
            return remote(sc_ref.at[t], scg_ref.at[col], scsend.at[t], screcv.at[col], z, 2 * t + c)

        def cnt_out(t):
            return remote(cnt_ref, cntg_ref.at[col], ksend.at[t], krecv.at[col], z, 2 * t + c)

        x_own = pltpu.make_async_copy(rows_ref.at[col], x_ref.at[col], xloc)
        x_own.start()
        for t in plane:
            sc_out(t).start()
            x_out(t).start()
            cnt_out(t).start()
        scg_ref[col] = sc_ref[col]
        cntg_ref[col] = cnt_ref[...]

        hop_two = lax.rem(z + 2, blocks)
        pair = z + 1 - 2 * lax.rem(z, 2)

        lo_half, hi_half = pl.ds(0, part), pl.ds(part, part)

        def views(s, which):
            return (in_ref.at[s, :, which], out_ref.at[s, which])

        sources = ((wi_ref, we_ref), (bi_ref, bo_ref))

        def w_own(i, k):
            return pltpu.make_async_copy(
                sources[k][i], views(z, (lo_half, hi_half)[k])[i], wloc.at[i, k]
            )

        def beside(side):
            return z - 1 if side == 0 else z + 1

        def w_near(side):
            return pltpu.make_async_copy(li_ref.at[side], views(beside(side), lo_half)[0], wloc.at[2, side])

        def w_near_sib(side):
            s = beside(side)
            return remote(li_ref.at[side], views(s, hi_half)[0], vsend.at[0, s], vrecv.at[0, s], z, sib)

        def w_hop(side):
            return remote(we_ref, views(z, lo_half)[1], wsend.at[1, side], wrecv.at[1, z], beside(side), e)

        def w_pass(i, side):
            s = beside(side)
            src = li_ref.at[side] if i == 0 else views(s, lo_half)[1]
            return remote(src, views(s, lo_half)[i], wsend.at[2 + i, side], wrecv.at[i, s], beside(1 - side), e)

        def w_got(i, s):
            return remote(views(s, lo_half)[i], views(s, lo_half)[i], wsend.at[0, 0], wrecv.at[i, s], z, e)

        def w_sib(i, s):
            return remote(views(s, lo_half)[i], views(s, hi_half)[i], vsend.at[i, s], vrecv.at[i, s], z, sib)

        def w_sib_got(i, s):
            return remote(views(s, lo_half)[i], views(s, hi_half)[i], vsend.at[i, z], vrecv.at[i, s], z, sib)

        def w_last(i):
            s = hop_two
            to = jnp.where(z == 1, 0, blocks - 1)
            return remote(views(s, lo_half)[i], views(s, lo_half)[i], wsend.at[4 + i, 0], wrecv.at[i, s], to, e)

        def has(side):
            return z > 0 if side == 0 else z < blocks - 1

        for side in range(2):

            @pl.when(has(side))
            def _():
                w_hop(side).start()

        for side in range(2):

            @pl.when(inner)
            def _():
                w_pass(0, side).start()

        for side in range(2):

            @pl.when(has(side))
            def _():
                w_near(side).start()
                w_near_sib(side).start()

        for i in range(2):
            for k in range(2):
                w_own(i, k).start()

        order = slice_order(z)
        far = order[3]
        oacc[...] = jnp.zeros_like(oacc)
        dacc[...] = jnp.zeros_like(dacc)
        first_block = col // per

        def at_block(b):
            return pl.ds(pl.multiple_of(b * per, per), per)

        def row_step(s, b, fresh):
            x_b = x_ref[at_block(b)].reshape(block, width)
            r = pl.ds(pl.multiple_of(b * block, block), block)
            if fresh:
                row = jnp.concatenate(
                    [scg_ref[b * per + i, :, 0:capacity] for i in range(per)], axis=1
                )
                column = jnp.transpose(row)[:, 0:1]
                cots = cot_ref[at_block(b)].reshape(block, width).astype(f32)
                d_ref[r, :] = (column * cots).astype(bf16)
            pre = dot(x_b, in_ref[s])
            cdf = 0.5 * (1.0 + lax.erf(pre * (0.5**0.5)))
            act = (pre * cdf).astype(bf16)
            slope = cdf + pre * (jnp.exp(-0.5 * pre * pre) * ((2 * jnp.pi) ** -0.5))
            d_act = dot_nt(d_ref[r, :], out_ref[s])
            d_pre = (d_act * slope).astype(bf16)
            act_ref[r, :] = act
            dpre_ref[r, :] = d_pre
            oacc[r, :] += dot(act, out_ref[s])
            dacc[r, :] += dot_nt(d_pre, in_ref[s])

        def grads(s):
            g_inner = dot(xt_ref[...], dpre_ref[...])
            gi_ref[s] = g_inner[:, :part].astype(bf16)
            sgi_ref[s] = g_inner[:, part:].astype(bf16)
            g_outer = dot_tn(act_ref[...], d_ref[...])
            go_ref[s] = g_outer[:part].astype(bf16)
            sgo_ref[s] = g_outer[part:].astype(bf16)
            for i in range(2):
                g_sib(i, s).start()

        def g_sib(i, s):
            src, dst = ((sgi_ref, ggi_ref), (sgo_ref, ggo_ref))[i]
            return remote(src.at[s], dst.at[s], gsend.at[i, s], grecv.at[i, s], z, sib)

        def join(s):
            for i, (total_ref, got_ref) in enumerate(((gi_ref, ggi_ref), (go_ref, ggo_ref))):
                g_sib(i, s).wait_recv()
                total_ref[s] = (total_ref[s].astype(f32) + got_ref[s].astype(f32)).astype(bf16)

        def s_out(i, s):
            src, dst = ((gi_ref, ei_ref), (go_ref, eo_ref))[i]
            return remote(src.at[s], dst.at[z], ssend.at[i, s], srecv.at[i, z], s, e)

        def block_at(m):
            return lax.rem(first_block + count - m, count)

        for side in range(2):

            @pl.when(has(side))
            def _():
                w_got(1, beside(side)).wait_recv()
                w_sib(1, beside(side)).start()

            @pl.when(inner)
            def _():
                w_pass(1, side).start()

        for side in range(2):

            @pl.when(has(side))
            def _():
                w_near(side).wait()
                for i in range(2):
                    w_sib_got(i, beside(side)).wait_recv()

        for m in range(count):
            b = block_at(m)
            for i in range(per):
                t = b * per + i

                @pl.when(t == col)
                def _():
                    x_own.wait()

                @pl.when(t != col)
                def _():
                    remote(sc_ref.at[0], scg_ref.at[t], scsend.at[t], screcv.at[t], z, e).wait_recv()
                    remote(rows_ref.at[0], x_ref.at[t], xsend.at[t], xrecv.at[t], z, e).wait_recv()

            row_step(order[0], b, True)
        def hand_on(i):
            w_got(i, hop_two).wait_recv()
            w_sib(i, hop_two).start()

            @pl.when(inner)
            def _():
                w_last(i).start()

        hand_on(0)
        xt_ref[...] = jnp.transpose(x_ref[...].reshape(total, width))
        grads(order[0])
        hand_on(1)
        for i in range(2):
            w_sib_got(i, hop_two).wait_recv()

        def loop(s, start):
            def body(b, _):
                row_step(s, b, False)
                return 0

            lax.fori_loop(start, count, body, 0)

        row_step(order[1], 0, False)
        join(order[0])
        for i in range(2):
            s_out(i, order[0]).start()
        loop(order[1], 1)
        grads(order[1])
        for i in range(2):
            for k in range(2):
                w_own(i, k).wait()
        row_step(order[2], 0, False)
        join(order[1])
        for i in range(2):
            s_out(i, order[1]).start()
        loop(order[2], 1)

        @pl.when(end)
        def _():
            for i in range(2):
                w_got(i, far).wait_recv()
                w_sib(i, far).start()

        grads(order[2])

        @pl.when(end)
        def _():
            for i in range(2):
                w_sib_got(i, far).wait_recv()

        def d_out(t):
            return remote(dr_ref.at[t], back_ref.at[col], dsend.at[0, t], drecv.at[0, col], z, 2 * t + c)

        def dots_out(t):
            return remote(dots_own.at[t], dots_ref.at[col], dsend.at[1, t], drecv.at[1, col], z, 2 * t + c)

        b_own = pltpu.make_async_copy(dr_ref.at[col], back_ref.at[col], bloc)
        for m in list(range(1, count)) + [0]:
            b = block_at(m)
            row_step(order[3], b, False)
            if m == 1:
                join(order[2])
            r = pl.ds(pl.multiple_of(b * block, block), block)
            made = oacc[r, :].astype(bf16)
            made_ref[at_block(b)] = made.reshape(per, capacity, width)
            dr_ref[at_block(b)] = dacc[r, :].astype(bf16).reshape(per, capacity, width)
            cots = cot_ref[at_block(b)].reshape(block, width).astype(f32)
            sums = jnp.sum(cots * made.astype(f32), axis=1, keepdims=True)
            row = jnp.transpose(jnp.broadcast_to(sums, (block, 128)))[0:8]
            for i in range(per):
                t = b * per + i
                if cap_lanes != capacity:
                    dots_own[t] = jnp.zeros((8, cap_lanes), f32)
                dots_own[t, :, 0:capacity] = row[:, i * capacity : (i + 1) * capacity]

                @pl.when(t == col)
                def _():
                    b_own.start()
                    dots_ref[t] = dots_own[t]

                @pl.when(t != col)
                def _():
                    d_out(t).start()
                    dots_out(t).start()

        grads(order[3])
        join(order[3])

        for t in plane:
            x_out(t).wait_send()
            sc_out(t).wait_send()
            cnt_out(t).wait_send()
            remote(cnt_ref, cntg_ref.at[t], ksend.at[t], krecv.at[t], z, e).wait_recv()
        tot = cntg_ref[0]
        for t in range(1, columns):
            tot = tot + cntg_ref[t]
        tot_ref[...] = tot
        for i in range(2):
            for side in range(2):

                @pl.when(inner)
                def _():
                    w_pass(i, side).wait_send()

            w_sib(i, hop_two).wait_send()

            @pl.when(end)
            def _():
                w_sib(i, far).wait_send()

            for n in range(blocks):
                g_sib(i, n).wait_send()
            s_out(i, order[0]).wait_send()
            s_out(i, order[1]).wait_send()
            got = (ei_ref, eo_ref)[i]

            def arrived(zs):
                return remote(got.at[0], got.at[zs], ssend.at[i, 0], srecv.at[i, zs], z, e)

            arrived(pair).wait_recv()

            @pl.when(inner)
            def _():
                w_last(i).wait_send()
                for k in range(2):
                    arrived(lax.rem(2 * (z // 2) + 2 + k, blocks)).wait_recv()

        for side in range(2):

            @pl.when(has(side))
            def _():
                w_hop(side).wait_send()
                w_near_sib(side).wait_send()
                w_sib(1, beside(side)).wait_send()

        b_own.wait()
        for t in plane:
            d_out(t).wait_send()
            dots_out(t).wait_send()
            remote(dr_ref.at[0], back_ref.at[t], dsend.at[0, t], drecv.at[0, t], z, e).wait_recv()
            remote(dots_own.at[0], dots_ref.at[t], dsend.at[1, t], drecv.at[1, t], z, e).wait_recv()

    out_shapes = [
        ((columns, capacity, width), bf16),
        ((columns, 8, cap_lanes), f32),
        ((columns, capacity, width), bf16),
        ((8, 128), f32),
        ((blocks, width, part), bf16),
        ((blocks, part, width), bf16),
        ((blocks, width, part), bf16),
        ((blocks, part, width), bf16),
    ]
    return pl.pallas_call(
        kernel,
        name="experts",
        out_shape=[jax.ShapeDtypeStruct(a, b) for a, b in out_shapes],
        in_specs=[VMEM] * 4 + [ANY] * 5,
        out_specs=[VMEM] * 6 + [ANY] * 2,
        scratch_shapes=[
            pltpu.VMEM((columns, capacity, width), bf16),
            pltpu.VMEM((width, total), bf16),
            pltpu.VMEM((total, width), bf16),
            pltpu.VMEM((columns, 8, cap_lanes), f32),
            pltpu.VMEM((columns, 8, 128), f32),
            pltpu.VMEM((blocks, width, 2 * part), bf16),
            pltpu.VMEM((blocks, 2 * part, width), bf16),
            pltpu.VMEM((total, width), f32),
            pltpu.VMEM((total, width), f32),
            pltpu.VMEM((total, 2 * part), bf16),
            pltpu.VMEM((total, 2 * part), bf16),
            pltpu.VMEM((columns, capacity, width), bf16),
            pltpu.VMEM((columns, 8, cap_lanes), f32),
            pltpu.VMEM((blocks, width, part), bf16),
            pltpu.VMEM((blocks, part, width), bf16),
            pltpu.VMEM((blocks, width, part), bf16),
            pltpu.VMEM((blocks, part, width), bf16),
            DMA,
            DMA((columns,)),
            DMA((columns,)),
            DMA((columns,)),
            DMA((columns,)),
            DMA((columns,)),
            DMA((columns,)),
            DMA((3, 2)),
            DMA((6, 2)),
            DMA((2, blocks)),
            DMA((2, blocks)),
            DMA((2, blocks)),
            DMA,
            DMA((2, columns)),
            DMA((2, columns)),
            DMA((2, blocks)),
            DMA((2, blocks)),
            DMA((2, blocks)),
            DMA((2, blocks)),
        ],
        compiler_params=params(2),
    )(rows, scales, cot, counts, w_inner, w_outer, sib_inner, sib_outer, near_inner)


class PieceSum:
    def __init__(self, at, part, got1, got2, got3, gotr, full, sem, rsem, zsem, zrsem, order, finish):
        self.at, self.part, self.full = at, part, full
        self.got1, self.got2, self.got3, self.gotr = got1, got2, got3, gotr
        self.sem, self.rsem, self.zsem, self.zrsem = sem, rsem, zsem, zrsem
        z, e, c, bit, mate, blocks, sib = at
        self.first, self.second = order
        self.finish = finish
        self.rest = len(bit) - 2

    def swap(self, n, src, dst, e):
        return remote(src, dst, self.sem.at[n], self.rsem.at[n], self.at[0], e)

    def halves(self):
        z, e, c, bit, mate, blocks, sib = self.at
        return self.swap(0, self.part.at[1 - bit[self.first]], self.got1, mate[self.first])

    def quarters(self):
        z, e, c, bit, mate, blocks, sib = self.at
        b1, b2 = bit[self.first], bit[self.second]
        return self.swap(1, self.part.at[b1, 1 - b2], self.got2, mate[self.second])

    def to_z(self, zt):
        z, e, c, bit, mate, blocks, sib = self.at
        b1, b2 = bit[self.first], bit[self.second]
        return remote(
            self.part.at[b1, b2, zt], self.got3.at[z], self.zsem.at[0, zt], self.zrsem.at[0, z], zt, e
        )

    def own(self):
        z, e, c, bit, mate, blocks, sib = self.at
        return self.full.at[c, bit[self.first], bit[self.second], z]

    def back_z(self, zt):
        z, e, c, bit, mate, blocks, sib = self.at
        return remote(self.own(), self.own(), self.zsem.at[1, zt], self.zrsem.at[1, z], zt, e)

    def back_quarter(self):
        z, e, c, bit, mate, blocks, sib = self.at
        at = self.full.at[c, bit[self.first], bit[self.second]]
        return self.swap(2, at, at, mate[self.second])

    def back_half(self):
        z, e, c, bit, mate, blocks, sib = self.at
        at = self.full.at[c, bit[self.first]]
        return self.swap(3, at, at, mate[self.first])

    def to_sibling(self):
        z, e, c, bit, mate, blocks, sib = self.at
        return self.swap(4, self.full.at[c], self.full.at[c], sib)

    def step(self, n):
        z, e, c, bit, mate, blocks, sib = self.at
        b1, b2 = bit[self.first], bit[self.second]
        others = [lax.rem(z + step, blocks) for step in range(1, blocks)]
        if n == 0:
            self.halves().start()
        elif n == 1:
            self.halves().wait()
            self.part[b1] = (self.part[b1].astype(f32) + self.got1[...].astype(f32)).astype(bf16)
            self.quarters().start()
        elif n == 2:
            self.quarters().wait()
            self.part[b1, b2] = (self.part[b1, b2].astype(f32) + self.got2[...].astype(f32)).astype(bf16)
            for zt in others:
                self.to_z(zt).start()
        elif n == 3:
            for zs in others:
                remote(
                    self.got3.at[0], self.got3.at[zs], self.zsem.at[0, zs], self.zrsem.at[0, zs], z, e
                ).wait_recv()
            for zt in others:
                self.to_z(zt).wait_send()
            self.got3[z] = self.part[b1, b2, z]
            total = self.got3[0].astype(f32)
            for j in range(1, blocks):
                total = total + self.got3[j].astype(f32)
            own = self.own()
            own[...] = total.astype(bf16)
            for r in range(self.rest):
                copy = self.swap(5 + r, own, self.gotr.at[r], mate[2 + r])
                copy.start()
                copy.wait()
                own[...] = (own[...].astype(f32) + self.gotr[r].astype(f32)).astype(bf16)
            for zt in others:
                self.back_z(zt).start()
        elif n == 4:
            for zs in others:
                at = self.full.at[c, b1, b2, zs]
                remote(at, at, self.zsem.at[1, zs], self.zrsem.at[1, zs], z, e).wait_recv()
            for zt in others:
                self.back_z(zt).wait_send()
            self.back_quarter().start()
        elif n == 5:
            self.back_quarter().wait()
            self.back_half().start()
        elif n == 6:
            self.back_half().wait()
            self.to_sibling().start()
        elif n == 7:
            self.to_sibling().wait()
            for k in range(2):
                self.finish(k, self.full[k])

    @staticmethod
    def scratch(blocks, piece, lanes, rest):
        return [
            pltpu.VMEM((2, 2, blocks, piece, lanes), bf16),
            pltpu.VMEM((2, blocks, piece, lanes), bf16),
            pltpu.VMEM((blocks, piece, lanes), bf16),
            pltpu.VMEM((blocks, piece, lanes), bf16),
            pltpu.VMEM((max(1, rest), piece, lanes), bf16),
            pltpu.VMEM((2, 2, 2, blocks, piece, lanes), bf16),
            DMA((5 + rest,)),
            DMA((5 + rest,)),
            DMA((2, blocks)),
            DMA((2, blocks)),
        ]


def backward(
    rows_t, weights, qkv, att_t, lse, length, attended, middle, flat, gate, slot, ids, lengths, cotangent,
    back, dots, counts, made, hidden, gain_one, gain_two, w_output, w_router, g_inner, g_outer, e_inner, e_outer,
    experts_n,
):
    width, total = rows_t.shape
    half = weights.shape[1] // 3
    pairs = half // 128
    seqs, _, span, _ = attended.shape
    blocks = total // span
    columns, capacity, _ = back.shape
    slots = columns * capacity
    tokens = seqs * span
    hs = span // 2
    scale = HEAD**-0.5
    part = g_inner.shape[2]
    bits = columns.bit_length() - 1
    assert columns == 1 << bits and bits >= 2 and blocks == 4
    rest = bits - 2
    small_rows = -(-(5 + experts_n) // 8) * 8
    out_piece, pair_piece = width // (4 * blocks), 3 * width // (4 * blocks)
    n_sum = 10

    def kernel(*refs):
        (
            xt_ref, w_ref, qkv_ref, attt_ref, lse_ref, len_ref, t_ref, mid_ref, flat_ref, gate_ref, slot_ref, ids_ref,
            lens_ref, cot_ref, back_ref, dots_ref, cnt_ref, made_ref, hid_ref, g1_ref, g2_ref, wo_ref, wr_ref,
            gi_ref, go_ref, ei_ref, eo_ref,
        ) = refs[:27]
        grads_ref, sums_ref, fi_ref, fo_ref, gh_ref, y_ref = refs[27:33]
        (
            do_ref, dqkv_ref, kt_ref, dk_ref, dv_ref, dn_ref, dsib_ref, dsum_ref, dnt_ref,
            zi, zo, ci, co, osib, sgot, szgot, datt_ref, op_ref, dmid_ref, mg_ref,
            loc_sem, dsend, drecv, rloc, rsend, rrecv,
            nsend, nrecv, ssend, srecv, osend, orecv, tsend, trecv, tzsend, tzrecv, msend, mrecv,
        ) = refs[33:71]
        sums_scratch = refs[71:]
        z, e, c, base = place()
        col = e // 2
        sib = base + 1 - c
        seq_core, seq = z // 2, lax.rem(z, 2)
        bit = [lax.rem(col // (1 << i), 2) for i in range(bits)]
        mate = [2 * (col + (1 - 2 * bit[i]) * (1 << i)) + c for i in range(bits)]
        others = [lax.rem(z + step, blocks) for step in range(1, blocks)]
        plane = [lax.rem(col + step, columns) for step in range(1, columns)]
        inner = (z > 0) & (z < blocks - 1)
        order = slice_order(z)
        across = [lax.rem(2 * (z // 2) + 2 + k, blocks) for k in range(2)]
        greet(column_partners(blocks, z, c, base) + [(z, 2 * t + c) for t in plane])

        def m_out(t):
            return remote(made_ref.at[t], mg_ref.at[col], msend.at[t], mrecv.at[col], z, 2 * t + c)

        m_own = pltpu.make_async_copy(made_ref.at[col], mg_ref.at[col], loc_sem.at[2])
        m_own.start()
        for t in plane:
            m_out(t).start()

        far = order[3]
        pair = z + 1 - 2 * lax.rem(z, 2)

        def r_load(i, src, s, slot):
            return pltpu.make_async_copy(src.at[s], (zi, zo)[i].at[slot], rloc.at[i, slot])

        def r_chain(i):
            src, dst = ((gi_ref, ci), (go_ref, co))[i]
            return remote(src.at[far], dst, rsend.at[i], rrecv.at[i], pair, e)

        def r_sum(i):
            src, dst = ((zi, ci), (zo, co))[i]
            return remote(src.at[0], dst, rsend.at[i], rrecv.at[i], far, e)

        def chain(i):
            @pl.when(inner)
            def _():
                buf, got = ((zi, ci), (zo, co))[i]
                r_load(i, (gi_ref, go_ref)[i], far, 0).wait()
                r_chain(i).wait_recv()
                buf[0] = (buf[0].astype(f32) + got[...].astype(f32)).astype(bf16)
                r_sum(i).start()

        for i in range(2):

            @pl.when(jnp.logical_not(inner))
            def _():
                r_chain(i).start()
                r_load(i, (gi_ref, go_ref)[i], z, 0).start()

            @pl.when(inner)
            def _():
                r_load(i, (gi_ref, go_ref)[i], far, 0).start()

            r_load(i, (ei_ref, eo_ref)[i], pair, 1).start()

        lane = lane_of((tokens, 128), 1)
        onehot = (lane == ids_ref[...]).astype(f32)
        place_in = z * span + lane_of((span, 1), 0)
        valid = jnp.concatenate(
            [(place_in < lens_ref[s, 0:1, 0:1]).astype(f32) for s in range(seqs)], axis=0
        )
        from_slots = lane_of((tokens, slots), 1).astype(f32) == slot_ref[...]
        dots_row = jnp.concatenate([dots_ref[t, 0:1, 0:capacity] for t in range(columns)], axis=1)
        dot_rows = jnp.sum(jnp.where(from_slots, dots_row, 0.0), axis=1, keepdims=True)
        picks = from_slots.astype(f32).astype(bf16)
        d_rows = dot(picks, back_ref[...].reshape(slots, width))
        count_row = cnt_ref[0:1]
        mean_load = jnp.sum(count_row, axis=1, keepdims=True) / experts_n
        ratio_rows = jnp.sum(onehot * ((count_row - mean_load) / mean_load), axis=1, keepdims=True)
        gates = gate_ref[...]
        d_gate = valid * (dot_rows + balance_weight * ratio_rows)
        d_logits = (onehot * (d_gate * gates * (1.0 - gates))).astype(bf16)
        router_t = dot_tn(d_logits, flat_ref[...])
        balance_part = jnp.sum(valid * gates * ratio_rows, axis=0, keepdims=True) / jnp.sum(
            count_row, axis=1, keepdims=True
        )
        gain_sum = jnp.zeros((1, width), f32)
        shift_sum = jnp.zeros((1, width), f32)
        for s in range(seqs):
            lo, hi = s * span, (s + 1) * span
            v = mid_ref[lo:hi]
            centered = v - jnp.mean(v, axis=-1, keepdims=True)
            inverse = lax.rsqrt(jnp.mean(centered * centered, axis=-1, keepdims=True) + epsilon)
            unit = centered * inverse
            dy = d_rows[lo:hi] + dot_nt(d_logits[lo:hi], wr_ref[...])
            gain_sum = gain_sum + jnp.sum(dy * unit, axis=0, keepdims=True)
            shift_sum = shift_sum + jnp.sum(dy, axis=0, keepdims=True)
            du = dy * g2_ref[...].reshape(1, width)
            dx = inverse * (
                du
                - jnp.mean(du, axis=-1, keepdims=True)
                - unit * jnp.mean(du * unit, axis=-1, keepdims=True)
            )
            dmid_ref[lo:hi] = cot_ref[lo:hi].astype(f32) + dx
            d_branch = dmid_ref[lo:hi].astype(bf16)
            for k in range(2):
                datt_ref[s, k] = dot_nt(d_branch, wo_ref[k * half : (k + 1) * half]).astype(bf16)

        at = (z, e, c, bit, mate, blocks, sib)

        def finish_out(k, g):
            grads_ref[3, :, k * half : (k + 1) * half] = g.reshape(width, half)

        def finish_pair(p):
            def finish(k, g):
                g = g.reshape(3, width, 128)
                for m in range(3):
                    grads_ref[m, :, k * half + p * 128 : k * half + (p + 1) * 128] = g[m]

            return finish

        out_sum = PieceSum(at, *sums_scratch[:n_sum], (0, 1), finish_out)
        pair_sums = [
            PieceSum(
                at,
                *sums_scratch[n_sum * (p + 1) : n_sum * (p + 2)],
                (1, 0) if p % 2 == 0 else (0, 1),
                finish_pair(p),
            )
            for p in range(pairs)
        ]

        def d_out(s, k):
            return remote(
                datt_ref.at[s, k], do_ref.at[z], dsend.at[s, k], drecv.at[z], 2 * c + s, base + k
            )

        def d_own(s, k):
            return pltpu.make_async_copy(datt_ref.at[s, k], do_ref.at[z], loc_sem.at[0])

        for k in range(2):
            for s in range(seqs):
                to_self = (2 * c + s == z) & (c == k)

                @pl.when(to_self)
                def _():
                    d_own(s, k).start()

                @pl.when(jnp.logical_not(to_self))
                def _():
                    d_out(s, k).start()

        sums_ref[...] = jnp.zeros_like(sums_ref)
        sums_ref[2:3] = gain_sum
        sums_ref[3:4] = shift_sum
        sums_ref[4 : 4 + experts_n] = router_t[0:experts_n]
        sums_ref[4 + experts_n : 5 + experts_n] = jnp.broadcast_to(balance_part, (1, width))
        d_branch = dmid_ref[...].astype(bf16)
        for k in range(2):
            att_k = jnp.concatenate([t_ref[s, k] for s in range(seqs)], axis=0)
            made_k = dot_tn(att_k, d_branch).astype(bf16)
            op_ref[0, k * half : (k + 1) * half] = made_k[:, :half]
            op_ref[1, k * half : (k + 1) * half] = made_k[:, half:]
        o_first = remote(op_ref.at[1 - c], osib, osend, orecv, z, sib)
        o_first.start()
        o_first.wait()
        out_sum.part[...] = (op_ref[c].astype(f32) + osib[...].astype(f32)).astype(bf16).reshape(
            2, 2, blocks, out_piece, half
        )
        out_sum.step(0)

        @pl.when(c == seq_core)
        def _():
            d_own(0, 0).wait()

        @pl.when(c != seq_core)
        def _():
            remote(datt_ref.at[0, 0], do_ref.at[z], dsend.at[0, 0], drecv.at[z], z, base).wait_recv()

        for zs in others:
            remote(datt_ref.at[0, 0], do_ref.at[zs], dsend.at[0, 0], drecv.at[zs], z, base).wait_recv()

        chain(0)
        key_bias = jnp.where(lane_of((total, 1), 0) < len_ref[0:1, 0:1], 0.0, masked_fill)
        lane = lane_of((1, 128), 1)
        later = lax.broadcasted_iota(jnp.int32, (span, span), 0) > lax.broadcasted_iota(
            jnp.int32, (span, span), 1
        )

        def pair_step(p):
            first = p * 128
            k_all = qkv_ref[:, pl.ds(half + first, 128)]
            kt_ref[...] = jnp.transpose(k_all)
            v_all = qkv_ref[:, pl.ds(2 * half + first, 128)]
            k_heads = key_heads(k_all, key_bias)
            dk_ref[...] = jnp.zeros_like(dk_ref)
            dv_ref[...] = jnp.zeros_like(dv_ref)
            for j in range(blocks):
                n = (j + 1) * span
                r = pl.ds(j * span, span)
                q = qkv_ref[r, pl.ds(first, 128)].astype(f32) * scale
                d_o = do_ref[j, :, pl.ds(first, 128)].astype(f32)
                prod_t = jnp.transpose(d_o) * attt_ref[pl.ds(first, 128), r]
                dq_t = []
                for h in range(2):
                    inside = (lane // HEAD) == h
                    spare = lane == (1 - h) * HEAD
                    q_h = jnp.where(inside, q, jnp.where(spare, 1.0, 0.0)).astype(bf16)
                    q_only = jnp.where(inside, q, 0.0).astype(bf16)
                    do_h = jnp.where(inside, d_o, 0.0).astype(bf16)
                    delta = jnp.sum(prod_t[h * HEAD : (h + 1) * HEAD], axis=0, keepdims=True)
                    s = dot_nt(k_heads[h][:n], q_h)
                    last = jnp.where(later, masked_fill, s[n - span :])
                    s = last if j == 0 else jnp.concatenate([s[: n - span], last], axis=0)
                    w = jnp.exp(s - lse_ref[pl.ds(2 * p + h, 1), r])
                    d_w = dot_nt(v_all[:n], do_h)
                    d_s = (w * (d_w - delta)).astype(bf16)
                    dv_ref[:n] += dot(w.astype(bf16), do_h)
                    dk_ref[:n] += dot(d_s, q_only)
                    dq_t.append(dot(kt_ref[h * HEAD : (h + 1) * HEAD, :n], d_s))
                dq = jnp.transpose(jnp.concatenate(dq_t, axis=0)) * scale
                dqkv_ref[r, pl.ds(first, 128)] = dq.astype(bf16)
            dqkv_ref[:, pl.ds(half + first, 128)] = dk_ref[...].astype(bf16)
            dqkv_ref[:, pl.ds(2 * half + first, 128)] = dv_ref[...].astype(bf16)
            joined = jnp.concatenate(
                [dqkv_ref[:, pl.ds(m * half + first, 128)] for m in range(3)], axis=1
            )
            grads = dot(xt_ref[...], joined).astype(bf16)
            pair_sums[p].part[...] = jnp.concatenate(
                [grads[:, m * 128 : (m + 1) * 128] for m in range(3)], axis=0
            ).reshape(2, 2, blocks, pair_piece, 128)

        todo = [(out_sum, 1)]

        def advance():
            nexts = []
            for one, n in todo:
                one.step(n)
                if n < 7:
                    nexts.append((one, n + 1))
            todo[:] = nexts

        for p in range(pairs):
            pair_step(p)
            advance()
            pair_sums[p].step(0)
            todo.append((pair_sums[p], 1))
            if p == 0:
                chain(1)

        for j in range(blocks):
            r = pl.ds(j * span, span)
            dn_ref[j] = dot_nt(dqkv_ref[r, :], w_ref[...]).astype(bf16).reshape(2, hs, width)

        def n_sib(j):
            return remote(dn_ref.at[j, 1 - c], dsib_ref.at[j], nsend.at[j], nrecv.at[j], z, sib)

        def n_out(j):
            return remote(
                dsum_ref.at[j], dnt_ref.at[seq, c], ssend.at[j], srecv.at[seq, c], j, base + seq_core
            )

        def n_own():
            return pltpu.make_async_copy(dsum_ref.at[z], dnt_ref.at[seq, c], loc_sem.at[1])

        n_order = others[1:2] + others[0:1] + others[2:] + [z]
        for j in n_order:
            n_sib(j).start()
        for i, j in enumerate(n_order):
            n_sib(j).wait_recv()
            dsum_ref[j] = (dn_ref[j, c].astype(f32) + dsib_ref[j].astype(f32)).astype(bf16)
            if i < blocks - 1:
                n_out(j).start()
            else:

                @pl.when(seq_core == c)
                def _():
                    n_own().start()

                @pl.when(seq_core != c)
                def _():
                    n_out(j).start()

        advance()
        for t in plane:
            remote(made_ref.at[0], mg_ref.at[t], msend.at[t], mrecv.at[t], z, e).wait_recv()
        m_own.wait()
        scaled = valid * gates
        expert_out = dot(picks, mg_ref[...].reshape(slots, width))
        y_ref[...] = (mid_ref[...] + scaled * expert_out).astype(bf16)
        advance()
        for s in range(seqs):
            for k in range(2):
                from_self = (2 * c + s == z) & (c == k)

                @pl.when(jnp.logical_not(from_self))
                def _():
                    remote(
                        dsum_ref.at[0], dnt_ref.at[s, k], ssend.at[0], srecv.at[s, k], z, base
                    ).wait_recv()

                @pl.when(from_self)
                def _():
                    n_own().wait()

        gains = g1_ref[...].reshape(1, width)
        gain_sum = jnp.zeros((1, width), f32)
        shift_sum = jnp.zeros((1, width), f32)
        for s in range(seqs):
            for k in range(2):
                v = hid_ref[s, k].astype(f32)
                centered = v - jnp.mean(v, axis=-1, keepdims=True)
                inverse = lax.rsqrt(jnp.mean(centered * centered, axis=-1, keepdims=True) + epsilon)
                unit = centered * inverse
                dy = dnt_ref[s, k].astype(f32)
                gain_sum = gain_sum + jnp.sum(dy * unit, axis=0, keepdims=True)
                shift_sum = shift_sum + jnp.sum(dy, axis=0, keepdims=True)
                du = dy * gains
                dx = inverse * (
                    du
                    - jnp.mean(du, axis=-1, keepdims=True)
                    - unit * jnp.mean(du * unit, axis=-1, keepdims=True)
                )
                gh_ref[s, k] = dmid_ref[(2 * s + k) * hs : (2 * s + k + 1) * hs] + dx

        sums_ref[0:1] = gain_sum
        sums_ref[1:2] = shift_sum

        def t_swap(n, te):
            return remote(sums_ref, sgot.at[n], tsend.at[n], trecv.at[n], z, te)

        partners = [sib] + mate
        for n, te in enumerate(partners):
            copy = t_swap(n, te)
            copy.start()
            if n in (1, 2):
                advance()
            copy.wait()
            sums_ref[...] = sums_ref[...] + sgot[n]

        def t_z(zt):
            return remote(sums_ref, szgot.at[z], tzsend.at[zt], tzrecv.at[z], zt, e)

        for zt in others:
            t_z(zt).start()
        advance()
        for zs in others:
            remote(sums_ref, szgot.at[zs], tzsend.at[zs], tzrecv.at[zs], z, e).wait_recv()
        for zt in others:
            t_z(zt).wait_send()
        szgot[z] = sums_ref[...]
        tot = szgot[0]
        for j in range(1, blocks):
            tot = tot + szgot[j]
        sums_ref[...] = tot

        advance()
        for i, (buf, got, final) in enumerate(((zi, ci, fi_ref), (zo, co, fo_ref))):

            @pl.when(inner)
            def _():
                r_sum(i).wait_send()
                r_load(i, (gi_ref, go_ref)[i], z, 0).start()

            r_load(i, (gi_ref, go_ref)[i], z, 0).wait()
            r_load(i, (ei_ref, eo_ref)[i], pair, 1).wait()
            final[...] = buf[0].astype(f32) + buf[1].astype(f32)

            @pl.when(inner)
            def _():
                for k in range(2):
                    r_load(i, (ei_ref, eo_ref)[i], across[k], k).start()
                for k in range(2):
                    r_load(i, (ei_ref, eo_ref)[i], across[k], k).wait()
                final[...] = final[...] + (buf[0].astype(f32) + buf[1].astype(f32))

            @pl.when(jnp.logical_not(inner))
            def _():
                r_sum(i).wait_recv()
                r_chain(i).wait_send()
                final[...] = final[...] + got[...].astype(f32)

            advance()
        while todo:
            advance()

        for s in range(seqs):
            for k in range(2):

                @pl.when(jnp.logical_not((2 * c + s == z) & (c == k)))
                def _():
                    d_out(s, k).wait_send()

        for j in n_order[:-1]:
            n_out(j).wait_send()

        @pl.when(seq_core != c)
        def _():
            n_out(z).wait_send()

        for j in n_order:
            n_sib(j).wait_send()
        for t in plane:
            m_out(t).wait_send()

    stage = blocks
    scratch = [
        pltpu.VMEM((blocks, span, half), bf16),
        pltpu.VMEM((total, 3 * half), bf16),
        pltpu.VMEM((128, total), bf16),
        pltpu.VMEM((total, 128), f32),
        pltpu.VMEM((total, 128), f32),
        pltpu.VMEM((blocks, 2, hs, width), bf16),
        pltpu.VMEM((blocks, hs, width), bf16),
        pltpu.VMEM((blocks, hs, width), bf16),
        pltpu.VMEM((seqs, 2, hs, width), bf16),
        pltpu.VMEM((2, width, part), bf16),
        pltpu.VMEM((2, part, width), bf16),
        pltpu.VMEM((width, part), bf16),
        pltpu.VMEM((part, width), bf16),
        pltpu.VMEM((width, half), bf16),
        pltpu.VMEM((1 + bits, small_rows, width), f32),
        pltpu.VMEM((blocks, small_rows, width), f32),
        pltpu.VMEM((seqs, 2, span, half), bf16),
        pltpu.VMEM((2, width, half), bf16),
        pltpu.VMEM((tokens, width), f32),
        pltpu.VMEM((columns, capacity, width), bf16),
        DMA((3,)),
        DMA((seqs, 2)),
        DMA((stage,)),
        DMA((2, 2)),
        DMA((2,)),
        DMA((2,)),
        DMA((stage,)),
        DMA((stage,)),
        DMA((stage,)),
        DMA((seqs, 2)),
        DMA,
        DMA,
        DMA((1 + bits,)),
        DMA((1 + bits,)),
        DMA((stage,)),
        DMA((stage,)),
        DMA((columns,)),
        DMA((columns,)),
    ]
    scratch += PieceSum.scratch(blocks, out_piece, half, rest)
    for _ in range(pairs):
        scratch += PieceSum.scratch(blocks, pair_piece, 128, rest)
    grads, sums, f_inner, f_outer, g_hidden, output = pl.pallas_call(
        kernel,
        name="backward",
        out_shape=[
            jax.ShapeDtypeStruct((4, width, width), bf16),
            jax.ShapeDtypeStruct((small_rows, width), f32),
            jax.ShapeDtypeStruct((width, part), f32),
            jax.ShapeDtypeStruct((part, width), f32),
            jax.ShapeDtypeStruct((seqs, 2, hs, width), f32),
            jax.ShapeDtypeStruct((tokens, width), bf16),
        ],
        in_specs=[VMEM] * 17 + [ANY] + [VMEM] * 5 + [ANY] * 4,
        out_specs=[VMEM] * 6,
        scratch_shapes=scratch,
        compiler_params=params(3),
    )(
        rows_t, weights, qkv, att_t, lse, length, attended, middle, flat, gate, slot, ids, lengths, cotangent,
        back, dots, counts, made, hidden.reshape(seqs, 2, hs, width), gain_one,
        gain_two, w_output, w_router, g_inner, g_outer, e_inner, e_outer,
    )
    return (
        grads, sums, f_inner, f_outer, g_hidden.reshape(seqs, span, width), output.reshape(seqs, span, width)
    )


def on_device(
    hidden_in,
    cotangent,
    query_weight,
    key_weight,
    value_weight,
    output_weight,
    gain_one,
    shift_one,
    gain_two,
    shift_two,
    w_router,
    w_inner,
    w_outer,
    expert_ids,
    seq_lengths,
):
    seqs, span, width = hidden_in.shape
    tokens = seqs * span
    blocks = lax.axis_size("blk")
    columns = lax.axis_size("ep") // 2
    experts_n = w_router.shape[1]
    capacity = max(2, 2 * tokens // experts_n)
    total = blocks * span
    half = width // 2
    assert seqs * 2 == blocks and experts_n == columns

    ids = expert_ids.reshape(tokens, 1)
    lengths = jnp.broadcast_to(seq_lengths[:, None, None], (seqs, 8, 128))
    router = jnp.pad(w_router, ((0, 0), (0, 128 - experts_n)))
    cot = cotangent.reshape(tokens, width)
    (
        rows_t, w_qkv, qkv, att_t, lse, attended, middle, flat, gate, slot, to_rows, scales, cot_rows, length, counts,
        near_inner, sib_inner, sib_outer,
    ) = forward(
        hidden_in, cotangent, gain_one, shift_one, gain_two, shift_two, query_weight, key_weight, value_weight,
        output_weight, router, ids, lengths, w_inner[0], w_outer[0], blocks, columns, capacity, experts_n,
    )
    back, dots, made, counts, g_inner, g_outer, e_inner, e_outer = experts(
        to_rows, scales, cot_rows, counts, w_inner[0], w_outer[0], sib_inner, sib_outer, near_inner, blocks
    )
    grads, sums, grad_inner, grad_outer, grad_hidden, output = backward(
        rows_t, w_qkv, qkv.reshape(total, 3 * half), att_t, lse, length, attended, middle, flat, gate,
        slot, ids, lengths, cot, back, dots, counts, made, hidden_in, gain_one, gain_two, output_weight, router,
        g_inner, g_outer, e_inner, e_outer, experts_n,
    )
    balance = sums[4 + experts_n, 0]
    return (
        output,
        grad_hidden,
        grads[0].astype(f32),
        grads[1].astype(f32),
        grads[2].astype(f32),
        grads[3].astype(f32),
        sums[0],
        sums[1],
        sums[2],
        sums[3],
        jnp.transpose(sums[4 : 4 + experts_n]),
        grad_inner[None],
        grad_outer[None],
        balance,
    )


def solution(mesh):
    tokens = P("ep", "blk", None)
    return jax.shard_map(
        on_device,
        mesh=mesh,
        in_specs=(tokens, tokens)
        + (P(),) * 9
        + (P("ep", None, "blk"), P("ep", "blk", None), P("ep", "blk", None, None, None), P("ep")),
        out_specs=(tokens, tokens) + (P(),) * 9 + (P("ep", None, "blk"), P("ep", "blk", None), P()),
        check_vma=False,
    )
```

```python
import functools

import jax
import jax.numpy as jnp
from jax import lax
from jax.experimental import pallas as pl
from jax.experimental.pallas import tpu as pltpu
from jax.sharding import PartitionSpec as P

HEAD = 64
MESH = pl.DeviceIdType.MESH
ANY = pl.BlockSpec(memory_space=pl.ANY)
VMEM = pl.BlockSpec(memory_space=pltpu.VMEM)
SMEM = pl.BlockSpec(memory_space=pltpu.SMEM)
DMA = pltpu.SemaphoreType.DMA
f32 = jnp.float32
bf16 = jnp.bfloat16

epsilon = 1e-05
balance_weight = 6.0
masked_fill = -1e30
VMEM_BYTES = 57 * 1024 * 1024


def dot(a, b):
    return lax.dot_general(a, b, (((1,), (0,)), ((), ())), preferred_element_type=f32)


def dot_nt(a, b):
    return lax.dot_general(a, b, (((1,), (1,)), ((), ())), preferred_element_type=f32)


def dot_tn(a, b):
    return lax.dot_general(a, b, (((0,), (0,)), ((), ())), preferred_element_type=f32)


def place():
    z = lax.axis_index("blk")
    e = lax.axis_index("ep")
    c = lax.rem(e, 2)
    return z, e, c, e - c


def remote(src, dst, send_sem, recv_sem, z, e):
    return pltpu.make_async_remote_copy(
        src, dst, send_sem, recv_sem, device_id=(z, e), device_id_type=MESH
    )


def greet(partners):
    barrier = pltpu.get_barrier_semaphore()
    for z, e in partners:
        pl.semaphore_signal(barrier, inc=1, device_id=(z, e), device_id_type=MESH)
    pl.semaphore_wait(barrier, len(partners))


def column_partners(blocks, z, c, base):
    found = [(z, base + 1 - c)]
    for step in range(1, blocks):
        for k in range(2):
            found.append((lax.rem(z + step, blocks), base + k))
    return found


def params(collective_id):
    return pltpu.CompilerParams(
        collective_id=collective_id, has_side_effects=True, vmem_limit_bytes=VMEM_BYTES
    )


def lane_of(shape, dimension):
    return lax.broadcasted_iota(jnp.int32, shape, dimension)


def key_heads(k_all, key_bias):
    lane = lane_of((1, 128), 1)
    found = []
    for h in range(2):
        inside = (lane // HEAD) == h
        spare = lane == (1 - h) * HEAD
        found.append(
            jnp.where(inside, k_all.astype(f32), jnp.where(spare, key_bias, 0.0)).astype(bf16)
        )
    return found


def forward(
    hidden, cotangent, gain_one, shift_one, gain_two, shift_two, w_query, w_key, w_value, w_output, w_router,
    ids, lengths, w_inner, w_outer, blocks, columns, capacity, experts_n,
):
    seqs, span, width = hidden.shape
    hs = span // 2
    half = width // 2
    pairs = half // 128
    total = blocks * span
    tokens = seqs * span
    slots = experts_n * capacity
    part = w_inner.shape[1]
    cap_lanes = max(128, capacity)

    def kernel(*refs):
        (
            hid_ref, cot_ref, g1_ref, s1_ref, g2_ref, s2_ref, wq_ref, wk_ref, wv_ref, wo_ref, wr_ref,
            ids_ref, lens_ref, wi_ref, we_ref,
        ) = refs[:15]
        (
            xt_out, w_out, qkv_out, attt_out, lse_ref, t_ref, mid_ref, flat_ref, gate_ref, slot_ref,
            rows_ref, sc_ref, cote_ref, len_ref, cnt_ref, li_ref, bi_ref, bo_ref,
        ) = refs[15:33]
        (
            x_ref, nb_ref, kh_ref, vt_ref, att_ref, cots_ref, lgot_ref, cown_ref, cgot_ref,
            wload, nloc, nsend, nrecv, fsend, frecv, aloc, asend, arecv, closs, csend, crecv,
            lsend, lrecv, ksend, krecv, hsend, hrecv, bsend, brecv,
            xt_ref, w_ref, qkv_ref, attt_ref, out_sem,
        ) = refs[33:]
        z, e, c, base = place()
        col = e // 2
        sib = base + 1 - c
        seq_core, seq = z // 2, lax.rem(z, 2)
        others = [lax.rem(z + step, blocks) for step in range(1, blocks)]
        plane = [lax.rem(col + step, columns) for step in range(1, columns)]
        column = column_partners(blocks, z, c, base)

        def load_w(m, ref):
            return pltpu.make_async_copy(
                ref.at[:, pl.ds(pl.multiple_of(c * half, half), half)],
                w_ref.at[:, pl.ds(m * half, half)],
                wload.at[m],
            )

        for m, ref in enumerate((wq_ref, wk_ref, wv_ref)):
            load_w(m, ref).start()
        gain_row, shift_row = g1_ref[...].reshape(1, width), s1_ref[...].reshape(1, width)
        for s in range(seqs):
            for k in range(2):
                v = hid_ref[s, k].astype(f32)
                centered = v - jnp.mean(v, axis=-1, keepdims=True)
                inverse = lax.rsqrt(jnp.mean(centered * centered, axis=-1, keepdims=True) + epsilon)
                nb_ref[s, k] = (centered * inverse * gain_row + shift_row).astype(bf16)
        greet(column + [(z, 2 * t + c) for t in plane])

        def n_out(s, k):
            return remote(
                nb_ref.at[s, k], x_ref.at[z, k], nsend.at[s, k], nrecv.at[z], 2 * c + s, base + k
            )

        def n_own(s, k):
            return pltpu.make_async_copy(nb_ref.at[s, k], x_ref.at[z, k], nloc)

        for k in range(2):
            for s in range(seqs):
                to_self = (2 * c + s == z) & (c == k)

                @pl.when(to_self)
                def _():
                    n_own(s, k).start()

                @pl.when(jnp.logical_not(to_self))
                def _():
                    n_out(s, k).start()

        to_lens = remote(lens_ref, lgot_ref, lsend, lrecv, z, sib)
        to_lens.start()
        lane = lane_of((tokens, 128), 1)
        onehot = (lane == ids_ref[...]).astype(f32)
        place_in = z * span + lane_of((span, 1), 0)
        valid = jnp.concatenate(
            [(place_in < lens_ref[s, 0:1, 0:1]).astype(f32) for s in range(seqs)], axis=0
        )
        cown_ref[...] = jnp.broadcast_to(jnp.sum(onehot * valid, axis=0, keepdims=True), (8, 128))

        def k_out(n, to_z, to_e):
            return remote(cown_ref, cgot_ref.at[z, c], ksend.at[n], krecv.at[z, c], to_z, to_e)

        for n, (to_z, to_e) in enumerate(column):
            k_out(n, to_z, to_e).start()
        earlier = (lane_of((tokens, tokens), 0) > lane_of((tokens, tokens), 1)).astype(f32).astype(bf16)
        rank = dot(earlier, onehot.astype(bf16))
        slot = jnp.sum(onehot * (rank + (lane * capacity).astype(f32)), axis=1, keepdims=True)
        slot_ref[...] = slot
        slot_row = jnp.transpose(jnp.broadcast_to(slot, (tokens, 128)))[0:1]
        to_slots = (lane_of((slots, tokens), 0).astype(f32) == slot_row).astype(f32).astype(bf16)
        cots_ref[...] = (
            dot(to_slots, cot_ref[...]).astype(bf16).reshape(columns, capacity, width)
        )

        def c_out(t):
            return remote(cots_ref.at[t], cote_ref.at[col], csend.at[t], crecv.at[col], z, 2 * t + c)

        c_own = pltpu.make_async_copy(cots_ref.at[col], cote_ref.at[col], closs)
        c_own.start()
        for t in plane:
            c_out(t).start()
        for m, ref in enumerate((wq_ref, wk_ref, wv_ref)):
            load_w(m, ref).wait()

        def n_sib(zs):
            return remote(x_ref.at[zs, c], x_ref.at[zs, c], fsend.at[zs], frecv.at[zs], z, sib)

        for zs in [z] + others:
            if zs is z:

                @pl.when(c == seq_core)
                def _():
                    n_own(0, 0).wait()

                @pl.when(c != seq_core)
                def _():
                    remote(nb_ref.at[0, 0], x_ref.at[z, c], nsend.at[0, 0], nrecv.at[z], z, base).wait_recv()
            else:
                remote(nb_ref.at[0, 0], x_ref.at[zs, c], nsend.at[0, 0], nrecv.at[zs], z, base).wait_recv()
            n_sib(zs).start()

        def h_out(step):
            side = 0 if step == 1 else 1
            return remote(wi_ref, li_ref.at[side], hsend.at[side], hrecv.at[side], z + step, e)

        def b_out(i):
            src, dst = ((wi_ref, bi_ref), (we_ref, bo_ref))[i]
            return remote(src, dst, bsend.at[i], brecv.at[i], z, sib)

        @pl.when(z < blocks - 1)
        def _():
            h_out(1).start()

        @pl.when(z > 0)
        def _():
            h_out(-1).start()

        for zs in [z] + others:
            remote(
                x_ref.at[zs, 1 - c], x_ref.at[zs, 1 - c], fsend.at[zs], frecv.at[zs], z, sib
            ).wait_recv()
            x_z = x_ref[zs].reshape(span, width)
            qkv_ref[zs] = dot(x_z, w_ref[...]).astype(bf16)
            xt_ref[:, pl.ds(pl.multiple_of(zs * span, span), span)] = jnp.transpose(x_z)
        for i in range(2):
            b_out(i).start()
        to_lens.wait()
        seq_len = jnp.where(c == seq_core, lens_ref[seq], lgot_ref[seq])
        len_ref[...] = seq_len
        key_bias = jnp.where(lane_of((total, 1), 0) < seq_len[0:1, 0:1], 0.0, masked_fill)
        for p in range(pairs):
            k_all = jnp.concatenate(
                [qkv_ref[j, :, half + p * 128 : half + (p + 1) * 128] for j in range(blocks)], axis=0
            )
            for h, k_h in enumerate(key_heads(k_all, key_bias)):
                kh_ref[2 * p + h] = k_h
            for j in range(blocks):
                vt_ref[p * 128 : (p + 1) * 128, j * span : (j + 1) * span] = jnp.transpose(
                    qkv_ref[j, :, 2 * half + p * 128 : 2 * half + (p + 1) * 128]
                )
        outs = [
            pltpu.make_async_copy(src, dst, out_sem.at[n])
            for n, (src, dst) in enumerate(
                ((xt_ref, xt_out), (w_ref, w_out), (qkv_ref, qkv_out), (attt_ref, attt_out))
            )
        ]
        for out in outs[:3]:
            out.start()
        later = lane_of((span, span), 0) > lane_of((span, span), 1)
        lane_row = lane_of((1, 128), 1)

        def a_out(j):
            return remote(
                att_ref.at[j], t_ref.at[seq, c], asend.at[j], arecv.at[seq, c], j, base + seq_core
            )

        def a_own(j):
            return pltpu.make_async_copy(att_ref.at[j], t_ref.at[seq, c], aloc)

        for j in [0] + list(range(blocks - 1, 0, -1)):
            n = (j + 1) * span

            def pair_step(p, _):
                first = pl.multiple_of(p * 128, 128)
                q = qkv_ref[j, :, pl.ds(first, 128)].astype(f32) * (HEAD**-0.5)
                out_t = []
                for h in range(2):
                    inside = (lane_row // HEAD) == h
                    spare = lane_row == (1 - h) * HEAD
                    q_h = jnp.where(inside, q, jnp.where(spare, 1.0, 0.0)).astype(bf16)
                    s = dot_nt(kh_ref[2 * p + h, :n], q_h)
                    last = jnp.where(later, masked_fill, s[n - span :])
                    s = last if j == 0 else jnp.concatenate([s[: n - span], last], axis=0)
                    top = jnp.max(s, axis=0, keepdims=True)
                    w = jnp.exp(s - top)
                    total_w = jnp.sum(w, axis=0, keepdims=True)
                    o_t = dot(vt_ref[pl.ds(pl.multiple_of(first + h * HEAD, HEAD), HEAD), :n], w.astype(bf16))
                    out_t.append(o_t / total_w)
                    lse_ref[pl.ds(2 * p + h, 1), pl.ds(j * span, span)] = top + jnp.log(total_w)
                o = jnp.concatenate(out_t, axis=0)
                attt_ref[pl.ds(first, 128), pl.ds(j * span, span)] = o
                att_ref[j, :, pl.ds(first, 128)] = jnp.transpose(o).astype(bf16)
                return 0

            lax.fori_loop(0, pairs, pair_step, 0)
            to_self = (z == j) & (c == seq_core)

            @pl.when(to_self)
            def _():
                a_own(j).start()

            @pl.when(jnp.logical_not(to_self))
            def _():
                a_out(j).start()

        outs[3].start()
        for s in range(seqs):
            for k in range(2):
                from_self = (2 * c + s == z) & (c == k)

                @pl.when(from_self)
                def _():
                    a_own(0).wait()

                @pl.when(jnp.logical_not(from_self))
                def _():
                    remote(att_ref.at[0], t_ref.at[s, k], asend.at[0], arecv.at[s, k], z, base).wait_recv()

        for s in range(seqs):
            r = pl.ds(s * span, span)
            branch = dot(t_ref[s, 0], wo_ref[0:half]) + dot(t_ref[s, 1], wo_ref[half:])
            v = hid_ref[s].reshape(span, width).astype(f32) + branch
            mid_ref[r, :] = v
            centered = v - jnp.mean(v, axis=-1, keepdims=True)
            inverse = lax.rsqrt(jnp.mean(centered * centered, axis=-1, keepdims=True) + epsilon)
            flat_ref[r, :] = (
                centered * inverse * g2_ref[...].reshape(1, width) + s2_ref[...].reshape(1, width)
            ).astype(bf16)
        logits = dot(flat_ref[...], wr_ref[...])
        gate = jax.nn.sigmoid(jnp.sum(logits * onehot, axis=1, keepdims=True))
        gate_ref[...] = gate
        rows_ref[...] = (
            dot(to_slots, flat_ref[...]).astype(bf16).reshape(columns, capacity, width)
        )
        from_slots = lane_of((tokens, slots), 1).astype(f32) == slot_ref[...]
        scales = jnp.sum(jnp.where(from_slots, valid * gate, 0.0), axis=0, keepdims=True)
        if cap_lanes != capacity:
            sc_ref[...] = jnp.zeros_like(sc_ref)
        for t in range(columns):
            sc_ref[t, :, 0:capacity] = jnp.broadcast_to(
                scales[:, t * capacity : (t + 1) * capacity], (8, capacity)
            )

        for out in outs:
            out.wait()
        for n, (to_z, to_e) in enumerate(column):
            remote(cown_ref, cgot_ref.at[to_z, lax.rem(to_e, 2)], ksend.at[n], krecv.at[to_z, lax.rem(to_e, 2)], z, sib).wait_recv()
            k_out(n, to_z, to_e).wait_send()
        cgot_ref[z, c] = cown_ref[...]
        tot = jnp.zeros((8, 128), f32)
        for zs in range(blocks):
            for k in range(2):
                tot = tot + cgot_ref[zs, k]
        cnt_ref[...] = tot
        c_own.wait()
        for t in plane:
            c_out(t).wait_send()
            remote(cots_ref.at[t], cote_ref.at[t], csend.at[t], crecv.at[t], z, e).wait_recv()
        for s in range(seqs):
            for k in range(2):

                @pl.when(jnp.logical_not((2 * c + s == z) & (c == k)))
                def _():
                    n_out(s, k).wait_send()

        for zs in [z] + others:
            n_sib(zs).wait_send()
        for j in range(blocks):

            @pl.when(jnp.logical_not((z == j) & (c == seq_core)))
            def _():
                a_out(j).wait_send()

        for i in range(2):
            b_out(i).wait()

        @pl.when(z < blocks - 1)
        def _():
            h_out(1).wait_send()
            remote(wi_ref, li_ref.at[1], hsend.at[1], hrecv.at[1], z, e).wait_recv()

        @pl.when(z > 0)
        def _():
            h_out(-1).wait_send()
            remote(wi_ref, li_ref.at[0], hsend.at[0], hrecv.at[0], z, e).wait_recv()

    out_shapes = [
        ((width, total), bf16),
        ((width, 3 * half), bf16),
        ((blocks, span, 3 * half), bf16),
        ((half, total), f32),
        ((2 * pairs, total), f32),
        ((seqs, 2, span, half), bf16),
        ((tokens, width), f32),
        ((tokens, width), bf16),
        ((tokens, 1), f32),
        ((tokens, 1), f32),
        ((columns, capacity, width), bf16),
        ((columns, 8, cap_lanes), f32),
        ((columns, capacity, width), bf16),
        ((8, 128), jnp.int32),
        ((8, 128), f32),
        ((2, width, part), bf16),
        ((width, part), bf16),
        ((part, width), bf16),
    ]
    return pl.pallas_call(
        kernel,
        name="forward",
        out_shape=[jax.ShapeDtypeStruct(a, b) for a, b in out_shapes],
        in_specs=[VMEM] * 6 + [ANY] * 3 + [VMEM] * 4 + [ANY] * 2,
        out_specs=[ANY] * 4 + [VMEM] * 8 + [ANY] + [VMEM] * 2 + [ANY] * 3,
        scratch_shapes=[
            pltpu.VMEM((blocks, 2, hs, width), bf16),
            pltpu.VMEM((seqs, 2, hs, width), bf16),
            pltpu.VMEM((2 * pairs, total, 128), bf16),
            pltpu.VMEM((half, total), bf16),
            pltpu.VMEM((blocks, span, half), bf16),
            pltpu.VMEM((columns, capacity, width), bf16),
            pltpu.VMEM((seqs, 8, 128), jnp.int32),
            pltpu.VMEM((8, 128), f32),
            pltpu.VMEM((blocks, 2, 8, 128), f32),
            DMA((3,)),
            DMA,
            DMA((seqs, 2)),
            DMA((blocks,)),
            DMA((blocks,)),
            DMA((blocks,)),
            DMA,
            DMA((blocks,)),
            DMA((seqs, 2)),
            DMA,
            DMA((columns,)),
            DMA((columns,)),
            DMA,
            DMA,
            DMA((2 * blocks - 1,)),
            DMA((blocks, 2)),
            DMA((2,)),
            DMA((2,)),
            DMA((2,)),
            DMA((2,)),
            pltpu.VMEM((width, total), bf16),
            pltpu.VMEM((width, 3 * half), bf16),
            pltpu.VMEM((blocks, span, 3 * half), bf16),
            pltpu.VMEM((half, total), f32),
            DMA((4,)),
        ],
        compiler_params=params(1),
    )(
        hidden.reshape(seqs, 2, hs, width), cotangent.reshape(tokens, width),
        gain_one, shift_one, gain_two, shift_two,
        w_query, w_key, w_value, w_output, w_router, ids, lengths, w_inner, w_outer,
    )


def slice_order(z):
    near = z + 1 - 2 * lax.rem(z, 2)
    across = jnp.where(z < 2, 2, 1)
    inner = (z > 0) & (z < 3)
    return [jnp.where(inner, across, near), jnp.where(inner, near, across), z, jnp.where(z < 2, 3, 0)]


def experts(
    rows, scales, cot, counts, w_inner, w_outer, sib_inner, sib_outer, near_inner, blocks
):
    columns, capacity, width = rows.shape
    cap_lanes = scales.shape[2]
    total = columns * capacity
    part = w_inner.shape[1]
    block = 256
    count = total // block
    per = block // capacity
    assert blocks == 4 and columns == count * per

    def kernel(*refs):
        rows_ref, sc_ref, cot_ref, cnt_ref, wi_ref, we_ref, bi_ref, bo_ref, li_ref = refs[:9]
        back_ref, dots_ref, made_ref, tot_ref, gi_out, go_out, ei_ref, eo_ref = refs[9:17]
        (
            x_ref, xt_ref, d_ref, scg_ref, cntg_ref, in_ref, out_ref, oacc, dacc, act_ref, dpre_ref,
            dr_ref, dots_own, sgi_ref, sgo_ref, ggi_ref, ggo_ref,
            xloc, xsend, xrecv, scsend, screcv, ksend, krecv, wloc, wsend, wrecv, vsend, vrecv,
            bloc, dsend, drecv, gsend, grecv, ssend, srecv, gi_ref, go_ref, keep_sem,
        ) = refs[17:]
        z, e, c, base = place()
        col = e // 2
        sib = base + 1 - c
        inner = (z > 0) & (z < blocks - 1)
        end = jnp.logical_not(inner)
        plane = [lax.rem(col + step, columns) for step in range(1, columns)]
        greet(column_partners(blocks, z, c, base) + [(z, 2 * t + c) for t in plane])

        def x_out(t):
            return remote(rows_ref.at[t], x_ref.at[col], xsend.at[t], xrecv.at[col], z, 2 * t + c)

        def sc_out(t):
            return remote(sc_ref.at[t], scg_ref.at[col], scsend.at[t], screcv.at[col], z, 2 * t + c)

        def cnt_out(t):
            return remote(cnt_ref, cntg_ref.at[col], ksend.at[t], krecv.at[col], z, 2 * t + c)

        x_own = pltpu.make_async_copy(rows_ref.at[col], x_ref.at[col], xloc)
        x_own.start()
        for t in plane:
            sc_out(t).start()
            x_out(t).start()
            cnt_out(t).start()
        scg_ref[col] = sc_ref[col]
        cntg_ref[col] = cnt_ref[...]

        hop_two = lax.rem(z + 2, blocks)
        pair = z + 1 - 2 * lax.rem(z, 2)

        lo_half, hi_half = pl.ds(0, part), pl.ds(part, part)

        def views(s, which):
            return (in_ref.at[s, :, which], out_ref.at[s, which])

        sources = ((wi_ref, we_ref), (bi_ref, bo_ref))

        def w_own(i, k):
            return pltpu.make_async_copy(
                sources[k][i], views(z, (lo_half, hi_half)[k])[i], wloc.at[i, k]
            )

        def beside(side):
            return z - 1 if side == 0 else z + 1

        def w_near(side):
            return pltpu.make_async_copy(li_ref.at[side], views(beside(side), lo_half)[0], wloc.at[2, side])

        def w_near_sib(side):
            s = beside(side)
            return remote(li_ref.at[side], views(s, hi_half)[0], vsend.at[0, s], vrecv.at[0, s], z, sib)

        def w_hop(side):
            return remote(we_ref, views(z, lo_half)[1], wsend.at[1, side], wrecv.at[1, z], beside(side), e)

        def w_pass(i, side):
            s = beside(side)
            src = li_ref.at[side] if i == 0 else views(s, lo_half)[1]
            return remote(src, views(s, lo_half)[i], wsend.at[2 + i, side], wrecv.at[i, s], beside(1 - side), e)

        def w_got(i, s):
            return remote(views(s, lo_half)[i], views(s, lo_half)[i], wsend.at[0, 0], wrecv.at[i, s], z, e)

        def w_sib(i, s):
            return remote(views(s, lo_half)[i], views(s, hi_half)[i], vsend.at[i, s], vrecv.at[i, s], z, sib)

        def w_sib_got(i, s):
            return remote(views(s, lo_half)[i], views(s, hi_half)[i], vsend.at[i, z], vrecv.at[i, s], z, sib)

        def w_last(i):
            s = hop_two
            to = jnp.where(z == 1, 0, blocks - 1)
            return remote(views(s, lo_half)[i], views(s, lo_half)[i], wsend.at[4 + i, 0], wrecv.at[i, s], to, e)

        def has(side):
            return z > 0 if side == 0 else z < blocks - 1

        for side in range(2):

            @pl.when(has(side))
            def _():
                w_hop(side).start()

        for side in range(2):

            @pl.when(inner)
            def _():
                w_pass(0, side).start()

        for side in range(2):

            @pl.when(has(side))
            def _():
                w_near(side).start()
                w_near_sib(side).start()

        for i in range(2):
            for k in range(2):
                w_own(i, k).start()

        order = slice_order(z)
        far = order[3]
        oacc[...] = jnp.zeros_like(oacc)
        dacc[...] = jnp.zeros_like(dacc)
        first_block = col // per

        def at_block(b):
            return pl.ds(pl.multiple_of(b * per, per), per)

        def row_step(s, b, fresh):
            x_b = x_ref[at_block(b)].reshape(block, width)
            r = pl.ds(pl.multiple_of(b * block, block), block)
            if fresh:
                row = jnp.concatenate(
                    [scg_ref[b * per + i, :, 0:capacity] for i in range(per)], axis=1
                )
                column = jnp.transpose(row)[:, 0:1]
                cots = cot_ref[at_block(b)].reshape(block, width).astype(f32)
                d_ref[r, :] = (column * cots).astype(bf16)
            pre = dot(x_b, in_ref[s])
            cdf = 0.5 * (1.0 + lax.erf(pre * (0.5**0.5)))
            act = (pre * cdf).astype(bf16)
            slope = cdf + pre * (jnp.exp(-0.5 * pre * pre) * ((2 * jnp.pi) ** -0.5))
            d_act = dot_nt(d_ref[r, :], out_ref[s])
            d_pre = (d_act * slope).astype(bf16)
            act_ref[r, :] = act
            dpre_ref[r, :] = d_pre
            oacc[r, :] += dot(act, out_ref[s])
            dacc[r, :] += dot_nt(d_pre, in_ref[s])

        def grads(s):
            g_inner = dot(xt_ref[...], dpre_ref[...])
            gi_ref[s] = g_inner[:, :part].astype(bf16)
            sgi_ref[s] = g_inner[:, part:].astype(bf16)
            g_outer = dot_tn(act_ref[...], d_ref[...])
            go_ref[s] = g_outer[:part].astype(bf16)
            sgo_ref[s] = g_outer[part:].astype(bf16)
            for i in range(2):
                g_sib(i, s).start()

        def g_keep(i, n):
            return pltpu.make_async_copy(
                (gi_ref, go_ref)[i].at[order[2 + n]], (gi_out, go_out)[i].at[n], keep_sem.at[i, n]
            )

        def g_sib(i, s):
            src, dst = ((sgi_ref, ggi_ref), (sgo_ref, ggo_ref))[i]
            return remote(src.at[s], dst.at[s], gsend.at[i, s], grecv.at[i, s], z, sib)

        def join(s):
            for i, (total_ref, got_ref) in enumerate(((gi_ref, ggi_ref), (go_ref, ggo_ref))):
                g_sib(i, s).wait_recv()
                total_ref[s] = (total_ref[s].astype(f32) + got_ref[s].astype(f32)).astype(bf16)

        def s_out(i, s):
            src, dst = ((gi_ref, ei_ref), (go_ref, eo_ref))[i]
            return remote(src.at[s], dst.at[z], ssend.at[i, s], srecv.at[i, z], s, e)

        def block_at(m):
            return lax.rem(first_block + count - m, count)

        for side in range(2):

            @pl.when(has(side))
            def _():
                w_got(1, beside(side)).wait_recv()
                w_sib(1, beside(side)).start()

            @pl.when(inner)
            def _():
                w_pass(1, side).start()

        for side in range(2):

            @pl.when(has(side))
            def _():
                w_near(side).wait()
                for i in range(2):
                    w_sib_got(i, beside(side)).wait_recv()

        for m in range(count):
            b = block_at(m)
            for i in range(per):
                t = b * per + i

                @pl.when(t == col)
                def _():
                    x_own.wait()

                @pl.when(t != col)
                def _():
                    remote(sc_ref.at[0], scg_ref.at[t], scsend.at[t], screcv.at[t], z, e).wait_recv()
                    remote(rows_ref.at[0], x_ref.at[t], xsend.at[t], xrecv.at[t], z, e).wait_recv()

            row_step(order[0], b, True)
        def hand_on(i):
            w_got(i, hop_two).wait_recv()
            w_sib(i, hop_two).start()

            @pl.when(inner)
            def _():
                w_last(i).start()

        hand_on(0)
        xt_ref[...] = jnp.transpose(x_ref[...].reshape(total, width))
        grads(order[0])

        @pl.when(end)
        def _():
            hand_on(1)
            for i in range(2):
                w_sib_got(i, hop_two).wait_recv()

        def loop(s, start):
            def body(b, _):
                row_step(s, b, False)
                return 0

            lax.fori_loop(start, count, body, 0)

        row_step(order[1], 0, False)
        join(order[0])
        for i in range(2):
            s_out(i, order[0]).start()
        loop(order[1], 1)

        @pl.when(inner)
        def _():
            hand_on(1)

        grads(order[1])
        for i in range(2):
            for k in range(2):
                w_own(i, k).wait()
        row_step(order[2], 0, False)
        join(order[1])
        for i in range(2):
            s_out(i, order[1]).start()
        loop(order[2], 1)

        @pl.when(inner)
        def _():
            for i in range(2):
                w_sib_got(i, hop_two).wait_recv()

        @pl.when(end)
        def _():
            for i in range(2):
                w_got(i, far).wait_recv()
                w_sib(i, far).start()

        grads(order[2])

        @pl.when(end)
        def _():
            for i in range(2):
                w_sib_got(i, far).wait_recv()

        def d_out(t):
            return remote(dr_ref.at[t], back_ref.at[col], dsend.at[0, t], drecv.at[0, col], z, 2 * t + c)

        def dots_out(t):
            return remote(dots_own.at[t], dots_ref.at[col], dsend.at[1, t], drecv.at[1, col], z, 2 * t + c)

        b_own = pltpu.make_async_copy(dr_ref.at[col], back_ref.at[col], bloc)
        for m in list(range(1, count)) + [0]:
            b = block_at(m)
            row_step(order[3], b, False)
            if m == 1:
                join(order[2])
                for i in range(2):
                    g_keep(i, 0).start()
            r = pl.ds(pl.multiple_of(b * block, block), block)
            made = oacc[r, :].astype(bf16)
            made_ref[at_block(b)] = made.reshape(per, capacity, width)
            dr_ref[at_block(b)] = dacc[r, :].astype(bf16).reshape(per, capacity, width)
            cots = cot_ref[at_block(b)].reshape(block, width).astype(f32)
            sums = jnp.sum(cots * made.astype(f32), axis=1, keepdims=True)
            row = jnp.transpose(jnp.broadcast_to(sums, (block, 128)))[0:8]
            for i in range(per):
                t = b * per + i
                if cap_lanes != capacity:
                    dots_own[t] = jnp.zeros((8, cap_lanes), f32)
                dots_own[t, :, 0:capacity] = row[:, i * capacity : (i + 1) * capacity]

                @pl.when(t == col)
                def _():
                    b_own.start()
                    dots_ref[t] = dots_own[t]

                @pl.when(t != col)
                def _():
                    d_out(t).start()
                    dots_out(t).start()

        grads(order[3])
        join(order[3])
        for i in range(2):
            g_keep(i, 1).start()

        for t in plane:
            x_out(t).wait_send()
            sc_out(t).wait_send()
            cnt_out(t).wait_send()
            remote(cnt_ref, cntg_ref.at[t], ksend.at[t], krecv.at[t], z, e).wait_recv()
        tot = cntg_ref[0]
        for t in range(1, columns):
            tot = tot + cntg_ref[t]
        tot_ref[...] = tot
        for i in range(2):
            for side in range(2):

                @pl.when(inner)
                def _():
                    w_pass(i, side).wait_send()

            w_sib(i, hop_two).wait_send()

            @pl.when(end)
            def _():
                w_sib(i, far).wait_send()

            for n in range(blocks):
                g_sib(i, n).wait_send()
            for n in range(2):
                g_keep(i, n).wait()
            s_out(i, order[0]).wait_send()
            s_out(i, order[1]).wait_send()
            got = (ei_ref, eo_ref)[i]

            def arrived(zs):
                return remote(got.at[0], got.at[zs], ssend.at[i, 0], srecv.at[i, zs], z, e)

            arrived(pair).wait_recv()

            @pl.when(inner)
            def _():
                w_last(i).wait_send()
                for k in range(2):
                    arrived(lax.rem(2 * (z // 2) + 2 + k, blocks)).wait_recv()

        for side in range(2):

            @pl.when(has(side))
            def _():
                w_hop(side).wait_send()
                w_near_sib(side).wait_send()
                w_sib(1, beside(side)).wait_send()

        b_own.wait()
        for t in plane:
            d_out(t).wait_send()
            dots_out(t).wait_send()
            remote(dr_ref.at[0], back_ref.at[t], dsend.at[0, t], drecv.at[0, t], z, e).wait_recv()
            remote(dots_own.at[0], dots_ref.at[t], dsend.at[1, t], drecv.at[1, t], z, e).wait_recv()

    out_shapes = [
        ((columns, capacity, width), bf16),
        ((columns, 8, cap_lanes), f32),
        ((columns, capacity, width), bf16),
        ((8, 128), f32),
        ((2, width, part), bf16),
        ((2, part, width), bf16),
        ((blocks, width, part), bf16),
        ((blocks, part, width), bf16),
    ]
    return pl.pallas_call(
        kernel,
        name="experts",
        out_shape=[jax.ShapeDtypeStruct(a, b) for a, b in out_shapes],
        in_specs=[VMEM] * 4 + [ANY] * 5,
        out_specs=[ANY] + [VMEM] * 3 + [ANY] * 4,
        scratch_shapes=[
            pltpu.VMEM((columns, capacity, width), bf16),
            pltpu.VMEM((width, total), bf16),
            pltpu.VMEM((total, width), bf16),
            pltpu.VMEM((columns, 8, cap_lanes), f32),
            pltpu.VMEM((columns, 8, 128), f32),
            pltpu.VMEM((blocks, width, 2 * part), bf16),
            pltpu.VMEM((blocks, 2 * part, width), bf16),
            pltpu.VMEM((total, width), f32),
            pltpu.VMEM((total, width), f32),
            pltpu.VMEM((total, 2 * part), bf16),
            pltpu.VMEM((total, 2 * part), bf16),
            pltpu.VMEM((columns, capacity, width), bf16),
            pltpu.VMEM((columns, 8, cap_lanes), f32),
            pltpu.VMEM((blocks, width, part), bf16),
            pltpu.VMEM((blocks, part, width), bf16),
            pltpu.VMEM((blocks, width, part), bf16),
            pltpu.VMEM((blocks, part, width), bf16),
            DMA,
            DMA((columns,)),
            DMA((columns,)),
            DMA((columns,)),
            DMA((columns,)),
            DMA((columns,)),
            DMA((columns,)),
            DMA((3, 2)),
            DMA((6, 2)),
            DMA((2, blocks)),
            DMA((2, blocks)),
            DMA((2, blocks)),
            DMA,
            DMA((2, columns)),
            DMA((2, columns)),
            DMA((2, blocks)),
            DMA((2, blocks)),
            DMA((2, blocks)),
            DMA((2, blocks)),
            pltpu.VMEM((blocks, width, part), bf16),
            pltpu.VMEM((blocks, part, width), bf16),
            DMA((2, 2)),
        ],
        compiler_params=params(2),
    )(rows, scales, cot, counts, w_inner, w_outer, sib_inner, sib_outer, near_inner)


class PieceSum:
    def __init__(self, at, part, got1, got2, got3, gotr, full, sem, rsem, zsem, zrsem, order, finish):
        self.at, self.part, self.full = at, part, full
        self.got1, self.got2, self.got3, self.gotr = got1, got2, got3, gotr
        self.sem, self.rsem, self.zsem, self.zrsem = sem, rsem, zsem, zrsem
        z, e, c, bit, mate, blocks, sib = at
        self.first, self.second = order
        self.finish = finish
        self.rest = len(bit) - 2

    def swap(self, n, src, dst, e):
        return remote(src, dst, self.sem.at[n], self.rsem.at[n], self.at[0], e)

    def halves(self):
        z, e, c, bit, mate, blocks, sib = self.at
        return self.swap(0, self.part.at[1 - bit[self.first]], self.got1, mate[self.first])

    def quarters(self):
        z, e, c, bit, mate, blocks, sib = self.at
        b1, b2 = bit[self.first], bit[self.second]
        return self.swap(1, self.part.at[b1, 1 - b2], self.got2, mate[self.second])

    def to_z(self, zt):
        z, e, c, bit, mate, blocks, sib = self.at
        b1, b2 = bit[self.first], bit[self.second]
        return remote(
            self.part.at[b1, b2, zt], self.got3.at[z], self.zsem.at[0, zt], self.zrsem.at[0, z], zt, e
        )

    def own(self):
        z, e, c, bit, mate, blocks, sib = self.at
        return self.full.at[c, bit[self.first], bit[self.second], z]

    def back_z(self, zt):
        z, e, c, bit, mate, blocks, sib = self.at
        return remote(self.own(), self.own(), self.zsem.at[1, zt], self.zrsem.at[1, z], zt, e)

    def back_quarter(self):
        z, e, c, bit, mate, blocks, sib = self.at
        at = self.full.at[c, bit[self.first], bit[self.second]]
        return self.swap(2, at, at, mate[self.second])

    def back_half(self):
        z, e, c, bit, mate, blocks, sib = self.at
        at = self.full.at[c, bit[self.first]]
        return self.swap(3, at, at, mate[self.first])

    def to_sibling(self):
        z, e, c, bit, mate, blocks, sib = self.at
        return self.swap(4, self.full.at[c], self.full.at[c], sib)

    def step(self, n):
        z, e, c, bit, mate, blocks, sib = self.at
        b1, b2 = bit[self.first], bit[self.second]
        others = [lax.rem(z + step, blocks) for step in range(1, blocks)]
        if n == 0:
            self.halves().start()
        elif n == 1:
            self.halves().wait()
            self.part[b1] = (self.part[b1].astype(f32) + self.got1[...].astype(f32)).astype(bf16)
            self.quarters().start()
        elif n == 2:
            self.quarters().wait()
            self.part[b1, b2] = (self.part[b1, b2].astype(f32) + self.got2[...].astype(f32)).astype(bf16)
            for zt in others:
                self.to_z(zt).start()
        elif n == 3:
            for zs in others:
                remote(
                    self.got3.at[0], self.got3.at[zs], self.zsem.at[0, zs], self.zrsem.at[0, zs], z, e
                ).wait_recv()
            for zt in others:
                self.to_z(zt).wait_send()
            self.got3[z] = self.part[b1, b2, z]
            total = self.got3[0].astype(f32)
            for j in range(1, blocks):
                total = total + self.got3[j].astype(f32)
            own = self.own()
            own[...] = total.astype(bf16)
            for r in range(self.rest):
                copy = self.swap(5 + r, own, self.gotr.at[r], mate[2 + r])
                copy.start()
                copy.wait()
                own[...] = (own[...].astype(f32) + self.gotr[r].astype(f32)).astype(bf16)
            for zt in others:
                self.back_z(zt).start()
        elif n == 4:
            for zs in others:
                at = self.full.at[c, b1, b2, zs]
                remote(at, at, self.zsem.at[1, zs], self.zrsem.at[1, zs], z, e).wait_recv()
            for zt in others:
                self.back_z(zt).wait_send()
            self.back_quarter().start()
        elif n == 5:
            self.back_quarter().wait()
            self.back_half().start()
        elif n == 6:
            self.back_half().wait()
            self.to_sibling().start()
        elif n == 7:
            self.to_sibling().wait()
            for k in range(2):
                self.finish(k, self.full[k])

    @staticmethod
    def scratch(blocks, piece, lanes, rest):
        return [
            pltpu.VMEM((2, 2, blocks, piece, lanes), bf16),
            pltpu.VMEM((2, blocks, piece, lanes), bf16),
            pltpu.VMEM((blocks, piece, lanes), bf16),
            pltpu.VMEM((blocks, piece, lanes), bf16),
            pltpu.VMEM((max(1, rest), piece, lanes), bf16),
            pltpu.VMEM((2, 2, 2, blocks, piece, lanes), bf16),
            DMA((5 + rest,)),
            DMA((5 + rest,)),
            DMA((2, blocks)),
            DMA((2, blocks)),
        ]


def backward(
    rows_t, weights, qkv, att_t, lse, length, attended, middle, flat, gate, slot, ids, lengths, cotangent,
    back, dots, counts, made, hidden, gain_one, gain_two, w_output, w_router, g_inner, g_outer, e_inner, e_outer,
    experts_n,
):
    width, total = rows_t.shape
    half = weights.shape[1] // 3
    pairs = half // 128
    seqs, _, span, _ = attended.shape
    blocks = total // span
    columns, capacity, _ = back.shape
    slots = columns * capacity
    tokens = seqs * span
    hs = span // 2
    scale = HEAD**-0.5
    part = g_inner.shape[2]
    bits = columns.bit_length() - 1
    assert columns == 1 << bits and bits >= 2 and blocks == 4
    rest = bits - 2
    small_rows = -(-(5 + experts_n) // 8) * 8
    out_piece, pair_piece = width // (4 * blocks), 3 * width // (4 * blocks)
    n_sum = 10

    def kernel(*refs):
        (
            xt_in, w_in, qkv_in, attt_in, lse_ref, len_ref, t_in, mid_in, flat_in, gate_ref, slot_ref, ids_ref,
            lens_ref, cot_in, back_in, dots_ref, cnt_ref, made_ref, hid_in, g1_ref, g2_ref, wo_in, wr_ref,
            gi_ref, go_ref, ei_ref, eo_ref,
        ) = refs[:27]
        grads_ref, sums_ref, fi_ref, fo_ref, gh_ref, y_ref = refs[27:33]
        (
            do_ref, dqkv_ref, kt_ref, dk_ref, dv_ref, dn_ref, dsib_ref, dsum_ref, dnt_ref,
            zi, zo, ci, co, osib, sgot, szgot, datt_ref, op_ref, dmid_ref, mg_ref,
            loc_sem, dsend, drecv, rloc, rsend, rrecv,
            nsend, nrecv, ssend, srecv, osend, orecv, tsend, trecv, tzsend, tzrecv, msend, mrecv,
            back_ref, mid_ref, cot_ref, flat_ref, wo_ref, t_ref, qkv_ref, attt_ref, xt_ref, w_ref, hid_ref, load_sem,
        ) = refs[33:83]
        sums_scratch = refs[83:]
        z, e, c, base = place()
        col = e // 2
        sib = base + 1 - c
        seq_core, seq = z // 2, lax.rem(z, 2)
        bit = [lax.rem(col // (1 << i), 2) for i in range(bits)]
        mate = [2 * (col + (1 - 2 * bit[i]) * (1 << i)) + c for i in range(bits)]
        others = [lax.rem(z + step, blocks) for step in range(1, blocks)]
        plane = [lax.rem(col + step, columns) for step in range(1, columns)]
        inner = (z > 0) & (z < blocks - 1)
        order = slice_order(z)
        across = [lax.rem(2 * (z // 2) + 2 + k, blocks) for k in range(2)]
        loads = [
            pltpu.make_async_copy(src, dst, load_sem.at[n])
            for n, (src, dst) in enumerate(
                (
                    (back_in, back_ref), (mid_in, mid_ref), (cot_in, cot_ref), (flat_in, flat_ref), (wo_in, wo_ref),
                    (t_in, t_ref), (qkv_in, qkv_ref), (attt_in, attt_ref), (xt_in, xt_ref), (w_in, w_ref), (hid_in, hid_ref),
                )
            )
        ]
        for load in loads:
            load.start()
        greet(column_partners(blocks, z, c, base) + [(z, 2 * t + c) for t in plane])

        def m_out(t):
            return remote(made_ref.at[t], mg_ref.at[col], msend.at[t], mrecv.at[col], z, 2 * t + c)

        m_own = pltpu.make_async_copy(made_ref.at[col], mg_ref.at[col], loc_sem.at[2])
        m_own.start()

        far = order[3]
        pair = z + 1 - 2 * lax.rem(z, 2)

        def r_load(i, src, s, slot):
            return pltpu.make_async_copy(src.at[s], (zi, zo)[i].at[slot], rloc.at[i, slot])

        def r_chain(i):
            src, dst = ((gi_ref, ci), (go_ref, co))[i]
            return remote(src.at[1], dst, rsend.at[i], rrecv.at[i], pair, e)

        def r_sum(i):
            src, dst = ((zi, ci), (zo, co))[i]
            return remote(src.at[0], dst, rsend.at[i], rrecv.at[i], far, e)

        def chain(i):
            @pl.when(inner)
            def _():
                buf, got = ((zi, ci), (zo, co))[i]
                r_load(i, (gi_ref, go_ref)[i], 1, 0).wait()
                r_chain(i).wait_recv()
                buf[0] = (buf[0].astype(f32) + got[...].astype(f32)).astype(bf16)
                r_sum(i).start()

        for i in range(2):

            @pl.when(jnp.logical_not(inner))
            def _():
                r_load(i, (gi_ref, go_ref)[i], 0, 0).start()

            @pl.when(inner)
            def _():
                r_load(i, (gi_ref, go_ref)[i], 1, 0).start()

            r_load(i, (ei_ref, eo_ref)[i], pair, 1).start()

        lane = lane_of((tokens, 128), 1)
        onehot = (lane == ids_ref[...]).astype(f32)
        place_in = z * span + lane_of((span, 1), 0)
        valid = jnp.concatenate(
            [(place_in < lens_ref[s, 0:1, 0:1]).astype(f32) for s in range(seqs)], axis=0
        )
        from_slots = lane_of((tokens, slots), 1).astype(f32) == slot_ref[...]
        dots_row = jnp.concatenate([dots_ref[t, 0:1, 0:capacity] for t in range(columns)], axis=1)
        dot_rows = jnp.sum(jnp.where(from_slots, dots_row, 0.0), axis=1, keepdims=True)
        picks = from_slots.astype(f32).astype(bf16)
        for load in loads[:5]:
            load.wait()
        d_rows = dot(picks, back_ref[...].reshape(slots, width))
        count_row = cnt_ref[0:1]
        mean_load = jnp.sum(count_row, axis=1, keepdims=True) / experts_n
        ratio_rows = jnp.sum(onehot * ((count_row - mean_load) / mean_load), axis=1, keepdims=True)
        gates = gate_ref[...]
        d_gate = valid * (dot_rows + balance_weight * ratio_rows)
        d_logits = (onehot * (d_gate * gates * (1.0 - gates))).astype(bf16)
        router_t = dot_tn(d_logits, flat_ref[...])
        balance_part = jnp.sum(valid * gates * ratio_rows, axis=0, keepdims=True) / jnp.sum(
            count_row, axis=1, keepdims=True
        )
        gain_sum = jnp.zeros((1, width), f32)
        shift_sum = jnp.zeros((1, width), f32)
        for s in range(seqs):
            lo, hi = s * span, (s + 1) * span
            v = mid_ref[lo:hi]
            centered = v - jnp.mean(v, axis=-1, keepdims=True)
            inverse = lax.rsqrt(jnp.mean(centered * centered, axis=-1, keepdims=True) + epsilon)
            unit = centered * inverse
            dy = d_rows[lo:hi] + dot_nt(d_logits[lo:hi], wr_ref[...])
            gain_sum = gain_sum + jnp.sum(dy * unit, axis=0, keepdims=True)
            shift_sum = shift_sum + jnp.sum(dy, axis=0, keepdims=True)
            du = dy * g2_ref[...].reshape(1, width)
            dx = inverse * (
                du
                - jnp.mean(du, axis=-1, keepdims=True)
                - unit * jnp.mean(du * unit, axis=-1, keepdims=True)
            )
            dmid_ref[lo:hi] = cot_ref[lo:hi].astype(f32) + dx
            d_branch = dmid_ref[lo:hi].astype(bf16)
            for k in range(2):
                datt_ref[s, k] = dot_nt(d_branch, wo_ref[k * half : (k + 1) * half]).astype(bf16)

        at = (z, e, c, bit, mate, blocks, sib)

        def finish_out(k, g):
            grads_ref[3, :, k * half : (k + 1) * half] = g.reshape(width, half)

        def finish_pair(p):
            def finish(k, g):
                g = g.reshape(3, width, 128)
                for m in range(3):
                    grads_ref[m, :, k * half + p * 128 : k * half + (p + 1) * 128] = g[m]

            return finish

        out_sum = PieceSum(at, *sums_scratch[:n_sum], (0, 1), finish_out)
        pair_sums = [
            PieceSum(
                at,
                *sums_scratch[n_sum * (p + 1) : n_sum * (p + 2)],
                (1, 0) if p % 2 == 0 else (0, 1),
                finish_pair(p),
            )
            for p in range(pairs)
        ]

        def d_out(s, k):
            return remote(
                datt_ref.at[s, k], do_ref.at[z], dsend.at[s, k], drecv.at[z], 2 * c + s, base + k
            )

        def d_own(s, k):
            return pltpu.make_async_copy(datt_ref.at[s, k], do_ref.at[z], loc_sem.at[0])

        for k in range(2):
            for s in range(seqs):
                to_self = (2 * c + s == z) & (c == k)

                @pl.when(to_self)
                def _():
                    d_own(s, k).start()

                @pl.when(jnp.logical_not(to_self))
                def _():
                    d_out(s, k).start()

        @pl.when(jnp.logical_not(inner))
        def _():
            r_chain(0).start()

        sums_ref[...] = jnp.zeros_like(sums_ref)
        sums_ref[2:3] = gain_sum
        sums_ref[3:4] = shift_sum
        sums_ref[4 : 4 + experts_n] = router_t[0:experts_n]
        sums_ref[4 + experts_n : 5 + experts_n] = jnp.broadcast_to(balance_part, (1, width))
        d_branch = dmid_ref[...].astype(bf16)
        loads[5].wait()
        for k in range(2):
            att_k = jnp.concatenate([t_ref[s, k] for s in range(seqs)], axis=0)
            made_k = dot_tn(att_k, d_branch).astype(bf16)
            op_ref[0, k * half : (k + 1) * half] = made_k[:, :half]
            op_ref[1, k * half : (k + 1) * half] = made_k[:, half:]
        o_first = remote(op_ref.at[1 - c], osib, osend, orecv, z, sib)
        o_first.start()
        o_first.wait()
        out_sum.part[...] = (op_ref[c].astype(f32) + osib[...].astype(f32)).astype(bf16).reshape(
            2, 2, blocks, out_piece, half
        )
        out_sum.step(0)
        out_sum.step(1)

        @pl.when(c == seq_core)
        def _():
            d_own(0, 0).wait()

        @pl.when(c != seq_core)
        def _():
            remote(datt_ref.at[0, 0], do_ref.at[z], dsend.at[0, 0], drecv.at[z], z, base).wait_recv()

        for zs in others:
            remote(datt_ref.at[0, 0], do_ref.at[zs], dsend.at[0, 0], drecv.at[zs], z, base).wait_recv()

        for load in loads[6:]:
            load.wait()
        key_bias = jnp.where(lane_of((total, 1), 0) < len_ref[0:1, 0:1], 0.0, masked_fill)
        lane = lane_of((1, 128), 1)
        later = lax.broadcasted_iota(jnp.int32, (span, span), 0) > lax.broadcasted_iota(
            jnp.int32, (span, span), 1
        )

        def pair_step(p):
            first = p * 128
            k_all = qkv_ref[:, pl.ds(half + first, 128)]
            kt_ref[...] = jnp.transpose(k_all)
            v_all = qkv_ref[:, pl.ds(2 * half + first, 128)]
            k_heads = key_heads(k_all, key_bias)
            dk_ref[...] = jnp.zeros_like(dk_ref)
            dv_ref[...] = jnp.zeros_like(dv_ref)
            for j in range(blocks):
                n = (j + 1) * span
                r = pl.ds(j * span, span)
                q = qkv_ref[r, pl.ds(first, 128)].astype(f32) * scale
                d_o = do_ref[j, :, pl.ds(first, 128)].astype(f32)
                prod_t = jnp.transpose(d_o) * attt_ref[pl.ds(first, 128), r]
                dq_t = []
                for h in range(2):
                    inside = (lane // HEAD) == h
                    spare = lane == (1 - h) * HEAD
                    q_h = jnp.where(inside, q, jnp.where(spare, 1.0, 0.0)).astype(bf16)
                    q_only = jnp.where(inside, q, 0.0).astype(bf16)
                    do_h = jnp.where(inside, d_o, 0.0).astype(bf16)
                    delta = jnp.sum(prod_t[h * HEAD : (h + 1) * HEAD], axis=0, keepdims=True)
                    s = dot_nt(k_heads[h][:n], q_h)
                    last = jnp.where(later, masked_fill, s[n - span :])
                    s = last if j == 0 else jnp.concatenate([s[: n - span], last], axis=0)
                    w = jnp.exp(s - lse_ref[pl.ds(2 * p + h, 1), r])
                    d_w = dot_nt(v_all[:n], do_h)
                    d_s = (w * (d_w - delta)).astype(bf16)
                    dv_ref[:n] += dot(w.astype(bf16), do_h)
                    dk_ref[:n] += dot(d_s, q_only)
                    dq_t.append(dot(kt_ref[h * HEAD : (h + 1) * HEAD, :n], d_s))
                dq = jnp.transpose(jnp.concatenate(dq_t, axis=0)) * scale
                dqkv_ref[r, pl.ds(first, 128)] = dq.astype(bf16)
            dqkv_ref[:, pl.ds(half + first, 128)] = dk_ref[...].astype(bf16)
            dqkv_ref[:, pl.ds(2 * half + first, 128)] = dv_ref[...].astype(bf16)
            joined = jnp.concatenate(
                [dqkv_ref[:, pl.ds(m * half + first, 128)] for m in range(3)], axis=1
            )
            grads = dot(xt_ref[...], joined).astype(bf16)
            pair_sums[p].part[...] = jnp.concatenate(
                [grads[:, m * 128 : (m + 1) * 128] for m in range(3)], axis=0
            ).reshape(2, 2, blocks, pair_piece, 128)

        state = {out_sum: 2}

        def advance(*chosen):
            for one in chosen or list(state):
                n = state.setdefault(one, 0)
                if n <= 7:
                    one.step(n)
                    state[one] = n + 1

        plan = ([out_sum], [pair_sums[0]], [out_sum]) if pairs == 3 else ([],) * pairs
        for p in range(pairs):
            pair_step(p)
            if plan[p]:
                advance(*plan[p])
            advance(pair_sums[p])
            if p == 1:
                chain(0)

        for t in plane:
            m_out(t).start()

        for j in range(blocks):
            r = pl.ds(j * span, span)
            dn_ref[j] = dot_nt(dqkv_ref[r, :], w_ref[...]).astype(bf16).reshape(2, hs, width)

        def n_sib(j):
            return remote(dn_ref.at[j, 1 - c], dsib_ref.at[j], nsend.at[j], nrecv.at[j], z, sib)

        def n_out(j):
            return remote(
                dsum_ref.at[j], dnt_ref.at[seq, c], ssend.at[j], srecv.at[seq, c], j, base + seq_core
            )

        def n_own():
            return pltpu.make_async_copy(dsum_ref.at[z], dnt_ref.at[seq, c], loc_sem.at[1])

        n_order = others[1:2] + others[0:1] + others[2:] + [z]
        for j in n_order:
            n_sib(j).start()
        advance(*pair_sums[:2])
        for i, j in enumerate(n_order):
            n_sib(j).wait_recv()
            dsum_ref[j] = (dn_ref[j, c].astype(f32) + dsib_ref[j].astype(f32)).astype(bf16)
            if i < blocks - 1:
                n_out(j).start()
            else:

                @pl.when(seq_core == c)
                def _():
                    n_own().start()

                @pl.when(seq_core != c)
                def _():
                    n_out(j).start()

        @pl.when(jnp.logical_not(inner))
        def _():
            r_chain(1).start()

        advance(*pair_sums[2:])
        advance()
        for s in range(seqs):
            for k in range(2):
                from_self = (2 * c + s == z) & (c == k)

                @pl.when(jnp.logical_not(from_self))
                def _():
                    remote(
                        dsum_ref.at[0], dnt_ref.at[s, k], ssend.at[0], srecv.at[s, k], z, base
                    ).wait_recv()

                @pl.when(from_self)
                def _():
                    n_own().wait()

        gains = g1_ref[...].reshape(1, width)
        gain_sum = jnp.zeros((1, width), f32)
        shift_sum = jnp.zeros((1, width), f32)
        for s in range(seqs):
            for k in range(2):
                v = hid_ref[s, k].astype(f32)
                centered = v - jnp.mean(v, axis=-1, keepdims=True)
                inverse = lax.rsqrt(jnp.mean(centered * centered, axis=-1, keepdims=True) + epsilon)
                unit = centered * inverse
                dy = dnt_ref[s, k].astype(f32)
                gain_sum = gain_sum + jnp.sum(dy * unit, axis=0, keepdims=True)
                shift_sum = shift_sum + jnp.sum(dy, axis=0, keepdims=True)
                du = dy * gains
                dx = inverse * (
                    du
                    - jnp.mean(du, axis=-1, keepdims=True)
                    - unit * jnp.mean(du * unit, axis=-1, keepdims=True)
                )
                gh_ref[s, k] = dmid_ref[(2 * s + k) * hs : (2 * s + k + 1) * hs] + dx

        sums_ref[0:1] = gain_sum
        sums_ref[1:2] = shift_sum

        def t_swap(n, te):
            return remote(sums_ref, sgot.at[n], tsend.at[n], trecv.at[n], z, te)

        partners = [sib] + mate
        for n, te in enumerate(partners):
            copy = t_swap(n, te)
            copy.start()
            if n in (1, 2):
                advance()
            copy.wait()
            sums_ref[...] = sums_ref[...] + sgot[n]

        def t_z(zt):
            return remote(sums_ref, szgot.at[z], tzsend.at[zt], tzrecv.at[z], zt, e)

        for zt in others:
            t_z(zt).start()
        chain(1)
        for t in plane:
            remote(made_ref.at[0], mg_ref.at[t], msend.at[t], mrecv.at[t], z, e).wait_recv()
        m_own.wait()
        scaled = valid * gates
        expert_out = dot(picks, mg_ref[...].reshape(slots, width))
        y_ref[...] = (mid_ref[...] + scaled * expert_out).astype(bf16)
        advance()
        for zs in others:
            remote(sums_ref, szgot.at[zs], tzsend.at[zs], tzrecv.at[zs], z, e).wait_recv()
        for zt in others:
            t_z(zt).wait_send()
        szgot[z] = sums_ref[...]
        tot = szgot[0]
        for j in range(1, blocks):
            tot = tot + szgot[j]
        sums_ref[...] = tot

        advance()
        for i, (buf, got, final) in enumerate(((zi, ci, fi_ref), (zo, co, fo_ref))):

            @pl.when(inner)
            def _():
                r_sum(i).wait_send()
                r_load(i, (gi_ref, go_ref)[i], 0, 0).start()

            r_load(i, (gi_ref, go_ref)[i], 0, 0).wait()
            r_load(i, (ei_ref, eo_ref)[i], pair, 1).wait()
            final[...] = buf[0].astype(f32) + buf[1].astype(f32)

            @pl.when(inner)
            def _():
                for k in range(2):
                    r_load(i, (ei_ref, eo_ref)[i], across[k], k).start()
                for k in range(2):
                    r_load(i, (ei_ref, eo_ref)[i], across[k], k).wait()
                final[...] = final[...] + (buf[0].astype(f32) + buf[1].astype(f32))

            @pl.when(jnp.logical_not(inner))
            def _():
                r_sum(i).wait_recv()
                r_chain(i).wait_send()
                final[...] = final[...] + got[...].astype(f32)

            advance()
        while min(state.values()) <= 7:
            advance()

        for s in range(seqs):
            for k in range(2):

                @pl.when(jnp.logical_not((2 * c + s == z) & (c == k)))
                def _():
                    d_out(s, k).wait_send()

        for j in n_order[:-1]:
            n_out(j).wait_send()

        @pl.when(seq_core != c)
        def _():
            n_out(z).wait_send()

        for j in n_order:
            n_sib(j).wait_send()
        for t in plane:
            m_out(t).wait_send()

    stage = blocks
    scratch = [
        pltpu.VMEM((blocks, span, half), bf16),
        pltpu.VMEM((total, 3 * half), bf16),
        pltpu.VMEM((128, total), bf16),
        pltpu.VMEM((total, 128), f32),
        pltpu.VMEM((total, 128), f32),
        pltpu.VMEM((blocks, 2, hs, width), bf16),
        pltpu.VMEM((blocks, hs, width), bf16),
        pltpu.VMEM((blocks, hs, width), bf16),
        pltpu.VMEM((seqs, 2, hs, width), bf16),
        pltpu.VMEM((2, width, part), bf16),
        pltpu.VMEM((2, part, width), bf16),
        pltpu.VMEM((width, part), bf16),
        pltpu.VMEM((part, width), bf16),
        pltpu.VMEM((width, half), bf16),
        pltpu.VMEM((1 + bits, small_rows, width), f32),
        pltpu.VMEM((blocks, small_rows, width), f32),
        pltpu.VMEM((seqs, 2, span, half), bf16),
        pltpu.VMEM((2, width, half), bf16),
        pltpu.VMEM((tokens, width), f32),
        pltpu.VMEM((columns, capacity, width), bf16),
        DMA((3,)),
        DMA((seqs, 2)),
        DMA((stage,)),
        DMA((2, 2)),
        DMA((2,)),
        DMA((2,)),
        DMA((stage,)),
        DMA((stage,)),
        DMA((stage,)),
        DMA((seqs, 2)),
        DMA,
        DMA,
        DMA((1 + bits,)),
        DMA((1 + bits,)),
        DMA((stage,)),
        DMA((stage,)),
        DMA((columns,)),
        DMA((columns,)),
        pltpu.VMEM((columns, capacity, width), bf16),
        pltpu.VMEM((tokens, width), f32),
        pltpu.VMEM((tokens, width), bf16),
        pltpu.VMEM((tokens, width), bf16),
        pltpu.VMEM((width, width), bf16),
        pltpu.VMEM((seqs, 2, span, half), bf16),
        pltpu.VMEM((total, 3 * half), bf16),
        pltpu.VMEM((half, total), f32),
        pltpu.VMEM((width, total), bf16),
        pltpu.VMEM((width, 3 * half), bf16),
        pltpu.VMEM((seqs, 2, hs, width), bf16),
        DMA((11,)),
    ]
    scratch += PieceSum.scratch(blocks, out_piece, half, rest)
    for _ in range(pairs):
        scratch += PieceSum.scratch(blocks, pair_piece, 128, rest)
    grads, sums, f_inner, f_outer, g_hidden, output = pl.pallas_call(
        kernel,
        name="backward",
        out_shape=[
            jax.ShapeDtypeStruct((4, width, width), bf16),
            jax.ShapeDtypeStruct((small_rows, width), f32),
            jax.ShapeDtypeStruct((width, part), f32),
            jax.ShapeDtypeStruct((part, width), f32),
            jax.ShapeDtypeStruct((seqs, 2, hs, width), f32),
            jax.ShapeDtypeStruct((tokens, width), bf16),
        ],
        in_specs=[ANY] * 4 + [VMEM] * 2 + [ANY] * 3 + [VMEM] * 4 + [ANY] * 2 + [VMEM] * 2 + [ANY] * 2 + [VMEM] * 2 + [ANY]
        + [VMEM] + [ANY] * 4,
        out_specs=[VMEM] * 6,
        scratch_shapes=scratch,
        compiler_params=params(3),
    )(
        rows_t, weights, qkv, att_t, lse, length, attended, middle, flat, gate, slot, ids, lengths, cotangent,
        back, dots, counts, made, hidden.reshape(seqs, 2, hs, width), gain_one,
        gain_two, w_output, w_router, g_inner, g_outer, e_inner, e_outer,
    )
    return finish(grads, sums, f_inner, f_outer, g_hidden.reshape(tokens, width), output, experts_n)


def finish(grads, sums, g_inner, g_outer, g_hidden, output, experts_n):
    steps = 8
    width = grads.shape[2]
    tokens = output.shape[0]
    part = g_inner.shape[1]
    rows = width // steps

    def kernel(g_ref, s_ref, i_ref, o_ref, h_ref, y_ref, *outs):
        for m in range(4):
            outs[m][...] = g_ref[m].astype(f32)
        outs[4][...] = i_ref[...]
        outs[5][...] = o_ref[...]
        outs[6][...] = h_ref[...]
        outs[7][...] = y_ref[...]

        @pl.when(pl.program_id(0) == 0)
        def _():
            for m in range(4):
                outs[8 + m][...] = s_ref[m]
            outs[12][...] = jnp.transpose(s_ref[...])[:, 4 : 4 + experts_n]
            outs[13][...] = s_ref[4 + experts_n : 5 + experts_n, 0:1]

    def by_rows(shape):
        return pl.BlockSpec((shape[0] // steps,) + shape[1:], lambda i: (i,) + (0,) * (len(shape) - 1))

    def whole(shape):
        return pl.BlockSpec(shape, lambda i: (0,) * len(shape))

    split = [(width, width)] * 4 + [(width, part), (part, width), (tokens, width), (tokens, width)]
    kept = [(width,)] * 4 + [(width, experts_n), (1, 1)]
    return pl.pallas_call(
        kernel,
        name="finish",
        grid=(steps,),
        out_shape=[jax.ShapeDtypeStruct(a, bf16 if n == 7 else f32) for n, a in enumerate(split + kept)],
        in_specs=[pl.BlockSpec((4, rows, width), lambda i: (0, i, 0)), whole(sums.shape)]
        + [by_rows(a) for a in split[4:]],
        out_specs=[by_rows(a) for a in split] + [whole(a) for a in kept],
        compiler_params=pltpu.CompilerParams(dimension_semantics=("arbitrary",), vmem_limit_bytes=VMEM_BYTES),
    )(grads, sums, g_inner, g_outer, g_hidden, output)


def on_device(
    hidden_in,
    cotangent,
    query_weight,
    key_weight,
    value_weight,
    output_weight,
    gain_one,
    shift_one,
    gain_two,
    shift_two,
    w_router,
    w_inner,
    w_outer,
    expert_ids,
    seq_lengths,
):
    seqs, span, width = hidden_in.shape
    tokens = seqs * span
    blocks = lax.axis_size("blk")
    columns = lax.axis_size("ep") // 2
    experts_n = w_router.shape[1]
    capacity = max(2, 2 * tokens // experts_n)
    total = blocks * span
    half = width // 2
    assert seqs * 2 == blocks and experts_n == columns

    ids = expert_ids.reshape(tokens, 1)
    lengths = jnp.broadcast_to(seq_lengths[:, None, None], (seqs, 8, 128))
    router = jnp.pad(w_router, ((0, 0), (0, 128 - experts_n)))
    cot = cotangent.reshape(tokens, width)
    (
        rows_t, w_qkv, qkv, att_t, lse, attended, middle, flat, gate, slot, to_rows, scales, cot_rows, length, counts,
        near_inner, sib_inner, sib_outer,
    ) = forward(
        hidden_in, cotangent, gain_one, shift_one, gain_two, shift_two, query_weight, key_weight, value_weight,
        output_weight, router, ids, lengths, w_inner[0], w_outer[0], blocks, columns, capacity, experts_n,
    )
    back, dots, made, counts, g_inner, g_outer, e_inner, e_outer = experts(
        to_rows, scales, cot_rows, counts, w_inner[0], w_outer[0], sib_inner, sib_outer, near_inner, blocks
    )
    results = backward(
        rows_t, w_qkv, qkv.reshape(total, 3 * half), att_t, lse, length, attended, middle, flat, gate,
        slot, ids, lengths, cot, back, dots, counts, made, hidden_in, gain_one, gain_two, output_weight, router,
        g_inner, g_outer, e_inner, e_outer, experts_n,
    )
    dense, (grad_inner, grad_outer, grad_hidden, output) = results[:4], results[4:8]
    gains, (grad_router, balance) = results[8:12], results[12:]
    return (
        output.reshape(seqs, span, width),
        grad_hidden.reshape(seqs, span, width),
        *dense,
        *gains,
        grad_router,
        grad_inner[None],
        grad_outer[None],
        balance[0, 0],
    )


def solution(mesh):
    tokens = P("ep", "blk", None)
    return jax.shard_map(
        on_device,
        mesh=mesh,
        in_specs=(tokens, tokens)
        + (P(),) * 9
        + (P("ep", None, "blk"), P("ep", "blk", None), P("ep", "blk", None, None, None), P("ep")),
        out_specs=(tokens, tokens) + (P(),) * 9 + (P("ep", None, "blk"), P("ep", "blk", None), P()),
        check_vma=False,
    )
```

```python
import functools

import jax
import jax.numpy as jnp
from jax import lax
from jax.experimental import pallas as pl
from jax.experimental.pallas import tpu as pltpu
from jax.sharding import PartitionSpec as P

HEAD = 64
MESH = pl.DeviceIdType.MESH
ANY = pl.BlockSpec(memory_space=pl.ANY)
VMEM = pl.BlockSpec(memory_space=pltpu.VMEM)
SMEM = pl.BlockSpec(memory_space=pltpu.SMEM)
DMA = pltpu.SemaphoreType.DMA
f32 = jnp.float32
bf16 = jnp.bfloat16

epsilon = 1e-05
balance_weight = 6.0
masked_fill = -1e30
VMEM_BYTES = 57 * 1024 * 1024


def dot(a, b):
    return lax.dot_general(a, b, (((1,), (0,)), ((), ())), preferred_element_type=f32)


def dot_nt(a, b):
    return lax.dot_general(a, b, (((1,), (1,)), ((), ())), preferred_element_type=f32)


def dot_tn(a, b):
    return lax.dot_general(a, b, (((0,), (0,)), ((), ())), preferred_element_type=f32)


def place():
    z = lax.axis_index("blk")
    e = lax.axis_index("ep")
    c = lax.rem(e, 2)
    return z, e, c, e - c


def remote(src, dst, send_sem, recv_sem, z, e):
    return pltpu.make_async_remote_copy(
        src, dst, send_sem, recv_sem, device_id=(z, e), device_id_type=MESH
    )


def greet(partners):
    barrier = pltpu.get_barrier_semaphore()
    for z, e in partners:
        pl.semaphore_signal(barrier, inc=1, device_id=(z, e), device_id_type=MESH)


def await_greetings(partners):
    pl.semaphore_wait(pltpu.get_barrier_semaphore(), len(partners))


def column_partners(blocks, z, c, base):
    found = [(z, base + 1 - c)]
    for step in range(1, blocks):
        for k in range(2):
            found.append((lax.rem(z + step, blocks), base + k))
    return found


def params(collective_id):
    return pltpu.CompilerParams(
        collective_id=collective_id, has_side_effects=True, vmem_limit_bytes=VMEM_BYTES
    )


def lane_of(shape, dimension):
    return lax.broadcasted_iota(jnp.int32, shape, dimension)


def one_hot(ids_ref, seqs, span):
    columns = [
        jnp.transpose(jnp.broadcast_to(ids_ref[s : s + 1], (128, span))) for s in range(seqs)
    ]
    ids = jnp.concatenate(columns, axis=0)
    return (lane_of(ids.shape, 1) == ids).astype(f32)


def valid_rows(len_ref, z, seqs, span):
    place_in = z * span + lane_of((span, 1), 0)
    return jnp.concatenate([(place_in < len_ref[s]).astype(f32) for s in range(seqs)], axis=0)


def key_heads(k_all, key_bias):
    lane = lane_of((1, 128), 1)
    found = []
    for h in range(2):
        inside = (lane // HEAD) == h
        spare = lane == (1 - h) * HEAD
        found.append(
            jnp.where(inside, k_all.astype(f32), jnp.where(spare, key_bias, 0.0)).astype(bf16)
        )
    return found


def forward(
    hidden, cotangent, gain_one, shift_one, gain_two, shift_two, w_query, w_key, w_value, w_output, w_router,
    ids, lengths, w_inner, w_outer, blocks, columns, capacity, experts_n,
):
    seqs, span, width = hidden.shape
    hs = span // 2
    half = width // 2
    pairs = half // 128
    total = blocks * span
    tokens = seqs * span
    slots = experts_n * capacity
    part = w_inner.shape[1]
    cap_lanes = max(128, capacity)

    def kernel(*refs):
        (
            hid_ref, cot_ref, g1_ref, s1_ref, g2_ref, s2_ref, wq_ref, wk_ref, wv_ref, wo_ref, wr_ref,
            ids_ref, len_in, wi_ref, we_ref,
        ) = refs[:15]
        (
            xt_out, w_out, qkv_out, attt_out, lse_ref, t_ref, mid_ref, flat_ref, gate_ref, slot_ref,
            rows_ref, sc_ref, cote_ref, len_ref, cnt_ref, li_ref, bi_ref, bo_ref,
        ) = refs[15:33]
        (
            x_ref, nb_ref, kh_ref, vt_ref, att_ref, cots_ref, lens_ref, lgot_ref, cown_ref, cgot_ref,
            wload, nloc, nsend, nrecv, fsend, frecv, aloc, asend, arecv, closs, csend, crecv,
            lsend, lrecv, ksend, krecv, hsend, hrecv, bsend, brecv,
            xt_ref, w_ref, qkv_ref, attt_ref, out_sem,
        ) = refs[33:]
        z, e, c, base = place()
        col = e // 2
        sib = base + 1 - c
        seq_core, seq = z // 2, lax.rem(z, 2)
        others = [lax.rem(z + step, blocks) for step in range(1, blocks)]
        plane = [lax.rem(col + step, columns) for step in range(1, columns)]
        column = column_partners(blocks, z, c, base)
        greet(column + [(z, 2 * t + c) for t in plane])

        def load_w(m, ref):
            return pltpu.make_async_copy(
                ref.at[:, pl.ds(pl.multiple_of(c * half, half), half)],
                w_ref.at[:, pl.ds(m * half, half)],
                wload.at[m],
            )

        for m, ref in enumerate((wq_ref, wk_ref, wv_ref)):
            load_w(m, ref).start()
        gain_row, shift_row = g1_ref[...].reshape(1, width), s1_ref[...].reshape(1, width)
        for s in range(seqs):
            for k in range(2):
                v = hid_ref[s, k].astype(f32)
                centered = v - jnp.mean(v, axis=-1, keepdims=True)
                inverse = lax.rsqrt(jnp.mean(centered * centered, axis=-1, keepdims=True) + epsilon)
                nb_ref[s, k] = (centered * inverse * gain_row + shift_row).astype(bf16)
        await_greetings(column + plane)

        def n_out(s, k):
            return remote(
                nb_ref.at[s, k], x_ref.at[z, k], nsend.at[s, k], nrecv.at[z], 2 * c + s, base + k
            )

        def n_own(s, k):
            return pltpu.make_async_copy(nb_ref.at[s, k], x_ref.at[z, k], nloc)

        for k, s in ((0, 0), (0, 1), (1, 1), (1, 0)):
            if True:
                to_self = (2 * c + s == z) & (c == k)

                @pl.when(to_self)
                def _():
                    n_own(s, k).start()

                @pl.when(jnp.logical_not(to_self))
                def _():
                    n_out(s, k).start()

        for s in range(seqs):
            lens_ref[s] = jnp.full((8, 128), len_in[s], jnp.int32)
        to_lens = remote(lens_ref, lgot_ref, lsend, lrecv, z, sib)
        to_lens.start()
        lane = lane_of((tokens, 128), 1)
        onehot = one_hot(ids_ref, seqs, span)
        valid = valid_rows(len_in, z, seqs, span)
        cown_ref[...] = jnp.broadcast_to(jnp.sum(onehot * valid, axis=0, keepdims=True), (8, 128))

        def k_out(n, to_z, to_e):
            return remote(cown_ref, cgot_ref.at[z, c], ksend.at[n], krecv.at[z, c], to_z, to_e)

        for n, (to_z, to_e) in enumerate(column):
            k_out(n, to_z, to_e).start()
        earlier = (lane_of((tokens, tokens), 0) > lane_of((tokens, tokens), 1)).astype(f32).astype(bf16)
        rank = dot(earlier, onehot.astype(bf16))
        slot = jnp.sum(onehot * (rank + (lane * capacity).astype(f32)), axis=1, keepdims=True)
        slot_ref[...] = slot
        slot_row = jnp.transpose(jnp.broadcast_to(slot, (tokens, 128)))[0:1]
        to_slots = (lane_of((slots, tokens), 0).astype(f32) == slot_row).astype(f32).astype(bf16)
        cots_ref[...] = (
            dot(to_slots, cot_ref[...]).astype(bf16).reshape(columns, capacity, width)
        )

        def c_out(t):
            return remote(cots_ref.at[t], cote_ref.at[col], csend.at[t], crecv.at[col], z, 2 * t + c)

        c_own = pltpu.make_async_copy(cots_ref.at[col], cote_ref.at[col], closs)
        c_own.start()
        for t in plane:
            c_out(t).start()
        for m, ref in enumerate((wq_ref, wk_ref, wv_ref)):
            load_w(m, ref).wait()

        def n_sib(zs):
            return remote(x_ref.at[zs, c], x_ref.at[zs, c], fsend.at[zs], frecv.at[zs], z, sib)

        for zs in [z] + others:
            if zs is z:

                @pl.when(c == seq_core)
                def _():
                    n_own(0, 0).wait()

                @pl.when(c != seq_core)
                def _():
                    remote(nb_ref.at[0, 0], x_ref.at[z, c], nsend.at[0, 0], nrecv.at[z], z, base).wait_recv()
            else:
                remote(nb_ref.at[0, 0], x_ref.at[zs, c], nsend.at[0, 0], nrecv.at[zs], z, base).wait_recv()
            n_sib(zs).start()

        def h_out(step):
            side = 0 if step == 1 else 1
            return remote(wi_ref, li_ref.at[side], hsend.at[side], hrecv.at[side], z + step, e)

        def b_out(i):
            src, dst = ((wi_ref, bi_ref), (we_ref, bo_ref))[i]
            return remote(src, dst, bsend.at[i], brecv.at[i], z, sib)

        @pl.when(z < blocks - 1)
        def _():
            h_out(1).start()

        @pl.when(z > 0)
        def _():
            h_out(-1).start()

        for zs in [z] + others:
            remote(
                x_ref.at[zs, 1 - c], x_ref.at[zs, 1 - c], fsend.at[zs], frecv.at[zs], z, sib
            ).wait_recv()
            x_z = x_ref[zs].reshape(span, width)
            qkv_ref[zs] = dot(x_z, w_ref[...]).astype(bf16)
            xt_ref[:, pl.ds(pl.multiple_of(zs * span, span), span)] = jnp.transpose(x_z)
        for i in range(2):
            b_out(i).start()
        to_lens.wait()
        seq_len = jnp.where(c == seq_core, lens_ref[seq], lgot_ref[seq])
        len_ref[...] = seq_len
        key_bias = jnp.where(lane_of((total, 1), 0) < seq_len[0:1, 0:1], 0.0, masked_fill)
        for p in range(pairs):
            k_all = jnp.concatenate(
                [qkv_ref[j, :, half + p * 128 : half + (p + 1) * 128] for j in range(blocks)], axis=0
            )
            for h, k_h in enumerate(key_heads(k_all, key_bias)):
                kh_ref[2 * p + h] = k_h
            for j in range(blocks):
                vt_ref[p * 128 : (p + 1) * 128, j * span : (j + 1) * span] = jnp.transpose(
                    qkv_ref[j, :, 2 * half + p * 128 : 2 * half + (p + 1) * 128]
                )
        outs = [
            pltpu.make_async_copy(src, dst, out_sem.at[n])
            for n, (src, dst) in enumerate(
                ((xt_ref, xt_out), (w_ref, w_out), (qkv_ref, qkv_out), (attt_ref, attt_out))
            )
        ]
        for out in outs[:3]:
            out.start()
        later = lane_of((span, span), 0) > lane_of((span, span), 1)
        lane_row = lane_of((1, 128), 1)

        def a_out(j):
            return remote(
                att_ref.at[j], t_ref.at[seq, c], asend.at[j], arecv.at[seq, c], j, base + seq_core
            )

        def a_own(j):
            return pltpu.make_async_copy(att_ref.at[j], t_ref.at[seq, c], aloc)

        for j in [0] + list(range(blocks - 1, 0, -1)):
            n = (j + 1) * span

            def pair_step(p, _):
                first = pl.multiple_of(p * 128, 128)
                q = qkv_ref[j, :, pl.ds(first, 128)].astype(f32) * (HEAD**-0.5)
                out_t = []
                for h in range(2):
                    inside = (lane_row // HEAD) == h
                    spare = lane_row == (1 - h) * HEAD
                    q_h = jnp.where(inside, q, jnp.where(spare, 1.0, 0.0)).astype(bf16)
                    s = dot_nt(kh_ref[2 * p + h, :n], q_h)
                    last = jnp.where(later, masked_fill, s[n - span :])
                    s = last if j == 0 else jnp.concatenate([s[: n - span], last], axis=0)
                    top = jnp.max(s, axis=0, keepdims=True)
                    w = jnp.exp(s - top)
                    total_w = jnp.sum(w, axis=0, keepdims=True)
                    o_t = dot(vt_ref[pl.ds(pl.multiple_of(first + h * HEAD, HEAD), HEAD), :n], w.astype(bf16))
                    out_t.append(o_t / total_w)
                    lse_ref[pl.ds(2 * p + h, 1), pl.ds(j * span, span)] = top + jnp.log(total_w)
                o = jnp.concatenate(out_t, axis=0)
                attt_ref[pl.ds(first, 128), pl.ds(j * span, span)] = o
                att_ref[j, :, pl.ds(first, 128)] = jnp.transpose(o).astype(bf16)
                return 0

            lax.fori_loop(0, pairs, pair_step, 0)
            to_self = (z == j) & (c == seq_core)

            @pl.when(to_self)
            def _():
                a_own(j).start()

            @pl.when(jnp.logical_not(to_self))
            def _():
                a_out(j).start()

        outs[3].start()
        for s in range(seqs):
            for k in range(2):
                from_self = (2 * c + s == z) & (c == k)

                @pl.when(from_self)
                def _():
                    a_own(0).wait()

                @pl.when(jnp.logical_not(from_self))
                def _():
                    remote(att_ref.at[0], t_ref.at[s, k], asend.at[0], arecv.at[s, k], z, base).wait_recv()

        for s in range(seqs):
            r = pl.ds(s * span, span)
            branch = dot(t_ref[s, 0], wo_ref[0:half]) + dot(t_ref[s, 1], wo_ref[half:])
            v = hid_ref[s].reshape(span, width).astype(f32) + branch
            mid_ref[r, :] = v
            centered = v - jnp.mean(v, axis=-1, keepdims=True)
            inverse = lax.rsqrt(jnp.mean(centered * centered, axis=-1, keepdims=True) + epsilon)
            flat_ref[r, :] = (
                centered * inverse * g2_ref[...].reshape(1, width) + s2_ref[...].reshape(1, width)
            ).astype(bf16)
        logits = dot_nt(flat_ref[...], wr_ref[...])
        gate = jax.nn.sigmoid(
            jnp.sum(logits * onehot[:, :experts_n], axis=1, keepdims=True)
        )
        gate_ref[...] = gate
        rows_ref[...] = (
            dot(to_slots, flat_ref[...]).astype(bf16).reshape(columns, capacity, width)
        )
        from_slots = lane_of((tokens, slots), 1).astype(f32) == slot_ref[...]
        scales = jnp.sum(jnp.where(from_slots, valid * gate, 0.0), axis=0, keepdims=True)
        if cap_lanes != capacity:
            sc_ref[...] = jnp.zeros_like(sc_ref)
        for t in range(columns):
            sc_ref[t, :, 0:capacity] = jnp.broadcast_to(
                scales[:, t * capacity : (t + 1) * capacity], (8, capacity)
            )

        for out in outs:
            out.wait()
        for n, (to_z, to_e) in enumerate(column):
            remote(cown_ref, cgot_ref.at[to_z, lax.rem(to_e, 2)], ksend.at[n], krecv.at[to_z, lax.rem(to_e, 2)], z, sib).wait_recv()
            k_out(n, to_z, to_e).wait_send()
        cgot_ref[z, c] = cown_ref[...]
        tot = jnp.zeros((8, 128), f32)
        for zs in range(blocks):
            for k in range(2):
                tot = tot + cgot_ref[zs, k]
        cnt_ref[...] = tot
        c_own.wait()
        for t in plane:
            c_out(t).wait_send()
            remote(cots_ref.at[t], cote_ref.at[t], csend.at[t], crecv.at[t], z, e).wait_recv()
        for s in range(seqs):
            for k in range(2):

                @pl.when(jnp.logical_not((2 * c + s == z) & (c == k)))
                def _():
                    n_out(s, k).wait_send()

        for zs in [z] + others:
            n_sib(zs).wait_send()
        for j in range(blocks):

            @pl.when(jnp.logical_not((z == j) & (c == seq_core)))
            def _():
                a_out(j).wait_send()

        for i in range(2):
            b_out(i).wait()

        @pl.when(z < blocks - 1)
        def _():
            h_out(1).wait_send()
            remote(wi_ref, li_ref.at[1], hsend.at[1], hrecv.at[1], z, e).wait_recv()

        @pl.when(z > 0)
        def _():
            h_out(-1).wait_send()
            remote(wi_ref, li_ref.at[0], hsend.at[0], hrecv.at[0], z, e).wait_recv()

    out_shapes = [
        ((width, total), bf16),
        ((width, 3 * half), bf16),
        ((blocks, span, 3 * half), bf16),
        ((half, total), f32),
        ((2 * pairs, total), f32),
        ((seqs, 2, span, half), bf16),
        ((tokens, width), f32),
        ((tokens, width), bf16),
        ((tokens, 1), f32),
        ((tokens, 1), f32),
        ((columns, capacity, width), bf16),
        ((columns, 8, cap_lanes), f32),
        ((columns, capacity, width), bf16),
        ((8, 128), jnp.int32),
        ((8, 128), f32),
        ((2, width, part), bf16),
        ((width, part), bf16),
        ((part, width), bf16),
    ]
    return pl.pallas_call(
        kernel,
        name="forward",
        out_shape=[jax.ShapeDtypeStruct(a, b) for a, b in out_shapes],
        in_specs=[VMEM] * 6 + [ANY] * 3 + [VMEM] * 3 + [SMEM] + [ANY] * 2,
        out_specs=[ANY] * 4 + [VMEM] * 8 + [ANY] + [VMEM] * 2 + [ANY] * 3,
        scratch_shapes=[
            pltpu.VMEM((blocks, 2, hs, width), bf16),
            pltpu.VMEM((seqs, 2, hs, width), bf16),
            pltpu.VMEM((2 * pairs, total, 128), bf16),
            pltpu.VMEM((half, total), bf16),
            pltpu.VMEM((blocks, span, half), bf16),
            pltpu.VMEM((columns, capacity, width), bf16),
            pltpu.VMEM((seqs, 8, 128), jnp.int32),
            pltpu.VMEM((seqs, 8, 128), jnp.int32),
            pltpu.VMEM((8, 128), f32),
            pltpu.VMEM((blocks, 2, 8, 128), f32),
            DMA((3,)),
            DMA,
            DMA((seqs, 2)),
            DMA((blocks,)),
            DMA((blocks,)),
            DMA((blocks,)),
            DMA,
            DMA((blocks,)),
            DMA((seqs, 2)),
            DMA,
            DMA((columns,)),
            DMA((columns,)),
            DMA,
            DMA,
            DMA((2 * blocks - 1,)),
            DMA((blocks, 2)),
            DMA((2,)),
            DMA((2,)),
            DMA((2,)),
            DMA((2,)),
            pltpu.VMEM((width, total), bf16),
            pltpu.VMEM((width, 3 * half), bf16),
            pltpu.VMEM((blocks, span, 3 * half), bf16),
            pltpu.VMEM((half, total), f32),
            DMA((4,)),
        ],
        compiler_params=params(1),
    )(
        hidden.reshape(seqs, 2, hs, width), cotangent.reshape(tokens, width),
        gain_one, shift_one, gain_two, shift_two,
        w_query, w_key, w_value, w_output, w_router, ids, lengths, w_inner, w_outer,
    )


def slice_order(z):
    near = z + 1 - 2 * lax.rem(z, 2)
    across = jnp.where(z < 2, 2, 1)
    inner = (z > 0) & (z < 3)
    return [jnp.where(inner, across, near), jnp.where(inner, near, across), z, jnp.where(z < 2, 3, 0)]


def experts(
    rows, scales, cot, counts, w_inner, w_outer, sib_inner, sib_outer, near_inner, blocks
):
    columns, capacity, width = rows.shape
    cap_lanes = scales.shape[2]
    total = columns * capacity
    part = w_inner.shape[1]
    block = 256
    count = total // block
    per = block // capacity
    assert blocks == 4 and columns == count * per

    def kernel(*refs):
        rows_ref, sc_ref, cot_ref, cnt_ref, wi_ref, we_ref, bi_ref, bo_ref, li_ref = refs[:9]
        back_ref, dots_ref, made_ref, tot_ref, gi_out, go_out, ei_ref, eo_ref = refs[9:17]
        (
            x_ref, xt_ref, d_ref, scg_ref, cntg_ref, in_ref, out_ref, oacc, dacc, act_ref, dpre_ref,
            dr_ref, dots_own, sgi_ref, sgo_ref, ggi_ref, ggo_ref,
            xloc, xsend, xrecv, scsend, screcv, ksend, krecv, wloc, wsend, wrecv, vsend, vrecv,
            bloc, dsend, drecv, gsend, grecv, ssend, srecv, gi_ref, go_ref, keep_sem,
        ) = refs[17:]
        z, e, c, base = place()
        col = e // 2
        sib = base + 1 - c
        inner = (z > 0) & (z < blocks - 1)
        end = jnp.logical_not(inner)
        plane = [lax.rem(col + step, columns) for step in range(1, columns)]
        partners = column_partners(blocks, z, c, base) + [(z, 2 * t + c) for t in plane]
        greet(partners)

        def x_out(t):
            return remote(rows_ref.at[t], x_ref.at[col], xsend.at[t], xrecv.at[col], z, 2 * t + c)

        def sc_out(t):
            return remote(sc_ref.at[t], scg_ref.at[col], scsend.at[t], screcv.at[col], z, 2 * t + c)

        def cnt_out(t):
            return remote(cnt_ref, cntg_ref.at[col], ksend.at[t], krecv.at[col], z, 2 * t + c)

        x_own = pltpu.make_async_copy(rows_ref.at[col], x_ref.at[col], xloc)
        x_own.start()
        await_greetings(partners)
        for t in plane:
            sc_out(t).start()
            x_out(t).start()
            cnt_out(t).start()
        scg_ref[col] = sc_ref[col]
        cntg_ref[col] = cnt_ref[...]

        hop_two = lax.rem(z + 2, blocks)
        pair = z + 1 - 2 * lax.rem(z, 2)

        lo_half, hi_half = pl.ds(0, part), pl.ds(part, part)

        def views(s, which):
            return (in_ref.at[s, :, which], out_ref.at[s, which])

        sources = ((wi_ref, we_ref), (bi_ref, bo_ref))

        def w_own(i, k):
            return pltpu.make_async_copy(
                sources[k][i], views(z, (lo_half, hi_half)[k])[i], wloc.at[i, k]
            )

        def beside(side):
            return z - 1 if side == 0 else z + 1

        def w_near(side):
            return pltpu.make_async_copy(li_ref.at[side], views(beside(side), lo_half)[0], wloc.at[2, side])

        def w_near_sib(side):
            s = beside(side)
            return remote(li_ref.at[side], views(s, hi_half)[0], vsend.at[0, s], vrecv.at[0, s], z, sib)

        def w_hop(side):
            return remote(we_ref, views(z, lo_half)[1], wsend.at[1, side], wrecv.at[1, z], beside(side), e)

        def w_pass(i, side):
            s = beside(side)
            src = li_ref.at[side] if i == 0 else views(s, lo_half)[1]
            return remote(src, views(s, lo_half)[i], wsend.at[2 + i, side], wrecv.at[i, s], beside(1 - side), e)

        def w_got(i, s):
            return remote(views(s, lo_half)[i], views(s, lo_half)[i], wsend.at[0, 0], wrecv.at[i, s], z, e)

        def w_sib(i, s):
            return remote(views(s, lo_half)[i], views(s, hi_half)[i], vsend.at[i, s], vrecv.at[i, s], z, sib)

        def w_sib_got(i, s):
            return remote(views(s, lo_half)[i], views(s, hi_half)[i], vsend.at[i, z], vrecv.at[i, s], z, sib)

        def w_last(i):
            s = hop_two
            to = jnp.where(z == 1, 0, blocks - 1)
            return remote(views(s, lo_half)[i], views(s, lo_half)[i], wsend.at[4 + i, 0], wrecv.at[i, s], to, e)

        def has(side):
            return z > 0 if side == 0 else z < blocks - 1

        for side in range(2):

            @pl.when(has(side))
            def _():
                w_hop(side).start()

        for side in range(2):

            @pl.when(inner)
            def _():
                w_pass(0, side).start()

        for side in range(2):

            @pl.when(has(side))
            def _():
                w_near(side).start()
                w_near_sib(side).start()

        for i in range(2):
            for k in range(2):
                w_own(i, k).start()

        order = slice_order(z)
        far = order[3]
        oacc[...] = jnp.zeros_like(oacc)
        dacc[...] = jnp.zeros_like(dacc)
        first_block = col // per

        def at_block(b):
            return pl.ds(pl.multiple_of(b * per, per), per)

        def row_step(s, b, fresh):
            x_b = x_ref[at_block(b)].reshape(block, width)
            r = pl.ds(pl.multiple_of(b * block, block), block)
            if fresh:
                row = jnp.concatenate(
                    [scg_ref[b * per + i, :, 0:capacity] for i in range(per)], axis=1
                )
                column = jnp.transpose(row)[:, 0:1]
                cots = cot_ref[at_block(b)].reshape(block, width).astype(f32)
                d_ref[r, :] = (column * cots).astype(bf16)
            pre = dot(x_b, in_ref[s])
            cdf = 0.5 * (1.0 + lax.erf(pre * (0.5**0.5)))
            act = (pre * cdf).astype(bf16)
            slope = cdf + pre * (jnp.exp(-0.5 * pre * pre) * ((2 * jnp.pi) ** -0.5))
            d_act = dot_nt(d_ref[r, :], out_ref[s])
            d_pre = (d_act * slope).astype(bf16)
            act_ref[r, :] = act
            dpre_ref[r, :] = d_pre
            oacc[r, :] += dot(act, out_ref[s])
            dacc[r, :] += dot_nt(d_pre, in_ref[s])

        def grads(s):
            g_inner = dot(xt_ref[...], dpre_ref[...])
            gi_ref[s] = g_inner[:, :part].astype(bf16)
            sgi_ref[s] = g_inner[:, part:].astype(bf16)
            g_outer = dot_tn(act_ref[...], d_ref[...])
            go_ref[s] = g_outer[:part].astype(bf16)
            sgo_ref[s] = g_outer[part:].astype(bf16)
            for i in range(2):
                g_sib(i, s).start()

        def g_keep(i, n):
            return pltpu.make_async_copy(
                (gi_ref, go_ref)[i].at[order[2 + n]], (gi_out, go_out)[i].at[n], keep_sem.at[i, n]
            )

        def g_sib(i, s):
            src, dst = ((sgi_ref, ggi_ref), (sgo_ref, ggo_ref))[i]
            return remote(src.at[s], dst.at[s], gsend.at[i, s], grecv.at[i, s], z, sib)

        def join(s):
            for i, (total_ref, got_ref) in enumerate(((gi_ref, ggi_ref), (go_ref, ggo_ref))):
                g_sib(i, s).wait_recv()
                total_ref[s] = (total_ref[s].astype(f32) + got_ref[s].astype(f32)).astype(bf16)

        def s_out(i, s):
            src, dst = ((gi_ref, ei_ref), (go_ref, eo_ref))[i]
            return remote(src.at[s], dst.at[z], ssend.at[i, s], srecv.at[i, z], s, e)

        def block_at(m):
            return lax.rem(first_block + count - m, count)

        for side in range(2):

            @pl.when(has(side))
            def _():
                w_got(1, beside(side)).wait_recv()
                w_sib(1, beside(side)).start()

            @pl.when(inner)
            def _():
                w_pass(1, side).start()

        for side in range(2):

            @pl.when(has(side))
            def _():
                w_near(side).wait()
                for i in range(2):
                    w_sib_got(i, beside(side)).wait_recv()

        for m in range(count):
            b = block_at(m)
            for i in range(per):
                t = b * per + i

                @pl.when(t == col)
                def _():
                    x_own.wait()

                @pl.when(t != col)
                def _():
                    remote(sc_ref.at[0], scg_ref.at[t], scsend.at[t], screcv.at[t], z, e).wait_recv()
                    remote(rows_ref.at[0], x_ref.at[t], xsend.at[t], xrecv.at[t], z, e).wait_recv()

            row_step(order[0], b, True)
        def hand_on(i):
            w_got(i, hop_two).wait_recv()
            w_sib(i, hop_two).start()

            @pl.when(inner)
            def _():
                w_last(i).start()

        hand_on(0)
        xt_ref[...] = jnp.transpose(x_ref[...].reshape(total, width))
        grads(order[0])

        @pl.when(end)
        def _():
            hand_on(1)
            for i in range(2):
                w_sib_got(i, hop_two).wait_recv()

        def loop(s, start):
            def body(b, _):
                row_step(s, b, False)
                return 0

            lax.fori_loop(start, count, body, 0)

        row_step(order[1], 0, False)
        join(order[0])
        for i in range(2):
            s_out(i, order[0]).start()
        loop(order[1], 1)

        @pl.when(inner)
        def _():
            hand_on(1)

        grads(order[1])
        for i in range(2):
            for k in range(2):
                w_own(i, k).wait()
        row_step(order[2], 0, False)
        join(order[1])
        for i in range(2):
            s_out(i, order[1]).start()
        loop(order[2], 1)

        @pl.when(inner)
        def _():
            for i in range(2):
                w_sib_got(i, hop_two).wait_recv()

        @pl.when(end)
        def _():
            for i in range(2):
                w_got(i, far).wait_recv()
                w_sib(i, far).start()

        grads(order[2])

        @pl.when(end)
        def _():
            for i in range(2):
                w_sib_got(i, far).wait_recv()

        def d_out(t):
            return remote(dr_ref.at[t], back_ref.at[col], dsend.at[0, t], drecv.at[0, col], z, 2 * t + c)

        def dots_out(t):
            return remote(dots_own.at[t], dots_ref.at[col], dsend.at[1, t], drecv.at[1, col], z, 2 * t + c)

        b_own = pltpu.make_async_copy(dr_ref.at[col], back_ref.at[col], bloc)
        for m in list(range(1, count)) + [0]:
            b = block_at(m)
            row_step(order[3], b, False)
            if m == 1:
                join(order[2])
                for i in range(2):
                    g_keep(i, 0).start()
            r = pl.ds(pl.multiple_of(b * block, block), block)
            made = oacc[r, :].astype(bf16)
            made_ref[at_block(b)] = made.reshape(per, capacity, width)
            dr_ref[at_block(b)] = dacc[r, :].astype(bf16).reshape(per, capacity, width)
            cots = cot_ref[at_block(b)].reshape(block, width).astype(f32)
            sums = jnp.sum(cots * made.astype(f32), axis=1, keepdims=True)
            row = jnp.transpose(jnp.broadcast_to(sums, (block, 128)))[0:8]
            for i in range(per):
                t = b * per + i
                if cap_lanes != capacity:
                    dots_own[t] = jnp.zeros((8, cap_lanes), f32)
                dots_own[t, :, 0:capacity] = row[:, i * capacity : (i + 1) * capacity]

                @pl.when(t == col)
                def _():
                    b_own.start()
                    dots_ref[t] = dots_own[t]

                @pl.when(t != col)
                def _():
                    d_out(t).start()
                    dots_out(t).start()

        grads(order[3])
        join(order[3])
        for i in range(2):
            g_keep(i, 1).start()

        for t in plane:
            x_out(t).wait_send()
            sc_out(t).wait_send()
            cnt_out(t).wait_send()
            remote(cnt_ref, cntg_ref.at[t], ksend.at[t], krecv.at[t], z, e).wait_recv()
        tot = cntg_ref[0]
        for t in range(1, columns):
            tot = tot + cntg_ref[t]
        tot_ref[...] = tot
        for i in range(2):
            for side in range(2):

                @pl.when(inner)
                def _():
                    w_pass(i, side).wait_send()

            w_sib(i, hop_two).wait_send()

            @pl.when(end)
            def _():
                w_sib(i, far).wait_send()

            for n in range(blocks):
                g_sib(i, n).wait_send()
            for n in range(2):
                g_keep(i, n).wait()
            s_out(i, order[0]).wait_send()
            s_out(i, order[1]).wait_send()
            got = (ei_ref, eo_ref)[i]

            def arrived(zs):
                return remote(got.at[0], got.at[zs], ssend.at[i, 0], srecv.at[i, zs], z, e)

            arrived(pair).wait_recv()

            @pl.when(inner)
            def _():
                w_last(i).wait_send()
                for k in range(2):
                    arrived(lax.rem(2 * (z // 2) + 2 + k, blocks)).wait_recv()

        for side in range(2):

            @pl.when(has(side))
            def _():
                w_hop(side).wait_send()
                w_near_sib(side).wait_send()
                w_sib(1, beside(side)).wait_send()

        b_own.wait()
        for t in plane:
            d_out(t).wait_send()
            dots_out(t).wait_send()
            remote(dr_ref.at[0], back_ref.at[t], dsend.at[0, t], drecv.at[0, t], z, e).wait_recv()
            remote(dots_own.at[0], dots_ref.at[t], dsend.at[1, t], drecv.at[1, t], z, e).wait_recv()

    out_shapes = [
        ((columns, capacity, width), bf16),
        ((columns, 8, cap_lanes), f32),
        ((columns, capacity, width), bf16),
        ((8, 128), f32),
        ((2, width, part), bf16),
        ((2, part, width), bf16),
        ((blocks, width, part), bf16),
        ((blocks, part, width), bf16),
    ]
    return pl.pallas_call(
        kernel,
        name="experts",
        out_shape=[jax.ShapeDtypeStruct(a, b) for a, b in out_shapes],
        in_specs=[VMEM] * 4 + [ANY] * 5,
        out_specs=[ANY] + [VMEM] * 3 + [ANY] * 4,
        scratch_shapes=[
            pltpu.VMEM((columns, capacity, width), bf16),
            pltpu.VMEM((width, total), bf16),
            pltpu.VMEM((total, width), bf16),
            pltpu.VMEM((columns, 8, cap_lanes), f32),
            pltpu.VMEM((columns, 8, 128), f32),
            pltpu.VMEM((blocks, width, 2 * part), bf16),
            pltpu.VMEM((blocks, 2 * part, width), bf16),
            pltpu.VMEM((total, width), f32),
            pltpu.VMEM((total, width), f32),
            pltpu.VMEM((total, 2 * part), bf16),
            pltpu.VMEM((total, 2 * part), bf16),
            pltpu.VMEM((columns, capacity, width), bf16),
            pltpu.VMEM((columns, 8, cap_lanes), f32),
            pltpu.VMEM((blocks, width, part), bf16),
            pltpu.VMEM((blocks, part, width), bf16),
            pltpu.VMEM((blocks, width, part), bf16),
            pltpu.VMEM((blocks, part, width), bf16),
            DMA,
            DMA((columns,)),
            DMA((columns,)),
            DMA((columns,)),
            DMA((columns,)),
            DMA((columns,)),
            DMA((columns,)),
            DMA((3, 2)),
            DMA((6, 2)),
            DMA((2, blocks)),
            DMA((2, blocks)),
            DMA((2, blocks)),
            DMA,
            DMA((2, columns)),
            DMA((2, columns)),
            DMA((2, blocks)),
            DMA((2, blocks)),
            DMA((2, blocks)),
            DMA((2, blocks)),
            pltpu.VMEM((blocks, width, part), bf16),
            pltpu.VMEM((blocks, part, width), bf16),
            DMA((2, 2)),
        ],
        compiler_params=params(2),
    )(rows, scales, cot, counts, w_inner, w_outer, sib_inner, sib_outer, near_inner)


class PieceSum:
    def __init__(self, at, part, got1, got2, got3, gotr, full, sem, rsem, zsem, zrsem, order, finish):
        self.at, self.part, self.full = at, part, full
        self.got1, self.got2, self.got3, self.gotr = got1, got2, got3, gotr
        self.sem, self.rsem, self.zsem, self.zrsem = sem, rsem, zsem, zrsem
        z, e, c, bit, mate, blocks, sib = at
        self.first, self.second = order
        self.finish = finish
        self.rest = len(bit) - 2

    def swap(self, n, src, dst, e):
        return remote(src, dst, self.sem.at[n], self.rsem.at[n], self.at[0], e)

    def halves(self):
        z, e, c, bit, mate, blocks, sib = self.at
        return self.swap(0, self.part.at[1 - bit[self.first]], self.got1, mate[self.first])

    def quarters(self):
        z, e, c, bit, mate, blocks, sib = self.at
        b1, b2 = bit[self.first], bit[self.second]
        return self.swap(1, self.part.at[b1, 1 - b2], self.got2, mate[self.second])

    def to_z(self, zt):
        z, e, c, bit, mate, blocks, sib = self.at
        b1, b2 = bit[self.first], bit[self.second]
        return remote(
            self.part.at[b1, b2, zt], self.got3.at[z], self.zsem.at[0, zt], self.zrsem.at[0, z], zt, e
        )

    def own(self):
        z, e, c, bit, mate, blocks, sib = self.at
        return self.full.at[c, bit[self.first], bit[self.second], z]

    def back_z(self, zt):
        z, e, c, bit, mate, blocks, sib = self.at
        return remote(self.own(), self.own(), self.zsem.at[1, zt], self.zrsem.at[1, z], zt, e)

    def back_quarter(self):
        z, e, c, bit, mate, blocks, sib = self.at
        at = self.full.at[c, bit[self.first], bit[self.second]]
        return self.swap(2, at, at, mate[self.second])

    def back_half(self):
        z, e, c, bit, mate, blocks, sib = self.at
        at = self.full.at[c, bit[self.first]]
        return self.swap(3, at, at, mate[self.first])

    def to_sibling(self):
        z, e, c, bit, mate, blocks, sib = self.at
        return self.swap(4, self.full.at[c], self.full.at[c], sib)

    def step(self, n):
        z, e, c, bit, mate, blocks, sib = self.at
        b1, b2 = bit[self.first], bit[self.second]
        others = [lax.rem(z + step, blocks) for step in range(1, blocks)]
        if n == 0:
            self.halves().start()
        elif n == 1:
            self.halves().wait()
            self.part[b1] = (self.part[b1].astype(f32) + self.got1[...].astype(f32)).astype(bf16)
            self.quarters().start()
        elif n == 2:
            self.quarters().wait()
            self.part[b1, b2] = (self.part[b1, b2].astype(f32) + self.got2[...].astype(f32)).astype(bf16)
            for zt in others:
                self.to_z(zt).start()
        elif n == 3:
            for zs in others:
                remote(
                    self.got3.at[0], self.got3.at[zs], self.zsem.at[0, zs], self.zrsem.at[0, zs], z, e
                ).wait_recv()
            for zt in others:
                self.to_z(zt).wait_send()
            self.got3[z] = self.part[b1, b2, z]
            total = self.got3[0].astype(f32)
            for j in range(1, blocks):
                total = total + self.got3[j].astype(f32)
            own = self.own()
            own[...] = total.astype(bf16)
            for r in range(self.rest):
                copy = self.swap(5 + r, own, self.gotr.at[r], mate[2 + r])
                copy.start()
                copy.wait()
                own[...] = (own[...].astype(f32) + self.gotr[r].astype(f32)).astype(bf16)
            for zt in others:
                self.back_z(zt).start()
        elif n == 4:
            for zs in others:
                at = self.full.at[c, b1, b2, zs]
                remote(at, at, self.zsem.at[1, zs], self.zrsem.at[1, zs], z, e).wait_recv()
            for zt in others:
                self.back_z(zt).wait_send()
            self.back_quarter().start()
        elif n == 5:
            self.back_quarter().wait()
            self.back_half().start()
        elif n == 6:
            self.back_half().wait()
            self.to_sibling().start()
        elif n == 7:
            self.to_sibling().wait()
            for k in range(2):
                self.finish(k, self.full[k])

    @staticmethod
    def scratch(blocks, piece, lanes, rest):
        return [
            pltpu.VMEM((2, 2, blocks, piece, lanes), bf16),
            pltpu.VMEM((2, blocks, piece, lanes), bf16),
            pltpu.VMEM((blocks, piece, lanes), bf16),
            pltpu.VMEM((blocks, piece, lanes), bf16),
            pltpu.VMEM((max(1, rest), piece, lanes), bf16),
            pltpu.VMEM((2, 2, 2, blocks, piece, lanes), bf16),
            DMA((5 + rest,)),
            DMA((5 + rest,)),
            DMA((2, blocks)),
            DMA((2, blocks)),
        ]


def backward(
    rows_t, weights, qkv, att_t, lse, length, attended, middle, flat, gate, slot, ids, lengths, cotangent,
    back, dots, counts, made, hidden, gain_one, gain_two, w_output, w_router, g_inner, g_outer, e_inner, e_outer,
    experts_n,
):
    width, total = rows_t.shape
    half = weights.shape[1] // 3
    pairs = half // 128
    seqs, _, span, _ = attended.shape
    blocks = total // span
    columns, capacity, _ = back.shape
    slots = columns * capacity
    tokens = seqs * span
    hs = span // 2
    scale = HEAD**-0.5
    part = g_inner.shape[2]
    bits = columns.bit_length() - 1
    assert columns == 1 << bits and bits >= 2 and blocks == 4
    rest = bits - 2
    small_rows = -(-(5 + experts_n) // 8) * 8
    out_piece, pair_piece = width // (4 * blocks), 3 * width // (4 * blocks)
    n_sum = 10

    def kernel(*refs):
        (
            xt_in, w_in, qkv_in, attt_in, lse_ref, len_ref, t_in, mid_in, flat_in, gate_ref, slot_ref, ids_ref,
            lens_ref, cot_in, back_in, dots_ref, cnt_ref, made_ref, hid_in, g1_ref, g2_ref, wo_in, wr_ref,
            gi_ref, go_ref, ei_ref, eo_ref,
        ) = refs[:27]
        grads_ref, sums_ref, fi_ref, fo_ref, gh_ref, y_ref = refs[27:33]
        (
            do_ref, dqkv_ref, kt_ref, dk_ref, dv_ref, dn_ref, dsib_ref, dsum_ref, dnt_ref,
            zi, zo, ci, co, osib, sgot, szgot, datt_ref, op_ref, dmid_ref, mg_ref,
            loc_sem, dsend, drecv, rloc, rsend, rrecv,
            nsend, nrecv, ssend, srecv, osend, orecv, tsend, trecv, tzsend, tzrecv, msend, mrecv,
            back_ref, mid_ref, cot_ref, flat_ref, wo_ref, t_ref, qkv_ref, attt_ref, xt_ref, w_ref, hid_ref, load_sem,
        ) = refs[33:83]
        sums_scratch = refs[83:]
        z, e, c, base = place()
        col = e // 2
        sib = base + 1 - c
        seq_core, seq = z // 2, lax.rem(z, 2)
        bit = [lax.rem(col // (1 << i), 2) for i in range(bits)]
        mate = [2 * (col + (1 - 2 * bit[i]) * (1 << i)) + c for i in range(bits)]
        others = [lax.rem(z + step, blocks) for step in range(1, blocks)]
        plane = [lax.rem(col + step, columns) for step in range(1, columns)]
        inner = (z > 0) & (z < blocks - 1)
        order = slice_order(z)
        across = [lax.rem(2 * (z // 2) + 2 + k, blocks) for k in range(2)]
        partners = column_partners(blocks, z, c, base) + [(z, 2 * t + c) for t in plane]
        greet(partners)
        loads = [
            pltpu.make_async_copy(src, dst, load_sem.at[n])
            for n, (src, dst) in enumerate(
                (
                    (back_in, back_ref), (mid_in, mid_ref), (cot_in, cot_ref), (flat_in, flat_ref), (wo_in, wo_ref),
                    (t_in, t_ref), (qkv_in, qkv_ref), (attt_in, attt_ref), (xt_in, xt_ref), (w_in, w_ref), (hid_in, hid_ref),
                )
            )
        ]
        for load in loads:
            load.start()

        def m_out(t):
            return remote(made_ref.at[t], mg_ref.at[col], msend.at[t], mrecv.at[col], z, 2 * t + c)

        m_own = pltpu.make_async_copy(made_ref.at[col], mg_ref.at[col], loc_sem.at[2])
        m_own.start()

        far = order[3]
        pair = z + 1 - 2 * lax.rem(z, 2)

        def r_load(i, src, s, slot):
            return pltpu.make_async_copy(src.at[s], (zi, zo)[i].at[slot], rloc.at[i, slot])

        def r_chain(i):
            src, dst = ((gi_ref, ci), (go_ref, co))[i]
            return remote(src.at[1], dst, rsend.at[i], rrecv.at[i], pair, e)

        def r_sum(i):
            src, dst = ((zi, ci), (zo, co))[i]
            return remote(src.at[0], dst, rsend.at[i], rrecv.at[i], far, e)

        def chain(i):
            @pl.when(inner)
            def _():
                buf, got = ((zi, ci), (zo, co))[i]
                r_load(i, (gi_ref, go_ref)[i], 1, 0).wait()
                r_chain(i).wait_recv()
                buf[0] = (buf[0].astype(f32) + got[...].astype(f32)).astype(bf16)
                r_sum(i).start()

        for i in range(2):

            @pl.when(jnp.logical_not(inner))
            def _():
                r_load(i, (gi_ref, go_ref)[i], 0, 0).start()

            @pl.when(inner)
            def _():
                r_load(i, (gi_ref, go_ref)[i], 1, 0).start()

            r_load(i, (ei_ref, eo_ref)[i], pair, 1).start()

        onehot = one_hot(ids_ref, seqs, span)
        valid = valid_rows(lens_ref, z, seqs, span)
        from_slots = lane_of((tokens, slots), 1).astype(f32) == slot_ref[...]
        dots_row = jnp.concatenate([dots_ref[t, 0:1, 0:capacity] for t in range(columns)], axis=1)
        dot_rows = jnp.sum(jnp.where(from_slots, dots_row, 0.0), axis=1, keepdims=True)
        picks = from_slots.astype(f32).astype(bf16)
        for load in loads[:5]:
            load.wait()
        d_rows = dot(picks, back_ref[...].reshape(slots, width))
        count_row = cnt_ref[0:1]
        mean_load = jnp.sum(count_row, axis=1, keepdims=True) / experts_n
        ratio_rows = jnp.sum(onehot * ((count_row - mean_load) / mean_load), axis=1, keepdims=True)
        gates = gate_ref[...]
        d_gate = valid * (dot_rows + balance_weight * ratio_rows)
        d_logits = (onehot * (d_gate * gates * (1.0 - gates))).astype(bf16)
        router_t = dot_tn(d_logits, flat_ref[...])
        balance_part = jnp.sum(valid * gates * ratio_rows, axis=0, keepdims=True) / jnp.sum(
            count_row, axis=1, keepdims=True
        )
        gain_sum = jnp.zeros((1, width), f32)
        shift_sum = jnp.zeros((1, width), f32)
        for s in range(seqs):
            lo, hi = s * span, (s + 1) * span
            v = mid_ref[lo:hi]
            centered = v - jnp.mean(v, axis=-1, keepdims=True)
            inverse = lax.rsqrt(jnp.mean(centered * centered, axis=-1, keepdims=True) + epsilon)
            unit = centered * inverse
            dy = d_rows[lo:hi] + dot(d_logits[lo:hi, :experts_n], wr_ref[...])
            gain_sum = gain_sum + jnp.sum(dy * unit, axis=0, keepdims=True)
            shift_sum = shift_sum + jnp.sum(dy, axis=0, keepdims=True)
            du = dy * g2_ref[...].reshape(1, width)
            dx = inverse * (
                du
                - jnp.mean(du, axis=-1, keepdims=True)
                - unit * jnp.mean(du * unit, axis=-1, keepdims=True)
            )
            dmid_ref[lo:hi] = cot_ref[lo:hi].astype(f32) + dx
            d_branch = dmid_ref[lo:hi].astype(bf16)
            for k in range(2):
                datt_ref[s, k] = dot_nt(d_branch, wo_ref[k * half : (k + 1) * half]).astype(bf16)

        at = (z, e, c, bit, mate, blocks, sib)

        def finish_out(k, g):
            grads_ref[3, :, k * half : (k + 1) * half] = g.reshape(width, half)

        def finish_pair(p):
            def finish(k, g):
                g = g.reshape(3, width, 128)
                for m in range(3):
                    grads_ref[m, :, k * half + p * 128 : k * half + (p + 1) * 128] = g[m]

            return finish

        out_sum = PieceSum(at, *sums_scratch[:n_sum], (0, 1), finish_out)
        pair_sums = [
            PieceSum(
                at,
                *sums_scratch[n_sum * (p + 1) : n_sum * (p + 2)],
                (1, 0) if p % 2 == 0 else (0, 1),
                finish_pair(p),
            )
            for p in range(pairs)
        ]

        await_greetings(partners)

        def d_out(s, k):
            return remote(
                datt_ref.at[s, k], do_ref.at[z], dsend.at[s, k], drecv.at[z], 2 * c + s, base + k
            )

        def d_own(s, k):
            return pltpu.make_async_copy(datt_ref.at[s, k], do_ref.at[z], loc_sem.at[0])

        for k, s in ((0, 0), (0, 1), (1, 1), (1, 0)):
            if True:
                to_self = (2 * c + s == z) & (c == k)

                @pl.when(to_self)
                def _():
                    d_own(s, k).start()

                @pl.when(jnp.logical_not(to_self))
                def _():
                    d_out(s, k).start()

        @pl.when(jnp.logical_not(inner))
        def _():
            r_chain(0).start()

        sums_ref[...] = jnp.zeros_like(sums_ref)
        sums_ref[2:3] = gain_sum
        sums_ref[3:4] = shift_sum
        sums_ref[4 : 4 + experts_n] = router_t[0:experts_n]
        sums_ref[4 + experts_n : 5 + experts_n] = jnp.broadcast_to(balance_part, (1, width))
        d_branch = dmid_ref[...].astype(bf16)
        loads[5].wait()
        for k in range(2):
            att_k = jnp.concatenate([t_ref[s, k] for s in range(seqs)], axis=0)
            made_k = dot_tn(att_k, d_branch).astype(bf16)
            op_ref[0, k * half : (k + 1) * half] = made_k[:, :half]
            op_ref[1, k * half : (k + 1) * half] = made_k[:, half:]
        o_first = remote(op_ref.at[1 - c], osib, osend, orecv, z, sib)
        o_first.start()
        o_first.wait()
        out_sum.part[...] = (op_ref[c].astype(f32) + osib[...].astype(f32)).astype(bf16).reshape(
            2, 2, blocks, out_piece, half
        )
        out_sum.step(0)
        out_sum.step(1)

        def d_got(j):
            mine = (z == j) & (c == seq_core)

            @pl.when(mine)
            def _():
                d_own(0, 0).wait()

            @pl.when(jnp.logical_not(mine))
            def _():
                remote(datt_ref.at[0, 0], do_ref.at[j], dsend.at[0, 0], drecv.at[j], z, base).wait_recv()

        for load in loads[6:]:
            load.wait()

        key_bias = jnp.where(lane_of((total, 1), 0) < len_ref[0:1, 0:1], 0.0, masked_fill)
        lane = lane_of((1, 128), 1)
        later = lax.broadcasted_iota(jnp.int32, (span, span), 0) > lax.broadcasted_iota(
            jnp.int32, (span, span), 1
        )

        def pair_step(p):
            first = p * 128
            k_all = qkv_ref[:, pl.ds(half + first, 128)]
            kt_ref[...] = jnp.transpose(k_all)
            v_all = qkv_ref[:, pl.ds(2 * half + first, 128)]
            k_heads = key_heads(k_all, key_bias)
            dk_ref[...] = jnp.zeros_like(dk_ref)
            dv_ref[...] = jnp.zeros_like(dv_ref)
            for j in range(blocks):
                n = (j + 1) * span
                r = pl.ds(j * span, span)
                if p == 0:
                    d_got(j)
                q = qkv_ref[r, pl.ds(first, 128)].astype(f32) * scale
                d_o = do_ref[j, :, pl.ds(first, 128)].astype(f32)
                prod_t = jnp.transpose(d_o) * attt_ref[pl.ds(first, 128), r]
                dq_t = []
                for h in range(2):
                    inside = (lane // HEAD) == h
                    spare = lane == (1 - h) * HEAD
                    q_h = jnp.where(inside, q, jnp.where(spare, 1.0, 0.0)).astype(bf16)
                    q_only = jnp.where(inside, q, 0.0).astype(bf16)
                    do_h = jnp.where(inside, d_o, 0.0).astype(bf16)
                    delta = jnp.sum(prod_t[h * HEAD : (h + 1) * HEAD], axis=0, keepdims=True)
                    s = dot_nt(k_heads[h][:n], q_h)
                    last = jnp.where(later, masked_fill, s[n - span :])
                    s = last if j == 0 else jnp.concatenate([s[: n - span], last], axis=0)
                    w = jnp.exp(s - lse_ref[pl.ds(2 * p + h, 1), r])
                    d_w = dot_nt(v_all[:n], do_h)
                    d_s = (w * (d_w - delta)).astype(bf16)
                    dv_ref[:n] += dot(w.astype(bf16), do_h)
                    dk_ref[:n] += dot(d_s, q_only)
                    dq_t.append(dot(kt_ref[h * HEAD : (h + 1) * HEAD, :n], d_s))
                dq = jnp.transpose(jnp.concatenate(dq_t, axis=0)) * scale
                dqkv_ref[r, pl.ds(first, 128)] = dq.astype(bf16)
            dqkv_ref[:, pl.ds(half + first, 128)] = dk_ref[...].astype(bf16)
            dqkv_ref[:, pl.ds(2 * half + first, 128)] = dv_ref[...].astype(bf16)
            joined = jnp.concatenate(
                [dqkv_ref[:, pl.ds(m * half + first, 128)] for m in range(3)], axis=1
            )
            grads = dot(xt_ref[...], joined).astype(bf16)
            pair_sums[p].part[...] = jnp.concatenate(
                [grads[:, m * 128 : (m + 1) * 128] for m in range(3)], axis=0
            ).reshape(2, 2, blocks, pair_piece, 128)

        state = {out_sum: 2}

        def advance(*chosen):
            for one in chosen or list(state):
                n = state.setdefault(one, 0)
                if n <= 7:
                    one.step(n)
                    state[one] = n + 1

        plan = ([out_sum], [pair_sums[0], out_sum], [pair_sums[0], out_sum]) if pairs == 3 else ([],) * pairs
        for p in range(pairs):
            pair_step(p)
            if plan[p]:
                advance(*plan[p])
            advance(pair_sums[p])
            if p == 1:
                chain(0)

        for t in plane:
            m_out(t).start()

        for j in range(blocks):
            r = pl.ds(j * span, span)
            dn_ref[j] = dot_nt(dqkv_ref[r, :], w_ref[...]).astype(bf16).reshape(2, hs, width)

        def n_sib(j):
            return remote(dn_ref.at[j, 1 - c], dsib_ref.at[j], nsend.at[j], nrecv.at[j], z, sib)

        def n_out(j):
            return remote(
                dsum_ref.at[j], dnt_ref.at[seq, c], ssend.at[j], srecv.at[seq, c], j, base + seq_core
            )

        def n_own():
            return pltpu.make_async_copy(dsum_ref.at[z], dnt_ref.at[seq, c], loc_sem.at[1])

        n_order = others[1:2] + others[0:1] + others[2:] + [z]
        for j in n_order:
            n_sib(j).start()
        advance(*pair_sums[1:2])
        for i, j in enumerate(n_order):
            n_sib(j).wait_recv()
            dsum_ref[j] = (dn_ref[j, c].astype(f32) + dsib_ref[j].astype(f32)).astype(bf16)
            if i < blocks - 1:
                n_out(j).start()
            else:

                @pl.when(seq_core == c)
                def _():
                    n_own().start()

                @pl.when(seq_core != c)
                def _():
                    n_out(j).start()

        @pl.when(jnp.logical_not(inner))
        def _():
            r_chain(1).start()

        advance(*pair_sums[1:], *pair_sums[:1], out_sum)
        for s in range(seqs):
            for k in range(2):
                from_self = (2 * c + s == z) & (c == k)

                @pl.when(jnp.logical_not(from_self))
                def _():
                    remote(
                        dsum_ref.at[0], dnt_ref.at[s, k], ssend.at[0], srecv.at[s, k], z, base
                    ).wait_recv()

                @pl.when(from_self)
                def _():
                    n_own().wait()

        gains = g1_ref[...].reshape(1, width)
        gain_sum = jnp.zeros((1, width), f32)
        shift_sum = jnp.zeros((1, width), f32)
        for s in range(seqs):
            for k in range(2):
                v = hid_ref[s, k].astype(f32)
                centered = v - jnp.mean(v, axis=-1, keepdims=True)
                inverse = lax.rsqrt(jnp.mean(centered * centered, axis=-1, keepdims=True) + epsilon)
                unit = centered * inverse
                dy = dnt_ref[s, k].astype(f32)
                gain_sum = gain_sum + jnp.sum(dy * unit, axis=0, keepdims=True)
                shift_sum = shift_sum + jnp.sum(dy, axis=0, keepdims=True)
                du = dy * gains
                dx = inverse * (
                    du
                    - jnp.mean(du, axis=-1, keepdims=True)
                    - unit * jnp.mean(du * unit, axis=-1, keepdims=True)
                )
                gh_ref[s, k] = dmid_ref[(2 * s + k) * hs : (2 * s + k + 1) * hs] + dx

        advance(*pair_sums[2:])

        sums_ref[0:1] = gain_sum
        sums_ref[1:2] = shift_sum

        def t_swap(n, te):
            return remote(sums_ref, sgot.at[n], tsend.at[n], trecv.at[n], z, te)

        partners = [sib] + mate
        for n, te in enumerate(partners):
            copy = t_swap(n, te)
            copy.start()
            if n in (1, 2):
                advance()
            if n == 1:
                chain(1)
            copy.wait()
            sums_ref[...] = sums_ref[...] + sgot[n]

        def t_z(zt):
            return remote(sums_ref, szgot.at[z], tzsend.at[zt], tzrecv.at[z], zt, e)

        for zt in others:
            t_z(zt).start()
        for t in plane:
            remote(made_ref.at[0], mg_ref.at[t], msend.at[t], mrecv.at[t], z, e).wait_recv()
        m_own.wait()
        scaled = valid * gates
        expert_out = dot(picks, mg_ref[...].reshape(slots, width))
        y_ref[...] = (mid_ref[...] + scaled * expert_out).astype(bf16)
        for _ in range(3):
            advance()
        for zs in others:
            remote(sums_ref, szgot.at[zs], tzsend.at[zs], tzrecv.at[zs], z, e).wait_recv()
        for zt in others:
            t_z(zt).wait_send()
        szgot[z] = sums_ref[...]
        tot = szgot[0]
        for j in range(1, blocks):
            tot = tot + szgot[j]
        sums_ref[...] = tot

        advance()
        for i, (buf, got, final) in enumerate(((zi, ci, fi_ref), (zo, co, fo_ref))):

            @pl.when(inner)
            def _():
                r_sum(i).wait_send()
                r_load(i, (gi_ref, go_ref)[i], 0, 0).start()

            r_load(i, (gi_ref, go_ref)[i], 0, 0).wait()
            r_load(i, (ei_ref, eo_ref)[i], pair, 1).wait()
            final[...] = buf[0].astype(f32) + buf[1].astype(f32)

            @pl.when(inner)
            def _():
                for k in range(2):
                    r_load(i, (ei_ref, eo_ref)[i], across[k], k).start()
                for k in range(2):
                    r_load(i, (ei_ref, eo_ref)[i], across[k], k).wait()
                final[...] = final[...] + (buf[0].astype(f32) + buf[1].astype(f32))

            @pl.when(jnp.logical_not(inner))
            def _():
                r_sum(i).wait_recv()
                r_chain(i).wait_send()
                final[...] = final[...] + got[...].astype(f32)

            advance()
        while min(state.values()) <= 7:
            advance()

        for s in range(seqs):
            for k in range(2):

                @pl.when(jnp.logical_not((2 * c + s == z) & (c == k)))
                def _():
                    d_out(s, k).wait_send()

        for j in n_order[:-1]:
            n_out(j).wait_send()

        @pl.when(seq_core != c)
        def _():
            n_out(z).wait_send()

        for j in n_order:
            n_sib(j).wait_send()
        for t in plane:
            m_out(t).wait_send()

    stage = blocks
    scratch = [
        pltpu.VMEM((blocks, span, half), bf16),
        pltpu.VMEM((total, 3 * half), bf16),
        pltpu.VMEM((128, total), bf16),
        pltpu.VMEM((total, 128), f32),
        pltpu.VMEM((total, 128), f32),
        pltpu.VMEM((blocks, 2, hs, width), bf16),
        pltpu.VMEM((blocks, hs, width), bf16),
        pltpu.VMEM((blocks, hs, width), bf16),
        pltpu.VMEM((seqs, 2, hs, width), bf16),
        pltpu.VMEM((2, width, part), bf16),
        pltpu.VMEM((2, part, width), bf16),
        pltpu.VMEM((width, part), bf16),
        pltpu.VMEM((part, width), bf16),
        pltpu.VMEM((width, half), bf16),
        pltpu.VMEM((1 + bits, small_rows, width), f32),
        pltpu.VMEM((blocks, small_rows, width), f32),
        pltpu.VMEM((seqs, 2, span, half), bf16),
        pltpu.VMEM((2, width, half), bf16),
        pltpu.VMEM((tokens, width), f32),
        pltpu.VMEM((columns, capacity, width), bf16),
        DMA((3,)),
        DMA((seqs, 2)),
        DMA((stage,)),
        DMA((2, 2)),
        DMA((2,)),
        DMA((2,)),
        DMA((stage,)),
        DMA((stage,)),
        DMA((stage,)),
        DMA((seqs, 2)),
        DMA,
        DMA,
        DMA((1 + bits,)),
        DMA((1 + bits,)),
        DMA((stage,)),
        DMA((stage,)),
        DMA((columns,)),
        DMA((columns,)),
        pltpu.VMEM((columns, capacity, width), bf16),
        pltpu.VMEM((tokens, width), f32),
        pltpu.VMEM((tokens, width), bf16),
        pltpu.VMEM((tokens, width), bf16),
        pltpu.VMEM((width, width), bf16),
        pltpu.VMEM((seqs, 2, span, half), bf16),
        pltpu.VMEM((total, 3 * half), bf16),
        pltpu.VMEM((half, total), f32),
        pltpu.VMEM((width, total), bf16),
        pltpu.VMEM((width, 3 * half), bf16),
        pltpu.VMEM((seqs, 2, hs, width), bf16),
        DMA((11,)),
    ]
    scratch += PieceSum.scratch(blocks, out_piece, half, rest)
    for _ in range(pairs):
        scratch += PieceSum.scratch(blocks, pair_piece, 128, rest)
    grads, sums, f_inner, f_outer, g_hidden, output = pl.pallas_call(
        kernel,
        name="backward",
        out_shape=[
            jax.ShapeDtypeStruct((4, width, width), bf16),
            jax.ShapeDtypeStruct((small_rows, width), f32),
            jax.ShapeDtypeStruct((width, part), f32),
            jax.ShapeDtypeStruct((part, width), f32),
            jax.ShapeDtypeStruct((seqs, 2, hs, width), f32),
            jax.ShapeDtypeStruct((tokens, width), bf16),
        ],
        in_specs=[ANY] * 4 + [VMEM] * 2 + [ANY] * 3 + [VMEM] * 3 + [SMEM] + [ANY] * 2 + [VMEM] * 2 + [ANY] * 2 + [VMEM] * 2
        + [ANY] + [VMEM] + [ANY] * 4,
        out_specs=[VMEM] * 6,
        scratch_shapes=scratch,
        compiler_params=params(3),
    )(
        rows_t, weights, qkv, att_t, lse, length, attended, middle, flat, gate, slot, ids, lengths, cotangent,
        back, dots, counts, made, hidden.reshape(seqs, 2, hs, width), gain_one,
        gain_two, w_output, w_router, g_inner, g_outer, e_inner, e_outer,
    )
    return finish(grads, sums, f_inner, f_outer, g_hidden.reshape(tokens, width), output, experts_n)


def finish(grads, sums, g_inner, g_outer, g_hidden, output, experts_n):
    steps = 8
    width = grads.shape[2]
    tokens = output.shape[0]
    part = g_inner.shape[1]
    rows = width // steps

    def kernel(g_ref, s_ref, i_ref, o_ref, h_ref, y_ref, *outs):
        for m in range(4):
            outs[m][...] = g_ref[m].astype(f32)
        outs[4][...] = i_ref[...]
        outs[5][...] = o_ref[...]
        outs[6][...] = h_ref[...]
        outs[7][...] = y_ref[...]

        @pl.when(pl.program_id(0) == 0)
        def _():
            for m in range(4):
                outs[8 + m][...] = s_ref[m]
            outs[12][...] = s_ref[4 : 4 + experts_n]
            outs[13][...] = s_ref[4 + experts_n : 5 + experts_n, 0:1]

    def by_rows(shape):
        return pl.BlockSpec((shape[0] // steps,) + shape[1:], lambda i: (i,) + (0,) * (len(shape) - 1))

    def whole(shape):
        return pl.BlockSpec(shape, lambda i: (0,) * len(shape))

    split = [(width, width)] * 4 + [(width, part), (part, width), (tokens, width), (tokens, width)]
    kept = [(width,)] * 4 + [(experts_n, width), (1, 1)]
    return pl.pallas_call(
        kernel,
        name="finish",
        grid=(steps,),
        out_shape=[jax.ShapeDtypeStruct(a, bf16 if n == 7 else f32) for n, a in enumerate(split + kept)],
        in_specs=[pl.BlockSpec((4, rows, width), lambda i: (0, i, 0)), whole(sums.shape)]
        + [by_rows(a) for a in split[4:]],
        out_specs=[by_rows(a) for a in split] + [whole(a) for a in kept],
        compiler_params=pltpu.CompilerParams(dimension_semantics=("arbitrary",), vmem_limit_bytes=VMEM_BYTES),
    )(grads, sums, g_inner, g_outer, g_hidden, output)


def on_device(
    hidden_in,
    cotangent,
    query_weight,
    key_weight,
    value_weight,
    output_weight,
    gain_one,
    shift_one,
    gain_two,
    shift_two,
    w_router,
    w_inner,
    w_outer,
    expert_ids,
    seq_lengths,
):
    seqs, span, width = hidden_in.shape
    tokens = seqs * span
    blocks = lax.axis_size("blk")
    columns = lax.axis_size("ep") // 2
    experts_n = w_router.shape[1]
    capacity = max(2, 2 * tokens // experts_n)
    total = blocks * span
    half = width // 2
    assert seqs * 2 == blocks and experts_n == columns

    ids = expert_ids.reshape(seqs, span)
    lengths = seq_lengths
    router = jnp.transpose(w_router)
    cot = cotangent.reshape(tokens, width)
    (
        rows_t, w_qkv, qkv, att_t, lse, attended, middle, flat, gate, slot, to_rows, scales, cot_rows, length, counts,
        near_inner, sib_inner, sib_outer,
    ) = forward(
        hidden_in, cotangent, gain_one, shift_one, gain_two, shift_two, query_weight, key_weight, value_weight,
        output_weight, router, ids, lengths, w_inner[0], w_outer[0], blocks, columns, capacity, experts_n,
    )
    back, dots, made, counts, g_inner, g_outer, e_inner, e_outer = experts(
        to_rows, scales, cot_rows, counts, w_inner[0], w_outer[0], sib_inner, sib_outer, near_inner, blocks
    )
    results = backward(
        rows_t, w_qkv, qkv.reshape(total, 3 * half), att_t, lse, length, attended, middle, flat, gate,
        slot, ids, lengths, cot, back, dots, counts, made, hidden_in, gain_one, gain_two, output_weight, router,
        g_inner, g_outer, e_inner, e_outer, experts_n,
    )
    dense, (grad_inner, grad_outer, grad_hidden, output) = results[:4], results[4:8]
    gains, (grad_router, balance) = results[8:12], results[12:]
    return (
        output.reshape(seqs, span, width),
        grad_hidden.reshape(seqs, span, width),
        *dense,
        *gains,
        jnp.transpose(grad_router),
        grad_inner[None],
        grad_outer[None],
        balance[0, 0],
    )


def solution(mesh):
    tokens = P("ep", "blk", None)
    return jax.shard_map(
        on_device,
        mesh=mesh,
        in_specs=(tokens, tokens)
        + (P(),) * 9
        + (P("ep", None, "blk"), P("ep", "blk", None), P("ep", "blk", None, None, None), P("ep")),
        out_specs=(tokens, tokens) + (P(),) * 9 + (P("ep", None, "blk"), P("ep", "blk", None), P()),
        check_vma=False,
    )
```

```python
import functools

import jax
import jax.numpy as jnp
from jax import lax
from jax.experimental import pallas as pl
from jax.experimental.pallas import tpu as pltpu
from jax.sharding import PartitionSpec as P

HEAD = 64
MESH = pl.DeviceIdType.MESH
ANY = pl.BlockSpec(memory_space=pl.ANY)
VMEM = pl.BlockSpec(memory_space=pltpu.VMEM)
SMEM = pl.BlockSpec(memory_space=pltpu.SMEM)
DMA = pltpu.SemaphoreType.DMA
f32 = jnp.float32
bf16 = jnp.bfloat16

epsilon = 1e-05
balance_weight = 6.0
masked_fill = -1e30
VMEM_BYTES = 57 * 1024 * 1024


def dot(a, b):
    return lax.dot_general(a, b, (((1,), (0,)), ((), ())), preferred_element_type=f32)


def dot_nt(a, b):
    return lax.dot_general(a, b, (((1,), (1,)), ((), ())), preferred_element_type=f32)


def dot_tn(a, b):
    return lax.dot_general(a, b, (((0,), (0,)), ((), ())), preferred_element_type=f32)


def place():
    z = lax.axis_index("blk")
    e = lax.axis_index("ep")
    c = lax.rem(e, 2)
    return z, e, c, e - c


def remote(src, dst, send_sem, recv_sem, z, e):
    return pltpu.make_async_remote_copy(
        src, dst, send_sem, recv_sem, device_id=(z, e), device_id_type=MESH
    )


def greet(partners):
    barrier = pltpu.get_barrier_semaphore()
    for z, e in partners:
        pl.semaphore_signal(barrier, inc=1, device_id=(z, e), device_id_type=MESH)


def await_greetings(partners):
    pl.semaphore_wait(pltpu.get_barrier_semaphore(), len(partners))


def column_partners(blocks, z, c, base):
    found = [(z, base + 1 - c)]
    for step in range(1, blocks):
        for k in range(2):
            found.append((lax.rem(z + step, blocks), base + k))
    return found


def params(collective_id):
    return pltpu.CompilerParams(
        collective_id=collective_id, has_side_effects=True, vmem_limit_bytes=VMEM_BYTES
    )


def lane_of(shape, dimension):
    return lax.broadcasted_iota(jnp.int32, shape, dimension)


def one_hot(ids_ref, seqs, span):
    columns = [
        jnp.transpose(jnp.broadcast_to(ids_ref[s : s + 1], (128, span))) for s in range(seqs)
    ]
    ids = jnp.concatenate(columns, axis=0)
    return (lane_of(ids.shape, 1) == ids).astype(f32)


def valid_rows(len_ref, z, seqs, span):
    place_in = z * span + lane_of((span, 1), 0)
    return jnp.concatenate([(place_in < len_ref[s]).astype(f32) for s in range(seqs)], axis=0)


def key_heads(k_all, key_bias):
    lane = lane_of((1, 128), 1)
    found = []
    for h in range(2):
        inside = (lane // HEAD) == h
        spare = lane == (1 - h) * HEAD
        found.append(
            jnp.where(inside, k_all.astype(f32), jnp.where(spare, key_bias, 0.0)).astype(bf16)
        )
    return found


def forward(
    hidden, cotangent, gain_one, shift_one, gain_two, shift_two, w_query, w_key, w_value, w_output, w_router,
    ids, lengths, w_inner, w_outer, blocks, columns, capacity, experts_n,
):
    seqs, span, width = hidden.shape
    hs = span // 2
    half = width // 2
    pairs = half // 128
    total = blocks * span
    tokens = seqs * span
    slots = experts_n * capacity
    part = w_inner.shape[1]
    cap_lanes = max(128, capacity)

    def kernel(*refs):
        (
            hid_ref, cot_ref, g1_ref, s1_ref, g2_ref, s2_ref, wq_ref, wk_ref, wv_ref, wo_ref, wr_ref,
            ids_ref, len_in, wi_ref, we_ref,
        ) = refs[:15]
        (
            xt_out, w_out, qkv_out, attt_out, lse_ref, t_out, mid_out, flat_out, gate_ref, slot_ref,
            rows_ref, sc_ref, cote_ref, len_ref, cnt_ref, li_ref, bi_ref, bo_ref,
        ) = refs[15:33]
        (
            x_ref, nb_ref, kh_ref, vt_ref, att_ref, cots_ref, lens_ref, lgot_ref, cown_ref, cgot_ref,
            wload, nloc, nsend, nrecv, fsend, frecv, aloc, asend, arecv, closs, csend, crecv,
            lsend, lrecv, ksend, krecv, hsend, hrecv, bsend, brecv,
            xt_ref, w_ref, qkv_ref, attt_ref, out_sem, t_ref, mid_ref, flat_ref,
        ) = refs[33:]
        z, e, c, base = place()
        col = e // 2
        sib = base + 1 - c
        seq_core, seq = z // 2, lax.rem(z, 2)
        others = [lax.rem(z + step, blocks) for step in range(1, blocks)]
        plane = [lax.rem(col + step, columns) for step in range(1, columns)]
        column = column_partners(blocks, z, c, base)
        greet(column + [(z, 2 * t + c) for t in plane])

        def load_w(m, ref):
            return pltpu.make_async_copy(
                ref.at[:, pl.ds(pl.multiple_of(c * half, half), half)],
                w_ref.at[:, pl.ds(m * half, half)],
                wload.at[m],
            )

        for m, ref in enumerate((wq_ref, wk_ref, wv_ref)):
            load_w(m, ref).start()
        gain_row, shift_row = g1_ref[...].reshape(1, width), s1_ref[...].reshape(1, width)
        for s in range(seqs):
            for k in range(2):
                v = hid_ref[s, k].astype(f32)
                centered = v - jnp.mean(v, axis=-1, keepdims=True)
                inverse = lax.rsqrt(jnp.mean(centered * centered, axis=-1, keepdims=True) + epsilon)
                nb_ref[s, k] = (centered * inverse * gain_row + shift_row).astype(bf16)
        await_greetings(column + plane)

        def n_out(s, k):
            return remote(
                nb_ref.at[s, k], x_ref.at[z, k], nsend.at[s, k], nrecv.at[z], 2 * c + s, base + k
            )

        def n_own(s, k):
            return pltpu.make_async_copy(nb_ref.at[s, k], x_ref.at[z, k], nloc)

        for k, s in ((0, 0), (0, 1), (1, 1), (1, 0)):
            if True:
                to_self = (2 * c + s == z) & (c == k)

                @pl.when(to_self)
                def _():
                    n_own(s, k).start()

                @pl.when(jnp.logical_not(to_self))
                def _():
                    n_out(s, k).start()

        for s in range(seqs):
            lens_ref[s] = jnp.full((8, 128), len_in[s], jnp.int32)
        to_lens = remote(lens_ref, lgot_ref, lsend, lrecv, z, sib)
        to_lens.start()
        lane = lane_of((tokens, 128), 1)
        onehot = one_hot(ids_ref, seqs, span)
        valid = valid_rows(len_in, z, seqs, span)
        cown_ref[...] = jnp.broadcast_to(jnp.sum(onehot * valid, axis=0, keepdims=True), (8, 128))

        def k_out(n, to_z, to_e):
            return remote(cown_ref, cgot_ref.at[z, c], ksend.at[n], krecv.at[z, c], to_z, to_e)

        for n, (to_z, to_e) in enumerate(column):
            k_out(n, to_z, to_e).start()
        earlier = (lane_of((tokens, tokens), 0) > lane_of((tokens, tokens), 1)).astype(f32).astype(bf16)
        rank = dot(earlier, onehot.astype(bf16))
        slot = jnp.sum(onehot * (rank + (lane * capacity).astype(f32)), axis=1, keepdims=True)
        slot_ref[...] = slot
        slot_row = jnp.transpose(jnp.broadcast_to(slot, (tokens, 128)))[0:1]
        to_slots = (lane_of((slots, tokens), 0).astype(f32) == slot_row).astype(f32).astype(bf16)
        cots_ref[...] = (
            dot(to_slots, cot_ref[...]).astype(bf16).reshape(columns, capacity, width)
        )

        def c_out(t):
            return remote(cots_ref.at[t], cote_ref.at[col], csend.at[t], crecv.at[col], z, 2 * t + c)

        c_own = pltpu.make_async_copy(cots_ref.at[col], cote_ref.at[col], closs)
        c_own.start()
        for t in plane:
            c_out(t).start()
        for m, ref in enumerate((wq_ref, wk_ref, wv_ref)):
            load_w(m, ref).wait()

        def n_sib(zs):
            return remote(x_ref.at[zs, c], x_ref.at[zs, c], fsend.at[zs], frecv.at[zs], z, sib)

        for zs in [z] + others:
            if zs is z:

                @pl.when(c == seq_core)
                def _():
                    n_own(0, 0).wait()

                @pl.when(c != seq_core)
                def _():
                    remote(nb_ref.at[0, 0], x_ref.at[z, c], nsend.at[0, 0], nrecv.at[z], z, base).wait_recv()
            else:
                remote(nb_ref.at[0, 0], x_ref.at[zs, c], nsend.at[0, 0], nrecv.at[zs], z, base).wait_recv()
            n_sib(zs).start()

        def h_out(step):
            side = 0 if step == 1 else 1
            return remote(wi_ref, li_ref.at[side], hsend.at[side], hrecv.at[side], z + step, e)

        def b_out(i):
            src, dst = ((wi_ref, bi_ref), (we_ref, bo_ref))[i]
            return remote(src, dst, bsend.at[i], brecv.at[i], z, sib)

        @pl.when(z < blocks - 1)
        def _():
            h_out(1).start()

        @pl.when(z > 0)
        def _():
            h_out(-1).start()

        for zs in [z] + others:
            remote(
                x_ref.at[zs, 1 - c], x_ref.at[zs, 1 - c], fsend.at[zs], frecv.at[zs], z, sib
            ).wait_recv()
            x_z = x_ref[zs].reshape(span, width)
            qkv_ref[zs] = dot(x_z, w_ref[...]).astype(bf16)
            xt_ref[:, pl.ds(pl.multiple_of(zs * span, span), span)] = jnp.transpose(x_z)
        for i in range(2):
            b_out(i).start()
        to_lens.wait()
        seq_len = jnp.where(c == seq_core, lens_ref[seq], lgot_ref[seq])
        len_ref[...] = seq_len
        key_bias = jnp.where(lane_of((total, 1), 0) < seq_len[0:1, 0:1], 0.0, masked_fill)
        for p in range(pairs):
            k_all = jnp.concatenate(
                [qkv_ref[j, :, half + p * 128 : half + (p + 1) * 128] for j in range(blocks)], axis=0
            )
            for h, k_h in enumerate(key_heads(k_all, key_bias)):
                kh_ref[2 * p + h] = k_h
            for j in range(blocks):
                vt_ref[p * 128 : (p + 1) * 128, j * span : (j + 1) * span] = jnp.transpose(
                    qkv_ref[j, :, 2 * half + p * 128 : 2 * half + (p + 1) * 128]
                )
        outs = [
            pltpu.make_async_copy(src, dst, out_sem.at[n])
            for n, (src, dst) in enumerate(
                (
                    (xt_ref, xt_out), (w_ref, w_out), (qkv_ref, qkv_out), (attt_ref, attt_out),
                    (t_ref, t_out), (mid_ref, mid_out), (flat_ref, flat_out),
                )
            )
        ]
        for out in outs[:3]:
            out.start()
        later = lane_of((span, span), 0) > lane_of((span, span), 1)
        lane_row = lane_of((1, 128), 1)

        def a_out(j):
            return remote(
                att_ref.at[j], t_ref.at[seq, c], asend.at[j], arecv.at[seq, c], j, base + seq_core
            )

        def a_own(j):
            return pltpu.make_async_copy(att_ref.at[j], t_ref.at[seq, c], aloc)

        for j in [0] + list(range(blocks - 1, 0, -1)):
            n = (j + 1) * span

            def pair_step(p, _):
                first = pl.multiple_of(p * 128, 128)
                q = qkv_ref[j, :, pl.ds(first, 128)].astype(f32) * (HEAD**-0.5)
                out_t = []
                for h in range(2):
                    inside = (lane_row // HEAD) == h
                    spare = lane_row == (1 - h) * HEAD
                    q_h = jnp.where(inside, q, jnp.where(spare, 1.0, 0.0)).astype(bf16)
                    s = dot_nt(kh_ref[2 * p + h, :n], q_h)
                    last = jnp.where(later, masked_fill, s[n - span :])
                    s = last if j == 0 else jnp.concatenate([s[: n - span], last], axis=0)
                    top = jnp.max(s, axis=0, keepdims=True)
                    w = jnp.exp(s - top)
                    total_w = jnp.sum(w, axis=0, keepdims=True)
                    o_t = dot(vt_ref[pl.ds(pl.multiple_of(first + h * HEAD, HEAD), HEAD), :n], w.astype(bf16))
                    out_t.append(o_t / total_w)
                    lse_ref[pl.ds(2 * p + h, 1), pl.ds(j * span, span)] = top + jnp.log(total_w)
                o = jnp.concatenate(out_t, axis=0)
                attt_ref[pl.ds(first, 128), pl.ds(j * span, span)] = o
                att_ref[j, :, pl.ds(first, 128)] = jnp.transpose(o).astype(bf16)
                return 0

            lax.fori_loop(0, pairs, pair_step, 0)
            to_self = (z == j) & (c == seq_core)

            @pl.when(to_self)
            def _():
                a_own(j).start()

            @pl.when(jnp.logical_not(to_self))
            def _():
                a_out(j).start()

        outs[3].start()
        for s in range(seqs):
            for k in range(2):
                from_self = (2 * c + s == z) & (c == k)

                @pl.when(from_self)
                def _():
                    a_own(0).wait()

                @pl.when(jnp.logical_not(from_self))
                def _():
                    remote(att_ref.at[0], t_ref.at[s, k], asend.at[0], arecv.at[s, k], z, base).wait_recv()

        for s in range(seqs):
            r = pl.ds(s * span, span)
            branch = dot(t_ref[s, 0], wo_ref[0:half]) + dot(t_ref[s, 1], wo_ref[half:])
            v = hid_ref[s].reshape(span, width).astype(f32) + branch
            mid_ref[r, :] = v
            centered = v - jnp.mean(v, axis=-1, keepdims=True)
            inverse = lax.rsqrt(jnp.mean(centered * centered, axis=-1, keepdims=True) + epsilon)
            flat_ref[r, :] = (
                centered * inverse * g2_ref[...].reshape(1, width) + s2_ref[...].reshape(1, width)
            ).astype(bf16)
        for out in outs[4:]:
            out.start()
        logits = dot_nt(flat_ref[...], wr_ref[...])
        gate = jax.nn.sigmoid(
            jnp.sum(logits * onehot[:, :experts_n], axis=1, keepdims=True)
        )
        gate_ref[...] = gate
        rows_ref[...] = (
            dot(to_slots, flat_ref[...]).astype(bf16).reshape(columns, capacity, width)
        )
        from_slots = lane_of((tokens, slots), 1).astype(f32) == slot_ref[...]
        scales = jnp.sum(jnp.where(from_slots, valid * gate, 0.0), axis=0, keepdims=True)
        if cap_lanes != capacity:
            sc_ref[...] = jnp.zeros_like(sc_ref)
        for t in range(columns):
            sc_ref[t, :, 0:capacity] = jnp.broadcast_to(
                scales[:, t * capacity : (t + 1) * capacity], (8, capacity)
            )

        for out in outs:
            out.wait()
        for n, (to_z, to_e) in enumerate(column):
            remote(cown_ref, cgot_ref.at[to_z, lax.rem(to_e, 2)], ksend.at[n], krecv.at[to_z, lax.rem(to_e, 2)], z, sib).wait_recv()
            k_out(n, to_z, to_e).wait_send()
        cgot_ref[z, c] = cown_ref[...]
        tot = jnp.zeros((8, 128), f32)
        for zs in range(blocks):
            for k in range(2):
                tot = tot + cgot_ref[zs, k]
        cnt_ref[...] = tot
        c_own.wait()
        for t in plane:
            c_out(t).wait_send()
            remote(cots_ref.at[t], cote_ref.at[t], csend.at[t], crecv.at[t], z, e).wait_recv()
        for s in range(seqs):
            for k in range(2):

                @pl.when(jnp.logical_not((2 * c + s == z) & (c == k)))
                def _():
                    n_out(s, k).wait_send()

        for zs in [z] + others:
            n_sib(zs).wait_send()
        for j in range(blocks):

            @pl.when(jnp.logical_not((z == j) & (c == seq_core)))
            def _():
                a_out(j).wait_send()

        for i in range(2):
            b_out(i).wait()

        @pl.when(z < blocks - 1)
        def _():
            h_out(1).wait_send()
            remote(wi_ref, li_ref.at[1], hsend.at[1], hrecv.at[1], z, e).wait_recv()

        @pl.when(z > 0)
        def _():
            h_out(-1).wait_send()
            remote(wi_ref, li_ref.at[0], hsend.at[0], hrecv.at[0], z, e).wait_recv()

    out_shapes = [
        ((width, total), bf16),
        ((width, 3 * half), bf16),
        ((blocks, span, 3 * half), bf16),
        ((half, total), f32),
        ((2 * pairs, total), f32),
        ((seqs, 2, span, half), bf16),
        ((tokens, width), f32),
        ((tokens, width), bf16),
        ((tokens, 1), f32),
        ((tokens, 1), f32),
        ((columns, capacity, width), bf16),
        ((columns, 8, cap_lanes), f32),
        ((columns, capacity, width), bf16),
        ((8, 128), jnp.int32),
        ((8, 128), f32),
        ((2, width, part), bf16),
        ((width, part), bf16),
        ((part, width), bf16),
    ]
    return pl.pallas_call(
        kernel,
        name="forward",
        out_shape=[jax.ShapeDtypeStruct(a, b) for a, b in out_shapes],
        in_specs=[VMEM] * 6 + [ANY] * 3 + [VMEM] * 3 + [SMEM] + [ANY] * 2,
        out_specs=[ANY] * 4 + [VMEM] + [ANY] * 3 + [VMEM] * 4 + [ANY] + [VMEM] * 2 + [ANY] * 3,
        scratch_shapes=[
            pltpu.VMEM((blocks, 2, hs, width), bf16),
            pltpu.VMEM((seqs, 2, hs, width), bf16),
            pltpu.VMEM((2 * pairs, total, 128), bf16),
            pltpu.VMEM((half, total), bf16),
            pltpu.VMEM((blocks, span, half), bf16),
            pltpu.VMEM((columns, capacity, width), bf16),
            pltpu.VMEM((seqs, 8, 128), jnp.int32),
            pltpu.VMEM((seqs, 8, 128), jnp.int32),
            pltpu.VMEM((8, 128), f32),
            pltpu.VMEM((blocks, 2, 8, 128), f32),
            DMA((3,)),
            DMA,
            DMA((seqs, 2)),
            DMA((blocks,)),
            DMA((blocks,)),
            DMA((blocks,)),
            DMA,
            DMA((blocks,)),
            DMA((seqs, 2)),
            DMA,
            DMA((columns,)),
            DMA((columns,)),
            DMA,
            DMA,
            DMA((2 * blocks - 1,)),
            DMA((blocks, 2)),
            DMA((2,)),
            DMA((2,)),
            DMA((2,)),
            DMA((2,)),
            pltpu.VMEM((width, total), bf16),
            pltpu.VMEM((width, 3 * half), bf16),
            pltpu.VMEM((blocks, span, 3 * half), bf16),
            pltpu.VMEM((half, total), f32),
            DMA((7,)),
            pltpu.VMEM((seqs, 2, span, half), bf16),
            pltpu.VMEM((tokens, width), f32),
            pltpu.VMEM((tokens, width), bf16),
        ],
        compiler_params=params(1),
    )(
        hidden.reshape(seqs, 2, hs, width), cotangent.reshape(tokens, width),
        gain_one, shift_one, gain_two, shift_two,
        w_query, w_key, w_value, w_output, w_router, ids, lengths, w_inner, w_outer,
    )


def slice_order(z):
    near = z + 1 - 2 * lax.rem(z, 2)
    across = jnp.where(z < 2, 2, 1)
    inner = (z > 0) & (z < 3)
    return [jnp.where(inner, across, near), jnp.where(inner, near, across), z, jnp.where(z < 2, 3, 0)]


def experts(
    rows, scales, cot, counts, w_inner, w_outer, sib_inner, sib_outer, near_inner, blocks
):
    columns, capacity, width = rows.shape
    cap_lanes = scales.shape[2]
    total = columns * capacity
    part = w_inner.shape[1]
    block = 256
    count = total // block
    per = block // capacity
    assert blocks == 4 and columns == count * per

    def kernel(*refs):
        rows_ref, sc_ref, cot_ref, cnt_ref, wi_ref, we_ref, bi_ref, bo_ref, li_ref = refs[:9]
        back_ref, dots_ref, made_out, tot_ref, gi_out, go_out, ei_ref, eo_ref = refs[9:17]
        (
            x_ref, xt_ref, d_ref, scg_ref, cntg_ref, in_ref, out_ref, oacc, dacc, act_ref, dpre_ref,
            dr_ref, dots_own, sgi_ref, sgo_ref, ggi_ref, ggo_ref,
            xloc, xsend, xrecv, scsend, screcv, ksend, krecv, wloc, wsend, wrecv, vsend, vrecv,
            bloc, dsend, drecv, gsend, grecv, ssend, srecv, gi_ref, go_ref, keep_sem, made_ref, made_sem,
        ) = refs[17:]
        z, e, c, base = place()
        col = e // 2
        sib = base + 1 - c
        inner = (z > 0) & (z < blocks - 1)
        end = jnp.logical_not(inner)
        plane = [lax.rem(col + step, columns) for step in range(1, columns)]
        partners = column_partners(blocks, z, c, base) + [(z, 2 * t + c) for t in plane]
        greet(partners)

        def x_out(t):
            return remote(rows_ref.at[t], x_ref.at[col], xsend.at[t], xrecv.at[col], z, 2 * t + c)

        def sc_out(t):
            return remote(sc_ref.at[t], scg_ref.at[col], scsend.at[t], screcv.at[col], z, 2 * t + c)

        def cnt_out(t):
            return remote(cnt_ref, cntg_ref.at[col], ksend.at[t], krecv.at[col], z, 2 * t + c)

        x_own = pltpu.make_async_copy(rows_ref.at[col], x_ref.at[col], xloc)
        x_own.start()
        await_greetings(partners)
        for t in plane:
            sc_out(t).start()
            x_out(t).start()
            cnt_out(t).start()
        scg_ref[col] = sc_ref[col]
        cntg_ref[col] = cnt_ref[...]

        hop_two = lax.rem(z + 2, blocks)
        pair = z + 1 - 2 * lax.rem(z, 2)

        lo_half, hi_half = pl.ds(0, part), pl.ds(part, part)

        def views(s, which):
            return (in_ref.at[s, :, which], out_ref.at[s, which])

        sources = ((wi_ref, we_ref), (bi_ref, bo_ref))

        def w_own(i, k):
            return pltpu.make_async_copy(
                sources[k][i], views(z, (lo_half, hi_half)[k])[i], wloc.at[i, k]
            )

        def beside(side):
            return z - 1 if side == 0 else z + 1

        def w_near(side):
            return pltpu.make_async_copy(li_ref.at[side], views(beside(side), lo_half)[0], wloc.at[2, side])

        def w_near_sib(side):
            s = beside(side)
            return remote(li_ref.at[side], views(s, hi_half)[0], vsend.at[0, s], vrecv.at[0, s], z, sib)

        def w_hop(side):
            return remote(we_ref, views(z, lo_half)[1], wsend.at[1, side], wrecv.at[1, z], beside(side), e)

        def w_pass(i, side):
            s = beside(side)
            src = li_ref.at[side] if i == 0 else views(s, lo_half)[1]
            return remote(src, views(s, lo_half)[i], wsend.at[2 + i, side], wrecv.at[i, s], beside(1 - side), e)

        def w_got(i, s):
            return remote(views(s, lo_half)[i], views(s, lo_half)[i], wsend.at[0, 0], wrecv.at[i, s], z, e)

        def w_sib(i, s):
            return remote(views(s, lo_half)[i], views(s, hi_half)[i], vsend.at[i, s], vrecv.at[i, s], z, sib)

        def w_sib_got(i, s):
            return remote(views(s, lo_half)[i], views(s, hi_half)[i], vsend.at[i, z], vrecv.at[i, s], z, sib)

        def w_last(i):
            s = hop_two
            to = jnp.where(z == 1, 0, blocks - 1)
            return remote(views(s, lo_half)[i], views(s, lo_half)[i], wsend.at[4 + i, 0], wrecv.at[i, s], to, e)

        def has(side):
            return z > 0 if side == 0 else z < blocks - 1

        for side in range(2):

            @pl.when(has(side))
            def _():
                w_hop(side).start()

        for side in range(2):

            @pl.when(inner)
            def _():
                w_pass(0, side).start()

        for side in range(2):

            @pl.when(has(side))
            def _():
                w_near(side).start()
                w_near_sib(side).start()

        for i in range(2):
            for k in range(2):
                w_own(i, k).start()

        order = slice_order(z)
        far = order[3]
        oacc[...] = jnp.zeros_like(oacc)
        dacc[...] = jnp.zeros_like(dacc)
        first_block = col // per

        def at_block(b):
            return pl.ds(pl.multiple_of(b * per, per), per)

        def row_step(s, b, fresh):
            x_b = x_ref[at_block(b)].reshape(block, width)
            r = pl.ds(pl.multiple_of(b * block, block), block)
            if fresh:
                row = jnp.concatenate(
                    [scg_ref[b * per + i, :, 0:capacity] for i in range(per)], axis=1
                )
                column = jnp.transpose(row)[:, 0:1]
                cots = cot_ref[at_block(b)].reshape(block, width).astype(f32)
                d_ref[r, :] = (column * cots).astype(bf16)
            pre = dot(x_b, in_ref[s])
            cdf = 0.5 * (1.0 + lax.erf(pre * (0.5**0.5)))
            act = (pre * cdf).astype(bf16)
            slope = cdf + pre * (jnp.exp(-0.5 * pre * pre) * ((2 * jnp.pi) ** -0.5))
            d_act = dot_nt(d_ref[r, :], out_ref[s])
            d_pre = (d_act * slope).astype(bf16)
            act_ref[r, :] = act
            dpre_ref[r, :] = d_pre
            oacc[r, :] += dot(act, out_ref[s])
            dacc[r, :] += dot_nt(d_pre, in_ref[s])

        def grads(s):
            g_inner = dot(xt_ref[...], dpre_ref[...])
            gi_ref[s] = g_inner[:, :part].astype(bf16)
            sgi_ref[s] = g_inner[:, part:].astype(bf16)
            g_outer = dot_tn(act_ref[...], d_ref[...])
            go_ref[s] = g_outer[:part].astype(bf16)
            sgo_ref[s] = g_outer[part:].astype(bf16)
            for i in range(2):
                g_sib(i, s).start()

        def g_keep(i, n):
            return pltpu.make_async_copy(
                (gi_ref, go_ref)[i].at[order[2 + n]], (gi_out, go_out)[i].at[n], keep_sem.at[i, n]
            )

        def g_sib(i, s):
            src, dst = ((sgi_ref, ggi_ref), (sgo_ref, ggo_ref))[i]
            return remote(src.at[s], dst.at[s], gsend.at[i, s], grecv.at[i, s], z, sib)

        def join(s):
            for i, (total_ref, got_ref) in enumerate(((gi_ref, ggi_ref), (go_ref, ggo_ref))):
                g_sib(i, s).wait_recv()
                total_ref[s] = (total_ref[s].astype(f32) + got_ref[s].astype(f32)).astype(bf16)

        def s_out(i, s):
            src, dst = ((gi_ref, ei_ref), (go_ref, eo_ref))[i]
            return remote(src.at[s], dst.at[z], ssend.at[i, s], srecv.at[i, z], s, e)

        def block_at(m):
            return lax.rem(first_block + count - m, count)

        for side in range(2):

            @pl.when(has(side))
            def _():
                w_got(1, beside(side)).wait_recv()
                w_sib(1, beside(side)).start()

            @pl.when(inner)
            def _():
                w_pass(1, side).start()

        for side in range(2):

            @pl.when(has(side))
            def _():
                w_near(side).wait()
                for i in range(2):
                    w_sib_got(i, beside(side)).wait_recv()

        for m in range(count):
            b = block_at(m)
            for i in range(per):
                t = b * per + i

                @pl.when(t == col)
                def _():
                    x_own.wait()

                @pl.when(t != col)
                def _():
                    remote(sc_ref.at[0], scg_ref.at[t], scsend.at[t], screcv.at[t], z, e).wait_recv()
                    remote(rows_ref.at[0], x_ref.at[t], xsend.at[t], xrecv.at[t], z, e).wait_recv()

            row_step(order[0], b, True)
        def hand_on(i):
            w_got(i, hop_two).wait_recv()
            w_sib(i, hop_two).start()

            @pl.when(inner)
            def _():
                w_last(i).start()

        hand_on(0)
        xt_ref[...] = jnp.transpose(x_ref[...].reshape(total, width))
        grads(order[0])

        @pl.when(end)
        def _():
            hand_on(1)
            for i in range(2):
                w_sib_got(i, hop_two).wait_recv()

        def loop(s, start):
            def body(b, _):
                row_step(s, b, False)
                return 0

            lax.fori_loop(start, count, body, 0)

        row_step(order[1], 0, False)
        join(order[0])
        for i in range(2):
            s_out(i, order[0]).start()
        loop(order[1], 1)

        @pl.when(inner)
        def _():
            hand_on(1)

        grads(order[1])
        for i in range(2):
            for k in range(2):
                w_own(i, k).wait()
        row_step(order[2], 0, False)
        join(order[1])
        for i in range(2):
            s_out(i, order[1]).start()
        loop(order[2], 1)

        @pl.when(inner)
        def _():
            for i in range(2):
                w_sib_got(i, hop_two).wait_recv()

        @pl.when(end)
        def _():
            for i in range(2):
                w_got(i, far).wait_recv()
                w_sib(i, far).start()

        grads(order[2])

        @pl.when(end)
        def _():
            for i in range(2):
                w_sib_got(i, far).wait_recv()

        def d_out(t):
            return remote(dr_ref.at[t], back_ref.at[col], dsend.at[0, t], drecv.at[0, col], z, 2 * t + c)

        def dots_out(t):
            return remote(dots_own.at[t], dots_ref.at[col], dsend.at[1, t], drecv.at[1, col], z, 2 * t + c)

        def made_copy(m):
            at = at_block(block_at(m))
            return pltpu.make_async_copy(made_ref.at[at], made_out.at[at], made_sem.at[m])

        b_own = pltpu.make_async_copy(dr_ref.at[col], back_ref.at[col], bloc)
        for m in list(range(1, count)) + [0]:
            b = block_at(m)
            row_step(order[3], b, False)
            if m == 1:
                join(order[2])
                for i in range(2):
                    g_keep(i, 0).start()
            r = pl.ds(pl.multiple_of(b * block, block), block)
            made = oacc[r, :].astype(bf16)
            made_ref[at_block(b)] = made.reshape(per, capacity, width)
            made_copy(m).start()
            dr_ref[at_block(b)] = dacc[r, :].astype(bf16).reshape(per, capacity, width)
            cots = cot_ref[at_block(b)].reshape(block, width).astype(f32)
            sums = jnp.sum(cots * made.astype(f32), axis=1, keepdims=True)
            row = jnp.transpose(jnp.broadcast_to(sums, (block, 128)))[0:8]
            for i in range(per):
                t = b * per + i
                if cap_lanes != capacity:
                    dots_own[t] = jnp.zeros((8, cap_lanes), f32)
                dots_own[t, :, 0:capacity] = row[:, i * capacity : (i + 1) * capacity]

                @pl.when(t == col)
                def _():
                    b_own.start()
                    dots_ref[t] = dots_own[t]

                @pl.when(t != col)
                def _():
                    d_out(t).start()
                    dots_out(t).start()

        grads(order[3])
        join(order[3])
        for i in range(2):
            g_keep(i, 1).start()

        for t in plane:
            x_out(t).wait_send()
            sc_out(t).wait_send()
            cnt_out(t).wait_send()
            remote(cnt_ref, cntg_ref.at[t], ksend.at[t], krecv.at[t], z, e).wait_recv()
        tot = cntg_ref[0]
        for t in range(1, columns):
            tot = tot + cntg_ref[t]
        tot_ref[...] = tot
        for i in range(2):
            for side in range(2):

                @pl.when(inner)
                def _():
                    w_pass(i, side).wait_send()

            w_sib(i, hop_two).wait_send()

            @pl.when(end)
            def _():
                w_sib(i, far).wait_send()

            for n in range(blocks):
                g_sib(i, n).wait_send()
            for n in range(2):
                g_keep(i, n).wait()
            s_out(i, order[0]).wait_send()
            s_out(i, order[1]).wait_send()
            got = (ei_ref, eo_ref)[i]

            def arrived(zs):
                return remote(got.at[0], got.at[zs], ssend.at[i, 0], srecv.at[i, zs], z, e)

            arrived(pair).wait_recv()

            @pl.when(inner)
            def _():
                w_last(i).wait_send()
                for k in range(2):
                    arrived(lax.rem(2 * (z // 2) + 2 + k, blocks)).wait_recv()

        for side in range(2):

            @pl.when(has(side))
            def _():
                w_hop(side).wait_send()
                w_near_sib(side).wait_send()
                w_sib(1, beside(side)).wait_send()

        for m in range(count):
            made_copy(m).wait()
        b_own.wait()
        for t in plane:
            d_out(t).wait_send()
            dots_out(t).wait_send()
            remote(dr_ref.at[0], back_ref.at[t], dsend.at[0, t], drecv.at[0, t], z, e).wait_recv()
            remote(dots_own.at[0], dots_ref.at[t], dsend.at[1, t], drecv.at[1, t], z, e).wait_recv()

    out_shapes = [
        ((columns, capacity, width), bf16),
        ((columns, 8, cap_lanes), f32),
        ((columns, capacity, width), bf16),
        ((8, 128), f32),
        ((2, width, part), bf16),
        ((2, part, width), bf16),
        ((blocks, width, part), bf16),
        ((blocks, part, width), bf16),
    ]
    return pl.pallas_call(
        kernel,
        name="experts",
        out_shape=[jax.ShapeDtypeStruct(a, b) for a, b in out_shapes],
        in_specs=[VMEM] * 4 + [ANY] * 5,
        out_specs=[ANY, VMEM, ANY, VMEM] + [ANY] * 4,
        scratch_shapes=[
            pltpu.VMEM((columns, capacity, width), bf16),
            pltpu.VMEM((width, total), bf16),
            pltpu.VMEM((total, width), bf16),
            pltpu.VMEM((columns, 8, cap_lanes), f32),
            pltpu.VMEM((columns, 8, 128), f32),
            pltpu.VMEM((blocks, width, 2 * part), bf16),
            pltpu.VMEM((blocks, 2 * part, width), bf16),
            pltpu.VMEM((total, width), f32),
            pltpu.VMEM((total, width), f32),
            pltpu.VMEM((total, 2 * part), bf16),
            pltpu.VMEM((total, 2 * part), bf16),
            pltpu.VMEM((columns, capacity, width), bf16),
            pltpu.VMEM((columns, 8, cap_lanes), f32),
            pltpu.VMEM((blocks, width, part), bf16),
            pltpu.VMEM((blocks, part, width), bf16),
            pltpu.VMEM((blocks, width, part), bf16),
            pltpu.VMEM((blocks, part, width), bf16),
            DMA,
            DMA((columns,)),
            DMA((columns,)),
            DMA((columns,)),
            DMA((columns,)),
            DMA((columns,)),
            DMA((columns,)),
            DMA((3, 2)),
            DMA((6, 2)),
            DMA((2, blocks)),
            DMA((2, blocks)),
            DMA((2, blocks)),
            DMA,
            DMA((2, columns)),
            DMA((2, columns)),
            DMA((2, blocks)),
            DMA((2, blocks)),
            DMA((2, blocks)),
            DMA((2, blocks)),
            pltpu.VMEM((blocks, width, part), bf16),
            pltpu.VMEM((blocks, part, width), bf16),
            DMA((2, 2)),
            pltpu.VMEM((columns, capacity, width), bf16),
            DMA((count,)),
        ],
        compiler_params=params(2),
    )(rows, scales, cot, counts, w_inner, w_outer, sib_inner, sib_outer, near_inner)


class PieceSum:
    def __init__(self, at, part, got1, got2, got3, gotr, full, sem, rsem, zsem, zrsem, order, finish):
        self.at, self.part, self.full = at, part, full
        self.got1, self.got2, self.got3, self.gotr = got1, got2, got3, gotr
        self.sem, self.rsem, self.zsem, self.zrsem = sem, rsem, zsem, zrsem
        z, e, c, bit, mate, blocks, sib = at
        self.first, self.second = order
        self.finish = finish
        self.rest = len(bit) - 2

    def swap(self, n, src, dst, e):
        return remote(src, dst, self.sem.at[n], self.rsem.at[n], self.at[0], e)

    def halves(self):
        z, e, c, bit, mate, blocks, sib = self.at
        return self.swap(0, self.part.at[1 - bit[self.first]], self.got1, mate[self.first])

    def quarters(self):
        z, e, c, bit, mate, blocks, sib = self.at
        b1, b2 = bit[self.first], bit[self.second]
        return self.swap(1, self.part.at[b1, 1 - b2], self.got2, mate[self.second])

    def to_z(self, zt):
        z, e, c, bit, mate, blocks, sib = self.at
        b1, b2 = bit[self.first], bit[self.second]
        return remote(
            self.part.at[b1, b2, zt], self.got3.at[z], self.zsem.at[0, zt], self.zrsem.at[0, z], zt, e
        )

    def own(self):
        z, e, c, bit, mate, blocks, sib = self.at
        return self.full.at[c, bit[self.first], bit[self.second], z]

    def back_z(self, zt):
        z, e, c, bit, mate, blocks, sib = self.at
        return remote(self.own(), self.own(), self.zsem.at[1, zt], self.zrsem.at[1, z], zt, e)

    def back_quarter(self):
        z, e, c, bit, mate, blocks, sib = self.at
        at = self.full.at[c, bit[self.first], bit[self.second]]
        return self.swap(2, at, at, mate[self.second])

    def back_half(self):
        z, e, c, bit, mate, blocks, sib = self.at
        at = self.full.at[c, bit[self.first]]
        return self.swap(3, at, at, mate[self.first])

    def to_sibling(self):
        z, e, c, bit, mate, blocks, sib = self.at
        return self.swap(4, self.full.at[c], self.full.at[c], sib)

    def step(self, n):
        z, e, c, bit, mate, blocks, sib = self.at
        b1, b2 = bit[self.first], bit[self.second]
        others = [lax.rem(z + step, blocks) for step in range(1, blocks)]
        if n == 0:
            self.halves().start()
        elif n == 1:
            self.halves().wait()
            self.part[b1] = (self.part[b1].astype(f32) + self.got1[...].astype(f32)).astype(bf16)
            self.quarters().start()
        elif n == 2:
            self.quarters().wait()
            self.part[b1, b2] = (self.part[b1, b2].astype(f32) + self.got2[...].astype(f32)).astype(bf16)
            for zt in others:
                self.to_z(zt).start()
        elif n == 3:
            for zs in others:
                remote(
                    self.got3.at[0], self.got3.at[zs], self.zsem.at[0, zs], self.zrsem.at[0, zs], z, e
                ).wait_recv()
            for zt in others:
                self.to_z(zt).wait_send()
            self.got3[z] = self.part[b1, b2, z]
            total = self.got3[0].astype(f32)
            for j in range(1, blocks):
                total = total + self.got3[j].astype(f32)
            own = self.own()
            own[...] = total.astype(bf16)
            for r in range(self.rest):
                copy = self.swap(5 + r, own, self.gotr.at[r], mate[2 + r])
                copy.start()
                copy.wait()
                own[...] = (own[...].astype(f32) + self.gotr[r].astype(f32)).astype(bf16)
            for zt in others:
                self.back_z(zt).start()
        elif n == 4:
            for zs in others:
                at = self.full.at[c, b1, b2, zs]
                remote(at, at, self.zsem.at[1, zs], self.zrsem.at[1, zs], z, e).wait_recv()
            for zt in others:
                self.back_z(zt).wait_send()
            self.back_quarter().start()
        elif n == 5:
            self.back_quarter().wait()
            self.back_half().start()
        elif n == 6:
            self.back_half().wait()
            self.to_sibling().start()
        elif n == 7:
            self.to_sibling().wait()
            for k in range(2):
                self.finish(k, self.full[k])

    @staticmethod
    def scratch(blocks, piece, lanes, rest):
        return [
            pltpu.VMEM((2, 2, blocks, piece, lanes), bf16),
            pltpu.VMEM((2, blocks, piece, lanes), bf16),
            pltpu.VMEM((blocks, piece, lanes), bf16),
            pltpu.VMEM((blocks, piece, lanes), bf16),
            pltpu.VMEM((max(1, rest), piece, lanes), bf16),
            pltpu.VMEM((2, 2, 2, blocks, piece, lanes), bf16),
            DMA((5 + rest,)),
            DMA((5 + rest,)),
            DMA((2, blocks)),
            DMA((2, blocks)),
        ]


def backward(
    rows_t, weights, qkv, att_t, lse, length, attended, middle, flat, gate, slot, ids, lengths, cotangent,
    back, dots, counts, made, hidden, gain_one, gain_two, w_output, w_router, g_inner, g_outer, e_inner, e_outer,
    experts_n,
):
    width, total = rows_t.shape
    half = weights.shape[1] // 3
    pairs = half // 128
    seqs, _, span, _ = attended.shape
    blocks = total // span
    columns, capacity, _ = back.shape
    slots = columns * capacity
    tokens = seqs * span
    hs = span // 2
    scale = HEAD**-0.5
    part = g_inner.shape[2]
    bits = columns.bit_length() - 1
    assert columns == 1 << bits and bits >= 2 and blocks == 4
    rest = bits - 2
    small_rows = -(-(5 + experts_n) // 8) * 8
    out_piece, pair_piece = width // (4 * blocks), 3 * width // (4 * blocks)
    n_sum = 10

    def kernel(*refs):
        (
            xt_in, w_in, qkv_in, attt_in, lse_ref, len_ref, t_in, mid_in, flat_in, gate_ref, slot_ref, ids_ref,
            lens_ref, cot_in, back_in, dots_ref, cnt_ref, made_ref, hid_in, g1_ref, g2_ref, wo_in, wr_ref,
            gi_ref, go_ref, ei_ref, eo_ref,
        ) = refs[:27]
        grads_out, sums_ref, fi_out, fo_out, gh_out, y_out = refs[27:33]
        (
            do_ref, dqkv_ref, kt_ref, dk_ref, dv_ref, dn_ref, dsib_ref, dsum_ref, dnt_ref,
            zi, zo, ci, co, osib, sgot, szgot, datt_ref, op_ref, dmid_ref, mg_ref,
            loc_sem, dsend, drecv, rloc, rsend, rrecv,
            nsend, nrecv, ssend, srecv, osend, orecv, tsend, trecv, tzsend, tzrecv, msend, mrecv,
            back_ref, mid_ref, cot_ref, flat_ref, wo_ref, t_ref, qkv_ref, attt_ref, xt_ref, w_ref, hid_ref, load_sem,
            grads_ref, fi_ref, fo_ref, gh_ref, y_ref, out_sem,
        ) = refs[33:89]
        sums_scratch = refs[89:]
        z, e, c, base = place()
        col = e // 2
        sib = base + 1 - c
        seq_core, seq = z // 2, lax.rem(z, 2)
        bit = [lax.rem(col // (1 << i), 2) for i in range(bits)]
        mate = [2 * (col + (1 - 2 * bit[i]) * (1 << i)) + c for i in range(bits)]
        others = [lax.rem(z + step, blocks) for step in range(1, blocks)]
        plane = [lax.rem(col + step, columns) for step in range(1, columns)]
        inner = (z > 0) & (z < blocks - 1)
        order = slice_order(z)
        across = [lax.rem(2 * (z // 2) + 2 + k, blocks) for k in range(2)]
        partners = column_partners(blocks, z, c, base) + [(z, 2 * t + c) for t in plane]
        greet(partners)
        outs = [
            pltpu.make_async_copy(src, dst, out_sem.at[n])
            for n, (src, dst) in enumerate(
                ((gh_ref, gh_out), (y_ref, y_out), (fi_ref, fi_out), (fo_ref, fo_out))
                + tuple((grads_ref.at[m], grads_out.at[m]) for m in range(4))
            )
        ]
        loads = [
            pltpu.make_async_copy(src, dst, load_sem.at[n])
            for n, (src, dst) in enumerate(
                (
                    (back_in, back_ref), (mid_in, mid_ref), (cot_in, cot_ref), (flat_in, flat_ref), (wo_in, wo_ref),
                    (t_in, t_ref), (qkv_in, qkv_ref), (attt_in, attt_ref), (xt_in, xt_ref), (w_in, w_ref), (hid_in, hid_ref),
                )
            )
        ]
        for load in loads:
            load.start()

        def m_out(t):
            return remote(made_ref.at[t], mg_ref.at[col], msend.at[t], mrecv.at[col], z, 2 * t + c)

        m_own = pltpu.make_async_copy(made_ref.at[col], mg_ref.at[col], loc_sem.at[2])
        m_own.start()

        far = order[3]
        pair = z + 1 - 2 * lax.rem(z, 2)

        def r_load(i, src, s, slot):
            return pltpu.make_async_copy(src.at[s], (zi, zo)[i].at[slot], rloc.at[i, slot])

        def r_chain(i):
            src, dst = ((gi_ref, ci), (go_ref, co))[i]
            return remote(src.at[1], dst, rsend.at[i], rrecv.at[i], pair, e)

        def r_sum(i):
            src, dst = ((zi, ci), (zo, co))[i]
            return remote(src.at[0], dst, rsend.at[i], rrecv.at[i], far, e)

        def chain(i):
            @pl.when(inner)
            def _():
                buf, got = ((zi, ci), (zo, co))[i]
                r_load(i, (gi_ref, go_ref)[i], 1, 0).wait()
                r_chain(i).wait_recv()
                buf[0] = (buf[0].astype(f32) + got[...].astype(f32)).astype(bf16)
                r_sum(i).start()

        for i in range(2):

            @pl.when(jnp.logical_not(inner))
            def _():
                r_load(i, (gi_ref, go_ref)[i], 0, 0).start()

            @pl.when(inner)
            def _():
                r_load(i, (gi_ref, go_ref)[i], 1, 0).start()

            r_load(i, (ei_ref, eo_ref)[i], pair, 1).start()

        onehot = one_hot(ids_ref, seqs, span)
        valid = valid_rows(lens_ref, z, seqs, span)
        from_slots = lane_of((tokens, slots), 1).astype(f32) == slot_ref[...]
        dots_row = jnp.concatenate([dots_ref[t, 0:1, 0:capacity] for t in range(columns)], axis=1)
        dot_rows = jnp.sum(jnp.where(from_slots, dots_row, 0.0), axis=1, keepdims=True)
        picks = from_slots.astype(f32).astype(bf16)
        for load in loads[:5]:
            load.wait()
        d_rows = dot(picks, back_ref[...].reshape(slots, width))
        count_row = cnt_ref[0:1]
        mean_load = jnp.sum(count_row, axis=1, keepdims=True) / experts_n
        ratio_rows = jnp.sum(onehot * ((count_row - mean_load) / mean_load), axis=1, keepdims=True)
        gates = gate_ref[...]
        d_gate = valid * (dot_rows + balance_weight * ratio_rows)
        d_logits = (onehot * (d_gate * gates * (1.0 - gates))).astype(bf16)
        router_t = dot_tn(d_logits, flat_ref[...])
        balance_part = jnp.sum(valid * gates * ratio_rows, axis=0, keepdims=True) / jnp.sum(
            count_row, axis=1, keepdims=True
        )
        gain_sum = jnp.zeros((1, width), f32)
        shift_sum = jnp.zeros((1, width), f32)
        for s in range(seqs):
            lo, hi = s * span, (s + 1) * span
            v = mid_ref[lo:hi]
            centered = v - jnp.mean(v, axis=-1, keepdims=True)
            inverse = lax.rsqrt(jnp.mean(centered * centered, axis=-1, keepdims=True) + epsilon)
            unit = centered * inverse
            dy = d_rows[lo:hi] + dot(d_logits[lo:hi, :experts_n], wr_ref[...])
            gain_sum = gain_sum + jnp.sum(dy * unit, axis=0, keepdims=True)
            shift_sum = shift_sum + jnp.sum(dy, axis=0, keepdims=True)
            du = dy * g2_ref[...].reshape(1, width)
            dx = inverse * (
                du
                - jnp.mean(du, axis=-1, keepdims=True)
                - unit * jnp.mean(du * unit, axis=-1, keepdims=True)
            )
            dmid_ref[lo:hi] = cot_ref[lo:hi].astype(f32) + dx
            d_branch = dmid_ref[lo:hi].astype(bf16)
            for k in range(2):
                datt_ref[s, k] = dot_nt(d_branch, wo_ref[k * half : (k + 1) * half]).astype(bf16)

        at = (z, e, c, bit, mate, blocks, sib)

        def finish_out(k, g):
            grads_ref[3, :, k * half : (k + 1) * half] = g.reshape(width, half)

        def finish_pair(p):
            def finish(k, g):
                g = g.reshape(3, width, 128)
                for m in range(3):
                    grads_ref[m, :, k * half + p * 128 : k * half + (p + 1) * 128] = g[m]

            return finish

        out_sum = PieceSum(at, *sums_scratch[:n_sum], (0, 1), finish_out)
        pair_sums = [
            PieceSum(
                at,
                *sums_scratch[n_sum * (p + 1) : n_sum * (p + 2)],
                (1, 0) if p % 2 == 0 else (0, 1),
                finish_pair(p),
            )
            for p in range(pairs)
        ]

        await_greetings(partners)

        def d_out(s, k):
            return remote(
                datt_ref.at[s, k], do_ref.at[z], dsend.at[s, k], drecv.at[z], 2 * c + s, base + k
            )

        def d_own(s, k):
            return pltpu.make_async_copy(datt_ref.at[s, k], do_ref.at[z], loc_sem.at[0])

        for k, s in ((0, 0), (0, 1), (1, 1), (1, 0)):
            if True:
                to_self = (2 * c + s == z) & (c == k)

                @pl.when(to_self)
                def _():
                    d_own(s, k).start()

                @pl.when(jnp.logical_not(to_self))
                def _():
                    d_out(s, k).start()

        @pl.when(jnp.logical_not(inner))
        def _():
            r_chain(0).start()

        sums_ref[...] = jnp.zeros_like(sums_ref)
        sums_ref[2:3] = gain_sum
        sums_ref[3:4] = shift_sum
        sums_ref[4 : 4 + experts_n] = router_t[0:experts_n]
        sums_ref[4 + experts_n : 5 + experts_n] = jnp.broadcast_to(balance_part, (1, width))
        d_branch = dmid_ref[...].astype(bf16)
        loads[5].wait()
        for k in range(2):
            att_k = jnp.concatenate([t_ref[s, k] for s in range(seqs)], axis=0)
            made_k = dot_tn(att_k, d_branch).astype(bf16)
            op_ref[0, k * half : (k + 1) * half] = made_k[:, :half]
            op_ref[1, k * half : (k + 1) * half] = made_k[:, half:]
        o_first = remote(op_ref.at[1 - c], osib, osend, orecv, z, sib)
        o_first.start()
        o_first.wait()
        out_sum.part[...] = (op_ref[c].astype(f32) + osib[...].astype(f32)).astype(bf16).reshape(
            2, 2, blocks, out_piece, half
        )
        out_sum.step(0)
        out_sum.step(1)

        def d_got(j):
            mine = (z == j) & (c == seq_core)

            @pl.when(mine)
            def _():
                d_own(0, 0).wait()

            @pl.when(jnp.logical_not(mine))
            def _():
                remote(datt_ref.at[0, 0], do_ref.at[j], dsend.at[0, 0], drecv.at[j], z, base).wait_recv()

        for load in loads[6:]:
            load.wait()

        key_bias = jnp.where(lane_of((total, 1), 0) < len_ref[0:1, 0:1], 0.0, masked_fill)
        lane = lane_of((1, 128), 1)
        later = lax.broadcasted_iota(jnp.int32, (span, span), 0) > lax.broadcasted_iota(
            jnp.int32, (span, span), 1
        )

        def pair_step(p):
            first = p * 128
            k_all = qkv_ref[:, pl.ds(half + first, 128)]
            kt_ref[...] = jnp.transpose(k_all)
            v_all = qkv_ref[:, pl.ds(2 * half + first, 128)]
            k_heads = key_heads(k_all, key_bias)
            dk_ref[...] = jnp.zeros_like(dk_ref)
            dv_ref[...] = jnp.zeros_like(dv_ref)
            for j in range(blocks):
                n = (j + 1) * span
                r = pl.ds(j * span, span)
                if p == 0:
                    d_got(j)
                q = qkv_ref[r, pl.ds(first, 128)].astype(f32) * scale
                d_o = do_ref[j, :, pl.ds(first, 128)].astype(f32)
                prod_t = jnp.transpose(d_o) * attt_ref[pl.ds(first, 128), r]
                dq_t = []
                for h in range(2):
                    inside = (lane // HEAD) == h
                    spare = lane == (1 - h) * HEAD
                    q_h = jnp.where(inside, q, jnp.where(spare, 1.0, 0.0)).astype(bf16)
                    q_only = jnp.where(inside, q, 0.0).astype(bf16)
                    do_h = jnp.where(inside, d_o, 0.0).astype(bf16)
                    delta = jnp.sum(prod_t[h * HEAD : (h + 1) * HEAD], axis=0, keepdims=True)
                    s = dot_nt(k_heads[h][:n], q_h)
                    last = jnp.where(later, masked_fill, s[n - span :])
                    s = last if j == 0 else jnp.concatenate([s[: n - span], last], axis=0)
                    w = jnp.exp(s - lse_ref[pl.ds(2 * p + h, 1), r])
                    d_w = dot_nt(v_all[:n], do_h)
                    d_s = (w * (d_w - delta)).astype(bf16)
                    dv_ref[:n] += dot(w.astype(bf16), do_h)
                    dk_ref[:n] += dot(d_s, q_only)
                    dq_t.append(dot(kt_ref[h * HEAD : (h + 1) * HEAD, :n], d_s))
                dq = jnp.transpose(jnp.concatenate(dq_t, axis=0)) * scale
                dqkv_ref[r, pl.ds(first, 128)] = dq.astype(bf16)
            dqkv_ref[:, pl.ds(half + first, 128)] = dk_ref[...].astype(bf16)
            dqkv_ref[:, pl.ds(2 * half + first, 128)] = dv_ref[...].astype(bf16)
            joined = jnp.concatenate(
                [dqkv_ref[:, pl.ds(m * half + first, 128)] for m in range(3)], axis=1
            )
            grads = dot(xt_ref[...], joined).astype(bf16)
            pair_sums[p].part[...] = jnp.concatenate(
                [grads[:, m * 128 : (m + 1) * 128] for m in range(3)], axis=0
            ).reshape(2, 2, blocks, pair_piece, 128)

        state = {out_sum: 2}

        def advance(*chosen):
            for one in chosen or list(state):
                n = state.setdefault(one, 0)
                if n <= 7:
                    one.step(n)
                    state[one] = n + 1

        plan = ([out_sum], [pair_sums[0]], [pair_sums[0]]) if pairs == 3 else ([],) * pairs
        for p in range(pairs):
            pair_step(p)
            if plan[p]:
                advance(*plan[p])
            advance(pair_sums[p])
            if p == 1:
                chain(0)

        for j in range(blocks):
            r = pl.ds(j * span, span)
            dn_ref[j] = dot_nt(dqkv_ref[r, :], w_ref[...]).astype(bf16).reshape(2, hs, width)

        def n_sib(j):
            return remote(dn_ref.at[j, 1 - c], dsib_ref.at[j], nsend.at[j], nrecv.at[j], z, sib)

        def n_out(j):
            return remote(
                dsum_ref.at[j], dnt_ref.at[seq, c], ssend.at[j], srecv.at[seq, c], j, base + seq_core
            )

        def n_own():
            return pltpu.make_async_copy(dsum_ref.at[z], dnt_ref.at[seq, c], loc_sem.at[1])

        n_order = others[1:2] + others[0:1] + others[2:] + [z]
        for j in n_order:
            n_sib(j).start()
        advance(*pair_sums[1:2])
        for i, j in enumerate(n_order):
            n_sib(j).wait_recv()
            dsum_ref[j] = (dn_ref[j, c].astype(f32) + dsib_ref[j].astype(f32)).astype(bf16)
            if i < blocks - 1:
                n_out(j).start()
            else:

                @pl.when(seq_core == c)
                def _():
                    n_own().start()

                @pl.when(seq_core != c)
                def _():
                    n_out(j).start()

        @pl.when(jnp.logical_not(inner))
        def _():
            r_chain(1).start()

        advance(*pair_sums[1:])
        for t in plane:
            m_out(t).start()
        advance(*pair_sums[2:])
        advance(out_sum, *pair_sums[:1])
        for s in range(seqs):
            for k in range(2):
                from_self = (2 * c + s == z) & (c == k)

                @pl.when(jnp.logical_not(from_self))
                def _():
                    remote(
                        dsum_ref.at[0], dnt_ref.at[s, k], ssend.at[0], srecv.at[s, k], z, base
                    ).wait_recv()

                @pl.when(from_self)
                def _():
                    n_own().wait()

        gains = g1_ref[...].reshape(1, width)
        gain_sum = jnp.zeros((1, width), f32)
        shift_sum = jnp.zeros((1, width), f32)
        for s in range(seqs):
            for k in range(2):
                v = hid_ref[s, k].astype(f32)
                centered = v - jnp.mean(v, axis=-1, keepdims=True)
                inverse = lax.rsqrt(jnp.mean(centered * centered, axis=-1, keepdims=True) + epsilon)
                unit = centered * inverse
                dy = dnt_ref[s, k].astype(f32)
                gain_sum = gain_sum + jnp.sum(dy * unit, axis=0, keepdims=True)
                shift_sum = shift_sum + jnp.sum(dy, axis=0, keepdims=True)
                du = dy * gains
                dx = inverse * (
                    du
                    - jnp.mean(du, axis=-1, keepdims=True)
                    - unit * jnp.mean(du * unit, axis=-1, keepdims=True)
                )
                gh_ref[s, k] = dmid_ref[(2 * s + k) * hs : (2 * s + k + 1) * hs] + dx
        outs[0].start()

        sums_ref[0:1] = gain_sum
        sums_ref[1:2] = shift_sum

        def t_swap(n, te):
            return remote(sums_ref, sgot.at[n], tsend.at[n], trecv.at[n], z, te)

        partners = [sib] + mate
        for n, te in enumerate(partners):
            copy = t_swap(n, te)
            copy.start()
            if n in (1, 2):
                advance()
            if n == 1:
                chain(1)
            copy.wait()
            sums_ref[...] = sums_ref[...] + sgot[n]

        def t_z(zt):
            return remote(sums_ref, szgot.at[z], tzsend.at[zt], tzrecv.at[z], zt, e)

        for zt in others:
            t_z(zt).start()
        for t in plane:
            remote(made_ref.at[0], mg_ref.at[t], msend.at[t], mrecv.at[t], z, e).wait_recv()
        m_own.wait()
        scaled = valid * gates
        expert_out = dot(picks, mg_ref[...].reshape(slots, width))
        y_ref[...] = (mid_ref[...] + scaled * expert_out).astype(bf16)
        outs[1].start()

        for i, (buf, final) in enumerate(((zi, fi_ref), (zo, fo_ref))):
            r_load(i, (ei_ref, eo_ref)[i], pair, 1).wait()
            final[...] = buf[1].astype(f32)

            @pl.when(inner)
            def _():
                for src, part_at in (
                    ((gi_ref, go_ref)[i], 0), ((ei_ref, eo_ref)[i], across[0]), ((ei_ref, eo_ref)[i], across[1])
                ):
                    load = r_load(i, src, part_at, 1)
                    load.start()
                    load.wait()
                    final[...] = final[...] + buf[1].astype(f32)

            @pl.when(jnp.logical_not(inner))
            def _():
                r_load(i, (gi_ref, go_ref)[i], 0, 0).wait()
                final[...] = final[...] + buf[0].astype(f32)

        for _ in range(3):
            advance()
        assert state[out_sum] == 8
        outs[7].start()
        for zs in others:
            remote(sums_ref, szgot.at[zs], tzsend.at[zs], tzrecv.at[zs], z, e).wait_recv()
        for zt in others:
            t_z(zt).wait_send()
        szgot[z] = sums_ref[...]
        tot = szgot[0]
        for j in range(1, blocks):
            tot = tot + szgot[j]
        sums_ref[...] = tot

        advance()
        for i, (got, final) in enumerate(((ci, fi_ref), (co, fo_ref))):

            @pl.when(inner)
            def _():
                r_sum(i).wait_send()

            @pl.when(jnp.logical_not(inner))
            def _():
                r_sum(i).wait_recv()
                r_chain(i).wait_send()
                final[...] = final[...] + got[...].astype(f32)

            outs[2 + i].start()
        while min(state.values()) <= 7:
            advance()
        for out in outs[4:7]:
            out.start()

        for s in range(seqs):
            for k in range(2):

                @pl.when(jnp.logical_not((2 * c + s == z) & (c == k)))
                def _():
                    d_out(s, k).wait_send()

        for j in n_order[:-1]:
            n_out(j).wait_send()

        @pl.when(seq_core != c)
        def _():
            n_out(z).wait_send()

        for j in n_order:
            n_sib(j).wait_send()
        for t in plane:
            m_out(t).wait_send()
        for out in outs:
            out.wait()

    stage = blocks
    scratch = [
        pltpu.VMEM((blocks, span, half), bf16),
        pltpu.VMEM((total, 3 * half), bf16),
        pltpu.VMEM((128, total), bf16),
        pltpu.VMEM((total, 128), f32),
        pltpu.VMEM((total, 128), f32),
        pltpu.VMEM((blocks, 2, hs, width), bf16),
        pltpu.VMEM((blocks, hs, width), bf16),
        pltpu.VMEM((blocks, hs, width), bf16),
        pltpu.VMEM((seqs, 2, hs, width), bf16),
        pltpu.VMEM((2, width, part), bf16),
        pltpu.VMEM((2, part, width), bf16),
        pltpu.VMEM((width, part), bf16),
        pltpu.VMEM((part, width), bf16),
        pltpu.VMEM((width, half), bf16),
        pltpu.VMEM((1 + bits, small_rows, width), f32),
        pltpu.VMEM((blocks, small_rows, width), f32),
        pltpu.VMEM((seqs, 2, span, half), bf16),
        pltpu.VMEM((2, width, half), bf16),
        pltpu.VMEM((tokens, width), f32),
        pltpu.VMEM((columns, capacity, width), bf16),
        DMA((3,)),
        DMA((seqs, 2)),
        DMA((stage,)),
        DMA((2, 2)),
        DMA((2,)),
        DMA((2,)),
        DMA((stage,)),
        DMA((stage,)),
        DMA((stage,)),
        DMA((seqs, 2)),
        DMA,
        DMA,
        DMA((1 + bits,)),
        DMA((1 + bits,)),
        DMA((stage,)),
        DMA((stage,)),
        DMA((columns,)),
        DMA((columns,)),
        pltpu.VMEM((columns, capacity, width), bf16),
        pltpu.VMEM((tokens, width), f32),
        pltpu.VMEM((tokens, width), bf16),
        pltpu.VMEM((tokens, width), bf16),
        pltpu.VMEM((width, width), bf16),
        pltpu.VMEM((seqs, 2, span, half), bf16),
        pltpu.VMEM((total, 3 * half), bf16),
        pltpu.VMEM((half, total), f32),
        pltpu.VMEM((width, total), bf16),
        pltpu.VMEM((width, 3 * half), bf16),
        pltpu.VMEM((seqs, 2, hs, width), bf16),
        DMA((11,)),
        pltpu.VMEM((4, width, width), bf16),
        pltpu.VMEM((width, part), f32),
        pltpu.VMEM((part, width), f32),
        pltpu.VMEM((seqs, 2, hs, width), f32),
        pltpu.VMEM((tokens, width), bf16),
        DMA((8,)),
    ]
    scratch += PieceSum.scratch(blocks, out_piece, half, rest)
    for _ in range(pairs):
        scratch += PieceSum.scratch(blocks, pair_piece, 128, rest)
    grads, sums, f_inner, f_outer, g_hidden, output = pl.pallas_call(
        kernel,
        name="backward",
        out_shape=[
            jax.ShapeDtypeStruct((4, width, width), bf16),
            jax.ShapeDtypeStruct((small_rows, width), f32),
            jax.ShapeDtypeStruct((width, part), f32),
            jax.ShapeDtypeStruct((part, width), f32),
            jax.ShapeDtypeStruct((seqs, 2, hs, width), f32),
            jax.ShapeDtypeStruct((tokens, width), bf16),
        ],
        in_specs=[ANY] * 4 + [VMEM] * 2 + [ANY] * 3 + [VMEM] * 3 + [SMEM] + [ANY] * 2 + [VMEM] * 2 + [ANY] * 2 + [VMEM] * 2
        + [ANY] + [VMEM] + [ANY] * 4,
        out_specs=[ANY, VMEM] + [ANY] * 4,
        scratch_shapes=scratch,
        compiler_params=params(3),
    )(
        rows_t, weights, qkv, att_t, lse, length, attended, middle, flat, gate, slot, ids, lengths, cotangent,
        back, dots, counts, made, hidden.reshape(seqs, 2, hs, width), gain_one,
        gain_two, w_output, w_router, g_inner, g_outer, e_inner, e_outer,
    )
    return finish(grads, sums, f_inner, f_outer, g_hidden.reshape(tokens, width), output, experts_n)


def finish(grads, sums, g_inner, g_outer, g_hidden, output, experts_n):
    steps = 8
    width = grads.shape[2]
    tokens = output.shape[0]
    part = g_inner.shape[1]
    rows = width // steps

    def kernel(g_ref, s_ref, i_ref, o_ref, h_ref, y_ref, *outs):
        for m in range(4):
            outs[m][...] = g_ref[m].astype(f32)
        outs[4][...] = i_ref[...]
        outs[5][...] = o_ref[...]
        outs[6][...] = h_ref[...]
        outs[7][...] = y_ref[...]

        @pl.when(pl.program_id(0) == 0)
        def _():
            for m in range(4):
                outs[8 + m][...] = s_ref[m]
            outs[12][...] = s_ref[4 : 4 + experts_n]
            outs[13][...] = s_ref[4 + experts_n : 5 + experts_n, 0:1]

    def by_rows(shape):
        return pl.BlockSpec((shape[0] // steps,) + shape[1:], lambda i: (i,) + (0,) * (len(shape) - 1))

    def whole(shape):
        return pl.BlockSpec(shape, lambda i: (0,) * len(shape))

    split = [(width, width)] * 4 + [(width, part), (part, width), (tokens, width), (tokens, width)]
    kept = [(width,)] * 4 + [(experts_n, width), (1, 1)]
    return pl.pallas_call(
        kernel,
        name="finish",
        grid=(steps,),
        out_shape=[jax.ShapeDtypeStruct(a, bf16 if n == 7 else f32) for n, a in enumerate(split + kept)],
        in_specs=[pl.BlockSpec((4, rows, width), lambda i: (0, i, 0)), whole(sums.shape)]
        + [by_rows(a) for a in split[4:]],
        out_specs=[by_rows(a) for a in split] + [whole(a) for a in kept],
        compiler_params=pltpu.CompilerParams(dimension_semantics=("arbitrary",), vmem_limit_bytes=VMEM_BYTES),
    )(grads, sums, g_inner, g_outer, g_hidden, output)


def on_device(
    hidden_in,
    cotangent,
    query_weight,
    key_weight,
    value_weight,
    output_weight,
    gain_one,
    shift_one,
    gain_two,
    shift_two,
    w_router,
    w_inner,
    w_outer,
    expert_ids,
    seq_lengths,
):
    seqs, span, width = hidden_in.shape
    tokens = seqs * span
    blocks = lax.axis_size("blk")
    columns = lax.axis_size("ep") // 2
    experts_n = w_router.shape[1]
    capacity = max(2, 2 * tokens // experts_n)
    total = blocks * span
    half = width // 2
    assert seqs * 2 == blocks and experts_n == columns

    ids = expert_ids.reshape(seqs, span)
    lengths = seq_lengths
    router = jnp.transpose(w_router)
    cot = cotangent.reshape(tokens, width)
    (
        rows_t, w_qkv, qkv, att_t, lse, attended, middle, flat, gate, slot, to_rows, scales, cot_rows, length, counts,
        near_inner, sib_inner, sib_outer,
    ) = forward(
        hidden_in, cotangent, gain_one, shift_one, gain_two, shift_two, query_weight, key_weight, value_weight,
        output_weight, router, ids, lengths, w_inner[0], w_outer[0], blocks, columns, capacity, experts_n,
    )
    back, dots, made, counts, g_inner, g_outer, e_inner, e_outer = experts(
        to_rows, scales, cot_rows, counts, w_inner[0], w_outer[0], sib_inner, sib_outer, near_inner, blocks
    )
    results = backward(
        rows_t, w_qkv, qkv.reshape(total, 3 * half), att_t, lse, length, attended, middle, flat, gate,
        slot, ids, lengths, cot, back, dots, counts, made, hidden_in, gain_one, gain_two, output_weight, router,
        g_inner, g_outer, e_inner, e_outer, experts_n,
    )
    dense, (grad_inner, grad_outer, grad_hidden, output) = results[:4], results[4:8]
    gains, (grad_router, balance) = results[8:12], results[12:]
    return (
        output.reshape(seqs, span, width),
        grad_hidden.reshape(seqs, span, width),
        *dense,
        *gains,
        jnp.transpose(grad_router),
        grad_inner[None],
        grad_outer[None],
        balance[0, 0],
    )


def solution(mesh):
    tokens = P("ep", "blk", None)
    return jax.shard_map(
        on_device,
        mesh=mesh,
        in_specs=(tokens, tokens)
        + (P(),) * 9
        + (P("ep", None, "blk"), P("ep", "blk", None), P("ep", "blk", None, None, None), P("ep")),
        out_specs=(tokens, tokens) + (P(),) * 9 + (P("ep", None, "blk"), P("ep", "blk", None), P()),
        check_vma=False,
    )
```

```python
import functools

import jax
import jax.numpy as jnp
from jax import lax
from jax.experimental import pallas as pl
from jax.experimental.pallas import tpu as pltpu
from jax.sharding import PartitionSpec as P

HEAD = 64
MESH = pl.DeviceIdType.MESH
ANY = pl.BlockSpec(memory_space=pl.ANY)
VMEM = pl.BlockSpec(memory_space=pltpu.VMEM)
SMEM = pl.BlockSpec(memory_space=pltpu.SMEM)
DMA = pltpu.SemaphoreType.DMA
f32 = jnp.float32
bf16 = jnp.bfloat16

epsilon = 1e-05
balance_weight = 6.0
masked_fill = -1e30
VMEM_BYTES = 57 * 1024 * 1024


def dot(a, b):
    return lax.dot_general(a, b, (((1,), (0,)), ((), ())), preferred_element_type=f32)


def dot_nt(a, b):
    return lax.dot_general(a, b, (((1,), (1,)), ((), ())), preferred_element_type=f32)


def dot_tn(a, b):
    return lax.dot_general(a, b, (((0,), (0,)), ((), ())), preferred_element_type=f32)


def place():
    z = lax.axis_index("blk")
    e = lax.axis_index("ep")
    c = lax.rem(e, 2)
    return z, e, c, e - c


def remote(src, dst, send_sem, recv_sem, z, e):
    return pltpu.make_async_remote_copy(
        src, dst, send_sem, recv_sem, device_id=(z, e), device_id_type=MESH
    )


def greet(partners):
    barrier = pltpu.get_barrier_semaphore()
    for z, e in partners:
        pl.semaphore_signal(barrier, inc=1, device_id=(z, e), device_id_type=MESH)


def await_greetings(partners):
    pl.semaphore_wait(pltpu.get_barrier_semaphore(), len(partners))


def column_partners(blocks, z, c, base):
    found = [(z, base + 1 - c)]
    for step in range(1, blocks):
        for k in range(2):
            found.append((lax.rem(z + step, blocks), base + k))
    return found


def params(collective_id):
    return pltpu.CompilerParams(
        collective_id=collective_id, has_side_effects=True, vmem_limit_bytes=VMEM_BYTES
    )


def lane_of(shape, dimension):
    return lax.broadcasted_iota(jnp.int32, shape, dimension)


def one_hot(ids_ref, seqs, span):
    columns = [
        jnp.transpose(jnp.broadcast_to(ids_ref[s : s + 1], (128, span))) for s in range(seqs)
    ]
    ids = jnp.concatenate(columns, axis=0)
    return (lane_of(ids.shape, 1) == ids).astype(f32)


def valid_rows(len_ref, z, seqs, span):
    place_in = z * span + lane_of((span, 1), 0)
    return jnp.concatenate([(place_in < len_ref[s]).astype(f32) for s in range(seqs)], axis=0)


def key_heads(k_all, key_bias):
    lane = lane_of((1, 128), 1)
    found = []
    for h in range(2):
        inside = (lane // HEAD) == h
        spare = lane == (1 - h) * HEAD
        found.append(
            jnp.where(inside, k_all.astype(f32), jnp.where(spare, key_bias, 0.0)).astype(bf16)
        )
    return found


def forward(
    hidden, cotangent, gain_one, shift_one, gain_two, shift_two, w_query, w_key, w_value, w_output, w_router,
    ids, lengths, w_inner, w_outer, blocks, columns, capacity, experts_n,
):
    seqs, span, width = hidden.shape
    hs = span // 2
    half = width // 2
    pairs = half // 128
    total = blocks * span
    tokens = seqs * span
    slots = experts_n * capacity
    part = w_inner.shape[1]
    cap_lanes = max(128, capacity)

    def kernel(*refs):
        (
            hid_ref, cot_ref, g1_ref, s1_ref, g2_ref, s2_ref, wq_ref, wk_ref, wv_ref, wo_ref, wr_ref,
            ids_ref, len_in, wi_ref, we_ref,
        ) = refs[:15]
        (
            xt_out, w_out, qkv_out, attt_out, lse_ref, t_out, mid_out, flat_out, gate_ref, slot_ref,
            rows_ref, sc_ref, cote_ref, len_ref, cnt_ref, li_ref, lo_ref, bi_ref, bo_ref,
        ) = refs[15:34]
        (
            x_ref, nb_ref, kh_ref, vt_ref, att_ref, cots_ref, lens_ref, lgot_ref, cown_ref, cgot_ref,
            wload, nloc, nsend, nrecv, fsend, frecv, aloc, asend, arecv, closs, csend, crecv,
            lsend, lrecv, ksend, krecv, hsend, hrecv, bsend, brecv,
            xt_ref, w_ref, qkv_ref, attt_ref, out_sem, t_ref, mid_ref, flat_ref,
        ) = refs[34:]
        z, e, c, base = place()
        col = e // 2
        sib = base + 1 - c
        seq_core, seq = z // 2, lax.rem(z, 2)
        others = [lax.rem(z + step, blocks) for step in range(1, blocks)]
        plane = [lax.rem(col + step, columns) for step in range(1, columns)]
        column = column_partners(blocks, z, c, base)
        greet(column + [(z, 2 * t + c) for t in plane])

        def load_w(m, ref):
            return pltpu.make_async_copy(
                ref.at[:, pl.ds(pl.multiple_of(c * half, half), half)],
                w_ref.at[:, pl.ds(m * half, half)],
                wload.at[m],
            )

        for m, ref in enumerate((wq_ref, wk_ref, wv_ref)):
            load_w(m, ref).start()
        gain_row, shift_row = g1_ref[...].reshape(1, width), s1_ref[...].reshape(1, width)
        for s in range(seqs):
            for k in range(2):
                v = hid_ref[s, k].astype(f32)
                centered = v - jnp.mean(v, axis=-1, keepdims=True)
                inverse = lax.rsqrt(jnp.mean(centered * centered, axis=-1, keepdims=True) + epsilon)
                nb_ref[s, k] = (centered * inverse * gain_row + shift_row).astype(bf16)
        await_greetings(column + plane)

        def n_out(s, k):
            return remote(
                nb_ref.at[s, k], x_ref.at[z, k], nsend.at[s, k], nrecv.at[z], 2 * c + s, base + k
            )

        def n_own(s, k):
            return pltpu.make_async_copy(nb_ref.at[s, k], x_ref.at[z, k], nloc)

        for k, s in ((0, 0), (0, 1), (1, 1), (1, 0)):
            if True:
                to_self = (2 * c + s == z) & (c == k)

                @pl.when(to_self)
                def _():
                    n_own(s, k).start()

                @pl.when(jnp.logical_not(to_self))
                def _():
                    n_out(s, k).start()

        for s in range(seqs):
            lens_ref[s] = jnp.full((8, 128), len_in[s], jnp.int32)
        to_lens = remote(lens_ref, lgot_ref, lsend, lrecv, z, sib)
        to_lens.start()
        lane = lane_of((tokens, 128), 1)
        onehot = one_hot(ids_ref, seqs, span)
        valid = valid_rows(len_in, z, seqs, span)
        cown_ref[...] = jnp.broadcast_to(jnp.sum(onehot * valid, axis=0, keepdims=True), (8, 128))

        def k_out(n, to_z, to_e):
            return remote(cown_ref, cgot_ref.at[z, c], ksend.at[n], krecv.at[z, c], to_z, to_e)

        for n, (to_z, to_e) in enumerate(column):
            k_out(n, to_z, to_e).start()
        earlier = (lane_of((tokens, tokens), 0) > lane_of((tokens, tokens), 1)).astype(f32).astype(bf16)
        rank = dot(earlier, onehot.astype(bf16))
        slot = jnp.sum(onehot * (rank + (lane * capacity).astype(f32)), axis=1, keepdims=True)
        slot_ref[...] = slot
        slot_row = jnp.transpose(jnp.broadcast_to(slot, (tokens, 128)))[0:1]
        to_slots = (lane_of((slots, tokens), 0).astype(f32) == slot_row).astype(f32).astype(bf16)
        cots_ref[...] = (
            dot(to_slots, cot_ref[...]).astype(bf16).reshape(columns, capacity, width)
        )

        def c_out(t):
            return remote(cots_ref.at[t], cote_ref.at[col], csend.at[t], crecv.at[col], z, 2 * t + c)

        c_own = pltpu.make_async_copy(cots_ref.at[col], cote_ref.at[col], closs)
        c_own.start()
        for t in plane:
            c_out(t).start()
        for m, ref in enumerate((wq_ref, wk_ref, wv_ref)):
            load_w(m, ref).wait()

        def n_sib(zs):
            return remote(x_ref.at[zs, c], x_ref.at[zs, c], fsend.at[zs], frecv.at[zs], z, sib)

        for zs in [z] + others:
            if zs is z:

                @pl.when(c == seq_core)
                def _():
                    n_own(0, 0).wait()

                @pl.when(c != seq_core)
                def _():
                    remote(nb_ref.at[0, 0], x_ref.at[z, c], nsend.at[0, 0], nrecv.at[z], z, base).wait_recv()
            else:
                remote(nb_ref.at[0, 0], x_ref.at[zs, c], nsend.at[0, 0], nrecv.at[zs], z, base).wait_recv()
            n_sib(zs).start()

        def h_out(i, step):
            side = 0 if step == 1 else 1
            src, dst = ((wi_ref, li_ref), (we_ref, lo_ref))[i]
            return remote(src, dst.at[side], hsend.at[i, side], hrecv.at[i, side], z + step, e)

        def h_start(i):
            @pl.when(z < blocks - 1)
            def _():
                h_out(i, 1).start()

            @pl.when(z > 0)
            def _():
                h_out(i, -1).start()

        def b_out(i):
            src, dst = ((wi_ref, bi_ref), (we_ref, bo_ref))[i]
            return remote(src, dst, bsend.at[i], brecv.at[i], z, sib)

        h_start(0)
        for zs in [z] + others:
            remote(
                x_ref.at[zs, 1 - c], x_ref.at[zs, 1 - c], fsend.at[zs], frecv.at[zs], z, sib
            ).wait_recv()
            x_z = x_ref[zs].reshape(span, width)
            qkv_ref[zs] = dot(x_z, w_ref[...]).astype(bf16)
            xt_ref[:, pl.ds(pl.multiple_of(zs * span, span), span)] = jnp.transpose(x_z)
        for i in range(2):
            b_out(i).start()
        to_lens.wait()
        seq_len = jnp.where(c == seq_core, lens_ref[seq], lgot_ref[seq])
        len_ref[...] = seq_len
        key_bias = jnp.where(lane_of((total, 1), 0) < seq_len[0:1, 0:1], 0.0, masked_fill)
        for p in range(pairs):
            k_all = jnp.concatenate(
                [qkv_ref[j, :, half + p * 128 : half + (p + 1) * 128] for j in range(blocks)], axis=0
            )
            for h, k_h in enumerate(key_heads(k_all, key_bias)):
                kh_ref[2 * p + h] = k_h
            for j in range(blocks):
                vt_ref[p * 128 : (p + 1) * 128, j * span : (j + 1) * span] = jnp.transpose(
                    qkv_ref[j, :, 2 * half + p * 128 : 2 * half + (p + 1) * 128]
                )
        outs = [
            pltpu.make_async_copy(src, dst, out_sem.at[n])
            for n, (src, dst) in enumerate(
                (
                    (xt_ref, xt_out), (w_ref, w_out), (qkv_ref, qkv_out), (attt_ref, attt_out),
                    (t_ref, t_out), (mid_ref, mid_out), (flat_ref, flat_out),
                )
            )
        ]
        for out in outs[:3]:
            out.start()
        later = lane_of((span, span), 0) > lane_of((span, span), 1)
        lane_row = lane_of((1, 128), 1)

        def a_out(j):
            return remote(
                att_ref.at[j], t_ref.at[seq, c], asend.at[j], arecv.at[seq, c], j, base + seq_core
            )

        def a_own(j):
            return pltpu.make_async_copy(att_ref.at[j], t_ref.at[seq, c], aloc)

        for j in [0] + list(range(blocks - 1, 0, -1)):
            n = (j + 1) * span

            def pair_step(p, _):
                first = pl.multiple_of(p * 128, 128)
                q = qkv_ref[j, :, pl.ds(first, 128)].astype(f32) * (HEAD**-0.5)
                out_t = []
                for h in range(2):
                    inside = (lane_row // HEAD) == h
                    spare = lane_row == (1 - h) * HEAD
                    q_h = jnp.where(inside, q, jnp.where(spare, 1.0, 0.0)).astype(bf16)
                    s = dot_nt(kh_ref[2 * p + h, :n], q_h)
                    last = jnp.where(later, masked_fill, s[n - span :])
                    s = last if j == 0 else jnp.concatenate([s[: n - span], last], axis=0)
                    top = jnp.max(s, axis=0, keepdims=True)
                    w = jnp.exp(s - top)
                    total_w = jnp.sum(w, axis=0, keepdims=True)
                    o_t = dot(vt_ref[pl.ds(pl.multiple_of(first + h * HEAD, HEAD), HEAD), :n], w.astype(bf16))
                    out_t.append(o_t / total_w)
                    lse_ref[pl.ds(2 * p + h, 1), pl.ds(j * span, span)] = top + jnp.log(total_w)
                o = jnp.concatenate(out_t, axis=0)
                attt_ref[pl.ds(first, 128), pl.ds(j * span, span)] = o
                att_ref[j, :, pl.ds(first, 128)] = jnp.transpose(o).astype(bf16)
                return 0

            lax.fori_loop(0, pairs, pair_step, 0)
            to_self = (z == j) & (c == seq_core)

            @pl.when(to_self)
            def _():
                a_own(j).start()

            @pl.when(jnp.logical_not(to_self))
            def _():
                a_out(j).start()

        outs[3].start()
        h_start(1)
        for s in range(seqs):
            for k in range(2):
                from_self = (2 * c + s == z) & (c == k)

                @pl.when(from_self)
                def _():
                    a_own(0).wait()

                @pl.when(jnp.logical_not(from_self))
                def _():
                    remote(att_ref.at[0], t_ref.at[s, k], asend.at[0], arecv.at[s, k], z, base).wait_recv()

        for s in range(seqs):
            r = pl.ds(s * span, span)
            branch = dot(t_ref[s, 0], wo_ref[0:half]) + dot(t_ref[s, 1], wo_ref[half:])
            v = hid_ref[s].reshape(span, width).astype(f32) + branch
            mid_ref[r, :] = v
            centered = v - jnp.mean(v, axis=-1, keepdims=True)
            inverse = lax.rsqrt(jnp.mean(centered * centered, axis=-1, keepdims=True) + epsilon)
            flat_ref[r, :] = (
                centered * inverse * g2_ref[...].reshape(1, width) + s2_ref[...].reshape(1, width)
            ).astype(bf16)
        for out in outs[4:]:
            out.start()
        logits = dot_nt(flat_ref[...], wr_ref[...])
        gate = jax.nn.sigmoid(
            jnp.sum(logits * onehot[:, :experts_n], axis=1, keepdims=True)
        )
        gate_ref[...] = gate
        rows_ref[...] = (
            dot(to_slots, flat_ref[...]).astype(bf16).reshape(columns, capacity, width)
        )
        from_slots = lane_of((tokens, slots), 1).astype(f32) == slot_ref[...]
        scales = jnp.sum(jnp.where(from_slots, valid * gate, 0.0), axis=0, keepdims=True)
        if cap_lanes != capacity:
            sc_ref[...] = jnp.zeros_like(sc_ref)
        for t in range(columns):
            sc_ref[t, :, 0:capacity] = jnp.broadcast_to(
                scales[:, t * capacity : (t + 1) * capacity], (8, capacity)
            )

        for out in outs:
            out.wait()
        for n, (to_z, to_e) in enumerate(column):
            remote(cown_ref, cgot_ref.at[to_z, lax.rem(to_e, 2)], ksend.at[n], krecv.at[to_z, lax.rem(to_e, 2)], z, sib).wait_recv()
            k_out(n, to_z, to_e).wait_send()
        cgot_ref[z, c] = cown_ref[...]
        tot = jnp.zeros((8, 128), f32)
        for zs in range(blocks):
            for k in range(2):
                tot = tot + cgot_ref[zs, k]
        cnt_ref[...] = tot
        c_own.wait()
        for t in plane:
            c_out(t).wait_send()
            remote(cots_ref.at[t], cote_ref.at[t], csend.at[t], crecv.at[t], z, e).wait_recv()
        for s in range(seqs):
            for k in range(2):

                @pl.when(jnp.logical_not((2 * c + s == z) & (c == k)))
                def _():
                    n_out(s, k).wait_send()

        for zs in [z] + others:
            n_sib(zs).wait_send()
        for j in range(blocks):

            @pl.when(jnp.logical_not((z == j) & (c == seq_core)))
            def _():
                a_out(j).wait_send()

        for i in range(2):
            b_out(i).wait()

        for i in range(2):
            src, dst = ((wi_ref, li_ref), (we_ref, lo_ref))[i]

            @pl.when(z < blocks - 1)
            def _():
                h_out(i, 1).wait_send()
                remote(src, dst.at[1], hsend.at[i, 1], hrecv.at[i, 1], z, e).wait_recv()

            @pl.when(z > 0)
            def _():
                h_out(i, -1).wait_send()
                remote(src, dst.at[0], hsend.at[i, 0], hrecv.at[i, 0], z, e).wait_recv()

    out_shapes = [
        ((width, total), bf16),
        ((width, 3 * half), bf16),
        ((blocks, span, 3 * half), bf16),
        ((half, total), f32),
        ((2 * pairs, total), f32),
        ((seqs, 2, span, half), bf16),
        ((tokens, width), f32),
        ((tokens, width), bf16),
        ((tokens, 1), f32),
        ((tokens, 1), f32),
        ((columns, capacity, width), bf16),
        ((columns, 8, cap_lanes), f32),
        ((columns, capacity, width), bf16),
        ((8, 128), jnp.int32),
        ((8, 128), f32),
        ((2, width, part), bf16),
        ((2, part, width), bf16),
        ((width, part), bf16),
        ((part, width), bf16),
    ]
    return pl.pallas_call(
        kernel,
        name="forward",
        out_shape=[jax.ShapeDtypeStruct(a, b) for a, b in out_shapes],
        in_specs=[VMEM] * 6 + [ANY] * 3 + [VMEM] * 3 + [SMEM] + [ANY] * 2,
        out_specs=[ANY] * 4 + [VMEM] + [ANY] * 3 + [VMEM] * 4 + [ANY] + [VMEM] * 2 + [ANY] * 4,
        scratch_shapes=[
            pltpu.VMEM((blocks, 2, hs, width), bf16),
            pltpu.VMEM((seqs, 2, hs, width), bf16),
            pltpu.VMEM((2 * pairs, total, 128), bf16),
            pltpu.VMEM((half, total), bf16),
            pltpu.VMEM((blocks, span, half), bf16),
            pltpu.VMEM((columns, capacity, width), bf16),
            pltpu.VMEM((seqs, 8, 128), jnp.int32),
            pltpu.VMEM((seqs, 8, 128), jnp.int32),
            pltpu.VMEM((8, 128), f32),
            pltpu.VMEM((blocks, 2, 8, 128), f32),
            DMA((3,)),
            DMA,
            DMA((seqs, 2)),
            DMA((blocks,)),
            DMA((blocks,)),
            DMA((blocks,)),
            DMA,
            DMA((blocks,)),
            DMA((seqs, 2)),
            DMA,
            DMA((columns,)),
            DMA((columns,)),
            DMA,
            DMA,
            DMA((2 * blocks - 1,)),
            DMA((blocks, 2)),
            DMA((2, 2)),
            DMA((2, 2)),
            DMA((2,)),
            DMA((2,)),
            pltpu.VMEM((width, total), bf16),
            pltpu.VMEM((width, 3 * half), bf16),
            pltpu.VMEM((blocks, span, 3 * half), bf16),
            pltpu.VMEM((half, total), f32),
            DMA((7,)),
            pltpu.VMEM((seqs, 2, span, half), bf16),
            pltpu.VMEM((tokens, width), f32),
            pltpu.VMEM((tokens, width), bf16),
        ],
        compiler_params=params(1),
    )(
        hidden.reshape(seqs, 2, hs, width), cotangent.reshape(tokens, width),
        gain_one, shift_one, gain_two, shift_two,
        w_query, w_key, w_value, w_output, w_router, ids, lengths, w_inner, w_outer,
    )


def slice_order(z):
    near = z + 1 - 2 * lax.rem(z, 2)
    across = jnp.where(z < 2, 2, 1)
    inner = (z > 0) & (z < 3)
    return [jnp.where(inner, across, near), jnp.where(inner, near, across), z, jnp.where(z < 2, 3, 0)]


def experts(
    rows, scales, cot, counts, w_inner, w_outer, sib_inner, sib_outer, near_inner, near_outer, blocks
):
    columns, capacity, width = rows.shape
    cap_lanes = scales.shape[2]
    total = columns * capacity
    part = w_inner.shape[1]
    block = 256
    count = total // block
    per = block // capacity
    assert blocks == 4 and columns == count * per

    def kernel(*refs):
        rows_ref, sc_ref, cot_ref, cnt_ref, wi_ref, we_ref, bi_ref, bo_ref, li_ref, lo_ref = refs[:10]
        back_ref, dots_ref, made_out, tot_ref, gi_out, go_out, ei_ref, eo_ref = refs[10:18]
        (
            x_ref, xt_ref, d_ref, scg_ref, cntg_ref, in_ref, out_ref, oacc, dacc, act_ref, dpre_ref,
            dr_ref, dots_own, sgi_ref, sgo_ref, ggi_ref, ggo_ref,
            xloc, xsend, xrecv, scsend, screcv, ksend, krecv, wloc, wsend, wrecv, vsend, vrecv,
            bloc, dsend, drecv, gsend, grecv, ssend, srecv, gi_ref, go_ref, keep_sem, made_ref, made_sem,
        ) = refs[18:]
        z, e, c, base = place()
        col = e // 2
        sib = base + 1 - c
        inner = (z > 0) & (z < blocks - 1)
        end = jnp.logical_not(inner)
        plane = [lax.rem(col + step, columns) for step in range(1, columns)]
        partners = column_partners(blocks, z, c, base) + [(z, 2 * t + c) for t in plane]
        greet(partners)

        def x_out(t):
            return remote(rows_ref.at[t], x_ref.at[col], xsend.at[t], xrecv.at[col], z, 2 * t + c)

        def sc_out(t):
            return remote(sc_ref.at[t], scg_ref.at[col], scsend.at[t], screcv.at[col], z, 2 * t + c)

        def cnt_out(t):
            return remote(cnt_ref, cntg_ref.at[col], ksend.at[t], krecv.at[col], z, 2 * t + c)

        x_own = pltpu.make_async_copy(rows_ref.at[col], x_ref.at[col], xloc)
        x_own.start()
        await_greetings(partners)
        for t in plane:
            sc_out(t).start()
            x_out(t).start()
            cnt_out(t).start()
        scg_ref[col] = sc_ref[col]
        cntg_ref[col] = cnt_ref[...]

        hop_two = lax.rem(z + 2, blocks)
        pair = z + 1 - 2 * lax.rem(z, 2)

        lo_half, hi_half = pl.ds(0, part), pl.ds(part, part)

        def views(s, which):
            return (in_ref.at[s, :, which], out_ref.at[s, which])

        sources = ((wi_ref, we_ref), (bi_ref, bo_ref))

        def w_own(i, k):
            return pltpu.make_async_copy(
                sources[k][i], views(z, (lo_half, hi_half)[k])[i], wloc.at[i, k]
            )

        def beside(side):
            return z - 1 if side == 0 else z + 1

        nears = (li_ref, lo_ref)

        def w_near(i, side):
            return pltpu.make_async_copy(nears[i].at[side], views(beside(side), lo_half)[i], wloc.at[2 + i, side])

        def w_near_sib(i, side):
            s = beside(side)
            return remote(nears[i].at[side], views(s, hi_half)[i], vsend.at[i, s], vrecv.at[i, s], z, sib)

        def w_pass(i, side):
            s = beside(side)
            return remote(
                nears[i].at[side], views(s, lo_half)[i], wsend.at[2 + i, side], wrecv.at[i, s], beside(1 - side), e
            )

        def w_got(i, s):
            return remote(views(s, lo_half)[i], views(s, lo_half)[i], wsend.at[0, 0], wrecv.at[i, s], z, e)

        def w_sib(i, s):
            return remote(views(s, lo_half)[i], views(s, hi_half)[i], vsend.at[i, s], vrecv.at[i, s], z, sib)

        def w_sib_got(i, s):
            return remote(views(s, lo_half)[i], views(s, hi_half)[i], vsend.at[i, z], vrecv.at[i, s], z, sib)

        def w_last(i):
            s = hop_two
            to = jnp.where(z == 1, 0, blocks - 1)
            return remote(views(s, lo_half)[i], views(s, lo_half)[i], wsend.at[4 + i, 0], wrecv.at[i, s], to, e)

        def has(side):
            return z > 0 if side == 0 else z < blocks - 1

        for i in range(2):
            for side in range(2):

                @pl.when(inner)
                def _():
                    w_pass(i, side).start()

        for i in range(2):
            for side in range(2):

                @pl.when(has(side))
                def _():
                    w_near(i, side).start()
                    w_near_sib(i, side).start()

        for i in range(2):
            for k in range(2):
                w_own(i, k).start()

        order = slice_order(z)
        far = order[3]
        oacc[...] = jnp.zeros_like(oacc)
        dacc[...] = jnp.zeros_like(dacc)
        first_block = col // per

        def at_block(b):
            return pl.ds(pl.multiple_of(b * per, per), per)

        def row_step(s, b, fresh):
            x_b = x_ref[at_block(b)].reshape(block, width)
            r = pl.ds(pl.multiple_of(b * block, block), block)
            if fresh:
                row = jnp.concatenate(
                    [scg_ref[b * per + i, :, 0:capacity] for i in range(per)], axis=1
                )
                column = jnp.transpose(row)[:, 0:1]
                cots = cot_ref[at_block(b)].reshape(block, width).astype(f32)
                d_ref[r, :] = (column * cots).astype(bf16)
            pre = dot(x_b, in_ref[s])
            cdf = 0.5 * (1.0 + lax.erf(pre * (0.5**0.5)))
            act = (pre * cdf).astype(bf16)
            slope = cdf + pre * (jnp.exp(-0.5 * pre * pre) * ((2 * jnp.pi) ** -0.5))
            d_act = dot_nt(d_ref[r, :], out_ref[s])
            d_pre = (d_act * slope).astype(bf16)
            act_ref[r, :] = act
            dpre_ref[r, :] = d_pre
            oacc[r, :] += dot(act, out_ref[s])
            dacc[r, :] += dot_nt(d_pre, in_ref[s])

        def grads(s):
            g_inner = dot(xt_ref[...], dpre_ref[...])
            gi_ref[s] = g_inner[:, :part].astype(bf16)
            sgi_ref[s] = g_inner[:, part:].astype(bf16)
            g_outer = dot_tn(act_ref[...], d_ref[...])
            go_ref[s] = g_outer[:part].astype(bf16)
            sgo_ref[s] = g_outer[part:].astype(bf16)
            for i in range(2):
                g_sib(i, s).start()

        def g_keep(i, n):
            return pltpu.make_async_copy(
                (gi_ref, go_ref)[i].at[order[2 + n]], (gi_out, go_out)[i].at[n], keep_sem.at[i, n]
            )

        def g_sib(i, s):
            src, dst = ((sgi_ref, ggi_ref), (sgo_ref, ggo_ref))[i]
            return remote(src.at[s], dst.at[s], gsend.at[i, s], grecv.at[i, s], z, sib)

        def join(s):
            for i, (total_ref, got_ref) in enumerate(((gi_ref, ggi_ref), (go_ref, ggo_ref))):
                g_sib(i, s).wait_recv()
                total_ref[s] = (total_ref[s].astype(f32) + got_ref[s].astype(f32)).astype(bf16)

        def s_out(i, s):
            src, dst = ((gi_ref, ei_ref), (go_ref, eo_ref))[i]
            return remote(src.at[s], dst.at[z], ssend.at[i, s], srecv.at[i, z], s, e)

        def block_at(m):
            return lax.rem(first_block + count - m, count)

        for i in range(2):
            for side in range(2):

                @pl.when(has(side))
                def _():
                    w_near(i, side).wait()
                    w_sib_got(i, beside(side)).wait_recv()

        for m in range(count):
            b = block_at(m)
            for i in range(per):
                t = b * per + i

                @pl.when(t == col)
                def _():
                    x_own.wait()

                @pl.when(t != col)
                def _():
                    remote(sc_ref.at[0], scg_ref.at[t], scsend.at[t], screcv.at[t], z, e).wait_recv()
                    remote(rows_ref.at[0], x_ref.at[t], xsend.at[t], xrecv.at[t], z, e).wait_recv()

            row_step(order[0], b, True)
        def hand_on(i):
            w_got(i, hop_two).wait_recv()
            w_sib(i, hop_two).start()

            @pl.when(inner)
            def _():
                w_last(i).start()

        hand_on(0)
        xt_ref[...] = jnp.transpose(x_ref[...].reshape(total, width))
        grads(order[0])

        @pl.when(end)
        def _():
            hand_on(1)
            for i in range(2):
                w_sib_got(i, hop_two).wait_recv()

        def loop(s, start):
            def body(b, _):
                row_step(s, b, False)
                return 0

            lax.fori_loop(start, count, body, 0)

        row_step(order[1], 0, False)
        join(order[0])
        for i in range(2):
            s_out(i, order[0]).start()
        loop(order[1], 1)

        @pl.when(inner)
        def _():
            hand_on(1)

        grads(order[1])
        for i in range(2):
            for k in range(2):
                w_own(i, k).wait()
        row_step(order[2], 0, False)
        join(order[1])
        for i in range(2):
            s_out(i, order[1]).start()
        loop(order[2], 1)

        @pl.when(inner)
        def _():
            for i in range(2):
                w_sib_got(i, hop_two).wait_recv()

        @pl.when(end)
        def _():
            for i in range(2):
                w_got(i, far).wait_recv()
                w_sib(i, far).start()

        grads(order[2])

        @pl.when(end)
        def _():
            for i in range(2):
                w_sib_got(i, far).wait_recv()

        def d_out(t):
            return remote(dr_ref.at[t], back_ref.at[col], dsend.at[0, t], drecv.at[0, col], z, 2 * t + c)

        def dots_out(t):
            return remote(dots_own.at[t], dots_ref.at[col], dsend.at[1, t], drecv.at[1, col], z, 2 * t + c)

        def made_copy(m):
            at = at_block(block_at(m))
            return pltpu.make_async_copy(made_ref.at[at], made_out.at[at], made_sem.at[m])

        b_own = pltpu.make_async_copy(dr_ref.at[col], back_ref.at[col], bloc)
        for m in list(range(1, count)) + [0]:
            b = block_at(m)
            row_step(order[3], b, False)
            if m == 1:
                join(order[2])
                for i in range(2):
                    g_keep(i, 0).start()
            r = pl.ds(pl.multiple_of(b * block, block), block)
            made = oacc[r, :].astype(bf16)
            made_ref[at_block(b)] = made.reshape(per, capacity, width)
            made_copy(m).start()
            dr_ref[at_block(b)] = dacc[r, :].astype(bf16).reshape(per, capacity, width)
            cots = cot_ref[at_block(b)].reshape(block, width).astype(f32)
            sums = jnp.sum(cots * made.astype(f32), axis=1, keepdims=True)
            row = jnp.transpose(jnp.broadcast_to(sums, (block, 128)))[0:8]
            for i in range(per):
                t = b * per + i
                if cap_lanes != capacity:
                    dots_own[t] = jnp.zeros((8, cap_lanes), f32)
                dots_own[t, :, 0:capacity] = row[:, i * capacity : (i + 1) * capacity]

                @pl.when(t == col)
                def _():
                    b_own.start()
                    dots_ref[t] = dots_own[t]

                @pl.when(t != col)
                def _():
                    d_out(t).start()
                    dots_out(t).start()

        grads(order[3])
        join(order[3])
        for i in range(2):
            g_keep(i, 1).start()

        for t in plane:
            x_out(t).wait_send()
            sc_out(t).wait_send()
            cnt_out(t).wait_send()
            remote(cnt_ref, cntg_ref.at[t], ksend.at[t], krecv.at[t], z, e).wait_recv()
        tot = cntg_ref[0]
        for t in range(1, columns):
            tot = tot + cntg_ref[t]
        tot_ref[...] = tot
        for i in range(2):
            for side in range(2):

                @pl.when(inner)
                def _():
                    w_pass(i, side).wait_send()

            w_sib(i, hop_two).wait_send()

            @pl.when(end)
            def _():
                w_sib(i, far).wait_send()

            for n in range(blocks):
                g_sib(i, n).wait_send()
            for n in range(2):
                g_keep(i, n).wait()
            s_out(i, order[0]).wait_send()
            s_out(i, order[1]).wait_send()
            got = (ei_ref, eo_ref)[i]

            def arrived(zs):
                return remote(got.at[0], got.at[zs], ssend.at[i, 0], srecv.at[i, zs], z, e)

            arrived(pair).wait_recv()

            @pl.when(inner)
            def _():
                w_last(i).wait_send()
                for k in range(2):
                    arrived(lax.rem(2 * (z // 2) + 2 + k, blocks)).wait_recv()

        for i in range(2):
            for side in range(2):

                @pl.when(has(side))
                def _():
                    w_near_sib(i, side).wait_send()

        for m in range(count):
            made_copy(m).wait()
        b_own.wait()
        for t in plane:
            d_out(t).wait_send()
            dots_out(t).wait_send()
            remote(dr_ref.at[0], back_ref.at[t], dsend.at[0, t], drecv.at[0, t], z, e).wait_recv()
            remote(dots_own.at[0], dots_ref.at[t], dsend.at[1, t], drecv.at[1, t], z, e).wait_recv()

    out_shapes = [
        ((columns, capacity, width), bf16),
        ((columns, 8, cap_lanes), f32),
        ((columns, capacity, width), bf16),
        ((8, 128), f32),
        ((2, width, part), bf16),
        ((2, part, width), bf16),
        ((blocks, width, part), bf16),
        ((blocks, part, width), bf16),
    ]
    return pl.pallas_call(
        kernel,
        name="experts",
        out_shape=[jax.ShapeDtypeStruct(a, b) for a, b in out_shapes],
        in_specs=[VMEM] * 4 + [ANY] * 6,
        out_specs=[ANY, VMEM, ANY, VMEM] + [ANY] * 4,
        scratch_shapes=[
            pltpu.VMEM((columns, capacity, width), bf16),
            pltpu.VMEM((width, total), bf16),
            pltpu.VMEM((total, width), bf16),
            pltpu.VMEM((columns, 8, cap_lanes), f32),
            pltpu.VMEM((columns, 8, 128), f32),
            pltpu.VMEM((blocks, width, 2 * part), bf16),
            pltpu.VMEM((blocks, 2 * part, width), bf16),
            pltpu.VMEM((total, width), f32),
            pltpu.VMEM((total, width), f32),
            pltpu.VMEM((total, 2 * part), bf16),
            pltpu.VMEM((total, 2 * part), bf16),
            pltpu.VMEM((columns, capacity, width), bf16),
            pltpu.VMEM((columns, 8, cap_lanes), f32),
            pltpu.VMEM((blocks, width, part), bf16),
            pltpu.VMEM((blocks, part, width), bf16),
            pltpu.VMEM((blocks, width, part), bf16),
            pltpu.VMEM((blocks, part, width), bf16),
            DMA,
            DMA((columns,)),
            DMA((columns,)),
            DMA((columns,)),
            DMA((columns,)),
            DMA((columns,)),
            DMA((columns,)),
            DMA((4, 2)),
            DMA((6, 2)),
            DMA((2, blocks)),
            DMA((2, blocks)),
            DMA((2, blocks)),
            DMA,
            DMA((2, columns)),
            DMA((2, columns)),
            DMA((2, blocks)),
            DMA((2, blocks)),
            DMA((2, blocks)),
            DMA((2, blocks)),
            pltpu.VMEM((blocks, width, part), bf16),
            pltpu.VMEM((blocks, part, width), bf16),
            DMA((2, 2)),
            pltpu.VMEM((columns, capacity, width), bf16),
            DMA((count,)),
        ],
        compiler_params=params(2),
    )(rows, scales, cot, counts, w_inner, w_outer, sib_inner, sib_outer, near_inner, near_outer)


class PieceSum:
    def __init__(self, at, part, got1, got2, got3, gotr, full, sem, rsem, zsem, zrsem, order, finish):
        self.at, self.part, self.full = at, part, full
        self.got1, self.got2, self.got3, self.gotr = got1, got2, got3, gotr
        self.sem, self.rsem, self.zsem, self.zrsem = sem, rsem, zsem, zrsem
        z, e, c, bit, mate, blocks, sib = at
        self.first, self.second = order
        self.finish = finish
        self.rest = len(bit) - 2

    def swap(self, n, src, dst, e):
        return remote(src, dst, self.sem.at[n], self.rsem.at[n], self.at[0], e)

    def halves(self):
        z, e, c, bit, mate, blocks, sib = self.at
        return self.swap(0, self.part.at[1 - bit[self.first]], self.got1, mate[self.first])

    def quarters(self):
        z, e, c, bit, mate, blocks, sib = self.at
        b1, b2 = bit[self.first], bit[self.second]
        return self.swap(1, self.part.at[b1, 1 - b2], self.got2, mate[self.second])

    def to_z(self, zt):
        z, e, c, bit, mate, blocks, sib = self.at
        b1, b2 = bit[self.first], bit[self.second]
        return remote(
            self.part.at[b1, b2, zt], self.got3.at[z], self.zsem.at[0, zt], self.zrsem.at[0, z], zt, e
        )

    def own(self):
        z, e, c, bit, mate, blocks, sib = self.at
        return self.full.at[c, bit[self.first], bit[self.second], z]

    def back_z(self, zt):
        z, e, c, bit, mate, blocks, sib = self.at
        return remote(self.own(), self.own(), self.zsem.at[1, zt], self.zrsem.at[1, z], zt, e)

    def back_quarter(self):
        z, e, c, bit, mate, blocks, sib = self.at
        at = self.full.at[c, bit[self.first], bit[self.second]]
        return self.swap(2, at, at, mate[self.second])

    def back_half(self):
        z, e, c, bit, mate, blocks, sib = self.at
        at = self.full.at[c, bit[self.first]]
        return self.swap(3, at, at, mate[self.first])

    def to_sibling(self):
        z, e, c, bit, mate, blocks, sib = self.at
        return self.swap(4, self.full.at[c], self.full.at[c], sib)

    def step(self, n):
        z, e, c, bit, mate, blocks, sib = self.at
        b1, b2 = bit[self.first], bit[self.second]
        others = [lax.rem(z + step, blocks) for step in range(1, blocks)]
        if n == 0:
            self.halves().start()
        elif n == 1:
            self.halves().wait()
            self.part[b1] = (self.part[b1].astype(f32) + self.got1[...].astype(f32)).astype(bf16)
            self.quarters().start()
        elif n == 2:
            self.quarters().wait()
            self.part[b1, b2] = (self.part[b1, b2].astype(f32) + self.got2[...].astype(f32)).astype(bf16)
            for zt in others:
                self.to_z(zt).start()
        elif n == 3:
            for zs in others:
                remote(
                    self.got3.at[0], self.got3.at[zs], self.zsem.at[0, zs], self.zrsem.at[0, zs], z, e
                ).wait_recv()
            for zt in others:
                self.to_z(zt).wait_send()
            self.got3[z] = self.part[b1, b2, z]
            total = self.got3[0].astype(f32)
            for j in range(1, blocks):
                total = total + self.got3[j].astype(f32)
            own = self.own()
            own[...] = total.astype(bf16)
            for r in range(self.rest):
                copy = self.swap(5 + r, own, self.gotr.at[r], mate[2 + r])
                copy.start()
                copy.wait()
                own[...] = (own[...].astype(f32) + self.gotr[r].astype(f32)).astype(bf16)
            for zt in others:
                self.back_z(zt).start()
        elif n == 4:
            for zs in others:
                at = self.full.at[c, b1, b2, zs]
                remote(at, at, self.zsem.at[1, zs], self.zrsem.at[1, zs], z, e).wait_recv()
            for zt in others:
                self.back_z(zt).wait_send()
            self.back_quarter().start()
        elif n == 5:
            self.back_quarter().wait()
            self.back_half().start()
        elif n == 6:
            self.back_half().wait()
            self.to_sibling().start()
        elif n == 7:
            self.to_sibling().wait()
            for k in range(2):
                self.finish(k, self.full[k])

    @staticmethod
    def scratch(blocks, piece, lanes, rest):
        return [
            pltpu.VMEM((2, 2, blocks, piece, lanes), bf16),
            pltpu.VMEM((2, blocks, piece, lanes), bf16),
            pltpu.VMEM((blocks, piece, lanes), bf16),
            pltpu.VMEM((blocks, piece, lanes), bf16),
            pltpu.VMEM((max(1, rest), piece, lanes), bf16),
            pltpu.VMEM((2, 2, 2, blocks, piece, lanes), bf16),
            DMA((5 + rest,)),
            DMA((5 + rest,)),
            DMA((2, blocks)),
            DMA((2, blocks)),
        ]


def backward(
    rows_t, weights, qkv, att_t, lse, length, attended, middle, flat, gate, slot, ids, lengths, cotangent,
    back, dots, counts, made, hidden, gain_one, gain_two, w_output, w_router, g_inner, g_outer, e_inner, e_outer,
    experts_n,
):
    width, total = rows_t.shape
    half = weights.shape[1] // 3
    pairs = half // 128
    seqs, _, span, _ = attended.shape
    blocks = total // span
    columns, capacity, _ = back.shape
    slots = columns * capacity
    tokens = seqs * span
    hs = span // 2
    scale = HEAD**-0.5
    part = g_inner.shape[2]
    bits = columns.bit_length() - 1
    assert columns == 1 << bits and bits >= 2 and blocks == 4
    rest = bits - 2
    small_rows = -(-(5 + experts_n) // 8) * 8
    out_piece, pair_piece = width // (4 * blocks), 3 * width // (4 * blocks)
    n_sum = 10

    def kernel(*refs):
        (
            xt_in, w_in, qkv_in, attt_in, lse_ref, len_ref, t_in, mid_in, flat_in, gate_ref, slot_ref, ids_ref,
            lens_ref, cot_in, back_in, dots_ref, cnt_ref, made_ref, hid_in, g1_ref, g2_ref, wo_in, wr_ref,
            gi_ref, go_ref, ei_ref, eo_ref,
        ) = refs[:27]
        grads_out, sums_ref, fi_out, fo_out, gh_out, y_out = refs[27:33]
        (
            do_ref, dqkv_ref, kt_ref, dk_ref, dv_ref, dn_ref, dsib_ref, dsum_ref, dnt_ref,
            zi, zo, ci, co, osib, sgot, szgot, datt_ref, op_ref, dmid_ref, mg_ref,
            loc_sem, dsend, drecv, rloc, rsend, rrecv,
            nsend, nrecv, ssend, srecv, osend, orecv, tsend, trecv, tzsend, tzrecv, msend, mrecv,
            back_ref, mid_ref, cot_ref, flat_ref, wo_ref, t_ref, qkv_ref, attt_ref, xt_ref, w_ref, hid_ref, load_sem,
            grads_ref, fi_ref, fo_ref, gh_ref, y_ref, out_sem,
        ) = refs[33:89]
        sums_scratch = refs[89:]
        z, e, c, base = place()
        col = e // 2
        sib = base + 1 - c
        seq_core, seq = z // 2, lax.rem(z, 2)
        bit = [lax.rem(col // (1 << i), 2) for i in range(bits)]
        mate = [2 * (col + (1 - 2 * bit[i]) * (1 << i)) + c for i in range(bits)]
        others = [lax.rem(z + step, blocks) for step in range(1, blocks)]
        plane = [lax.rem(col + step, columns) for step in range(1, columns)]
        inner = (z > 0) & (z < blocks - 1)
        order = slice_order(z)
        across = [lax.rem(2 * (z // 2) + 2 + k, blocks) for k in range(2)]
        partners = column_partners(blocks, z, c, base) + [(z, 2 * t + c) for t in plane]
        greet(partners)
        outs = [
            pltpu.make_async_copy(src, dst, out_sem.at[n])
            for n, (src, dst) in enumerate(
                ((gh_ref, gh_out), (y_ref, y_out), (fi_ref, fi_out), (fo_ref, fo_out))
                + tuple((grads_ref.at[m], grads_out.at[m]) for m in range(4))
            )
        ]
        loads = [
            pltpu.make_async_copy(src, dst, load_sem.at[n])
            for n, (src, dst) in enumerate(
                (
                    (back_in, back_ref), (mid_in, mid_ref), (cot_in, cot_ref), (flat_in, flat_ref), (wo_in, wo_ref),
                    (t_in, t_ref), (qkv_in, qkv_ref), (attt_in, attt_ref), (xt_in, xt_ref), (w_in, w_ref), (hid_in, hid_ref),
                )
            )
        ]
        for load in loads:
            load.start()

        def m_out(t):
            return remote(made_ref.at[t], mg_ref.at[col], msend.at[t], mrecv.at[col], z, 2 * t + c)

        m_own = pltpu.make_async_copy(made_ref.at[col], mg_ref.at[col], loc_sem.at[2])
        m_own.start()

        far = order[3]
        pair = z + 1 - 2 * lax.rem(z, 2)

        def r_load(i, src, s, slot):
            return pltpu.make_async_copy(src.at[s], (zi, zo)[i].at[slot], rloc.at[i, slot])

        def r_chain(i):
            src, dst = ((gi_ref, ci), (go_ref, co))[i]
            return remote(src.at[1], dst, rsend.at[i], rrecv.at[i], pair, e)

        def r_sum(i):
            src, dst = ((zi, ci), (zo, co))[i]
            return remote(src.at[0], dst, rsend.at[i], rrecv.at[i], far, e)

        def chain(i):
            @pl.when(inner)
            def _():
                buf, got = ((zi, ci), (zo, co))[i]
                r_load(i, (gi_ref, go_ref)[i], 1, 0).wait()
                r_chain(i).wait_recv()
                buf[0] = (buf[0].astype(f32) + got[...].astype(f32)).astype(bf16)
                r_sum(i).start()

        for i in range(2):

            @pl.when(jnp.logical_not(inner))
            def _():
                r_load(i, (gi_ref, go_ref)[i], 0, 0).start()

            @pl.when(inner)
            def _():
                r_load(i, (gi_ref, go_ref)[i], 1, 0).start()

            r_load(i, (ei_ref, eo_ref)[i], pair, 1).start()

        onehot = one_hot(ids_ref, seqs, span)
        valid = valid_rows(lens_ref, z, seqs, span)
        from_slots = lane_of((tokens, slots), 1).astype(f32) == slot_ref[...]
        dots_row = jnp.concatenate([dots_ref[t, 0:1, 0:capacity] for t in range(columns)], axis=1)
        dot_rows = jnp.sum(jnp.where(from_slots, dots_row, 0.0), axis=1, keepdims=True)
        picks = from_slots.astype(f32).astype(bf16)
        for load in loads[:5]:
            load.wait()
        d_rows = dot(picks, back_ref[...].reshape(slots, width))
        count_row = cnt_ref[0:1]
        mean_load = jnp.sum(count_row, axis=1, keepdims=True) / experts_n
        ratio_rows = jnp.sum(onehot * ((count_row - mean_load) / mean_load), axis=1, keepdims=True)
        gates = gate_ref[...]
        d_gate = valid * (dot_rows + balance_weight * ratio_rows)
        d_logits = (onehot * (d_gate * gates * (1.0 - gates))).astype(bf16)
        router_t = dot_tn(d_logits, flat_ref[...])
        balance_part = jnp.sum(valid * gates * ratio_rows, axis=0, keepdims=True) / jnp.sum(
            count_row, axis=1, keepdims=True
        )
        gain_sum = jnp.zeros((1, width), f32)
        shift_sum = jnp.zeros((1, width), f32)
        for s in range(seqs):
            lo, hi = s * span, (s + 1) * span
            v = mid_ref[lo:hi]
            centered = v - jnp.mean(v, axis=-1, keepdims=True)
            inverse = lax.rsqrt(jnp.mean(centered * centered, axis=-1, keepdims=True) + epsilon)
            unit = centered * inverse
            dy = d_rows[lo:hi] + dot(d_logits[lo:hi, :experts_n], wr_ref[...])
            gain_sum = gain_sum + jnp.sum(dy * unit, axis=0, keepdims=True)
            shift_sum = shift_sum + jnp.sum(dy, axis=0, keepdims=True)
            du = dy * g2_ref[...].reshape(1, width)
            dx = inverse * (
                du
                - jnp.mean(du, axis=-1, keepdims=True)
                - unit * jnp.mean(du * unit, axis=-1, keepdims=True)
            )
            dmid_ref[lo:hi] = cot_ref[lo:hi].astype(f32) + dx
            d_branch = dmid_ref[lo:hi].astype(bf16)
            for k in range(2):
                datt_ref[s, k] = dot_nt(d_branch, wo_ref[k * half : (k + 1) * half]).astype(bf16)

        at = (z, e, c, bit, mate, blocks, sib)

        def finish_out(k, g):
            grads_ref[3, :, k * half : (k + 1) * half] = g.reshape(width, half)

        def finish_pair(p):
            def finish(k, g):
                g = g.reshape(3, width, 128)
                for m in range(3):
                    grads_ref[m, :, k * half + p * 128 : k * half + (p + 1) * 128] = g[m]

            return finish

        out_sum = PieceSum(at, *sums_scratch[:n_sum], (0, 1), finish_out)
        pair_sums = [
            PieceSum(
                at,
                *sums_scratch[n_sum * (p + 1) : n_sum * (p + 2)],
                (1, 0) if p % 2 == 0 else (0, 1),
                finish_pair(p),
            )
            for p in range(pairs)
        ]

        await_greetings(partners)

        def d_out(s, k):
            return remote(
                datt_ref.at[s, k], do_ref.at[z], dsend.at[s, k], drecv.at[z], 2 * c + s, base + k
            )

        def d_own(s, k):
            return pltpu.make_async_copy(datt_ref.at[s, k], do_ref.at[z], loc_sem.at[0])

        for k, s in ((0, 0), (0, 1), (1, 1), (1, 0)):
            if True:
                to_self = (2 * c + s == z) & (c == k)

                @pl.when(to_self)
                def _():
                    d_own(s, k).start()

                @pl.when(jnp.logical_not(to_self))
                def _():
                    d_out(s, k).start()

        @pl.when(jnp.logical_not(inner))
        def _():
            r_chain(0).start()

        sums_ref[...] = jnp.zeros_like(sums_ref)
        sums_ref[2:3] = gain_sum
        sums_ref[3:4] = shift_sum
        sums_ref[4 : 4 + experts_n] = router_t[0:experts_n]
        sums_ref[4 + experts_n : 5 + experts_n] = jnp.broadcast_to(balance_part, (1, width))
        d_branch = dmid_ref[...].astype(bf16)
        loads[5].wait()
        for k in range(2):
            att_k = jnp.concatenate([t_ref[s, k] for s in range(seqs)], axis=0)
            made_k = dot_tn(att_k, d_branch).astype(bf16)
            op_ref[0, k * half : (k + 1) * half] = made_k[:, :half]
            op_ref[1, k * half : (k + 1) * half] = made_k[:, half:]
        o_first = remote(op_ref.at[1 - c], osib, osend, orecv, z, sib)
        o_first.start()
        o_first.wait()
        out_sum.part[...] = (op_ref[c].astype(f32) + osib[...].astype(f32)).astype(bf16).reshape(
            2, 2, blocks, out_piece, half
        )
        out_sum.step(0)
        out_sum.step(1)

        def d_got(j):
            mine = (z == j) & (c == seq_core)

            @pl.when(mine)
            def _():
                d_own(0, 0).wait()

            @pl.when(jnp.logical_not(mine))
            def _():
                remote(datt_ref.at[0, 0], do_ref.at[j], dsend.at[0, 0], drecv.at[j], z, base).wait_recv()

        for load in loads[6:]:
            load.wait()

        key_bias = jnp.where(lane_of((total, 1), 0) < len_ref[0:1, 0:1], 0.0, masked_fill)
        lane = lane_of((1, 128), 1)
        later = lax.broadcasted_iota(jnp.int32, (span, span), 0) > lax.broadcasted_iota(
            jnp.int32, (span, span), 1
        )

        def pair_step(p):
            first = p * 128
            k_all = qkv_ref[:, pl.ds(half + first, 128)]
            kt_ref[...] = jnp.transpose(k_all)
            v_all = qkv_ref[:, pl.ds(2 * half + first, 128)]
            k_heads = key_heads(k_all, key_bias)
            dk_ref[...] = jnp.zeros_like(dk_ref)
            dv_ref[...] = jnp.zeros_like(dv_ref)
            for j in range(blocks):
                n = (j + 1) * span
                r = pl.ds(j * span, span)
                if p == 0:
                    d_got(j)
                q = qkv_ref[r, pl.ds(first, 128)].astype(f32) * scale
                d_o = do_ref[j, :, pl.ds(first, 128)].astype(f32)
                prod_t = jnp.transpose(d_o) * attt_ref[pl.ds(first, 128), r]
                dq_t = []
                for h in range(2):
                    inside = (lane // HEAD) == h
                    spare = lane == (1 - h) * HEAD
                    q_h = jnp.where(inside, q, jnp.where(spare, 1.0, 0.0)).astype(bf16)
                    q_only = jnp.where(inside, q, 0.0).astype(bf16)
                    do_h = jnp.where(inside, d_o, 0.0).astype(bf16)
                    delta = jnp.sum(prod_t[h * HEAD : (h + 1) * HEAD], axis=0, keepdims=True)
                    s = dot_nt(k_heads[h][:n], q_h)
                    last = jnp.where(later, masked_fill, s[n - span :])
                    s = last if j == 0 else jnp.concatenate([s[: n - span], last], axis=0)
                    w = jnp.exp(s - lse_ref[pl.ds(2 * p + h, 1), r])
                    d_w = dot_nt(v_all[:n], do_h)
                    d_s = (w * (d_w - delta)).astype(bf16)
                    dv_ref[:n] += dot(w.astype(bf16), do_h)
                    dk_ref[:n] += dot(d_s, q_only)
                    dq_t.append(dot(kt_ref[h * HEAD : (h + 1) * HEAD, :n], d_s))
                dq = jnp.transpose(jnp.concatenate(dq_t, axis=0)) * scale
                dqkv_ref[r, pl.ds(first, 128)] = dq.astype(bf16)
            dqkv_ref[:, pl.ds(half + first, 128)] = dk_ref[...].astype(bf16)
            dqkv_ref[:, pl.ds(2 * half + first, 128)] = dv_ref[...].astype(bf16)
            joined = jnp.concatenate(
                [dqkv_ref[:, pl.ds(m * half + first, 128)] for m in range(3)], axis=1
            )
            grads = dot(xt_ref[...], joined).astype(bf16)
            pair_sums[p].part[...] = jnp.concatenate(
                [grads[:, m * 128 : (m + 1) * 128] for m in range(3)], axis=0
            ).reshape(2, 2, blocks, pair_piece, 128)

        state = {out_sum: 2}

        def advance(*chosen):
            for one in chosen or list(state):
                n = state.setdefault(one, 0)
                if n <= 7:
                    one.step(n)
                    state[one] = n + 1

        plan = ([out_sum], [pair_sums[0]], [pair_sums[0]]) if pairs == 3 else ([],) * pairs
        for p in range(pairs):
            pair_step(p)
            if plan[p]:
                advance(*plan[p])
            advance(pair_sums[p])
            if p == 1:
                chain(0)

        for j in range(blocks):
            r = pl.ds(j * span, span)
            dn_ref[j] = dot_nt(dqkv_ref[r, :], w_ref[...]).astype(bf16).reshape(2, hs, width)

        def n_sib(j):
            return remote(dn_ref.at[j, 1 - c], dsib_ref.at[j], nsend.at[j], nrecv.at[j], z, sib)

        def n_out(j):
            return remote(
                dsum_ref.at[j], dnt_ref.at[seq, c], ssend.at[j], srecv.at[seq, c], j, base + seq_core
            )

        def n_own():
            return pltpu.make_async_copy(dsum_ref.at[z], dnt_ref.at[seq, c], loc_sem.at[1])

        n_order = others[1:2] + others[0:1] + others[2:] + [z]
        for j in n_order:
            n_sib(j).start()
        advance(*pair_sums[1:2])
        for i, j in enumerate(n_order):
            n_sib(j).wait_recv()
            dsum_ref[j] = (dn_ref[j, c].astype(f32) + dsib_ref[j].astype(f32)).astype(bf16)
            if i < blocks - 1:
                n_out(j).start()
            else:

                @pl.when(seq_core == c)
                def _():
                    n_own().start()

                @pl.when(seq_core != c)
                def _():
                    n_out(j).start()

        @pl.when(jnp.logical_not(inner))
        def _():
            r_chain(1).start()

        advance(*pair_sums[1:])
        for t in plane:
            m_out(t).start()
        advance(*pair_sums[2:])
        advance(out_sum, *pair_sums[:1])
        for s in range(seqs):
            for k in range(2):
                from_self = (2 * c + s == z) & (c == k)

                @pl.when(jnp.logical_not(from_self))
                def _():
                    remote(
                        dsum_ref.at[0], dnt_ref.at[s, k], ssend.at[0], srecv.at[s, k], z, base
                    ).wait_recv()

                @pl.when(from_self)
                def _():
                    n_own().wait()

        gains = g1_ref[...].reshape(1, width)
        gain_sum = jnp.zeros((1, width), f32)
        shift_sum = jnp.zeros((1, width), f32)
        for s in range(seqs):
            for k in range(2):
                v = hid_ref[s, k].astype(f32)
                centered = v - jnp.mean(v, axis=-1, keepdims=True)
                inverse = lax.rsqrt(jnp.mean(centered * centered, axis=-1, keepdims=True) + epsilon)
                unit = centered * inverse
                dy = dnt_ref[s, k].astype(f32)
                gain_sum = gain_sum + jnp.sum(dy * unit, axis=0, keepdims=True)
                shift_sum = shift_sum + jnp.sum(dy, axis=0, keepdims=True)
                du = dy * gains
                dx = inverse * (
                    du
                    - jnp.mean(du, axis=-1, keepdims=True)
                    - unit * jnp.mean(du * unit, axis=-1, keepdims=True)
                )
                gh_ref[s, k] = dmid_ref[(2 * s + k) * hs : (2 * s + k + 1) * hs] + dx
        outs[0].start()

        sums_ref[0:1] = gain_sum
        sums_ref[1:2] = shift_sum

        def t_swap(n, te):
            return remote(sums_ref, sgot.at[n], tsend.at[n], trecv.at[n], z, te)

        partners = [sib] + mate
        for n, te in enumerate(partners):
            copy = t_swap(n, te)
            copy.start()
            if n in (1, 2):
                advance()
            if n == 1:
                chain(1)
            copy.wait()
            sums_ref[...] = sums_ref[...] + sgot[n]

        def t_z(zt):
            return remote(sums_ref, szgot.at[z], tzsend.at[zt], tzrecv.at[z], zt, e)

        for zt in others:
            t_z(zt).start()
        for t in plane:
            remote(made_ref.at[0], mg_ref.at[t], msend.at[t], mrecv.at[t], z, e).wait_recv()
        m_own.wait()
        scaled = valid * gates
        expert_out = dot(picks, mg_ref[...].reshape(slots, width))
        y_ref[...] = (mid_ref[...] + scaled * expert_out).astype(bf16)
        outs[1].start()

        for i, (buf, final) in enumerate(((zi, fi_ref), (zo, fo_ref))):
            r_load(i, (ei_ref, eo_ref)[i], pair, 1).wait()
            final[...] = buf[1].astype(f32)

            @pl.when(inner)
            def _():
                for src, part_at in (
                    ((gi_ref, go_ref)[i], 0), ((ei_ref, eo_ref)[i], across[0]), ((ei_ref, eo_ref)[i], across[1])
                ):
                    load = r_load(i, src, part_at, 1)
                    load.start()
                    load.wait()
                    final[...] = final[...] + buf[1].astype(f32)

            @pl.when(jnp.logical_not(inner))
            def _():
                r_load(i, (gi_ref, go_ref)[i], 0, 0).wait()
                final[...] = final[...] + buf[0].astype(f32)

        for _ in range(3):
            advance()
        assert state[out_sum] == 8
        outs[7].start()
        for zs in others:
            remote(sums_ref, szgot.at[zs], tzsend.at[zs], tzrecv.at[zs], z, e).wait_recv()
        for zt in others:
            t_z(zt).wait_send()
        szgot[z] = sums_ref[...]
        tot = szgot[0]
        for j in range(1, blocks):
            tot = tot + szgot[j]
        sums_ref[...] = tot

        advance()
        for i, (got, final) in enumerate(((ci, fi_ref), (co, fo_ref))):

            @pl.when(inner)
            def _():
                r_sum(i).wait_send()

            @pl.when(jnp.logical_not(inner))
            def _():
                r_sum(i).wait_recv()
                r_chain(i).wait_send()
                final[...] = final[...] + got[...].astype(f32)

            outs[2 + i].start()
        while min(state.values()) <= 7:
            advance()
        for out in outs[4:7]:
            out.start()

        for s in range(seqs):
            for k in range(2):

                @pl.when(jnp.logical_not((2 * c + s == z) & (c == k)))
                def _():
                    d_out(s, k).wait_send()

        for j in n_order[:-1]:
            n_out(j).wait_send()

        @pl.when(seq_core != c)
        def _():
            n_out(z).wait_send()

        for j in n_order:
            n_sib(j).wait_send()
        for t in plane:
            m_out(t).wait_send()
        for out in outs:
            out.wait()

    stage = blocks
    scratch = [
        pltpu.VMEM((blocks, span, half), bf16),
        pltpu.VMEM((total, 3 * half), bf16),
        pltpu.VMEM((128, total), bf16),
        pltpu.VMEM((total, 128), f32),
        pltpu.VMEM((total, 128), f32),
        pltpu.VMEM((blocks, 2, hs, width), bf16),
        pltpu.VMEM((blocks, hs, width), bf16),
        pltpu.VMEM((blocks, hs, width), bf16),
        pltpu.VMEM((seqs, 2, hs, width), bf16),
        pltpu.VMEM((2, width, part), bf16),
        pltpu.VMEM((2, part, width), bf16),
        pltpu.VMEM((width, part), bf16),
        pltpu.VMEM((part, width), bf16),
        pltpu.VMEM((width, half), bf16),
        pltpu.VMEM((1 + bits, small_rows, width), f32),
        pltpu.VMEM((blocks, small_rows, width), f32),
        pltpu.VMEM((seqs, 2, span, half), bf16),
        pltpu.VMEM((2, width, half), bf16),
        pltpu.VMEM((tokens, width), f32),
        pltpu.VMEM((columns, capacity, width), bf16),
        DMA((3,)),
        DMA((seqs, 2)),
        DMA((stage,)),
        DMA((2, 2)),
        DMA((2,)),
        DMA((2,)),
        DMA((stage,)),
        DMA((stage,)),
        DMA((stage,)),
        DMA((seqs, 2)),
        DMA,
        DMA,
        DMA((1 + bits,)),
        DMA((1 + bits,)),
        DMA((stage,)),
        DMA((stage,)),
        DMA((columns,)),
        DMA((columns,)),
        pltpu.VMEM((columns, capacity, width), bf16),
        pltpu.VMEM((tokens, width), f32),
        pltpu.VMEM((tokens, width), bf16),
        pltpu.VMEM((tokens, width), bf16),
        pltpu.VMEM((width, width), bf16),
        pltpu.VMEM((seqs, 2, span, half), bf16),
        pltpu.VMEM((total, 3 * half), bf16),
        pltpu.VMEM((half, total), f32),
        pltpu.VMEM((width, total), bf16),
        pltpu.VMEM((width, 3 * half), bf16),
        pltpu.VMEM((seqs, 2, hs, width), bf16),
        DMA((11,)),
        pltpu.VMEM((4, width, width), bf16),
        pltpu.VMEM((width, part), f32),
        pltpu.VMEM((part, width), f32),
        pltpu.VMEM((seqs, 2, hs, width), f32),
        pltpu.VMEM((tokens, width), bf16),
        DMA((8,)),
    ]
    scratch += PieceSum.scratch(blocks, out_piece, half, rest)
    for _ in range(pairs):
        scratch += PieceSum.scratch(blocks, pair_piece, 128, rest)
    grads, sums, f_inner, f_outer, g_hidden, output = pl.pallas_call(
        kernel,
        name="backward",
        out_shape=[
            jax.ShapeDtypeStruct((4, width, width), bf16),
            jax.ShapeDtypeStruct((small_rows, width), f32),
            jax.ShapeDtypeStruct((width, part), f32),
            jax.ShapeDtypeStruct((part, width), f32),
            jax.ShapeDtypeStruct((seqs, 2, hs, width), f32),
            jax.ShapeDtypeStruct((tokens, width), bf16),
        ],
        in_specs=[ANY] * 4 + [VMEM] * 2 + [ANY] * 3 + [VMEM] * 3 + [SMEM] + [ANY] * 2 + [VMEM] * 2 + [ANY] * 2 + [VMEM] * 2
        + [ANY] + [VMEM] + [ANY] * 4,
        out_specs=[ANY, VMEM] + [ANY] * 4,
        scratch_shapes=scratch,
        compiler_params=params(3),
    )(
        rows_t, weights, qkv, att_t, lse, length, attended, middle, flat, gate, slot, ids, lengths, cotangent,
        back, dots, counts, made, hidden.reshape(seqs, 2, hs, width), gain_one,
        gain_two, w_output, w_router, g_inner, g_outer, e_inner, e_outer,
    )
    return finish(grads, sums, f_inner, f_outer, g_hidden.reshape(tokens, width), output, experts_n)


def finish(grads, sums, g_inner, g_outer, g_hidden, output, experts_n):
    steps = 8
    width = grads.shape[2]
    tokens = output.shape[0]
    part = g_inner.shape[1]
    rows = width // steps

    def kernel(g_ref, s_ref, i_ref, o_ref, h_ref, y_ref, *outs):
        for m in range(4):
            outs[m][...] = g_ref[m].astype(f32)
        outs[4][...] = i_ref[...]
        outs[5][...] = o_ref[...]
        outs[6][...] = h_ref[...]
        outs[7][...] = y_ref[...]

        @pl.when(pl.program_id(0) == 0)
        def _():
            for m in range(4):
                outs[8 + m][...] = s_ref[m]
            outs[12][...] = s_ref[4 : 4 + experts_n]
            outs[13][...] = s_ref[4 + experts_n : 5 + experts_n, 0:1]

    def by_rows(shape):
        return pl.BlockSpec((shape[0] // steps,) + shape[1:], lambda i: (i,) + (0,) * (len(shape) - 1))

    def whole(shape):
        return pl.BlockSpec(shape, lambda i: (0,) * len(shape))

    split = [(width, width)] * 4 + [(width, part), (part, width), (tokens, width), (tokens, width)]
    kept = [(width,)] * 4 + [(experts_n, width), (1, 1)]
    return pl.pallas_call(
        kernel,
        name="finish",
        grid=(steps,),
        out_shape=[jax.ShapeDtypeStruct(a, bf16 if n == 7 else f32) for n, a in enumerate(split + kept)],
        in_specs=[pl.BlockSpec((4, rows, width), lambda i: (0, i, 0)), whole(sums.shape)]
        + [by_rows(a) for a in split[4:]],
        out_specs=[by_rows(a) for a in split] + [whole(a) for a in kept],
        compiler_params=pltpu.CompilerParams(dimension_semantics=("arbitrary",), vmem_limit_bytes=VMEM_BYTES),
    )(grads, sums, g_inner, g_outer, g_hidden, output)


def on_device(
    hidden_in,
    cotangent,
    query_weight,
    key_weight,
    value_weight,
    output_weight,
    gain_one,
    shift_one,
    gain_two,
    shift_two,
    w_router,
    w_inner,
    w_outer,
    expert_ids,
    seq_lengths,
):
    seqs, span, width = hidden_in.shape
    tokens = seqs * span
    blocks = lax.axis_size("blk")
    columns = lax.axis_size("ep") // 2
    experts_n = w_router.shape[1]
    capacity = max(2, 2 * tokens // experts_n)
    total = blocks * span
    half = width // 2
    assert seqs * 2 == blocks and experts_n == columns

    ids = expert_ids.reshape(seqs, span)
    lengths = seq_lengths
    router = jnp.transpose(w_router)
    cot = cotangent.reshape(tokens, width)
    (
        rows_t, w_qkv, qkv, att_t, lse, attended, middle, flat, gate, slot, to_rows, scales, cot_rows, length, counts,
        near_inner, near_outer, sib_inner, sib_outer,
    ) = forward(
        hidden_in, cotangent, gain_one, shift_one, gain_two, shift_two, query_weight, key_weight, value_weight,
        output_weight, router, ids, lengths, w_inner[0], w_outer[0], blocks, columns, capacity, experts_n,
    )
    back, dots, made, counts, g_inner, g_outer, e_inner, e_outer = experts(
        to_rows, scales, cot_rows, counts, w_inner[0], w_outer[0], sib_inner, sib_outer, near_inner, near_outer,
        blocks,
    )
    results = backward(
        rows_t, w_qkv, qkv.reshape(total, 3 * half), att_t, lse, length, attended, middle, flat, gate,
        slot, ids, lengths, cot, back, dots, counts, made, hidden_in, gain_one, gain_two, output_weight, router,
        g_inner, g_outer, e_inner, e_outer, experts_n,
    )
    dense, (grad_inner, grad_outer, grad_hidden, output) = results[:4], results[4:8]
    gains, (grad_router, balance) = results[8:12], results[12:]
    return (
        output.reshape(seqs, span, width),
        grad_hidden.reshape(seqs, span, width),
        *dense,
        *gains,
        jnp.transpose(grad_router),
        grad_inner[None],
        grad_outer[None],
        balance[0, 0],
    )


def solution(mesh):
    tokens = P("ep", "blk", None)
    return jax.shard_map(
        on_device,
        mesh=mesh,
        in_specs=(tokens, tokens)
        + (P(),) * 9
        + (P("ep", None, "blk"), P("ep", "blk", None), P("ep", "blk", None, None, None), P("ep")),
        out_specs=(tokens, tokens) + (P(),) * 9 + (P("ep", None, "blk"), P("ep", "blk", None), P()),
        check_vma=False,
    )
```

```python
import functools

import jax
import jax.numpy as jnp
from jax import lax
from jax.experimental import pallas as pl
from jax.experimental.pallas import tpu as pltpu
from jax.sharding import PartitionSpec as P

HEAD = 64
MESH = pl.DeviceIdType.MESH
ANY = pl.BlockSpec(memory_space=pl.ANY)
VMEM = pl.BlockSpec(memory_space=pltpu.VMEM)
SMEM = pl.BlockSpec(memory_space=pltpu.SMEM)
DMA = pltpu.SemaphoreType.DMA
f32 = jnp.float32
bf16 = jnp.bfloat16

epsilon = 1e-05
balance_weight = 6.0
masked_fill = -1e30
VMEM_BYTES = 57 * 1024 * 1024


def dot(a, b):
    return lax.dot_general(a, b, (((1,), (0,)), ((), ())), preferred_element_type=f32)


def dot_nt(a, b):
    return lax.dot_general(a, b, (((1,), (1,)), ((), ())), preferred_element_type=f32)


def dot_tn(a, b):
    return lax.dot_general(a, b, (((0,), (0,)), ((), ())), preferred_element_type=f32)


def place():
    z = lax.axis_index("blk")
    e = lax.axis_index("ep")
    c = lax.rem(e, 2)
    return z, e, c, e - c


def remote(src, dst, send_sem, recv_sem, z, e):
    return pltpu.make_async_remote_copy(
        src, dst, send_sem, recv_sem, device_id=(z, e), device_id_type=MESH
    )


def greet(partners):
    barrier = pltpu.get_barrier_semaphore()
    for z, e in partners:
        pl.semaphore_signal(barrier, inc=1, device_id=(z, e), device_id_type=MESH)


def await_greetings(partners):
    pl.semaphore_wait(pltpu.get_barrier_semaphore(), len(partners))


def column_partners(blocks, z, c, base):
    found = [(z, base + 1 - c)]
    for step in range(1, blocks):
        for k in range(2):
            found.append((lax.rem(z + step, blocks), base + k))
    return found


def params(collective_id):
    return pltpu.CompilerParams(
        collective_id=collective_id, has_side_effects=True, vmem_limit_bytes=VMEM_BYTES
    )


def lane_of(shape, dimension):
    return lax.broadcasted_iota(jnp.int32, shape, dimension)


def one_hot(ids_ref, seqs, span):
    columns = [
        jnp.transpose(jnp.broadcast_to(ids_ref[s : s + 1], (128, span))) for s in range(seqs)
    ]
    ids = jnp.concatenate(columns, axis=0)
    return (lane_of(ids.shape, 1) == ids).astype(f32)


def valid_rows(len_ref, z, seqs, span):
    place_in = z * span + lane_of((span, 1), 0)
    return jnp.concatenate([(place_in < len_ref[s]).astype(f32) for s in range(seqs)], axis=0)


def key_heads(k_all, key_bias):
    lane = lane_of((1, 128), 1)
    found = []
    for h in range(2):
        inside = (lane // HEAD) == h
        spare = lane == (1 - h) * HEAD
        found.append(
            jnp.where(inside, k_all.astype(f32), jnp.where(spare, key_bias, 0.0)).astype(bf16)
        )
    return found


def forward(
    hidden, cotangent, gain_one, shift_one, gain_two, shift_two, w_query, w_key, w_value, w_output, w_router,
    ids, lengths, w_inner, w_outer, blocks, columns, capacity, experts_n,
):
    seqs, span, width = hidden.shape
    hs = span // 2
    half = width // 2
    pairs = half // 128
    total = blocks * span
    tokens = seqs * span
    slots = experts_n * capacity
    part = w_inner.shape[1]
    cap_lanes = max(128, capacity)

    def kernel(*refs):
        (
            hid_ref, cot_ref, g1_ref, s1_ref, g2_ref, s2_ref, wq_ref, wk_ref, wv_ref, wo_ref, wr_ref,
            ids_ref, len_in, wi_ref, we_ref,
        ) = refs[:15]
        (
            xt_out, w_out, qkv_out, attt_out, lse_ref, t_out, mid_out, flat_out, gate_ref, slot_ref,
            rows_ref, sc_ref, cote_ref, len_ref, cnt_ref, li_ref, lo_ref, bi_ref, bo_ref,
        ) = refs[15:34]
        (
            x_ref, nb_ref, kh_ref, vt_ref, att_ref, cots_ref, lens_ref, lgot_ref, cown_ref, cgot_ref,
            wload, nloc, nsend, nrecv, fsend, frecv, aloc, asend, arecv, closs, csend, crecv,
            lsend, lrecv, ksend, krecv, hsend, hrecv, bsend, brecv,
            xt_ref, w_ref, qkv_ref, attt_ref, out_sem, t_ref, mid_ref, flat_ref,
        ) = refs[34:]
        z, e, c, base = place()
        col = e // 2
        sib = base + 1 - c
        seq_core, seq = z // 2, lax.rem(z, 2)
        others = [lax.rem(z + step, blocks) for step in range(1, blocks)]
        plane = [lax.rem(col + step, columns) for step in range(1, columns)]
        column = column_partners(blocks, z, c, base)
        greet(column + [(z, 2 * t + c) for t in plane])

        def load_w(m, ref):
            return pltpu.make_async_copy(
                ref.at[:, pl.ds(pl.multiple_of(c * half, half), half)],
                w_ref.at[:, pl.ds(m * half, half)],
                wload.at[m],
            )

        for m, ref in enumerate((wq_ref, wk_ref, wv_ref)):
            load_w(m, ref).start()
        gain_row, shift_row = g1_ref[...].reshape(1, width), s1_ref[...].reshape(1, width)
        for s in range(seqs):
            for k in range(2):
                v = hid_ref[s, k].astype(f32)
                centered = v - jnp.mean(v, axis=-1, keepdims=True)
                inverse = lax.rsqrt(jnp.mean(centered * centered, axis=-1, keepdims=True) + epsilon)
                nb_ref[s, k] = (centered * inverse * gain_row + shift_row).astype(bf16)
        await_greetings(column + plane)

        def n_out(s, k):
            return remote(
                nb_ref.at[s, k], x_ref.at[z, k], nsend.at[s, k], nrecv.at[z], 2 * c + s, base + k
            )

        def n_own(s, k):
            return pltpu.make_async_copy(nb_ref.at[s, k], x_ref.at[z, k], nloc)

        for k, s in ((0, 0), (0, 1), (1, 1), (1, 0)):
            if True:
                to_self = (2 * c + s == z) & (c == k)

                @pl.when(to_self)
                def _():
                    n_own(s, k).start()

                @pl.when(jnp.logical_not(to_self))
                def _():
                    n_out(s, k).start()

        for s in range(seqs):
            lens_ref[s] = jnp.full((8, 128), len_in[s], jnp.int32)
        to_lens = remote(lens_ref, lgot_ref, lsend, lrecv, z, sib)
        to_lens.start()
        lane = lane_of((tokens, 128), 1)
        onehot = one_hot(ids_ref, seqs, span)
        valid = valid_rows(len_in, z, seqs, span)
        cown_ref[...] = jnp.broadcast_to(jnp.sum(onehot * valid, axis=0, keepdims=True), (8, 128))

        def k_out(n, to_z, to_e):
            return remote(cown_ref, cgot_ref.at[z, c], ksend.at[n], krecv.at[z, c], to_z, to_e)

        for n, (to_z, to_e) in enumerate(column):
            k_out(n, to_z, to_e).start()
        earlier = (lane_of((tokens, tokens), 0) > lane_of((tokens, tokens), 1)).astype(f32).astype(bf16)
        rank = dot(earlier, onehot.astype(bf16))
        slot = jnp.sum(onehot * (rank + (lane * capacity).astype(f32)), axis=1, keepdims=True)
        slot_ref[...] = slot
        slot_row = jnp.transpose(jnp.broadcast_to(slot, (tokens, 128)))[0:1]
        to_slots = (lane_of((slots, tokens), 0).astype(f32) == slot_row).astype(f32).astype(bf16)
        cots_ref[...] = (
            dot(to_slots, cot_ref[...]).astype(bf16).reshape(columns, capacity, width)
        )

        def c_out(t):
            return remote(cots_ref.at[t], cote_ref.at[col], csend.at[t], crecv.at[col], z, 2 * t + c)

        c_own = pltpu.make_async_copy(cots_ref.at[col], cote_ref.at[col], closs)
        c_own.start()
        for t in plane:
            c_out(t).start()
        for m, ref in enumerate((wq_ref, wk_ref, wv_ref)):
            load_w(m, ref).wait()

        def n_sib(zs):
            return remote(x_ref.at[zs, c], x_ref.at[zs, c], fsend.at[zs], frecv.at[zs], z, sib)

        for zs in [z] + others:
            if zs is z:

                @pl.when(c == seq_core)
                def _():
                    n_own(0, 0).wait()

                @pl.when(c != seq_core)
                def _():
                    remote(nb_ref.at[0, 0], x_ref.at[z, c], nsend.at[0, 0], nrecv.at[z], z, base).wait_recv()
            else:
                remote(nb_ref.at[0, 0], x_ref.at[zs, c], nsend.at[0, 0], nrecv.at[zs], z, base).wait_recv()
            n_sib(zs).start()

        def h_out(i, step):
            side = 0 if step == 1 else 1
            src, dst = ((wi_ref, li_ref), (we_ref, lo_ref))[i]
            return remote(src, dst.at[side], hsend.at[i, side], hrecv.at[i, side], z + step, e)

        def h_start(i):
            @pl.when(z < blocks - 1)
            def _():
                h_out(i, 1).start()

            @pl.when(z > 0)
            def _():
                h_out(i, -1).start()

        def b_out(i):
            src, dst = ((wi_ref, bi_ref), (we_ref, bo_ref))[i]
            return remote(src, dst, bsend.at[i], brecv.at[i], z, sib)

        h_start(0)
        for zs in [z] + others:
            remote(
                x_ref.at[zs, 1 - c], x_ref.at[zs, 1 - c], fsend.at[zs], frecv.at[zs], z, sib
            ).wait_recv()
            x_z = x_ref[zs].reshape(span, width)
            qkv_ref[zs] = dot(x_z, w_ref[...]).astype(bf16)
            xt_ref[:, pl.ds(pl.multiple_of(zs * span, span), span)] = jnp.transpose(x_z)
        for i in range(2):
            b_out(i).start()
        to_lens.wait()
        seq_len = jnp.where(c == seq_core, lens_ref[seq], lgot_ref[seq])
        len_ref[...] = seq_len
        key_bias = jnp.where(lane_of((total, 1), 0) < seq_len[0:1, 0:1], 0.0, masked_fill)
        for p in range(pairs):
            k_all = jnp.concatenate(
                [qkv_ref[j, :, half + p * 128 : half + (p + 1) * 128] for j in range(blocks)], axis=0
            )
            for h, k_h in enumerate(key_heads(k_all, key_bias)):
                kh_ref[2 * p + h] = k_h
            for j in range(blocks):
                vt_ref[p * 128 : (p + 1) * 128, j * span : (j + 1) * span] = jnp.transpose(
                    qkv_ref[j, :, 2 * half + p * 128 : 2 * half + (p + 1) * 128]
                )
        outs = [
            pltpu.make_async_copy(src, dst, out_sem.at[n])
            for n, (src, dst) in enumerate(
                (
                    (xt_ref, xt_out), (w_ref, w_out), (qkv_ref, qkv_out), (attt_ref, attt_out),
                    (t_ref, t_out), (mid_ref, mid_out), (flat_ref, flat_out),
                )
            )
        ]
        for out in outs[:3]:
            out.start()
        later = lane_of((span, span), 0) > lane_of((span, span), 1)
        lane_row = lane_of((1, 128), 1)

        def a_out(j):
            return remote(
                att_ref.at[j], t_ref.at[seq, c], asend.at[j], arecv.at[seq, c], j, base + seq_core
            )

        def a_own(j):
            return pltpu.make_async_copy(att_ref.at[j], t_ref.at[seq, c], aloc)

        for j in [0] + list(range(blocks - 1, 0, -1)):
            n = (j + 1) * span

            def pair_step(p, _):
                first = pl.multiple_of(p * 128, 128)
                q = qkv_ref[j, :, pl.ds(first, 128)].astype(f32) * (HEAD**-0.5)
                out_t = []
                for h in range(2):
                    inside = (lane_row // HEAD) == h
                    spare = lane_row == (1 - h) * HEAD
                    q_h = jnp.where(inside, q, jnp.where(spare, 1.0, 0.0)).astype(bf16)
                    s = dot_nt(kh_ref[2 * p + h, :n], q_h)
                    last = jnp.where(later, masked_fill, s[n - span :])
                    s = last if j == 0 else jnp.concatenate([s[: n - span], last], axis=0)
                    top = jnp.max(s, axis=0, keepdims=True)
                    w = jnp.exp(s - top)
                    total_w = jnp.sum(w, axis=0, keepdims=True)
                    o_t = dot(vt_ref[pl.ds(pl.multiple_of(first + h * HEAD, HEAD), HEAD), :n], w.astype(bf16))
                    out_t.append(o_t / total_w)
                    lse_ref[pl.ds(2 * p + h, 1), pl.ds(j * span, span)] = top + jnp.log(total_w)
                o = jnp.concatenate(out_t, axis=0)
                attt_ref[pl.ds(first, 128), pl.ds(j * span, span)] = o
                att_ref[j, :, pl.ds(first, 128)] = jnp.transpose(o).astype(bf16)
                return 0

            lax.fori_loop(0, pairs, pair_step, 0)
            to_self = (z == j) & (c == seq_core)

            @pl.when(to_self)
            def _():
                a_own(j).start()

            @pl.when(jnp.logical_not(to_self))
            def _():
                a_out(j).start()

        outs[3].start()
        h_start(1)
        for s in range(seqs):
            for k in range(2):
                from_self = (2 * c + s == z) & (c == k)

                @pl.when(from_self)
                def _():
                    a_own(0).wait()

                @pl.when(jnp.logical_not(from_self))
                def _():
                    remote(att_ref.at[0], t_ref.at[s, k], asend.at[0], arecv.at[s, k], z, base).wait_recv()

        for s in range(seqs):
            r = pl.ds(s * span, span)
            branch = dot(t_ref[s, 0], wo_ref[0:half]) + dot(t_ref[s, 1], wo_ref[half:])
            v = hid_ref[s].reshape(span, width).astype(f32) + branch
            mid_ref[r, :] = v
            centered = v - jnp.mean(v, axis=-1, keepdims=True)
            inverse = lax.rsqrt(jnp.mean(centered * centered, axis=-1, keepdims=True) + epsilon)
            flat_ref[r, :] = (
                centered * inverse * g2_ref[...].reshape(1, width) + s2_ref[...].reshape(1, width)
            ).astype(bf16)
        for out in outs[4:]:
            out.start()
        logits = dot_nt(flat_ref[...], wr_ref[...])
        gate = jax.nn.sigmoid(
            jnp.sum(logits * onehot[:, :experts_n], axis=1, keepdims=True)
        )
        gate_ref[...] = gate
        rows_ref[...] = (
            dot(to_slots, flat_ref[...]).astype(bf16).reshape(columns, capacity, width)
        )
        from_slots = lane_of((tokens, slots), 1).astype(f32) == slot_ref[...]
        scales = jnp.sum(jnp.where(from_slots, valid * gate, 0.0), axis=0, keepdims=True)
        if cap_lanes != capacity:
            sc_ref[...] = jnp.zeros_like(sc_ref)
        for t in range(columns):
            sc_ref[t, :, 0:capacity] = jnp.broadcast_to(
                scales[:, t * capacity : (t + 1) * capacity], (8, capacity)
            )

        for out in outs:
            out.wait()
        for n, (to_z, to_e) in enumerate(column):
            remote(cown_ref, cgot_ref.at[to_z, lax.rem(to_e, 2)], ksend.at[n], krecv.at[to_z, lax.rem(to_e, 2)], z, sib).wait_recv()
            k_out(n, to_z, to_e).wait_send()
        cgot_ref[z, c] = cown_ref[...]
        tot = jnp.zeros((8, 128), f32)
        for zs in range(blocks):
            for k in range(2):
                tot = tot + cgot_ref[zs, k]
        cnt_ref[...] = tot
        c_own.wait()
        for t in plane:
            c_out(t).wait_send()
            remote(cots_ref.at[t], cote_ref.at[t], csend.at[t], crecv.at[t], z, e).wait_recv()
        for s in range(seqs):
            for k in range(2):

                @pl.when(jnp.logical_not((2 * c + s == z) & (c == k)))
                def _():
                    n_out(s, k).wait_send()

        for zs in [z] + others:
            n_sib(zs).wait_send()
        for j in range(blocks):

            @pl.when(jnp.logical_not((z == j) & (c == seq_core)))
            def _():
                a_out(j).wait_send()

        for i in range(2):
            b_out(i).wait()

        for i in range(2):
            src, dst = ((wi_ref, li_ref), (we_ref, lo_ref))[i]

            @pl.when(z < blocks - 1)
            def _():
                h_out(i, 1).wait_send()
                remote(src, dst.at[1], hsend.at[i, 1], hrecv.at[i, 1], z, e).wait_recv()

            @pl.when(z > 0)
            def _():
                h_out(i, -1).wait_send()
                remote(src, dst.at[0], hsend.at[i, 0], hrecv.at[i, 0], z, e).wait_recv()

    out_shapes = [
        ((width, total), bf16),
        ((width, 3 * half), bf16),
        ((blocks, span, 3 * half), bf16),
        ((half, total), f32),
        ((2 * pairs, total), f32),
        ((seqs, 2, span, half), bf16),
        ((tokens, width), f32),
        ((tokens, width), bf16),
        ((tokens, 1), f32),
        ((tokens, 1), f32),
        ((columns, capacity, width), bf16),
        ((columns, 8, cap_lanes), f32),
        ((columns, capacity, width), bf16),
        ((8, 128), jnp.int32),
        ((8, 128), f32),
        ((2, width, part), bf16),
        ((2, part, width), bf16),
        ((width, part), bf16),
        ((part, width), bf16),
    ]
    return pl.pallas_call(
        kernel,
        name="forward",
        out_shape=[jax.ShapeDtypeStruct(a, b) for a, b in out_shapes],
        in_specs=[VMEM] * 6 + [ANY] * 3 + [VMEM] * 3 + [SMEM] + [ANY] * 2,
        out_specs=[ANY] * 4 + [VMEM] + [ANY] * 3 + [VMEM] * 4 + [ANY] + [VMEM] * 2 + [ANY] * 4,
        scratch_shapes=[
            pltpu.VMEM((blocks, 2, hs, width), bf16),
            pltpu.VMEM((seqs, 2, hs, width), bf16),
            pltpu.VMEM((2 * pairs, total, 128), bf16),
            pltpu.VMEM((half, total), bf16),
            pltpu.VMEM((blocks, span, half), bf16),
            pltpu.VMEM((columns, capacity, width), bf16),
            pltpu.VMEM((seqs, 8, 128), jnp.int32),
            pltpu.VMEM((seqs, 8, 128), jnp.int32),
            pltpu.VMEM((8, 128), f32),
            pltpu.VMEM((blocks, 2, 8, 128), f32),
            DMA((3,)),
            DMA,
            DMA((seqs, 2)),
            DMA((blocks,)),
            DMA((blocks,)),
            DMA((blocks,)),
            DMA,
            DMA((blocks,)),
            DMA((seqs, 2)),
            DMA,
            DMA((columns,)),
            DMA((columns,)),
            DMA,
            DMA,
            DMA((2 * blocks - 1,)),
            DMA((blocks, 2)),
            DMA((2, 2)),
            DMA((2, 2)),
            DMA((2,)),
            DMA((2,)),
            pltpu.VMEM((width, total), bf16),
            pltpu.VMEM((width, 3 * half), bf16),
            pltpu.VMEM((blocks, span, 3 * half), bf16),
            pltpu.VMEM((half, total), f32),
            DMA((7,)),
            pltpu.VMEM((seqs, 2, span, half), bf16),
            pltpu.VMEM((tokens, width), f32),
            pltpu.VMEM((tokens, width), bf16),
        ],
        compiler_params=params(1),
    )(
        hidden.reshape(seqs, 2, hs, width), cotangent.reshape(tokens, width),
        gain_one, shift_one, gain_two, shift_two,
        w_query, w_key, w_value, w_output, w_router, ids, lengths, w_inner, w_outer,
    )


def slice_order(z):
    near = z + 1 - 2 * lax.rem(z, 2)
    across = jnp.where(z < 2, 2, 1)
    inner = (z > 0) & (z < 3)
    return [jnp.where(inner, across, near), jnp.where(inner, near, across), z, jnp.where(z < 2, 3, 0)]


def experts(
    rows, scales, cot, counts, w_inner, w_outer, sib_inner, sib_outer, near_inner, near_outer, blocks
):
    columns, capacity, width = rows.shape
    cap_lanes = scales.shape[2]
    total = columns * capacity
    part = w_inner.shape[1]
    block = 256
    count = total // block
    per = block // capacity
    assert blocks == 4 and columns == count * per

    def kernel(*refs):
        rows_ref, sc_ref, cot_ref, cnt_ref, wi_ref, we_ref, bi_ref, bo_ref, li_ref, lo_ref = refs[:10]
        back_ref, dots_ref, made_out, tot_ref, gi_out, go_out, ei_ref, eo_ref = refs[10:18]
        (
            x_ref, xt_ref, d_ref, scg_ref, cntg_ref, in_ref, out_ref, oacc, dacc, act_ref, dpre_ref,
            dr_ref, dots_own, sgi_ref, sgo_ref, ggi_ref, ggo_ref,
            xloc, xsend, xrecv, scsend, screcv, ksend, krecv, wloc, wsend, wrecv, vsend, vrecv,
            bloc, dsend, drecv, gsend, grecv, ssend, srecv, gi_ref, go_ref, keep_sem, made_ref, made_sem,
        ) = refs[18:]
        z, e, c, base = place()
        col = e // 2
        sib = base + 1 - c
        inner = (z > 0) & (z < blocks - 1)
        end = jnp.logical_not(inner)
        plane = [lax.rem(col + step, columns) for step in range(1, columns)]
        partners = column_partners(blocks, z, c, base) + [(z, 2 * t + c) for t in plane]
        greet(partners)

        def x_out(t):
            return remote(rows_ref.at[t], x_ref.at[col], xsend.at[t], xrecv.at[col], z, 2 * t + c)

        def sc_out(t):
            return remote(sc_ref.at[t], scg_ref.at[col], scsend.at[t], screcv.at[col], z, 2 * t + c)

        def cnt_out(t):
            return remote(cnt_ref, cntg_ref.at[col], ksend.at[t], krecv.at[col], z, 2 * t + c)

        x_own = pltpu.make_async_copy(rows_ref.at[col], x_ref.at[col], xloc)
        x_own.start()
        await_greetings(partners)
        for t in plane:
            sc_out(t).start()
            x_out(t).start()
            cnt_out(t).start()
        scg_ref[col] = sc_ref[col]
        cntg_ref[col] = cnt_ref[...]

        hop_two = lax.rem(z + 2, blocks)
        pair = z + 1 - 2 * lax.rem(z, 2)

        lo_half, hi_half = pl.ds(0, part), pl.ds(part, part)

        def views(s, which):
            return (in_ref.at[s, :, which], out_ref.at[s, which])

        sources = ((wi_ref, we_ref), (bi_ref, bo_ref))

        def w_own(i, k):
            return pltpu.make_async_copy(
                sources[k][i], views(z, (lo_half, hi_half)[k])[i], wloc.at[i, k]
            )

        def beside(side):
            return z - 1 if side == 0 else z + 1

        nears = (li_ref, lo_ref)

        def w_near(i, side):
            return pltpu.make_async_copy(nears[i].at[side], views(beside(side), lo_half)[i], wloc.at[2 + i, side])

        def w_near_sib(i, side):
            s = beside(side)
            return remote(nears[i].at[side], views(s, hi_half)[i], vsend.at[i, s], vrecv.at[i, s], z, sib)

        def w_pass(i, side):
            s = beside(side)
            return remote(
                nears[i].at[side], views(s, lo_half)[i], wsend.at[2 + i, side], wrecv.at[i, s], beside(1 - side), e
            )

        def w_got(i, s):
            return remote(views(s, lo_half)[i], views(s, lo_half)[i], wsend.at[0, 0], wrecv.at[i, s], z, e)

        def w_sib(i, s):
            return remote(views(s, lo_half)[i], views(s, hi_half)[i], vsend.at[i, s], vrecv.at[i, s], z, sib)

        def w_sib_got(i, s):
            return remote(views(s, lo_half)[i], views(s, hi_half)[i], vsend.at[i, z], vrecv.at[i, s], z, sib)

        def w_last(i):
            s = hop_two
            to = jnp.where(z == 1, 0, blocks - 1)
            return remote(views(s, lo_half)[i], views(s, lo_half)[i], wsend.at[4 + i, 0], wrecv.at[i, s], to, e)

        def has(side):
            return z > 0 if side == 0 else z < blocks - 1

        for i in range(2):
            for side in range(2):

                @pl.when(inner)
                def _():
                    w_pass(i, side).start()

        for i in range(2):
            for side in range(2):

                @pl.when(has(side))
                def _():
                    w_near(i, side).start()
                    w_near_sib(i, side).start()

        for i in range(2):
            for k in range(2):
                w_own(i, k).start()

        order = slice_order(z)
        far = order[3]
        oacc[...] = jnp.zeros_like(oacc)
        dacc[...] = jnp.zeros_like(dacc)
        first_block = col // per

        def at_block(b):
            return pl.ds(pl.multiple_of(b * per, per), per)

        def row_step(s, b, fresh):
            x_b = x_ref[at_block(b)].reshape(block, width)
            r = pl.ds(pl.multiple_of(b * block, block), block)
            if fresh:
                row = jnp.concatenate(
                    [scg_ref[b * per + i, :, 0:capacity] for i in range(per)], axis=1
                )
                column = jnp.transpose(row)[:, 0:1]
                cots = cot_ref[at_block(b)].reshape(block, width).astype(f32)
                d_ref[r, :] = (column * cots).astype(bf16)
            pre = dot(x_b, in_ref[s])
            cdf = 0.5 * (1.0 + lax.erf(pre * (0.5**0.5)))
            act = (pre * cdf).astype(bf16)
            slope = cdf + pre * (jnp.exp(-0.5 * pre * pre) * ((2 * jnp.pi) ** -0.5))
            d_act = dot_nt(d_ref[r, :], out_ref[s])
            d_pre = (d_act * slope).astype(bf16)
            act_ref[r, :] = act
            dpre_ref[r, :] = d_pre
            oacc[r, :] += dot(act, out_ref[s])
            dacc[r, :] += dot_nt(d_pre, in_ref[s])

        def grads(s):
            g_inner = dot(xt_ref[...], dpre_ref[...])
            gi_ref[s] = g_inner[:, :part].astype(bf16)
            sgi_ref[s] = g_inner[:, part:].astype(bf16)
            g_outer = dot_tn(act_ref[...], d_ref[...])
            go_ref[s] = g_outer[:part].astype(bf16)
            sgo_ref[s] = g_outer[part:].astype(bf16)
            for i in range(2):
                g_sib(i, s).start()

        def g_keep(i, n):
            return pltpu.make_async_copy(
                (gi_ref, go_ref)[i].at[order[2 + n]], (gi_out, go_out)[i].at[n], keep_sem.at[i, n]
            )

        def g_sib(i, s):
            src, dst = ((sgi_ref, ggi_ref), (sgo_ref, ggo_ref))[i]
            return remote(src.at[s], dst.at[s], gsend.at[i, s], grecv.at[i, s], z, sib)

        def join(s):
            for i, (total_ref, got_ref) in enumerate(((gi_ref, ggi_ref), (go_ref, ggo_ref))):
                g_sib(i, s).wait_recv()
                total_ref[s] = (total_ref[s].astype(f32) + got_ref[s].astype(f32)).astype(bf16)

        def s_out(i, s):
            src, dst = ((gi_ref, ei_ref), (go_ref, eo_ref))[i]
            return remote(src.at[s], dst.at[z], ssend.at[i, s], srecv.at[i, z], s, e)

        def block_at(m):
            return lax.rem(first_block + count - m, count)

        for i in range(2):
            for side in range(2):

                @pl.when(has(side))
                def _():
                    w_near(i, side).wait()
                    w_sib_got(i, beside(side)).wait_recv()

        for m in range(count):
            b = block_at(m)
            for i in range(per):
                t = b * per + i

                @pl.when(t == col)
                def _():
                    x_own.wait()

                @pl.when(t != col)
                def _():
                    remote(sc_ref.at[0], scg_ref.at[t], scsend.at[t], screcv.at[t], z, e).wait_recv()
                    remote(rows_ref.at[0], x_ref.at[t], xsend.at[t], xrecv.at[t], z, e).wait_recv()

            row_step(order[0], b, True)
        def hand_on(i):
            w_got(i, hop_two).wait_recv()
            w_sib(i, hop_two).start()

            @pl.when(inner)
            def _():
                w_last(i).start()

        hand_on(0)
        xt_ref[...] = jnp.transpose(x_ref[...].reshape(total, width))
        grads(order[0])

        @pl.when(end)
        def _():
            hand_on(1)
            for i in range(2):
                w_sib_got(i, hop_two).wait_recv()

        def loop(s, start):
            def body(b, _):
                row_step(s, b, False)
                return 0

            lax.fori_loop(start, count, body, 0)

        row_step(order[1], 0, False)
        join(order[0])
        for i in range(2):
            s_out(i, order[0]).start()
        loop(order[1], 1)

        @pl.when(inner)
        def _():
            hand_on(1)

        grads(order[1])
        for i in range(2):
            for k in range(2):
                w_own(i, k).wait()
        row_step(order[2], 0, False)
        join(order[1])
        for i in range(2):
            s_out(i, order[1]).start()
        loop(order[2], 1)

        @pl.when(inner)
        def _():
            for i in range(2):
                w_sib_got(i, hop_two).wait_recv()

        @pl.when(end)
        def _():
            for i in range(2):
                w_got(i, far).wait_recv()
                w_sib(i, far).start()

        grads(order[2])

        @pl.when(end)
        def _():
            for i in range(2):
                w_sib_got(i, far).wait_recv()

        def d_out(t):
            return remote(dr_ref.at[t], back_ref.at[col], dsend.at[0, t], drecv.at[0, col], z, 2 * t + c)

        def dots_out(t):
            return remote(dots_own.at[t], dots_ref.at[col], dsend.at[1, t], drecv.at[1, col], z, 2 * t + c)

        def made_copy(m):
            at = at_block(block_at(m))
            return pltpu.make_async_copy(made_ref.at[at], made_out.at[at], made_sem.at[m])

        b_own = pltpu.make_async_copy(dr_ref.at[col], back_ref.at[col], bloc)
        for m in list(range(1, count)) + [0]:
            b = block_at(m)
            row_step(order[3], b, False)
            if m == 1:
                join(order[2])
                for i in range(2):
                    g_keep(i, 0).start()
            r = pl.ds(pl.multiple_of(b * block, block), block)
            made = oacc[r, :].astype(bf16)
            made_ref[at_block(b)] = made.reshape(per, capacity, width)
            made_copy(m).start()
            dr_ref[at_block(b)] = dacc[r, :].astype(bf16).reshape(per, capacity, width)
            cots = cot_ref[at_block(b)].reshape(block, width).astype(f32)
            sums = jnp.sum(cots * made.astype(f32), axis=1, keepdims=True)
            row = jnp.transpose(jnp.broadcast_to(sums, (block, 128)))[0:8]
            for i in range(per):
                t = b * per + i
                if cap_lanes != capacity:
                    dots_own[t] = jnp.zeros((8, cap_lanes), f32)
                dots_own[t, :, 0:capacity] = row[:, i * capacity : (i + 1) * capacity]

                @pl.when(t == col)
                def _():
                    b_own.start()
                    dots_ref[t] = dots_own[t]

                @pl.when(t != col)
                def _():
                    d_out(t).start()
                    dots_out(t).start()

        grads(order[3])
        join(order[3])
        for i in range(2):
            g_keep(i, 1).start()

        for t in plane:
            x_out(t).wait_send()
            sc_out(t).wait_send()
            cnt_out(t).wait_send()
            remote(cnt_ref, cntg_ref.at[t], ksend.at[t], krecv.at[t], z, e).wait_recv()
        tot = cntg_ref[0]
        for t in range(1, columns):
            tot = tot + cntg_ref[t]
        tot_ref[...] = tot
        for i in range(2):
            for side in range(2):

                @pl.when(inner)
                def _():
                    w_pass(i, side).wait_send()

            w_sib(i, hop_two).wait_send()

            @pl.when(end)
            def _():
                w_sib(i, far).wait_send()

            for n in range(blocks):
                g_sib(i, n).wait_send()
            for n in range(2):
                g_keep(i, n).wait()
            s_out(i, order[0]).wait_send()
            s_out(i, order[1]).wait_send()
            got = (ei_ref, eo_ref)[i]

            def arrived(zs):
                return remote(got.at[0], got.at[zs], ssend.at[i, 0], srecv.at[i, zs], z, e)

            arrived(pair).wait_recv()

            @pl.when(inner)
            def _():
                w_last(i).wait_send()
                for k in range(2):
                    arrived(lax.rem(2 * (z // 2) + 2 + k, blocks)).wait_recv()

        for i in range(2):
            for side in range(2):

                @pl.when(has(side))
                def _():
                    w_near_sib(i, side).wait_send()

        for m in range(count):
            made_copy(m).wait()
        b_own.wait()
        for t in plane:
            d_out(t).wait_send()
            dots_out(t).wait_send()
            remote(dr_ref.at[0], back_ref.at[t], dsend.at[0, t], drecv.at[0, t], z, e).wait_recv()
            remote(dots_own.at[0], dots_ref.at[t], dsend.at[1, t], drecv.at[1, t], z, e).wait_recv()

    out_shapes = [
        ((columns, capacity, width), bf16),
        ((columns, 8, cap_lanes), f32),
        ((columns, capacity, width), bf16),
        ((8, 128), f32),
        ((2, width, part), bf16),
        ((2, part, width), bf16),
        ((blocks, width, part), bf16),
        ((blocks, part, width), bf16),
    ]
    return pl.pallas_call(
        kernel,
        name="experts",
        out_shape=[jax.ShapeDtypeStruct(a, b) for a, b in out_shapes],
        in_specs=[VMEM] * 4 + [ANY] * 6,
        out_specs=[ANY, VMEM, ANY, VMEM] + [ANY] * 4,
        scratch_shapes=[
            pltpu.VMEM((columns, capacity, width), bf16),
            pltpu.VMEM((width, total), bf16),
            pltpu.VMEM((total, width), bf16),
            pltpu.VMEM((columns, 8, cap_lanes), f32),
            pltpu.VMEM((columns, 8, 128), f32),
            pltpu.VMEM((blocks, width, 2 * part), bf16),
            pltpu.VMEM((blocks, 2 * part, width), bf16),
            pltpu.VMEM((total, width), f32),
            pltpu.VMEM((total, width), f32),
            pltpu.VMEM((total, 2 * part), bf16),
            pltpu.VMEM((total, 2 * part), bf16),
            pltpu.VMEM((columns, capacity, width), bf16),
            pltpu.VMEM((columns, 8, cap_lanes), f32),
            pltpu.VMEM((blocks, width, part), bf16),
            pltpu.VMEM((blocks, part, width), bf16),
            pltpu.VMEM((blocks, width, part), bf16),
            pltpu.VMEM((blocks, part, width), bf16),
            DMA,
            DMA((columns,)),
            DMA((columns,)),
            DMA((columns,)),
            DMA((columns,)),
            DMA((columns,)),
            DMA((columns,)),
            DMA((4, 2)),
            DMA((6, 2)),
            DMA((2, blocks)),
            DMA((2, blocks)),
            DMA((2, blocks)),
            DMA,
            DMA((2, columns)),
            DMA((2, columns)),
            DMA((2, blocks)),
            DMA((2, blocks)),
            DMA((2, blocks)),
            DMA((2, blocks)),
            pltpu.VMEM((blocks, width, part), bf16),
            pltpu.VMEM((blocks, part, width), bf16),
            DMA((2, 2)),
            pltpu.VMEM((columns, capacity, width), bf16),
            DMA((count,)),
        ],
        compiler_params=params(2),
    )(rows, scales, cot, counts, w_inner, w_outer, sib_inner, sib_outer, near_inner, near_outer)


class PieceSum:
    def __init__(self, at, part, got1, got2, got3, gotr, full, sem, rsem, zsem, zrsem, order, finish):
        self.at, self.part, self.full = at, part, full
        self.got1, self.got2, self.got3, self.gotr = got1, got2, got3, gotr
        self.sem, self.rsem, self.zsem, self.zrsem = sem, rsem, zsem, zrsem
        z, e, c, bit, mate, blocks, sib = at
        self.first, self.second = order
        self.finish = finish
        self.rest = len(bit) - 2

    def swap(self, n, src, dst, e):
        return remote(src, dst, self.sem.at[n], self.rsem.at[n], self.at[0], e)

    def halves(self):
        z, e, c, bit, mate, blocks, sib = self.at
        return self.swap(0, self.part.at[1 - bit[self.first]], self.got1, mate[self.first])

    def quarters(self):
        z, e, c, bit, mate, blocks, sib = self.at
        b1, b2 = bit[self.first], bit[self.second]
        return self.swap(1, self.part.at[b1, 1 - b2], self.got2, mate[self.second])

    def to_z(self, zt):
        z, e, c, bit, mate, blocks, sib = self.at
        b1, b2 = bit[self.first], bit[self.second]
        return remote(
            self.part.at[b1, b2, zt], self.got3.at[z], self.zsem.at[0, zt], self.zrsem.at[0, z], zt, e
        )

    def own(self):
        z, e, c, bit, mate, blocks, sib = self.at
        return self.full.at[c, bit[self.first], bit[self.second], z]

    def back_z(self, zt):
        z, e, c, bit, mate, blocks, sib = self.at
        return remote(self.own(), self.own(), self.zsem.at[1, zt], self.zrsem.at[1, z], zt, e)

    def back_quarter(self):
        z, e, c, bit, mate, blocks, sib = self.at
        at = self.full.at[c, bit[self.first], bit[self.second]]
        return self.swap(2, at, at, mate[self.second])

    def back_half(self):
        z, e, c, bit, mate, blocks, sib = self.at
        at = self.full.at[c, bit[self.first]]
        return self.swap(3, at, at, mate[self.first])

    def to_sibling(self):
        z, e, c, bit, mate, blocks, sib = self.at
        return self.swap(4, self.full.at[c], self.full.at[c], sib)

    def step(self, n):
        z, e, c, bit, mate, blocks, sib = self.at
        b1, b2 = bit[self.first], bit[self.second]
        others = [lax.rem(z + step, blocks) for step in range(1, blocks)]
        if n == 0:
            self.halves().start()
        elif n == 1:
            self.halves().wait()
            self.part[b1] = (self.part[b1].astype(f32) + self.got1[...].astype(f32)).astype(bf16)
            self.quarters().start()
        elif n == 2:
            self.quarters().wait()
            self.part[b1, b2] = (self.part[b1, b2].astype(f32) + self.got2[...].astype(f32)).astype(bf16)
            for zt in others:
                self.to_z(zt).start()
        elif n == 3:
            for zs in others:
                remote(
                    self.got3.at[0], self.got3.at[zs], self.zsem.at[0, zs], self.zrsem.at[0, zs], z, e
                ).wait_recv()
            for zt in others:
                self.to_z(zt).wait_send()
            self.got3[z] = self.part[b1, b2, z]
            total = self.got3[0].astype(f32)
            for j in range(1, blocks):
                total = total + self.got3[j].astype(f32)
            own = self.own()
            own[...] = total.astype(bf16)
            for r in range(self.rest):
                copy = self.swap(5 + r, own, self.gotr.at[r], mate[2 + r])
                copy.start()
                copy.wait()
                own[...] = (own[...].astype(f32) + self.gotr[r].astype(f32)).astype(bf16)
            for zt in others:
                self.back_z(zt).start()
        elif n == 4:
            for zs in others:
                at = self.full.at[c, b1, b2, zs]
                remote(at, at, self.zsem.at[1, zs], self.zrsem.at[1, zs], z, e).wait_recv()
            for zt in others:
                self.back_z(zt).wait_send()
            self.back_quarter().start()
        elif n == 5:
            self.back_quarter().wait()
            self.back_half().start()
        elif n == 6:
            self.back_half().wait()
            self.to_sibling().start()
        elif n == 7:
            self.to_sibling().wait()
            for k in range(2):
                self.finish(k, self.full[k])

    @staticmethod
    def scratch(blocks, piece, lanes, rest):
        return [
            pltpu.VMEM((2, 2, blocks, piece, lanes), bf16),
            pltpu.VMEM((2, blocks, piece, lanes), bf16),
            pltpu.VMEM((blocks, piece, lanes), bf16),
            pltpu.VMEM((blocks, piece, lanes), bf16),
            pltpu.VMEM((max(1, rest), piece, lanes), bf16),
            pltpu.VMEM((2, 2, 2, blocks, piece, lanes), bf16),
            DMA((5 + rest,)),
            DMA((5 + rest,)),
            DMA((2, blocks)),
            DMA((2, blocks)),
        ]


def backward(
    rows_t, weights, qkv, att_t, lse, length, attended, middle, flat, gate, slot, ids, lengths, cotangent,
    back, dots, counts, made, hidden, gain_one, gain_two, w_output, w_router, g_inner, g_outer, e_inner, e_outer,
    experts_n,
):
    width, total = rows_t.shape
    half = weights.shape[1] // 3
    pairs = half // 128
    seqs, _, span, _ = attended.shape
    blocks = total // span
    columns, capacity, _ = back.shape
    slots = columns * capacity
    tokens = seqs * span
    hs = span // 2
    scale = HEAD**-0.5
    part = g_inner.shape[2]
    bits = columns.bit_length() - 1
    assert columns == 1 << bits and bits >= 2 and blocks == 4
    rest = bits - 2
    small_rows = -(-(5 + experts_n) // 8) * 8
    out_piece, pair_piece = width // (4 * blocks), 3 * width // (4 * blocks)
    n_sum = 10

    def kernel(*refs):
        (
            xt_in, w_in, qkv_in, attt_in, lse_ref, len_ref, t_in, mid_in, flat_in, gate_ref, slot_ref, ids_ref,
            lens_ref, cot_in, back_in, dots_ref, cnt_ref, made_ref, hid_in, g1_ref, g2_ref, wo_in, wr_ref,
            gi_ref, go_ref, ei_ref, eo_ref,
        ) = refs[:27]
        grads_out, sums_ref, fi_out, fo_out, gh_out, y_out = refs[27:33]
        (
            do_ref, dqkv_ref, kt_ref, dk_ref, dv_ref, dn_ref, dsib_ref, dsum_ref, dnt_ref,
            zi, zo, ci, co, osib, sgot, szgot, datt_ref, op_ref, dmid_ref, mg_ref,
            loc_sem, dsend, drecv, rloc, rsend, rrecv,
            nsend, nrecv, ssend, srecv, osend, orecv, tsend, trecv, tzsend, tzrecv, msend, mrecv,
            back_ref, mid_ref, cot_ref, flat_ref, wo_ref, t_ref, qkv_ref, attt_ref, xt_ref, w_ref, hid_ref, load_sem,
            grads_ref, fi_ref, fo_ref, gh_ref, y_ref, out_sem,
        ) = refs[33:89]
        sums_scratch = refs[89:]
        z, e, c, base = place()
        col = e // 2
        sib = base + 1 - c
        seq_core, seq = z // 2, lax.rem(z, 2)
        bit = [lax.rem(col // (1 << i), 2) for i in range(bits)]
        mate = [2 * (col + (1 - 2 * bit[i]) * (1 << i)) + c for i in range(bits)]
        others = [lax.rem(z + step, blocks) for step in range(1, blocks)]
        plane = [lax.rem(col + step, columns) for step in range(1, columns)]
        inner = (z > 0) & (z < blocks - 1)
        order = slice_order(z)
        across = [lax.rem(2 * (z // 2) + 2 + k, blocks) for k in range(2)]
        partners = column_partners(blocks, z, c, base) + [(z, 2 * t + c) for t in plane]
        greet(partners)
        outs = [
            pltpu.make_async_copy(src, dst, out_sem.at[n])
            for n, (src, dst) in enumerate(
                ((gh_ref, gh_out), (y_ref, y_out), (fi_ref, fi_out), (fo_ref, fo_out))
                + tuple((grads_ref.at[m], grads_out.at[m]) for m in range(4))
            )
        ]
        loads = [
            pltpu.make_async_copy(src, dst, load_sem.at[n])
            for n, (src, dst) in enumerate(
                (
                    (back_in, back_ref), (mid_in, mid_ref), (cot_in, cot_ref), (flat_in, flat_ref), (wo_in, wo_ref),
                    (t_in, t_ref), (qkv_in, qkv_ref), (attt_in, attt_ref), (xt_in, xt_ref), (w_in, w_ref), (hid_in, hid_ref),
                )
            )
        ]
        for load in loads[:6]:
            load.start()

        def m_out(t):
            return remote(made_ref.at[t], mg_ref.at[col], msend.at[t], mrecv.at[col], z, 2 * t + c)

        m_own = pltpu.make_async_copy(made_ref.at[col], mg_ref.at[col], loc_sem.at[2])

        far = order[3]
        pair = z + 1 - 2 * lax.rem(z, 2)

        def r_load(i, src, s, slot):
            return pltpu.make_async_copy(src.at[s], (zi, zo)[i].at[slot], rloc.at[i, slot])

        def r_chain(i):
            src, dst = ((gi_ref, ci), (go_ref, co))[i]
            return remote(src.at[1], dst, rsend.at[i], rrecv.at[i], pair, e)

        def r_sum(i):
            src, dst = ((zi, ci), (zo, co))[i]
            return remote(src.at[0], dst, rsend.at[i], rrecv.at[i], far, e)

        def chain(i):
            @pl.when(inner)
            def _():
                buf, got = ((zi, ci), (zo, co))[i]
                r_load(i, (gi_ref, go_ref)[i], 1, 0).wait()
                r_chain(i).wait_recv()
                buf[0] = (buf[0].astype(f32) + got[...].astype(f32)).astype(bf16)
                r_sum(i).start()

        onehot = one_hot(ids_ref, seqs, span)
        valid = valid_rows(lens_ref, z, seqs, span)
        from_slots = lane_of((tokens, slots), 1).astype(f32) == slot_ref[...]
        dots_row = jnp.concatenate([dots_ref[t, 0:1, 0:capacity] for t in range(columns)], axis=1)
        dot_rows = jnp.sum(jnp.where(from_slots, dots_row, 0.0), axis=1, keepdims=True)
        picks = from_slots.astype(f32).astype(bf16)
        for load in loads[:5]:
            load.wait()
        for load in loads[6:]:
            load.start()
        m_own.start()
        for i in range(2):

            @pl.when(jnp.logical_not(inner))
            def _():
                r_load(i, (gi_ref, go_ref)[i], 0, 0).start()

            @pl.when(inner)
            def _():
                r_load(i, (gi_ref, go_ref)[i], 1, 0).start()

            r_load(i, (ei_ref, eo_ref)[i], pair, 1).start()

        d_rows = dot(picks, back_ref[...].reshape(slots, width))
        count_row = cnt_ref[0:1]
        mean_load = jnp.sum(count_row, axis=1, keepdims=True) / experts_n
        ratio_rows = jnp.sum(onehot * ((count_row - mean_load) / mean_load), axis=1, keepdims=True)
        gates = gate_ref[...]
        d_gate = valid * (dot_rows + balance_weight * ratio_rows)
        d_logits = (onehot * (d_gate * gates * (1.0 - gates))).astype(bf16)
        router_t = dot_tn(d_logits, flat_ref[...])
        balance_part = jnp.sum(valid * gates * ratio_rows, axis=0, keepdims=True) / jnp.sum(
            count_row, axis=1, keepdims=True
        )
        gain_sum = jnp.zeros((1, width), f32)
        shift_sum = jnp.zeros((1, width), f32)
        for s in range(seqs):
            lo, hi = s * span, (s + 1) * span
            v = mid_ref[lo:hi]
            centered = v - jnp.mean(v, axis=-1, keepdims=True)
            inverse = lax.rsqrt(jnp.mean(centered * centered, axis=-1, keepdims=True) + epsilon)
            unit = centered * inverse
            dy = d_rows[lo:hi] + dot(d_logits[lo:hi, :experts_n], wr_ref[...])
            gain_sum = gain_sum + jnp.sum(dy * unit, axis=0, keepdims=True)
            shift_sum = shift_sum + jnp.sum(dy, axis=0, keepdims=True)
            du = dy * g2_ref[...].reshape(1, width)
            dx = inverse * (
                du
                - jnp.mean(du, axis=-1, keepdims=True)
                - unit * jnp.mean(du * unit, axis=-1, keepdims=True)
            )
            dmid_ref[lo:hi] = cot_ref[lo:hi].astype(f32) + dx
            d_branch = dmid_ref[lo:hi].astype(bf16)
            for k in range(2):
                datt_ref[s, k] = dot_nt(d_branch, wo_ref[k * half : (k + 1) * half]).astype(bf16)

        at = (z, e, c, bit, mate, blocks, sib)

        def finish_out(k, g):
            grads_ref[3, :, k * half : (k + 1) * half] = g.reshape(width, half)

        def finish_pair(p):
            def finish(k, g):
                g = g.reshape(3, width, 128)
                for m in range(3):
                    grads_ref[m, :, k * half + p * 128 : k * half + (p + 1) * 128] = g[m]

            return finish

        out_sum = PieceSum(at, *sums_scratch[:n_sum], (0, 1), finish_out)
        pair_sums = [
            PieceSum(
                at,
                *sums_scratch[n_sum * (p + 1) : n_sum * (p + 2)],
                (1, 0) if p % 2 == 0 else (0, 1),
                finish_pair(p),
            )
            for p in range(pairs)
        ]

        await_greetings(partners)

        def d_out(s, k):
            return remote(
                datt_ref.at[s, k], do_ref.at[z], dsend.at[s, k], drecv.at[z], 2 * c + s, base + k
            )

        def d_own(s, k):
            return pltpu.make_async_copy(datt_ref.at[s, k], do_ref.at[z], loc_sem.at[0])

        for k, s in ((0, 0), (0, 1), (1, 1), (1, 0)):
            if True:
                to_self = (2 * c + s == z) & (c == k)

                @pl.when(to_self)
                def _():
                    d_own(s, k).start()

                @pl.when(jnp.logical_not(to_self))
                def _():
                    d_out(s, k).start()

        @pl.when(jnp.logical_not(inner))
        def _():
            r_chain(0).start()

        sums_ref[...] = jnp.zeros_like(sums_ref)
        sums_ref[2:3] = gain_sum
        sums_ref[3:4] = shift_sum
        sums_ref[4 : 4 + experts_n] = router_t[0:experts_n]
        sums_ref[4 + experts_n : 5 + experts_n] = jnp.broadcast_to(balance_part, (1, width))
        d_branch = dmid_ref[...].astype(bf16)
        loads[5].wait()
        for k in range(2):
            att_k = jnp.concatenate([t_ref[s, k] for s in range(seqs)], axis=0)
            made_k = dot_tn(att_k, d_branch).astype(bf16)
            op_ref[0, k * half : (k + 1) * half] = made_k[:, :half]
            op_ref[1, k * half : (k + 1) * half] = made_k[:, half:]
        o_first = remote(op_ref.at[1 - c], osib, osend, orecv, z, sib)
        o_first.start()
        o_first.wait()
        out_sum.part[...] = (op_ref[c].astype(f32) + osib[...].astype(f32)).astype(bf16).reshape(
            2, 2, blocks, out_piece, half
        )
        out_sum.step(0)
        out_sum.step(1)

        def d_got(j):
            mine = (z == j) & (c == seq_core)

            @pl.when(mine)
            def _():
                d_own(0, 0).wait()

            @pl.when(jnp.logical_not(mine))
            def _():
                remote(datt_ref.at[0, 0], do_ref.at[j], dsend.at[0, 0], drecv.at[j], z, base).wait_recv()

        for load in loads[6:]:
            load.wait()

        key_bias = jnp.where(lane_of((total, 1), 0) < len_ref[0:1, 0:1], 0.0, masked_fill)
        lane = lane_of((1, 128), 1)
        later = lax.broadcasted_iota(jnp.int32, (span, span), 0) > lax.broadcasted_iota(
            jnp.int32, (span, span), 1
        )

        def pair_step(p):
            first = p * 128
            k_all = qkv_ref[:, pl.ds(half + first, 128)]
            kt_ref[...] = jnp.transpose(k_all)
            v_all = qkv_ref[:, pl.ds(2 * half + first, 128)]
            k_heads = key_heads(k_all, key_bias)
            dk_ref[...] = jnp.zeros_like(dk_ref)
            dv_ref[...] = jnp.zeros_like(dv_ref)
            for j in range(blocks):
                n = (j + 1) * span
                r = pl.ds(j * span, span)
                if p == 0:
                    d_got(j)
                q = qkv_ref[r, pl.ds(first, 128)].astype(f32) * scale
                d_o = do_ref[j, :, pl.ds(first, 128)].astype(f32)
                prod_t = jnp.transpose(d_o) * attt_ref[pl.ds(first, 128), r]
                dq_t = []
                for h in range(2):
                    inside = (lane // HEAD) == h
                    spare = lane == (1 - h) * HEAD
                    q_h = jnp.where(inside, q, jnp.where(spare, 1.0, 0.0)).astype(bf16)
                    q_only = jnp.where(inside, q, 0.0).astype(bf16)
                    do_h = jnp.where(inside, d_o, 0.0).astype(bf16)
                    delta = jnp.sum(prod_t[h * HEAD : (h + 1) * HEAD], axis=0, keepdims=True)
                    s = dot_nt(k_heads[h][:n], q_h)
                    last = jnp.where(later, masked_fill, s[n - span :])
                    s = last if j == 0 else jnp.concatenate([s[: n - span], last], axis=0)
                    w = jnp.exp(s - lse_ref[pl.ds(2 * p + h, 1), r])
                    d_w = dot_nt(v_all[:n], do_h)
                    d_s = (w * (d_w - delta)).astype(bf16)
                    dv_ref[:n] += dot(w.astype(bf16), do_h)
                    dk_ref[:n] += dot(d_s, q_only)
                    dq_t.append(dot(kt_ref[h * HEAD : (h + 1) * HEAD, :n], d_s))
                dq = jnp.transpose(jnp.concatenate(dq_t, axis=0)) * scale
                dqkv_ref[r, pl.ds(first, 128)] = dq.astype(bf16)
            dqkv_ref[:, pl.ds(half + first, 128)] = dk_ref[...].astype(bf16)
            dqkv_ref[:, pl.ds(2 * half + first, 128)] = dv_ref[...].astype(bf16)
            joined = jnp.concatenate(
                [dqkv_ref[:, pl.ds(m * half + first, 128)] for m in range(3)], axis=1
            )
            grads = dot(xt_ref[...], joined).astype(bf16)
            pair_sums[p].part[...] = jnp.concatenate(
                [grads[:, m * 128 : (m + 1) * 128] for m in range(3)], axis=0
            ).reshape(2, 2, blocks, pair_piece, 128)

        state = {out_sum: 2}

        def advance(*chosen):
            for one in chosen or list(state):
                n = state.setdefault(one, 0)
                if n <= 7:
                    one.step(n)
                    state[one] = n + 1

        plan = ([out_sum], [pair_sums[0]], [pair_sums[0]]) if pairs == 3 else ([],) * pairs
        for p in range(pairs):
            pair_step(p)
            if plan[p]:
                advance(*plan[p])
            advance(pair_sums[p])
            if p == 1:
                chain(0)

        for j in range(blocks):
            r = pl.ds(j * span, span)
            dn_ref[j] = dot_nt(dqkv_ref[r, :], w_ref[...]).astype(bf16).reshape(2, hs, width)

        def n_sib(j):
            return remote(dn_ref.at[j, 1 - c], dsib_ref.at[j], nsend.at[j], nrecv.at[j], z, sib)

        def n_out(j):
            return remote(
                dsum_ref.at[j], dnt_ref.at[seq, c], ssend.at[j], srecv.at[seq, c], j, base + seq_core
            )

        def n_own():
            return pltpu.make_async_copy(dsum_ref.at[z], dnt_ref.at[seq, c], loc_sem.at[1])

        n_order = others[1:2] + others[0:1] + others[2:] + [z]
        for j in n_order:
            n_sib(j).start()
        advance(*pair_sums[1:2])
        for i, j in enumerate(n_order):
            n_sib(j).wait_recv()
            dsum_ref[j] = (dn_ref[j, c].astype(f32) + dsib_ref[j].astype(f32)).astype(bf16)
            if i < blocks - 1:
                n_out(j).start()
            else:

                @pl.when(seq_core == c)
                def _():
                    n_own().start()

                @pl.when(seq_core != c)
                def _():
                    n_out(j).start()

        @pl.when(jnp.logical_not(inner))
        def _():
            r_chain(1).start()

        advance(*pair_sums[1:])
        for t in plane:
            m_out(t).start()
        advance(*pair_sums[2:])
        advance(out_sum, *pair_sums[:1])
        for s in range(seqs):
            for k in range(2):
                from_self = (2 * c + s == z) & (c == k)

                @pl.when(jnp.logical_not(from_self))
                def _():
                    remote(
                        dsum_ref.at[0], dnt_ref.at[s, k], ssend.at[0], srecv.at[s, k], z, base
                    ).wait_recv()

                @pl.when(from_self)
                def _():
                    n_own().wait()

        gains = g1_ref[...].reshape(1, width)
        gain_sum = jnp.zeros((1, width), f32)
        shift_sum = jnp.zeros((1, width), f32)
        for s in range(seqs):
            for k in range(2):
                v = hid_ref[s, k].astype(f32)
                centered = v - jnp.mean(v, axis=-1, keepdims=True)
                inverse = lax.rsqrt(jnp.mean(centered * centered, axis=-1, keepdims=True) + epsilon)
                unit = centered * inverse
                dy = dnt_ref[s, k].astype(f32)
                gain_sum = gain_sum + jnp.sum(dy * unit, axis=0, keepdims=True)
                shift_sum = shift_sum + jnp.sum(dy, axis=0, keepdims=True)
                du = dy * gains
                dx = inverse * (
                    du
                    - jnp.mean(du, axis=-1, keepdims=True)
                    - unit * jnp.mean(du * unit, axis=-1, keepdims=True)
                )
                gh_ref[s, k] = dmid_ref[(2 * s + k) * hs : (2 * s + k + 1) * hs] + dx
        outs[0].start()

        sums_ref[0:1] = gain_sum
        sums_ref[1:2] = shift_sum

        def t_swap(n, te):
            return remote(sums_ref, sgot.at[n], tsend.at[n], trecv.at[n], z, te)

        partners = [sib] + mate
        for n, te in enumerate(partners):
            copy = t_swap(n, te)
            copy.start()
            if n in (1, 2):
                advance()
            if n == 1:
                chain(1)
            copy.wait()
            sums_ref[...] = sums_ref[...] + sgot[n]

        def t_z(zt):
            return remote(sums_ref, szgot.at[z], tzsend.at[zt], tzrecv.at[z], zt, e)

        for zt in others:
            t_z(zt).start()
        for t in plane:
            remote(made_ref.at[0], mg_ref.at[t], msend.at[t], mrecv.at[t], z, e).wait_recv()
        m_own.wait()
        scaled = valid * gates
        expert_out = dot(picks, mg_ref[...].reshape(slots, width))
        y_ref[...] = (mid_ref[...] + scaled * expert_out).astype(bf16)
        outs[1].start()

        for i, (buf, final) in enumerate(((zi, fi_ref), (zo, fo_ref))):
            r_load(i, (ei_ref, eo_ref)[i], pair, 1).wait()
            final[...] = buf[1].astype(f32)

            @pl.when(inner)
            def _():
                for src, part_at in (
                    ((gi_ref, go_ref)[i], 0), ((ei_ref, eo_ref)[i], across[0]), ((ei_ref, eo_ref)[i], across[1])
                ):
                    load = r_load(i, src, part_at, 1)
                    load.start()
                    load.wait()
                    final[...] = final[...] + buf[1].astype(f32)

            @pl.when(jnp.logical_not(inner))
            def _():
                r_load(i, (gi_ref, go_ref)[i], 0, 0).wait()
                final[...] = final[...] + buf[0].astype(f32)

        for _ in range(3):
            advance()
        assert state[out_sum] == 8
        outs[7].start()
        for zs in others:
            remote(sums_ref, szgot.at[zs], tzsend.at[zs], tzrecv.at[zs], z, e).wait_recv()
        for zt in others:
            t_z(zt).wait_send()
        szgot[z] = sums_ref[...]
        tot = szgot[0]
        for j in range(1, blocks):
            tot = tot + szgot[j]
        sums_ref[...] = tot

        advance()
        for i, (got, final) in enumerate(((ci, fi_ref), (co, fo_ref))):

            @pl.when(inner)
            def _():
                r_sum(i).wait_send()

            @pl.when(jnp.logical_not(inner))
            def _():
                r_sum(i).wait_recv()
                r_chain(i).wait_send()
                final[...] = final[...] + got[...].astype(f32)

            outs[2 + i].start()
        while min(state.values()) <= 7:
            advance()
        for out in outs[4:7]:
            out.start()

        for s in range(seqs):
            for k in range(2):

                @pl.when(jnp.logical_not((2 * c + s == z) & (c == k)))
                def _():
                    d_out(s, k).wait_send()

        for j in n_order[:-1]:
            n_out(j).wait_send()

        @pl.when(seq_core != c)
        def _():
            n_out(z).wait_send()

        for j in n_order:
            n_sib(j).wait_send()
        for t in plane:
            m_out(t).wait_send()
        for out in outs:
            out.wait()

    stage = blocks
    scratch = [
        pltpu.VMEM((blocks, span, half), bf16),
        pltpu.VMEM((total, 3 * half), bf16),
        pltpu.VMEM((128, total), bf16),
        pltpu.VMEM((total, 128), f32),
        pltpu.VMEM((total, 128), f32),
        pltpu.VMEM((blocks, 2, hs, width), bf16),
        pltpu.VMEM((blocks, hs, width), bf16),
        pltpu.VMEM((blocks, hs, width), bf16),
        pltpu.VMEM((seqs, 2, hs, width), bf16),
        pltpu.VMEM((2, width, part), bf16),
        pltpu.VMEM((2, part, width), bf16),
        pltpu.VMEM((width, part), bf16),
        pltpu.VMEM((part, width), bf16),
        pltpu.VMEM((width, half), bf16),
        pltpu.VMEM((1 + bits, small_rows, width), f32),
        pltpu.VMEM((blocks, small_rows, width), f32),
        pltpu.VMEM((seqs, 2, span, half), bf16),
        pltpu.VMEM((2, width, half), bf16),
        pltpu.VMEM((tokens, width), f32),
        pltpu.VMEM((columns, capacity, width), bf16),
        DMA((3,)),
        DMA((seqs, 2)),
        DMA((stage,)),
        DMA((2, 2)),
        DMA((2,)),
        DMA((2,)),
        DMA((stage,)),
        DMA((stage,)),
        DMA((stage,)),
        DMA((seqs, 2)),
        DMA,
        DMA,
        DMA((1 + bits,)),
        DMA((1 + bits,)),
        DMA((stage,)),
        DMA((stage,)),
        DMA((columns,)),
        DMA((columns,)),
        pltpu.VMEM((columns, capacity, width), bf16),
        pltpu.VMEM((tokens, width), f32),
        pltpu.VMEM((tokens, width), bf16),
        pltpu.VMEM((tokens, width), bf16),
        pltpu.VMEM((width, width), bf16),
        pltpu.VMEM((seqs, 2, span, half), bf16),
        pltpu.VMEM((total, 3 * half), bf16),
        pltpu.VMEM((half, total), f32),
        pltpu.VMEM((width, total), bf16),
        pltpu.VMEM((width, 3 * half), bf16),
        pltpu.VMEM((seqs, 2, hs, width), bf16),
        DMA((11,)),
        pltpu.VMEM((4, width, width), bf16),
        pltpu.VMEM((width, part), f32),
        pltpu.VMEM((part, width), f32),
        pltpu.VMEM((seqs, 2, hs, width), f32),
        pltpu.VMEM((tokens, width), bf16),
        DMA((8,)),
    ]
    scratch += PieceSum.scratch(blocks, out_piece, half, rest)
    for _ in range(pairs):
        scratch += PieceSum.scratch(blocks, pair_piece, 128, rest)
    grads, sums, f_inner, f_outer, g_hidden, output = pl.pallas_call(
        kernel,
        name="backward",
        out_shape=[
            jax.ShapeDtypeStruct((4, width, width), bf16),
            jax.ShapeDtypeStruct((small_rows, width), f32),
            jax.ShapeDtypeStruct((width, part), f32),
            jax.ShapeDtypeStruct((part, width), f32),
            jax.ShapeDtypeStruct((seqs, 2, hs, width), f32),
            jax.ShapeDtypeStruct((tokens, width), bf16),
        ],
        in_specs=[ANY] * 4 + [VMEM] * 2 + [ANY] * 3 + [VMEM] * 3 + [SMEM] + [ANY] * 2 + [VMEM] * 2 + [ANY] * 2 + [VMEM] * 2
        + [ANY] + [VMEM] + [ANY] * 4,
        out_specs=[ANY, VMEM] + [ANY] * 4,
        scratch_shapes=scratch,
        compiler_params=params(3),
    )(
        rows_t, weights, qkv, att_t, lse, length, attended, middle, flat, gate, slot, ids, lengths, cotangent,
        back, dots, counts, made, hidden.reshape(seqs, 2, hs, width), gain_one,
        gain_two, w_output, w_router, g_inner, g_outer, e_inner, e_outer,
    )
    return finish(grads, sums, f_inner, f_outer, g_hidden.reshape(tokens, width), output, experts_n)


def finish(grads, sums, g_inner, g_outer, g_hidden, output, experts_n):
    steps = 4
    width = grads.shape[2]
    tokens = output.shape[0]
    part = g_inner.shape[1]
    rows = width // steps

    def kernel(g_ref, s_ref, i_ref, o_ref, h_ref, y_ref, *outs):
        for m in range(4):
            outs[m][...] = g_ref[m].astype(f32)
        outs[4][...] = i_ref[...]
        outs[5][...] = o_ref[...]
        outs[6][...] = h_ref[...]
        outs[7][...] = y_ref[...]

        @pl.when(pl.program_id(0) == 0)
        def _():
            for m in range(4):
                outs[8 + m][...] = s_ref[m]
            outs[12][...] = s_ref[4 : 4 + experts_n]
            outs[13][...] = s_ref[4 + experts_n : 5 + experts_n, 0:1]

    def by_rows(shape):
        return pl.BlockSpec((shape[0] // steps,) + shape[1:], lambda i: (i,) + (0,) * (len(shape) - 1))

    def whole(shape):
        return pl.BlockSpec(shape, lambda i: (0,) * len(shape))

    split = [(width, width)] * 4 + [(width, part), (part, width), (tokens, width), (tokens, width)]
    kept = [(width,)] * 4 + [(experts_n, width), (1, 1)]
    return pl.pallas_call(
        kernel,
        name="finish",
        grid=(steps,),
        out_shape=[jax.ShapeDtypeStruct(a, bf16 if n == 7 else f32) for n, a in enumerate(split + kept)],
        in_specs=[pl.BlockSpec((4, rows, width), lambda i: (0, i, 0)), whole(sums.shape)]
        + [by_rows(a) for a in split[4:]],
        out_specs=[by_rows(a) for a in split] + [whole(a) for a in kept],
        compiler_params=pltpu.CompilerParams(dimension_semantics=("arbitrary",), vmem_limit_bytes=VMEM_BYTES),
    )(grads, sums, g_inner, g_outer, g_hidden, output)


def on_device(
    hidden_in,
    cotangent,
    query_weight,
    key_weight,
    value_weight,
    output_weight,
    gain_one,
    shift_one,
    gain_two,
    shift_two,
    w_router,
    w_inner,
    w_outer,
    expert_ids,
    seq_lengths,
):
    seqs, span, width = hidden_in.shape
    tokens = seqs * span
    blocks = lax.axis_size("blk")
    columns = lax.axis_size("ep") // 2
    experts_n = w_router.shape[1]
    capacity = max(2, 2 * tokens // experts_n)
    total = blocks * span
    half = width // 2
    assert seqs * 2 == blocks and experts_n == columns

    ids = expert_ids.reshape(seqs, span)
    lengths = seq_lengths
    router = jnp.transpose(w_router)
    cot = cotangent.reshape(tokens, width)
    (
        rows_t, w_qkv, qkv, att_t, lse, attended, middle, flat, gate, slot, to_rows, scales, cot_rows, length, counts,
        near_inner, near_outer, sib_inner, sib_outer,
    ) = forward(
        hidden_in, cotangent, gain_one, shift_one, gain_two, shift_two, query_weight, key_weight, value_weight,
        output_weight, router, ids, lengths, w_inner[0], w_outer[0], blocks, columns, capacity, experts_n,
    )
    back, dots, made, counts, g_inner, g_outer, e_inner, e_outer = experts(
        to_rows, scales, cot_rows, counts, w_inner[0], w_outer[0], sib_inner, sib_outer, near_inner, near_outer,
        blocks,
    )
    results = backward(
        rows_t, w_qkv, qkv.reshape(total, 3 * half), att_t, lse, length, attended, middle, flat, gate,
        slot, ids, lengths, cot, back, dots, counts, made, hidden_in, gain_one, gain_two, output_weight, router,
        g_inner, g_outer, e_inner, e_outer, experts_n,
    )
    dense, (grad_inner, grad_outer, grad_hidden, output) = results[:4], results[4:8]
    gains, (grad_router, balance) = results[8:12], results[12:]
    return (
        output.reshape(seqs, span, width),
        grad_hidden.reshape(seqs, span, width),
        *dense,
        *gains,
        jnp.transpose(grad_router),
        grad_inner[None],
        grad_outer[None],
        balance[0, 0],
    )


def solution(mesh):
    tokens = P("ep", "blk", None)
    return jax.shard_map(
        on_device,
        mesh=mesh,
        in_specs=(tokens, tokens)
        + (P(),) * 9
        + (P("ep", None, "blk"), P("ep", "blk", None), P("ep", "blk", None, None, None), P("ep")),
        out_specs=(tokens, tokens) + (P(),) * 9 + (P("ep", None, "blk"), P("ep", "blk", None), P()),
        check_vma=False,
    )
```
